32 devices in a mesh: grp: 8 (over y, x, core), rep: 4 (over z).
Axes of the slice: x: 2, y: 2, z: 4, core: 2. Of those that a mesh axis runs over, the one named last changes fastest.
Arguments:
- inputs: bfloat16 [32, 384, 1536], P(('grp', 'rep')), may hold values from -6 to 6
- conditioning: bfloat16 [32, 130, 768], P(('grp', 'rep')), may hold values from -6 to 6
- positions: int32 [32, 384], P(('grp', 'rep')), may hold values from 0 to 2047, as said below
- slot_valid: int32 [32], P(('grp', 'rep')), may hold values from 0 to 1, as said below
- cotangent: bfloat16 [32, 384, 1536], P(('grp', 'rep')), may hold values from -6 to 6
- norm1_gain: bfloat16 [1536], P('grp'), may hold values from 0.5 to 1.5
- norm1_shift: bfloat16 [1536], P('grp'), may hold values from -1.75 to 1.75
- norm2_gain: bfloat16 [1536], P('grp'), may hold values from 0.5 to 1.5
- norm2_shift: bfloat16 [1536], P('grp'), may hold values from -1.75 to 1.75
- norm3_gain: bfloat16 [1536], P('grp'), may hold values from 0.5 to 1.5
- norm3_shift: bfloat16 [1536], P('grp'), may hold values from -1.75 to 1.75
- w_qkv: bfloat16 [4608, 1536], P('grp'), may hold values from -0.15625 to 0.15625
- w_out: bfloat16 [1536, 1536], P('grp'), may hold values from -1.25 to 1.25
- w_query2: bfloat16 [1536, 1536], P('grp'), may hold values from -0.15625 to 0.15625
- w_kv2: bfloat16 [3072, 768], P('grp'), may hold values from -0.21875 to 0.21875
- w_out2: bfloat16 [1536, 1536], P('grp'), may hold values from -0.875 to 0.875
- w_gate: bfloat16 [6144, 1536], P('grp'), may hold values from -0.15625 to 0.15625
- w_up: bfloat16 [6144, 1536], P('grp'), may hold values from -0.15625 to 0.15625
- w_down: bfloat16 [6144, 1536], P('grp'), may hold values from -0.15625 to 0.15625
Outputs:
- outputs: bfloat16 [32, 384, 1536], P(('grp', 'rep'))
- d_inputs: float32 [32, 384, 1536], P(('grp', 'rep'))
- grad_norm1_gain: float32 [1536], P('grp')
- grad_norm1_shift: float32 [1536], P('grp')
- grad_norm2_gain: float32 [1536], P('grp')
- grad_norm2_shift: float32 [1536], P('grp')
- grad_norm3_gain: float32 [1536], P('grp')
- grad_norm3_shift: float32 [1536], P('grp')
- grad_w_qkv: float32 [4608, 1536], P('grp')
- grad_w_out: float32 [1536, 1536], P('grp')
- grad_w_query2: float32 [1536, 1536], P('grp')
- grad_w_kv2: float32 [3072, 768], P('grp')
- grad_w_out2: float32 [1536, 1536], P('grp')
- grad_w_gate: float32 [6144, 1536], P('grp')
- grad_w_up: float32 [6144, 1536], P('grp')
- grad_w_down: float32 [6144, 1536], P('grp')
The draws below stay inside these ranges and needn't reach their ends.
Inputs may be any that keep to these rules, and one draw needn't show every extreme that they name: Within a slot, positions rise by 1 or 2 from one token to the next; some slot starts at 0 and some slot ends at 2047. `slot_valid`: exactly 11 slots hold 1.
All inputs are finite; a program needn't handle non-finite values.
Results may differ from the reference program's by a relative error of at most 0.025.
Values may be sent and summed in bfloat16 or wider, within the bound.
A program may use at most 384 MiB of HBM per device.

```python
import math
import jax
import jax.numpy as jnp
from jax import lax

D = 1536
HEADS = 24
HD = 64
FF = 6144
CD = 768
NC = 130
L = 384
MAX_POS = 2048
SLOTS = 32
FILLED = 11


def draw_positions(key, part):
    increments = jax.random.randint(jax.random.fold_in(key, 13), (SLOTS, L), 1, 3).astype(jnp.int32)
    increments = increments.at[:, 0].set(0)
    offsets = jnp.cumsum(increments, axis=1).astype(jnp.int32)
    room = (MAX_POS - 1 - offsets[:, L - 1]).astype(jnp.int32)
    raw = jax.random.randint(jax.random.fold_in(key, 11), (SLOTS,), 0, MAX_POS).astype(jnp.int32)
    starts = (raw % (room + 1)).astype(jnp.int32)
    chosen = jax.random.permutation(jax.random.fold_in(key, 12), SLOTS)
    starts = starts.at[chosen[0]].set(0)
    starts = starts.at[chosen[1]].set(room[chosen[1]])
    return (starts[:, None] + offsets).astype(jnp.int32)


def draw_slot_valid(key, part):
    order = jax.random.permutation(jax.random.fold_in(key, 21), SLOTS)
    return (order < FILLED).astype(jnp.int32)


def block_scale(stream_key, dims, cuts, least, largest):
    factor_of = 1.0
    for axis_at, blocks in cuts:
        heights = jax.random.uniform(jax.random.fold_in(jax.random.fold_in(stream_key, 6), axis_at), (blocks,), jnp.float32, least / len(cuts), largest / len(cuts))
        factor_of = factor_of * jnp.repeat(jnp.exp(heights), dims[axis_at] // blocks).reshape((-1,) + (1,) * (len(dims) - 1 - axis_at))
    return factor_of


def bell_draw(key, extent, scale, reach, shards=(), kind=jnp.bfloat16):
    loudness = block_scale(key, extent, shards, -0.22, 0.18) if shards else 1.0
    drawn = jax.random.normal(key, extent, jnp.float32) * scale * loudness
    return jnp.minimum(jnp.maximum(drawn, -reach), reach).astype(kind)


def setup_inputs(seed: int = 0) -> dict:
    splits = jax.random.split(jax.random.key(seed), 20)
    inputs = bell_draw(splits[0], (SLOTS, L, D), 1.0, 6.0, ((0, 32),))
    conditioning = bell_draw(splits[1], (SLOTS, NC, CD), 1.0, 6.0, ((0, 32),))
    positions = draw_positions(jax.random.fold_in(splits[19], 71), 0)
    slot_valid = draw_slot_valid(jax.random.fold_in(splits[19], 71), 0)
    cotangent = bell_draw(splits[4], (SLOTS, L, D), 1.0, 6.0, ((0, 32),))
    norm1_gain = jnp.clip(1.0 + 0.1 * jax.random.normal(splits[5], (D,), jnp.float32), 0.5, 1.5).astype(jnp.bfloat16)
    norm1_shift = bell_draw(splits[6], (D,), 0.3, 1.75, ((0, 8),))
    norm2_gain = jnp.clip(1.0 + 0.1 * jax.random.normal(splits[7], (D,), jnp.float32), 0.5, 1.5).astype(jnp.bfloat16)
    norm2_shift = bell_draw(splits[8], (D,), 0.3, 1.75, ((0, 8),))
    norm3_gain = jnp.clip(1.0 + 0.1 * jax.random.normal(splits[9], (D,), jnp.float32), 0.5, 1.5).astype(jnp.bfloat16)
    norm3_shift = bell_draw(splits[10], (D,), 0.3, 1.75, ((0, 8),))
    w_qkv = bell_draw(splits[11], (3 * D, D), D ** -0.5, 0.15625, ((0, 8),))
    w_out = bell_draw(splits[12], (D, D), (D // 64) ** -0.5, 1.25, ((0, 8),))
    w_query2 = bell_draw(splits[13], (D, D), D ** -0.5, 0.15625, ((0, 8),))
    w_kv2 = bell_draw(splits[14], (2 * D, CD), CD ** -0.5, 0.21875, ((0, 8),))
    w_out2 = bell_draw(splits[15], (D, D), (D // 32) ** -0.5, 0.875, ((0, 8),))
    w_gate = bell_draw(splits[16], (FF, D), D ** -0.5, 0.15625, ((0, 8),))
    w_up = bell_draw(splits[17], (FF, D), D ** -0.5, 0.15625, ((0, 8),))
    w_down = bell_draw(splits[18], (FF, D), (FF // 4) ** -0.5, 0.15625, ((0, 8),))
    return {"inputs": inputs, "conditioning": conditioning, "positions": positions, "slot_valid": slot_valid, "cotangent": cotangent, "norm1_gain": norm1_gain, "norm1_shift": norm1_shift, "norm2_gain": norm2_gain, "norm2_shift": norm2_shift, "norm3_gain": norm3_gain, "norm3_shift": norm3_shift, "w_qkv": w_qkv, "w_out": w_out, "w_query2": w_query2, "w_kv2": w_kv2, "w_out2": w_out2, "w_gate": w_gate, "w_up": w_up, "w_down": w_down}


@jax.custom_vjp
def low(v):
    return lax.optimization_barrier(v.astype(jnp.bfloat16)).astype(jnp.float32)

@jax.custom_vjp
def low_back(v):
    return v

def low_keep(v):
    return (low(v), None)

def low_pass(kept, grad):
    return (grad,)

def back_keep(v):
    return (v, None)

def back_low(kept, grad):
    return (low(grad),)
low.defvjp(low_keep, low_pass)
low_back.defvjp(back_keep, back_low)

def matmul(left_side, right_side):
    return jnp.dot(left_side, right_side, precision=lax.Precision.HIGHEST, preferred_element_type=jnp.float32)

def layer_norm(tensor, gain, shift):
    center = tensor - lax.optimization_barrier(jnp.mean(tensor, axis=-1, keepdims=True))
    spread = lax.optimization_barrier(jnp.mean(center * center, axis=-1, keepdims=True))
    return center * lax.rsqrt(spread + 1e-05) * gain + shift

def angles(positions):
    quarter = HD // 4
    frequency = jnp.exp(jnp.arange(quarter, dtype=jnp.float32) * (-math.log(10000.0) / quarter))
    turned = positions.astype(jnp.float32)[:, None] * frequency[None, :]
    return (jnp.cos(turned)[:, None, :], jnp.sin(turned)[:, None, :])

def rotate(tensor, cosine, sin_table):
    quarter = tensor.shape[-1] // 4
    first_half = tensor[..., :quarter]
    second_half = tensor[..., quarter:2 * quarter]
    remainder = tensor[..., 2 * quarter:]
    return jnp.concatenate([first_half * cosine - second_half * sin_table, first_half * sin_table + second_half * cosine, remainder], axis=-1)

def attention(queries, key_heads, value_heads):
    scores = low_back(0.125 * jnp.einsum('qhd,khd->hqk', queries, key_heads, precision=lax.Precision.HIGHEST))
    probability = jax.nn.softmax(scores, axis=-1)
    return jnp.einsum('hqk,khd->qhd', low(probability), value_heads, precision=lax.Precision.HIGHEST)

def sequence(params, tokens, conditioning, positions):
    gain_one, shift_one, gain_two, shift_two, gain_three, shift_three, w_qkv, w_out, w_query2, w_kv2, w_out2, w_gate, w_up, w_down = params
    seq_len = tokens.shape[0]
    cosine, sin_table = angles(positions)
    act_one = low(layer_norm(tokens, gain_one, shift_one))
    qkv_rows = low_back(matmul(act_one, w_qkv.T))
    queries = low(rotate(qkv_rows[:, :D].reshape(seq_len, HEADS, HD), cosine, sin_table))
    key_heads = low(rotate(qkv_rows[:, D:2 * D].reshape(seq_len, HEADS, HD), cosine, sin_table))
    value_heads = low(qkv_rows[:, 2 * D:].reshape(seq_len, HEADS, HD))
    attended = low(low_back(attention(queries, key_heads, value_heads))).reshape(seq_len, D)
    section_one = tokens + low_back(matmul(attended, w_out.T))
    act_two = low(layer_norm(section_one, gain_two, shift_two))
    query_two = low(low_back(matmul(act_two, w_query2.T))).reshape(seq_len, HEADS, HD)
    kv_two = low(low_back(matmul(conditioning, w_kv2.T)))
    key_two = kv_two[:, :D].reshape(NC, HEADS, HD)
    value_two = kv_two[:, D:].reshape(NC, HEADS, HD)
    attended_two = low(low_back(attention(query_two, key_two, value_two))).reshape(seq_len, D)
    section_two = section_one + low_back(matmul(attended_two, w_out2.T))
    act_three = low(layer_norm(section_two, gain_three, shift_three))
    gate_pre = low_back(matmul(act_three, w_gate.T))
    up_pre = low_back(matmul(act_three, w_up.T))
    hidden = low(jax.nn.silu(gate_pre) * up_pre)
    return section_two + low_back(matmul(hidden, w_down))

def reference(inputs, conditioning, positions, slot_valid, cotangent, norm1_gain, norm1_shift, norm2_gain, norm2_shift, norm3_gain, norm3_shift, w_qkv, w_out, w_query2, w_kv2, w_out2, w_gate, w_up, w_down):
    params = tuple((weight_item.astype(jnp.float32) for weight_item in (norm1_gain, norm1_shift, norm2_gain, norm2_shift, norm3_gain, norm3_shift, w_qkv, w_out, w_query2, w_kv2, w_out2, w_gate, w_up, w_down)))
    tokens = inputs.astype(jnp.float32)
    cond_all = conditioning.astype(jnp.float32)

    def forward(params_in, tokens_in):

        def per_sequence(sample):
            return sequence(params_in, sample[0], sample[1], sample[2])
        return lax.map(jax.checkpoint(per_sequence), (tokens_in, cond_all, positions))
    outputs, pullback = jax.vjp(forward, params, tokens)
    weighted = cotangent.astype(jnp.float32) * slot_valid.astype(jnp.float32)[:, None, None]
    param_grads, d_inputs = pullback(weighted)
    return (outputs.astype(jnp.bfloat16), d_inputs, param_grads[0], param_grads[1], param_grads[2], param_grads[3], param_grads[4], param_grads[5], param_grads[6], param_grads[7], param_grads[8], param_grads[9], param_grads[10], param_grads[11], param_grads[12], param_grads[13])
```

```python
import functools
import math

import jax
import jax.numpy as jnp
from jax import lax
from jax.experimental import pallas as pl
from jax.experimental.pallas import tpu as pltpu
from jax.sharding import PartitionSpec as P

MESH = pl.DeviceIdType.MESH

D = 1536
HEADS = 24
HD = 64
NC = 130


epsilon = 1e-05
score_scale = 0.125


def layer_norm(tensor, gain, shift):
    center = tensor - jnp.mean(tensor, axis=-1, keepdims=True)
    spread = jnp.mean(center * center, axis=-1, keepdims=True)
    return center * lax.rsqrt(spread + epsilon) * gain + shift


def norm_back(tensor, gain, shift, d_normed):
    _, pullback = jax.vjp(layer_norm, tensor, gain, shift)
    return pullback(d_normed)


def swiglu(gate_part, up_part):
    return jax.nn.silu(gate_part) * up_part


def swiglu_back(gate_part, up_part, d_hidden):
    _, pullback = jax.vjp(swiglu, gate_part, up_part)
    return pullback(d_hidden)


def angles(positions, head_size):
    quarter = head_size // 4
    frequency = jnp.exp(jnp.arange(quarter, dtype=jnp.float32) * (-math.log(10000.0) / quarter))
    turned = positions.astype(jnp.float32)[:, None] * frequency[None, :]
    return (jnp.cos(turned)[:, None, :], jnp.sin(turned)[:, None, :])


def rotate(tensor, cosine, sin_table):
    quarter = tensor.shape[-1] // 4
    first_half = tensor[..., :quarter]
    second_half = tensor[..., quarter : 2 * quarter]
    remainder = tensor[..., 2 * quarter :]
    return jnp.concatenate(
        [
            first_half * cosine - second_half * sin_table,
            first_half * sin_table + second_half * cosine,
            remainder,
        ],
        axis=-1,
    )


def dot_nt(left_side, right_side):
    return lax.dot_general(
        left_side, right_side, (((1,), (1,)), ((), ())), preferred_element_type=jnp.float32
    )


def dot_tn(left_side, right_side):
    return lax.dot_general(
        left_side, right_side, (((0,), (0,)), ((), ())), preferred_element_type=jnp.float32
    )


def dot(left_side, right_side):
    return jnp.dot(left_side, right_side, preferred_element_type=jnp.float32)


def part_grad(grad_cols, activation):
    return dot_tn(grad_cols, activation).astype(jnp.bfloat16)


def attend(queries, key_heads, value_heads):
    seq_len = queries.shape[0]
    span = min(seq_len, 512)
    blocked = queries.reshape(seq_len // span, span, queries.shape[1], queries.shape[2])

    def one_block(query_block):
        scores = (
            jnp.einsum("qhd,khd->hqk", query_block, key_heads, preferred_element_type=jnp.float32)
            * score_scale
        )
        largest = jnp.max(scores, axis=-1, keepdims=True)
        shifted = jnp.exp(scores - largest)
        totals = jnp.sum(shifted, axis=-1, keepdims=True)
        probability = (shifted / totals).astype(jnp.bfloat16)
        result = jnp.einsum(
            "hqk,khd->qhd", probability, value_heads, preferred_element_type=jnp.float32
        )
        return (result.astype(jnp.bfloat16), (largest + jnp.log(totals))[..., 0])

    outcome, log_sums = lax.map(one_block, blocked)
    return (outcome.reshape(queries.shape), log_sums)


def attend_back(queries, key_heads, value_heads, log_sums, grad_heads):
    seq_len = queries.shape[0]
    span = min(seq_len, 512)
    block_count = seq_len // span
    query_blocks = queries.reshape(block_count, span, queries.shape[1], queries.shape[2])
    grad_blocks = grad_heads.reshape(block_count, span, queries.shape[1], queries.shape[2])

    def one_block(carried, inputs_block):
        query_block, log_block, grad_block = inputs_block
        scores = (
            jnp.einsum("qhd,khd->hqk", query_block, key_heads, preferred_element_type=jnp.float32)
            * score_scale
        )
        probability = jnp.exp(scores - log_block[..., None])
        d_prob = jnp.einsum(
            "qhd,khd->hqk", grad_block, value_heads, preferred_element_type=jnp.float32
        )
        inner = jnp.sum(probability * d_prob, axis=-1, keepdims=True)
        d_scores = (probability * (d_prob - inner)).astype(jnp.bfloat16)
        d_query = (
            jnp.einsum("hqk,khd->qhd", d_scores, key_heads, preferred_element_type=jnp.float32)
            * score_scale
        )
        d_key = (
            carried[0]
            + jnp.einsum("hqk,qhd->khd", d_scores, query_block, preferred_element_type=jnp.float32)
            * score_scale
        )
        d_value = carried[1] + jnp.einsum(
            "hqk,qhd->khd",
            probability.astype(jnp.bfloat16),
            grad_block,
            preferred_element_type=jnp.float32,
        )
        return ((d_key, d_value), d_query)

    start_zero = jnp.zeros(key_heads.shape, jnp.float32)
    (d_key, d_value), d_query = lax.scan(
        one_block, (start_zero, start_zero), (query_blocks, log_sums, grad_blocks)
    )
    return (d_query.reshape(queries.shape), d_key, d_value)


def meet(peers, lower=None, upper=None, rep_index=None):
    barrier = pltpu.get_barrier_semaphore()
    for peer in peers:
        pl.semaphore_signal(barrier, inc=1, device_id=peer, device_id_type=MESH)
    if lower is not None:

        @pl.when(rep_index > 0)
        def _():
            pl.semaphore_signal(barrier, inc=1, device_id=lower, device_id_type=MESH)

        @pl.when(rep_index < 3)
        def _():
            pl.semaphore_signal(barrier, inc=1, device_id=upper, device_id_type=MESH)

    expected = len(peers)
    if lower is not None:
        expected = expected + jnp.where(rep_index > 0, 1, 0) + jnp.where(rep_index < 3, 1, 0)
    pl.semaphore_wait(barrier, expected)


GATHER_WINDOW = 4


def gather_kernel(pieces, *refs):
    count = len(pieces)
    sources = refs[:count]
    fulls = refs[count : 2 * count]
    send_sem, recv_sem, local_sem = refs[2 * count :]
    me = lax.axis_index("grp")
    plane = lax.axis_index("rep")
    odd = lax.rem(plane, 2)
    first_bit = 2 + 2 * odd
    second_bit = 6 - first_bit
    first = me ^ first_bit
    second = me ^ second_bit
    across = me ^ 6
    first_dev = (first, plane)
    second_dev = (second, plane)
    rep_dev = (me, plane ^ 1)
    mate_dev = (me ^ 1, plane)
    meet([first_dev, second_dev, rep_dev, mate_dev])
    total = sum(n for n, _ in pieces)

    def each(i, body):
        base = 0
        for k, (n, rows) in enumerate(pieces):
            if n == 1:

                @pl.when(i == base)
                def _(k=k, rows=rows):
                    body(k, pl.ds(0, rows))

            else:

                @pl.when((i >= base) & (i < base + n))
                def _(k=k, rows=rows, base=base):
                    body(k, pl.ds(pl.multiple_of((i - base) * rows, 16), rows))

            base += n

    def push(k, cut, i, owner, lane, device, own=False):
        src = sources[k].at[cut] if own else fulls[k].at[owner, cut]
        return pltpu.make_async_remote_copy(
            src_ref=src,
            dst_ref=fulls[k].at[owner, cut],
            send_sem=send_sem.at[lane, i],
            recv_sem=recv_sem.at[lane, i],
            device_id=device,
            device_id_type=MESH,
        )

    def stage_own(i):
        def body(k, cut):
            push(k, cut, i, me, 0, first_dev, own=True).start()
            push(k, cut, i, me, 3, mate_dev, own=True).start()
            pltpu.make_async_copy(sources[k].at[cut], fulls[k].at[me, cut], local_sem.at[i]).start()

        each(i, body)

    def stage_first(i):
        def body(k, cut):
            push(k, cut, i, first, 0, first_dev).wait_recv()
            push(k, cut, i, first, 1, second_dev).start()
            push(k, cut, i, first, 2, rep_dev).start()
            push(k, cut, i, first, 4, mate_dev).start()

        each(i, body)

    def stage_rest(i):
        def body(k, cut):
            push(k, cut, i, across, 1, second_dev).wait_recv()
            push(k, cut, i, across, 5, mate_dev).start()
            push(k, cut, i, second, 2, rep_dev).wait_recv()
            push(k, cut, i, second, 6, mate_dev).start()

        each(i, body)

    def stage_end(i):
        def body(k, cut):
            pltpu.make_async_copy(
                sources[k].at[cut], fulls[k].at[me, cut], local_sem.at[i]
            ).wait()
            push(k, cut, i, me, 0, first_dev, own=True).wait_send()
            push(k, cut, i, first, 1, second_dev).wait_send()
            push(k, cut, i, first, 2, rep_dev).wait_send()
            push(k, cut, i, me, 3, mate_dev, own=True).wait()
            push(k, cut, i, first, 4, mate_dev).wait()
            push(k, cut, i, across, 5, mate_dev).wait()
            push(k, cut, i, second, 6, mate_dev).wait()

        each(i, body)

    def step(t, carry):
        for stage, lag in ((stage_own, 0), (stage_first, GATHER_WINDOW), (stage_rest, GATHER_WINDOW + 2)):
            i = t - lag

            @pl.when((i >= 0) & (i < total))
            def _(stage=stage, i=i):
                stage(i)

        return carry

    lax.fori_loop(0, total + GATHER_WINDOW + 2, step, 0)

    def finish(i, carry):
        stage_end(i)
        return carry

    lax.fori_loop(0, total, finish, 0)


def gather_all(arrays, rows):
    groups = lax.axis_size("grp")
    if groups != 8 or lax.axis_size("rep") % 2 != 0:
        return [lax.all_gather(a, "grp", axis=0) for a in arrays]
    pieces = tuple((a.shape[0] // n, n) for a, n in zip(arrays, rows))
    total = sum(n for n, _ in pieces)
    hbm = pl.BlockSpec(memory_space=pltpu.HBM)
    return pl.pallas_call(
        functools.partial(gather_kernel, pieces),
        out_shape=[jax.ShapeDtypeStruct((groups,) + a.shape, a.dtype) for a in arrays],
        in_specs=[hbm] * len(arrays),
        out_specs=[hbm] * len(arrays),
        scratch_shapes=[
            pltpu.SemaphoreType.DMA((7, total)),
            pltpu.SemaphoreType.DMA((7, total)),
            pltpu.SemaphoreType.DMA((total,)),
        ],
        compiler_params=pltpu.CompilerParams(collective_id=0, has_side_effects=True),
    )(*arrays)


CUT = 48
FCUT = 96
MATE_SLOTS = 6
OWN_SLOTS = 3
SUM_SLOTS = 8
FFN_SLOTS = 12


def reduce_kernel(pieces, ffn_count, *refs):
    count = len(pieces)
    parts = refs[:count]
    ffn = refs[count : count + 3]
    out_a, out_f = refs[count + 3 : count + 5]
    (
        mate_buf,
        own_buf,
        sums,
        one_buf,
        two_buf,
        done,
        ffn_buf,
        low_a,
        up_a,
        low_f,
        up_f,
        mate_send,
        mate_recv,
        own_sem,
        one_send,
        one_recv,
        two_send,
        two_recv,
        ffn_sem,
        chain_send,
        chain_recv,
        out_sem,
        credit,
    ) = refs[count + 5 :]
    me = lax.axis_index("grp")
    plane = lax.axis_index("rep")
    core = lax.rem(me, 2)
    x = lax.rem(me // 2, 2)
    y = me // 4
    mate_dev = (me ^ 1, plane)
    x_dev = (me ^ 2, plane)
    y_dev = (me ^ 4, plane)
    low_dev = (me, plane - 1)
    up_dev = (me, plane + 1)
    meet([mate_dev, x_dev, y_dev], low_dev, up_dev, plane)
    total = sum(pieces)
    chain_total = ffn_count + total

    def each(i, body):
        base = 0
        for k, n in enumerate(pieces):

            @pl.when((i >= base) & (i < base + n))
            def _(k=k, base=base):
                body(k, pl.ds(pl.multiple_of((i - base) * CUT, 16), CUT))

            base += n

    def mate_copy(k, cut, slot):
        return pltpu.make_async_remote_copy(
            src_ref=parts[k].at[:, :, 1 - core, cut],
            dst_ref=mate_buf.at[slot],
            send_sem=mate_send.at[slot],
            recv_sem=mate_recv.at[slot],
            device_id=mate_dev,
            device_id_type=MESH,
        )

    def own_copy(k, cut, slot):
        return pltpu.make_async_copy(
            parts[k].at[:, :, core, cut], own_buf.at[slot], own_sem.at[slot]
        )

    def load(i):
        @pl.when(i >= MATE_SLOTS)
        def _():
            pl.semaphore_wait(credit, 1)
            mate_copy(0, pl.ds(0, CUT), lax.rem(i, MATE_SLOTS)).wait_send()

        def body(k, cut):
            mate_copy(k, cut, lax.rem(i, MATE_SLOTS)).start()
            own_copy(k, cut, lax.rem(i, OWN_SLOTS)).start()

        each(i, body)

    def one_copy(i, slot, by_x):
        return pltpu.make_async_remote_copy(
            src_ref=sums.at[slot, :, 1 - x] if by_x else sums.at[slot, 1 - y],
            dst_ref=one_buf.at[i],
            send_sem=one_send.at[slot],
            recv_sem=one_recv.at[i],
            device_id=x_dev if by_x else y_dev,
            device_id_type=MESH,
        )

    def two_copy(i, slot, by_x):
        return pltpu.make_async_remote_copy(
            src_ref=sums.at[slot, 1 - y, x] if by_x else sums.at[slot, y, 1 - x],
            dst_ref=two_buf.at[i],
            send_sem=two_send.at[slot],
            recv_sem=two_recv.at[i],
            device_id=y_dev if by_x else x_dev,
            device_id_type=MESH,
        )

    def either(i, body):
        @pl.when(lax.rem(i, 2) == 0)
        def _():
            body(True)

        @pl.when(lax.rem(i, 2) == 1)
        def _():
            body(False)

    def add(a, b):
        return (a.astype(jnp.float32) + b.astype(jnp.float32)).astype(jnp.bfloat16)

    def pair(i):
        mate_slot, own_slot, slot = (
            lax.rem(i, MATE_SLOTS),
            lax.rem(i, OWN_SLOTS),
            lax.rem(i, SUM_SLOTS),
        )
        mate_copy(0, pl.ds(0, CUT), mate_slot).wait_recv()
        own_copy(0, pl.ds(0, CUT), own_slot).wait()
        for u in range(2):
            for v in range(2):
                sums[slot, u, v] = add(own_buf[own_slot, u, v], mate_buf[mate_slot, u, v])

        @pl.when(i + MATE_SLOTS < total)
        def _():
            pl.semaphore_signal(credit, inc=1, device_id=mate_dev, device_id_type=MESH)

        either(i, lambda by_x: one_copy(i, slot, by_x).start())

    def plane_one(i):
        slot = lax.rem(i, SUM_SLOTS)

        def body(by_x):
            one_copy(i, slot, by_x).wait_recv()
            for u in range(2):
                if by_x:
                    sums[slot, u, x] = add(sums[slot, u, x], one_buf[i, u])
                else:
                    sums[slot, y, u] = add(sums[slot, y, u], one_buf[i, u])
            two_copy(i, slot, by_x).start()

        either(i, body)

    def plane_two(i):
        slot = lax.rem(i, SUM_SLOTS)

        def body(by_x):
            two_copy(i, slot, by_x).wait_recv()
            done[i] = add(sums[slot, y, x], two_buf[i])
            one_copy(i, slot, by_x).wait_send()
            two_copy(i, slot, by_x).wait_send()

        either(i, body)

    def ffn_load(j):
        for k in range(3):

            @pl.when(j // (ffn_count // 3) == k)
            def _(k=k):
                row = pl.multiple_of((j - k * (ffn_count // 3)) * FCUT, 16)
                pltpu.make_async_copy(
                    ffn[k].at[pl.ds(row, FCUT)],
                    ffn_buf.at[lax.rem(j, FFN_SLOTS)],
                    ffn_sem.at[lax.rem(j, FFN_SLOTS)],
                ).start()

    def ffn_wait(j):
        pltpu.make_async_copy(
            ffn[0].at[pl.ds(0, FCUT)],
            ffn_buf.at[lax.rem(j, FFN_SLOTS)],
            ffn_sem.at[lax.rem(j, FFN_SLOTS)],
        ).wait()

    def views(j, is_ffn):
        if is_ffn:
            rows = pl.ds(pl.multiple_of(j * FCUT, 16), FCUT)
            return ffn_buf.at[lax.rem(j, FFN_SLOTS)], low_f.at[j], up_f.at[j], out_f.at[rows]
        i = j - ffn_count
        rows = pl.ds(pl.multiple_of(i * CUT, 16), CUT)
        return done.at[i], low_a.at[i], up_a.at[i], out_a.at[rows]

    def chain(j, lane, src, dst, device):
        return pltpu.make_async_remote_copy(
            src_ref=src,
            dst_ref=dst,
            send_sem=chain_send.at[lane, j],
            recv_sem=chain_recv.at[lane, j],
            device_id=device,
            device_id_type=MESH,
        )

    def kinds(j, body):
        @pl.when(j < ffn_count)
        def _():
            body(*views(j, True))

        @pl.when(j >= ffn_count)
        def _():
            body(*views(j, False))

    def inward(j):
        @pl.when(j < ffn_count)
        def _():
            ffn_wait(j)

        def body(mine, low, up, out):
            @pl.when(plane == 0)
            def _():
                chain(j, 0, mine, low, up_dev).start()

            @pl.when(plane == 3)
            def _():
                chain(j, 1, mine, up, low_dev).start()

        kinds(j, body)

    def middle(j):
        def body(mine, low, up, out):
            @pl.when(plane == 2)
            def _():
                chain(j, 1, mine, up, low_dev).wait_recv()
                mine[...] = add(mine[...], up[...])
                chain(j, 1, mine, up, low_dev).start()

        kinds(j, body)

    def root(j):
        def body(mine, low, up, out):
            @pl.when(plane == 1)
            def _():
                chain(j, 0, mine, low, up_dev).wait_recv()
                chain(j, 1, mine, up, low_dev).wait_recv()
                mine[...] = (
                    mine[...].astype(jnp.float32)
                    + low[...].astype(jnp.float32)
                    + up[...].astype(jnp.float32)
                ).astype(jnp.bfloat16)
                chain(j, 0, mine, out, up_dev).start()
                chain(j, 1, mine, out, low_dev).start()
                pltpu.make_async_copy(mine, out, out_sem.at[j]).start()

        kinds(j, body)

    def outward(j):
        def body(mine, low, up, out):
            @pl.when(plane == 2)
            def _():
                chain(j, 0, mine, out, up_dev).wait_recv()
                chain(j, 0, out, out, up_dev).start()

        kinds(j, body)

    def drain(j):
        def body(mine, low, up, out):
            @pl.when(plane == 0)
            def _():
                chain(j, 0, mine, low, up_dev).wait_send()
                chain(j, 1, mine, out, low_dev).wait_recv()

            @pl.when(plane == 3)
            def _():
                chain(j, 1, mine, up, low_dev).wait_send()
                chain(j, 0, mine, out, up_dev).wait_recv()

            @pl.when(plane == 1)
            def _():
                chain(j, 0, mine, out, up_dev).wait_send()
                chain(j, 1, mine, out, low_dev).wait_send()
                pltpu.make_async_copy(mine, out, out_sem.at[j]).wait()

            @pl.when(plane == 2)
            def _():
                chain(j, 1, mine, up, low_dev).wait_send()
                chain(j, 0, out, out, up_dev).wait_send()

        kinds(j, body)

    stages = (
        (load, 0, total),
        (ffn_load, 0, ffn_count),
        (inward, 1, chain_total),
        (pair, 1, total),
        (plane_one, 3, total),
        (middle, 3, chain_total),
        (plane_two, 5, total),
        (root, 5, chain_total),
        (outward, 7, chain_total),
        (drain, 9, chain_total),
    )

    def step(t, carry):
        for stage, lag, limit in stages:
            i = t - lag

            @pl.when((i >= 0) & (i < limit))
            def _(stage=stage, i=i):
                stage(i)

        return carry

    lax.fori_loop(0, chain_total + 9, step, 0)
    for i in range(max(total - MATE_SLOTS, 0), total):
        mate_copy(0, pl.ds(0, CUT), i % MATE_SLOTS).wait_send()


def reduce_all(parts, ffn):
    pieces = tuple(p.shape[3] // CUT for p in parts)
    total = sum(pieces)
    wide = parts[0].shape[-1]
    ffn_rows = sum(f.shape[0] for f in ffn)
    ffn_count = ffn_rows // FCUT
    chain_total = total + ffn_count
    hbm = pl.BlockSpec(memory_space=pltpu.HBM)
    low = jnp.bfloat16
    dma = pltpu.SemaphoreType.DMA
    return pl.pallas_call(
        functools.partial(reduce_kernel, pieces, ffn_count),
        out_shape=[
            jax.ShapeDtypeStruct((total * CUT, wide), low),
            jax.ShapeDtypeStruct((ffn_rows, wide), low),
        ],
        in_specs=[hbm] * (len(parts) + 3),
        out_specs=[hbm] * 2,
        scratch_shapes=[
            pltpu.VMEM((MATE_SLOTS, 2, 2, CUT, wide), low),
            pltpu.VMEM((OWN_SLOTS, 2, 2, CUT, wide), low),
            pltpu.VMEM((SUM_SLOTS, 2, 2, CUT, wide), low),
            pltpu.VMEM((total, 2, CUT, wide), low),
            pltpu.VMEM((total, CUT, wide), low),
            pltpu.VMEM((total, CUT, wide), low),
            pltpu.VMEM((FFN_SLOTS, FCUT, wide), low),
            pltpu.VMEM((total, CUT, wide), low),
            pltpu.VMEM((total, CUT, wide), low),
            pltpu.VMEM((ffn_count, FCUT, wide), low),
            pltpu.VMEM((ffn_count, FCUT, wide), low),
            dma((MATE_SLOTS,)),
            dma((MATE_SLOTS,)),
            dma((OWN_SLOTS,)),
            dma((SUM_SLOTS,)),
            dma((total,)),
            dma((SUM_SLOTS,)),
            dma((total,)),
            dma((FFN_SLOTS,)),
            dma((2, chain_total)),
            dma((2, chain_total)),
            dma((chain_total,)),
            pltpu.SemaphoreType.REGULAR,
        ],
        compiler_params=pltpu.CompilerParams(
            collective_id=1, has_side_effects=True, vmem_limit_bytes=60 * 1024 * 1024
        ),
    )(*parts, *ffn)


def per_device(
    inputs,
    conditioning,
    positions,
    slot_valid,
    cotangent,
    norm1_gain,
    norm1_shift,
    norm2_gain,
    norm2_shift,
    norm3_gain,
    norm3_shift,
    w_qkv,
    w_out,
    w_query2,
    w_kv2,
    w_out2,
    w_gate,
    w_up,
    w_down,
):
    tokens = inputs[0].astype(jnp.float32)
    seq_len = tokens.shape[0]
    cond_rows = conditioning[0]
    norms = jnp.stack(
        [norm1_gain, norm1_shift, norm2_gain, norm2_shift, norm3_gain, norm3_shift], axis=0
    )
    own_width = norms.shape[1]
    norms = jnp.pad(norms, ((0, 10), (0, -own_width % 128)))
    norms, full_qkv, full_out, full_kv2, full_query2, full_out2 = gather_all(
        [norms, w_qkv, w_out, w_kv2, w_query2, w_out2], [16, 48, 48, 96, 48, 48]
    )
    norms = jnp.swapaxes(norms[:, :6, :own_width], 0, 1).reshape(6, D).astype(jnp.float32)
    gain_one, shift_one, gain_two, shift_two, gain_three, shift_three = (norms[k] for k in range(6))
    full_qkv = full_qkv.reshape(-1, D)
    full_out = full_out.reshape(-1, D)
    full_kv2 = full_kv2.reshape(-1, cond_rows.shape[1])
    full_query2 = full_query2.reshape(-1, D)
    full_out2 = full_out2.reshape(-1, D)
    cosine, sin_table = angles(positions[0], HD)
    act_one = layer_norm(tokens, gain_one, shift_one).astype(jnp.bfloat16)
    qkv_rows = dot_nt(act_one, full_qkv)
    queries = rotate(qkv_rows[:, :D].reshape(seq_len, HEADS, HD), cosine, sin_table).astype(
        jnp.bfloat16
    )
    key_heads = rotate(
        qkv_rows[:, D : 2 * D].reshape(seq_len, HEADS, HD), cosine, sin_table
    ).astype(jnp.bfloat16)
    value_heads = qkv_rows[:, 2 * D :].reshape(seq_len, HEADS, HD).astype(jnp.bfloat16)
    attended, log_one = attend(queries, key_heads, value_heads)
    flat_one = attended.reshape(seq_len, D)
    section_one = tokens + dot_nt(flat_one, full_out)
    act_two = layer_norm(section_one, gain_two, shift_two).astype(jnp.bfloat16)
    query_two = dot_nt(act_two, full_query2).astype(jnp.bfloat16).reshape(seq_len, HEADS, HD)
    kv_two = dot_nt(cond_rows, full_kv2).astype(jnp.bfloat16)
    key_two = kv_two[:, :D].reshape(NC, HEADS, HD)
    value_two = kv_two[:, D:].reshape(NC, HEADS, HD)
    attended_two, log_two = attend(query_two, key_two, value_two)
    flat_two = attended_two.reshape(seq_len, D)
    section_two = section_one + dot_nt(flat_two, full_out2)
    act_three = layer_norm(section_two, gain_three, shift_three).astype(jnp.bfloat16)
    grad_out = cotangent[0].astype(jnp.float32) * slot_valid[0].astype(jnp.float32)
    grad_mlp = grad_out.astype(jnp.bfloat16)
    all_grad = lax.all_gather(grad_mlp, "grp", axis=0, tiled=True)
    all_act = lax.all_gather(act_three, "grp", axis=0, tiled=True)
    gate_pre = dot_nt(all_act, w_gate)
    up_pre = dot_nt(all_act, w_up)
    hidden = swiglu(gate_pre, up_pre).astype(jnp.bfloat16)
    mlp_part = dot(hidden, w_down).astype(jnp.bfloat16)
    mlp_out = lax.psum_scatter(mlp_part, "grp", scatter_dimension=0, tiled=True)
    outputs = (section_two + mlp_out.astype(jnp.float32)).astype(jnp.bfloat16)
    d_hidden = dot_nt(all_grad, w_down)
    d_gate_full, d_up_full = swiglu_back(gate_pre, up_pre, d_hidden)
    d_gate = d_gate_full.astype(jnp.bfloat16)
    d_up = d_up_full.astype(jnp.bfloat16)
    d_norm3_part = (dot(d_gate, w_gate) + dot(d_up, w_up)).astype(jnp.bfloat16)
    d_norm3 = lax.psum_scatter(d_norm3_part, "grp", scatter_dimension=0, tiled=True)
    d_norm3 = d_norm3.astype(jnp.float32)
    grad_gate = dot_tn(d_gate, all_act).astype(jnp.bfloat16)
    grad_up = dot_tn(d_up, all_act).astype(jnp.bfloat16)
    grad_down = dot_tn(hidden, all_grad).astype(jnp.bfloat16)
    d_ln_three, d_gain_three, d_shift_three = norm_back(
        section_two, gain_three, shift_three, d_norm3
    )
    d_section_two = grad_out + d_ln_three
    d_cross = d_section_two.astype(jnp.bfloat16)
    grad_out_two = part_grad(d_cross, flat_two)
    d_att_two = dot(d_cross, full_out2).astype(jnp.bfloat16).reshape(seq_len, HEADS, HD)
    d_query_full, d_key_full, d_value_full = attend_back(
        query_two, key_two, value_two, log_two, d_att_two
    )
    d_query_two = d_query_full.reshape(seq_len, D).astype(jnp.bfloat16)
    d_kv_two = jnp.concatenate(
        [d_key_full.reshape(NC, D), d_value_full.reshape(NC, D)], axis=1
    ).astype(jnp.bfloat16)
    grad_query_two = part_grad(d_query_two, act_two)
    grad_kv_two = part_grad(d_kv_two, cond_rows)
    d_norm2 = dot(d_query_two, full_query2)
    d_ln_two, d_gain_two, d_shift_two = norm_back(section_one, gain_two, shift_two, d_norm2)
    d_section_one = d_section_two + d_ln_two
    d_attn = d_section_one.astype(jnp.bfloat16)
    grad_out_one = part_grad(d_attn, flat_one)
    d_att = dot(d_attn, full_out).astype(jnp.bfloat16).reshape(seq_len, HEADS, HD)
    d_query, d_key, d_value = attend_back(queries, key_heads, value_heads, log_one, d_att)
    d_qkv = jnp.concatenate(
        [
            rotate(d_query, cosine, -sin_table).reshape(seq_len, D),
            rotate(d_key, cosine, -sin_table).reshape(seq_len, D),
            d_value.reshape(seq_len, D),
        ],
        axis=1,
    ).astype(jnp.bfloat16)
    grad_qkv = part_grad(d_qkv, act_one)
    d_norm1 = dot(d_qkv, full_qkv)
    d_ln_one, d_gain_one, d_shift_one = norm_back(tokens, gain_one, shift_one, d_norm1)
    d_tokens = d_section_one + d_ln_one
    norm_stack = jnp.stack(
        [d_gain_one, d_shift_one, d_gain_two, d_shift_two, d_gain_three, d_shift_three], axis=0
    ).astype(jnp.bfloat16)
    groups = lax.axis_size("grp")
    attention_parts = [grad_qkv, grad_out_one, grad_query_two, grad_out_two, grad_kv_two]
    ffn_parts = [grad_gate, grad_up, grad_down]
    if groups == 8 and lax.axis_size("rep") == 4:
        norm_part = jnp.swapaxes(norm_stack.reshape(6, groups, own_width), 0, 1)
        norm_part = norm_part.reshape(groups, 1, 6 * own_width)
        norm_part = jnp.pad(norm_part, ((0, 0), (0, CUT - 1), (0, D - 6 * own_width)))
        kv2_rows = grad_kv_two.shape[0] // groups // 2
        kv2_part = grad_kv_two.reshape(groups, 2, kv2_rows, D // 2)
        kv2_part = jnp.swapaxes(kv2_part, 1, 2).reshape(groups, kv2_rows, D)
        parts = attention_parts[:4] + [kv2_part, norm_part]
        parts = [p.reshape(2, 2, 2, -1, D) for p in parts]
        total_a, total_f = reduce_all(parts, ffn_parts)
        ends = []
        for p in parts:
            ends.append((ends[-1] if ends else 0) + p.shape[3])
        pieces = [total_a[e - p.shape[3] : e] for e, p in zip(ends, parts)]
        norm_total = pieces[5][0, : 6 * own_width].reshape(6, own_width)
        kv2_total = jnp.swapaxes(pieces[4].reshape(kv2_rows, 2, D // 2), 0, 1)
        pieces[4] = kv2_total.reshape(2 * kv2_rows, D // 2)
        attention_sums = pieces[:5]
        own = w_gate.shape[0]
        ffn_sums = [total_f[k * own : (k + 1) * own] for k in range(3)]
    else:
        norm_total = lax.psum(norm_stack, ("grp", "rep"))
        norm_total = lax.dynamic_slice_in_dim(
            norm_total, lax.axis_index("grp") * own_width, own_width, axis=1
        )
        attention_sums = [
            lax.psum_scatter(g, "grp", scatter_dimension=0, tiled=True) for g in attention_parts
        ]
        attention_sums = [lax.psum(g, "rep") for g in attention_sums]
        ffn_sums = [lax.psum(g, "rep") for g in ffn_parts]
    norm_total = norm_total.astype(jnp.float32)
    grad_qkv, grad_out_one, grad_query_two, grad_out_two, grad_kv_two = (
        g.astype(jnp.float32) for g in attention_sums
    )
    grad_gate, grad_up, grad_down = (g.astype(jnp.float32) for g in ffn_sums)
    return (
        outputs[None],
        d_tokens[None],
        norm_total[0],
        norm_total[1],
        norm_total[2],
        norm_total[3],
        norm_total[4],
        norm_total[5],
        grad_qkv,
        grad_out_one,
        grad_query_two,
        grad_kv_two,
        grad_out_two,
        grad_gate,
        grad_up,
        grad_down,
    )


def solution(mesh):
    return jax.shard_map(
        per_device,
        mesh=mesh,
        in_specs=(
            P(("grp", "rep"), None, None),
            P(("grp", "rep"), None, None),
            P(("grp", "rep"), None),
            P(("grp", "rep")),
            P(("grp", "rep"), None, None),
            P("grp"),
            P("grp"),
            P("grp"),
            P("grp"),
            P("grp"),
            P("grp"),
            P("grp", None),
            P("grp", None),
            P("grp", None),
            P("grp", None),
            P("grp", None),
            P("grp", None),
            P("grp", None),
            P("grp", None),
        ),
        out_specs=(
            P(("grp", "rep"), None, None),
            P(("grp", "rep"), None, None),
            P("grp"),
            P("grp"),
            P("grp"),
            P("grp"),
            P("grp"),
            P("grp"),
            P("grp", None),
            P("grp", None),
            P("grp", None),
            P("grp", None),
            P("grp", None),
            P("grp", None),
            P("grp", None),
            P("grp", None),
        ),
        check_vma=False,
    )
```

```python
import functools
import math

import jax
import jax.numpy as jnp
from jax import lax
from jax.experimental import pallas as pl
from jax.experimental.pallas import tpu as pltpu
from jax.sharding import PartitionSpec as P

MESH = pl.DeviceIdType.MESH
VMEM_LIMIT = 63 * 1024 * 1024

D = 1536
HEADS = 24
HD = 64
NC = 130


epsilon = 1e-05
score_scale = 0.125


def layer_norm(tensor, gain, shift):
    center = tensor - jnp.mean(tensor, axis=-1, keepdims=True)
    spread = jnp.mean(center * center, axis=-1, keepdims=True)
    return center * lax.rsqrt(spread + epsilon) * gain + shift


def norm_back(tensor, gain, shift, d_normed):
    _, pullback = jax.vjp(layer_norm, tensor, gain, shift)
    return pullback(d_normed)


def swiglu(gate_part, up_part):
    return jax.nn.silu(gate_part) * up_part


def swiglu_back(gate_part, up_part, d_hidden):
    _, pullback = jax.vjp(swiglu, gate_part, up_part)
    return pullback(d_hidden)


def angles(positions, head_size):
    quarter = head_size // 4
    frequency = jnp.exp(jnp.arange(quarter, dtype=jnp.float32) * (-math.log(10000.0) / quarter))
    turned = positions.astype(jnp.float32)[:, None] * frequency[None, :]
    return (jnp.cos(turned)[:, None, :], jnp.sin(turned)[:, None, :])


def rotate(tensor, cosine, sin_table):
    quarter = tensor.shape[-1] // 4
    first_half = tensor[..., :quarter]
    second_half = tensor[..., quarter : 2 * quarter]
    remainder = tensor[..., 2 * quarter :]
    return jnp.concatenate(
        [
            first_half * cosine - second_half * sin_table,
            first_half * sin_table + second_half * cosine,
            remainder,
        ],
        axis=-1,
    )


def dot_nt(left_side, right_side):
    return lax.dot_general(
        left_side, right_side, (((1,), (1,)), ((), ())), preferred_element_type=jnp.float32
    )


def dot_tn(left_side, right_side):
    return lax.dot_general(
        left_side, right_side, (((0,), (0,)), ((), ())), preferred_element_type=jnp.float32
    )


def dot(left_side, right_side):
    return jnp.dot(left_side, right_side, preferred_element_type=jnp.float32)


def part_grad(grad_cols, activation):
    return dot_tn(grad_cols, activation).astype(jnp.bfloat16)


def attend(queries, key_heads, value_heads):
    seq_len = queries.shape[0]
    span = min(seq_len, 512)
    blocked = queries.reshape(seq_len // span, span, queries.shape[1], queries.shape[2])

    def one_block(query_block):
        scores = (
            jnp.einsum("qhd,khd->hqk", query_block, key_heads, preferred_element_type=jnp.float32)
            * score_scale
        )
        largest = jnp.max(scores, axis=-1, keepdims=True)
        shifted = jnp.exp(scores - largest)
        totals = jnp.sum(shifted, axis=-1, keepdims=True)
        probability = (shifted / totals).astype(jnp.bfloat16)
        result = jnp.einsum(
            "hqk,khd->qhd", probability, value_heads, preferred_element_type=jnp.float32
        )
        return (result.astype(jnp.bfloat16), (largest + jnp.log(totals))[..., 0])

    outcome, log_sums = lax.map(one_block, blocked)
    return (outcome.reshape(queries.shape), log_sums)


def attend_back(queries, key_heads, value_heads, log_sums, grad_heads):
    seq_len = queries.shape[0]
    span = min(seq_len, 512)
    block_count = seq_len // span
    query_blocks = queries.reshape(block_count, span, queries.shape[1], queries.shape[2])
    grad_blocks = grad_heads.reshape(block_count, span, queries.shape[1], queries.shape[2])

    def one_block(carried, inputs_block):
        query_block, log_block, grad_block = inputs_block
        scores = (
            jnp.einsum("qhd,khd->hqk", query_block, key_heads, preferred_element_type=jnp.float32)
            * score_scale
        )
        probability = jnp.exp(scores - log_block[..., None])
        d_prob = jnp.einsum(
            "qhd,khd->hqk", grad_block, value_heads, preferred_element_type=jnp.float32
        )
        inner = jnp.sum(probability * d_prob, axis=-1, keepdims=True)
        d_scores = (probability * (d_prob - inner)).astype(jnp.bfloat16)
        d_query = (
            jnp.einsum("hqk,khd->qhd", d_scores, key_heads, preferred_element_type=jnp.float32)
            * score_scale
        )
        d_key = (
            carried[0]
            + jnp.einsum("hqk,qhd->khd", d_scores, query_block, preferred_element_type=jnp.float32)
            * score_scale
        )
        d_value = carried[1] + jnp.einsum(
            "hqk,qhd->khd",
            probability.astype(jnp.bfloat16),
            grad_block,
            preferred_element_type=jnp.float32,
        )
        return ((d_key, d_value), d_query)

    start_zero = jnp.zeros(key_heads.shape, jnp.float32)
    (d_key, d_value), d_query = lax.scan(
        one_block, (start_zero, start_zero), (query_blocks, log_sums, grad_blocks)
    )
    return (d_query.reshape(queries.shape), d_key, d_value)


def meet(peers, lower=None, upper=None, rep_index=None):
    barrier = pltpu.get_barrier_semaphore()
    for peer in peers:
        pl.semaphore_signal(barrier, inc=1, device_id=peer, device_id_type=MESH)
    if lower is not None:

        @pl.when(rep_index > 0)
        def _():
            pl.semaphore_signal(barrier, inc=1, device_id=lower, device_id_type=MESH)

        @pl.when(rep_index < 3)
        def _():
            pl.semaphore_signal(barrier, inc=1, device_id=upper, device_id_type=MESH)

    expected = len(peers)
    if lower is not None:
        expected = expected + jnp.where(rep_index > 0, 1, 0) + jnp.where(rep_index < 3, 1, 0)
    pl.semaphore_wait(barrier, expected)


GATHER_WINDOW = 4


def gather_kernel(pieces, *refs):
    count = len(pieces)
    sources = refs[:count]
    fulls = refs[count : 2 * count]
    send_sem, recv_sem, local_sem = refs[2 * count :]
    me = lax.axis_index("grp")
    plane = lax.axis_index("rep")
    odd = lax.rem(plane, 2)
    first_bit = 2 + 2 * odd
    second_bit = 6 - first_bit
    first = me ^ first_bit
    second = me ^ second_bit
    across = me ^ 6
    first_dev = (first, plane)
    second_dev = (second, plane)
    rep_dev = (me, plane ^ 1)
    mate_dev = (me ^ 1, plane)
    meet([first_dev, second_dev, rep_dev, mate_dev])
    total = sum(n for n, _ in pieces)

    def each(i, body):
        base = 0
        for k, (n, rows) in enumerate(pieces):
            if n == 1:

                @pl.when(i == base)
                def _(k=k, rows=rows):
                    body(k, pl.ds(0, rows))

            else:

                @pl.when((i >= base) & (i < base + n))
                def _(k=k, rows=rows, base=base):
                    body(k, pl.ds(pl.multiple_of((i - base) * rows, 16), rows))

            base += n

    def push(k, cut, i, owner, lane, device, own=False):
        src = sources[k].at[cut] if own else fulls[k].at[owner, cut]
        return pltpu.make_async_remote_copy(
            src_ref=src,
            dst_ref=fulls[k].at[owner, cut],
            send_sem=send_sem.at[lane, i],
            recv_sem=recv_sem.at[lane, i],
            device_id=device,
            device_id_type=MESH,
        )

    def stage_own(i):
        def body(k, cut):
            push(k, cut, i, me, 0, first_dev, own=True).start()
            push(k, cut, i, me, 3, mate_dev, own=True).start()
            pltpu.make_async_copy(sources[k].at[cut], fulls[k].at[me, cut], local_sem.at[i]).start()

        each(i, body)

    def stage_first(i):
        def body(k, cut):
            push(k, cut, i, first, 0, first_dev).wait_recv()
            push(k, cut, i, first, 1, second_dev).start()
            push(k, cut, i, first, 2, rep_dev).start()
            push(k, cut, i, first, 4, mate_dev).start()

        each(i, body)

    def stage_rest(i):
        def body(k, cut):
            push(k, cut, i, across, 1, second_dev).wait_recv()
            push(k, cut, i, across, 5, mate_dev).start()
            push(k, cut, i, second, 2, rep_dev).wait_recv()
            push(k, cut, i, second, 6, mate_dev).start()

        each(i, body)

    def stage_end(i):
        def body(k, cut):
            pltpu.make_async_copy(
                sources[k].at[cut], fulls[k].at[me, cut], local_sem.at[i]
            ).wait()
            push(k, cut, i, me, 0, first_dev, own=True).wait_send()
            push(k, cut, i, first, 1, second_dev).wait_send()
            push(k, cut, i, first, 2, rep_dev).wait_send()
            push(k, cut, i, me, 3, mate_dev, own=True).wait()
            push(k, cut, i, first, 4, mate_dev).wait()
            push(k, cut, i, across, 5, mate_dev).wait()
            push(k, cut, i, second, 6, mate_dev).wait()

        each(i, body)

    def step(t, carry):
        for stage, lag in ((stage_own, 0), (stage_first, GATHER_WINDOW), (stage_rest, GATHER_WINDOW + 2)):
            i = t - lag

            @pl.when((i >= 0) & (i < total))
            def _(stage=stage, i=i):
                stage(i)

        return carry

    lax.fori_loop(0, total + GATHER_WINDOW + 2, step, 0)

    def finish(i, carry):
        stage_end(i)
        return carry

    lax.fori_loop(0, total, finish, 0)


def gather_all(arrays, rows):
    groups = lax.axis_size("grp")
    if groups != 8 or lax.axis_size("rep") % 2 != 0:
        return [lax.all_gather(a, "grp", axis=0) for a in arrays]
    pieces = tuple((a.shape[0] // n, n) for a, n in zip(arrays, rows))
    total = sum(n for n, _ in pieces)
    hbm = pl.BlockSpec(memory_space=pltpu.HBM)
    return pl.pallas_call(
        functools.partial(gather_kernel, pieces),
        out_shape=[jax.ShapeDtypeStruct((groups,) + a.shape, a.dtype) for a in arrays],
        in_specs=[hbm] * len(arrays),
        out_specs=[hbm] * len(arrays),
        scratch_shapes=[
            pltpu.SemaphoreType.DMA((7, total)),
            pltpu.SemaphoreType.DMA((7, total)),
            pltpu.SemaphoreType.DMA((total,)),
        ],
        compiler_params=pltpu.CompilerParams(collective_id=0, has_side_effects=True),
    )(*arrays)


CUT = 48
FCUT = 96
MATE_SLOTS = 6
OWN_SLOTS = 3
SUM_SLOTS = 8
FFN_SLOTS = 12


def reduce_kernel(pieces, ffn_count, *refs):
    count = len(pieces)
    parts = refs[:count]
    ffn = refs[count : count + (3 if ffn_count else 0)]
    refs = refs[len(ffn) :]
    out_a = refs[count]
    out_f = refs[count + 1] if ffn_count else None
    refs = refs[count + (2 if ffn_count else 1) :]
    (
        mate_buf,
        own_buf,
        sums,
        one_buf,
        two_buf,
        done,
        ffn_buf,
        low_a,
        up_a,
        low_f,
        up_f,
        mate_send,
        mate_recv,
        own_sem,
        one_send,
        one_recv,
        two_send,
        two_recv,
        ffn_sem,
        chain_send,
        chain_recv,
        out_sem,
        credit,
    ) = refs
    me = lax.axis_index("grp")
    plane = lax.axis_index("rep")
    core = lax.rem(me, 2)
    x = lax.rem(me // 2, 2)
    y = me // 4
    mate_dev = (me ^ 1, plane)
    x_dev = (me ^ 2, plane)
    y_dev = (me ^ 4, plane)
    low_dev = (me, plane - 1)
    up_dev = (me, plane + 1)
    meet([mate_dev, x_dev, y_dev], low_dev, up_dev, plane)
    total = sum(pieces)
    chain_total = ffn_count + total

    def each(i, body):
        base = 0
        for k, n in enumerate(pieces):

            @pl.when((i >= base) & (i < base + n))
            def _(k=k, base=base):
                body(k, pl.ds(pl.multiple_of((i - base) * CUT, 16), CUT))

            base += n

    def mate_copy(k, cut, slot):
        return pltpu.make_async_remote_copy(
            src_ref=parts[k].at[:, :, 1 - core, cut],
            dst_ref=mate_buf.at[slot],
            send_sem=mate_send.at[slot],
            recv_sem=mate_recv.at[slot],
            device_id=mate_dev,
            device_id_type=MESH,
        )

    def own_copy(k, cut, slot):
        return pltpu.make_async_copy(
            parts[k].at[:, :, core, cut], own_buf.at[slot], own_sem.at[slot]
        )

    def load(i):
        @pl.when(i >= MATE_SLOTS)
        def _():
            pl.semaphore_wait(credit, 1)
            mate_copy(0, pl.ds(0, CUT), lax.rem(i, MATE_SLOTS)).wait_send()

        def body(k, cut):
            mate_copy(k, cut, lax.rem(i, MATE_SLOTS)).start()
            own_copy(k, cut, lax.rem(i, OWN_SLOTS)).start()

        each(i, body)

    def one_copy(i, slot, by_x):
        return pltpu.make_async_remote_copy(
            src_ref=sums.at[slot, :, 1 - x] if by_x else sums.at[slot, 1 - y],
            dst_ref=one_buf.at[i],
            send_sem=one_send.at[slot],
            recv_sem=one_recv.at[i],
            device_id=x_dev if by_x else y_dev,
            device_id_type=MESH,
        )

    def two_copy(i, slot, by_x):
        return pltpu.make_async_remote_copy(
            src_ref=sums.at[slot, 1 - y, x] if by_x else sums.at[slot, y, 1 - x],
            dst_ref=two_buf.at[i],
            send_sem=two_send.at[slot],
            recv_sem=two_recv.at[i],
            device_id=y_dev if by_x else x_dev,
            device_id_type=MESH,
        )

    def either(i, body):
        @pl.when(lax.rem(i, 2) == 0)
        def _():
            body(True)

        @pl.when(lax.rem(i, 2) == 1)
        def _():
            body(False)

    def add(a, b):
        return (a.astype(jnp.float32) + b.astype(jnp.float32)).astype(jnp.bfloat16)

    def pair(i):
        mate_slot, own_slot, slot = (
            lax.rem(i, MATE_SLOTS),
            lax.rem(i, OWN_SLOTS),
            lax.rem(i, SUM_SLOTS),
        )
        mate_copy(0, pl.ds(0, CUT), mate_slot).wait_recv()
        own_copy(0, pl.ds(0, CUT), own_slot).wait()
        for u in range(2):
            for v in range(2):
                sums[slot, u, v] = add(own_buf[own_slot, u, v], mate_buf[mate_slot, u, v])

        @pl.when(i + MATE_SLOTS < total)
        def _():
            pl.semaphore_signal(credit, inc=1, device_id=mate_dev, device_id_type=MESH)

        either(i, lambda by_x: one_copy(i, slot, by_x).start())

    def plane_one(i):
        slot = lax.rem(i, SUM_SLOTS)

        def body(by_x):
            one_copy(i, slot, by_x).wait_recv()
            for u in range(2):
                if by_x:
                    sums[slot, u, x] = add(sums[slot, u, x], one_buf[i, u])
                else:
                    sums[slot, y, u] = add(sums[slot, y, u], one_buf[i, u])
            two_copy(i, slot, by_x).start()

        either(i, body)

    def plane_two(i):
        slot = lax.rem(i, SUM_SLOTS)

        def body(by_x):
            two_copy(i, slot, by_x).wait_recv()
            done[i] = add(sums[slot, y, x], two_buf[i])
            one_copy(i, slot, by_x).wait_send()
            two_copy(i, slot, by_x).wait_send()

        either(i, body)

    def ffn_load(j):
        for k in range(3):

            @pl.when(j // (ffn_count // 3) == k)
            def _(k=k):
                row = pl.multiple_of((j - k * (ffn_count // 3)) * FCUT, 16)
                pltpu.make_async_copy(
                    ffn[k].at[pl.ds(row, FCUT)],
                    ffn_buf.at[lax.rem(j, FFN_SLOTS)],
                    ffn_sem.at[lax.rem(j, FFN_SLOTS)],
                ).start()

    def ffn_wait(j):
        pltpu.make_async_copy(
            ffn[0].at[pl.ds(0, FCUT)],
            ffn_buf.at[lax.rem(j, FFN_SLOTS)],
            ffn_sem.at[lax.rem(j, FFN_SLOTS)],
        ).wait()

    def views(j, is_ffn):
        if is_ffn:
            rows = pl.ds(pl.multiple_of(j * FCUT, 16), FCUT)
            return ffn_buf.at[lax.rem(j, FFN_SLOTS)], low_f.at[j], up_f.at[j], out_f.at[rows]
        i = j - ffn_count
        rows = pl.ds(pl.multiple_of(i * CUT, 16), CUT)
        return done.at[i], low_a.at[i], up_a.at[i], out_a.at[rows]

    def chain(j, lane, src, dst, device):
        return pltpu.make_async_remote_copy(
            src_ref=src,
            dst_ref=dst,
            send_sem=chain_send.at[lane, j],
            recv_sem=chain_recv.at[lane, j],
            device_id=device,
            device_id_type=MESH,
        )

    def kinds(j, body):
        if ffn_count:

            @pl.when(j < ffn_count)
            def _():
                body(*views(j, True))

        @pl.when(j >= ffn_count)
        def _():
            body(*views(j, False))

    def inward(j):
        if ffn_count:

            @pl.when(j < ffn_count)
            def _():
                ffn_wait(j)

        def body(mine, low, up, out):
            @pl.when(plane == 0)
            def _():
                chain(j, 0, mine, low, up_dev).start()

            @pl.when(plane == 3)
            def _():
                chain(j, 1, mine, up, low_dev).start()

        kinds(j, body)

    def middle(j):
        def body(mine, low, up, out):
            @pl.when(plane == 2)
            def _():
                chain(j, 1, mine, up, low_dev).wait_recv()
                mine[...] = add(mine[...], up[...])
                chain(j, 1, mine, up, low_dev).start()

        kinds(j, body)

    def root(j):
        def body(mine, low, up, out):
            @pl.when(plane == 1)
            def _():
                chain(j, 0, mine, low, up_dev).wait_recv()
                chain(j, 1, mine, up, low_dev).wait_recv()
                mine[...] = (
                    mine[...].astype(jnp.float32)
                    + low[...].astype(jnp.float32)
                    + up[...].astype(jnp.float32)
                ).astype(jnp.bfloat16)
                chain(j, 0, mine, out, up_dev).start()
                chain(j, 1, mine, out, low_dev).start()
                pltpu.make_async_copy(mine, out, out_sem.at[j]).start()

        kinds(j, body)

    def outward(j):
        def body(mine, low, up, out):
            @pl.when(plane == 2)
            def _():
                chain(j, 0, mine, out, up_dev).wait_recv()
                chain(j, 0, out, out, up_dev).start()

        kinds(j, body)

    def drain(j):
        def body(mine, low, up, out):
            @pl.when(plane == 0)
            def _():
                chain(j, 0, mine, low, up_dev).wait_send()
                chain(j, 1, mine, out, low_dev).wait_recv()

            @pl.when(plane == 3)
            def _():
                chain(j, 1, mine, up, low_dev).wait_send()
                chain(j, 0, mine, out, up_dev).wait_recv()

            @pl.when(plane == 1)
            def _():
                chain(j, 0, mine, out, up_dev).wait_send()
                chain(j, 1, mine, out, low_dev).wait_send()
                pltpu.make_async_copy(mine, out, out_sem.at[j]).wait()

            @pl.when(plane == 2)
            def _():
                chain(j, 1, mine, up, low_dev).wait_send()
                chain(j, 0, out, out, up_dev).wait_send()

        kinds(j, body)

    stages = (
        (load, 0, total),
        (ffn_load, 0, ffn_count),
        (pair, 1, total),
        (plane_one, 3, total),
        (plane_two, 5, total),
        (inward, 5, chain_total),
        (middle, 7, chain_total),
        (root, 9, chain_total),
        (outward, 11, chain_total),
        (drain, 13, chain_total),
    )
    if not ffn_count:
        stages = stages[:1] + stages[2:]

    def step(t, carry):
        for stage, lag, limit in stages:
            i = t - lag

            @pl.when((i >= 0) & (i < limit))
            def _(stage=stage, i=i):
                stage(i)

        return carry

    lax.fori_loop(0, chain_total + 13, step, 0)
    for i in range(max(total - MATE_SLOTS, 0), total):
        mate_copy(0, pl.ds(0, CUT), i % MATE_SLOTS).wait_send()


def reduce_all(parts, ffn):
    pieces = tuple(p.shape[3] // CUT for p in parts)
    total = sum(pieces)
    wide = parts[0].shape[-1]
    ffn_rows = sum(f.shape[0] for f in ffn)
    ffn_count = ffn_rows // FCUT
    chain_total = total + ffn_count
    hbm = pl.BlockSpec(memory_space=pltpu.HBM)
    low = jnp.bfloat16
    dma = pltpu.SemaphoreType.DMA
    return pl.pallas_call(
        functools.partial(reduce_kernel, pieces, ffn_count),
        out_shape=[
            jax.ShapeDtypeStruct((total * CUT, wide), low),
            jax.ShapeDtypeStruct((ffn_rows, wide), low),
        ][: 2 if ffn else 1],
        in_specs=[hbm] * (len(parts) + len(ffn)),
        out_specs=[hbm] * (2 if ffn else 1),
        scratch_shapes=[
            pltpu.VMEM((MATE_SLOTS, 2, 2, CUT, wide), low),
            pltpu.VMEM((OWN_SLOTS, 2, 2, CUT, wide), low),
            pltpu.VMEM((SUM_SLOTS, 2, 2, CUT, wide), low),
            pltpu.VMEM((total, 2, CUT, wide), low),
            pltpu.VMEM((total, CUT, wide), low),
            pltpu.VMEM((total, CUT, wide), low),
            pltpu.VMEM((FFN_SLOTS if ffn else 1, FCUT, wide), low),
            pltpu.VMEM((total, CUT, wide), low),
            pltpu.VMEM((total, CUT, wide), low),
            pltpu.VMEM((max(ffn_count, 1), FCUT, wide), low),
            pltpu.VMEM((max(ffn_count, 1), FCUT, wide), low),
            dma((MATE_SLOTS,)),
            dma((MATE_SLOTS,)),
            dma((OWN_SLOTS,)),
            dma((SUM_SLOTS,)),
            dma((total,)),
            dma((SUM_SLOTS,)),
            dma((total,)),
            dma((FFN_SLOTS,)),
            dma((2, chain_total)),
            dma((2, chain_total)),
            dma((chain_total,)),
            pltpu.SemaphoreType.REGULAR,
        ],
        compiler_params=pltpu.CompilerParams(
            collective_id=1, has_side_effects=True, vmem_limit_bytes=VMEM_LIMIT
        ),
    )(*parts, *ffn)


STEP_CHIP = (0, 0, 1, 2, 1, 2, 3, 3)
STEP_HALF = (0, 1, 0, 1, 1, 0, 0, 1)
TILE = 256


def ffn_kernel(
    act_in,
    cot_in,
    gate_in,
    up_in,
    down_in,
    out_ref,
    dn_ref,
    grad_gate,
    grad_up,
    grad_down,
    act,
    cot,
    w_gate,
    w_up,
    w_down,
    hidden,
    d_gate,
    d_up,
    pair,
    mine,
    stage,
    passed,
    final,
    tile_buf,
    weight_sem,
    cot_sem,
    own_sem,
    act_send,
    act_recv,
    pair_send,
    pair_recv,
    flow_send,
    flow_recv,
    tile_sem,
    end_sem,
):
    me = lax.axis_index("grp")
    plane = lax.axis_index("rep")
    mate_dev, x_dev, y_dev = (me ^ 1, plane), (me ^ 2, plane), (me ^ 4, plane)
    half = act.shape[2]
    seq_len = 2 * half
    rows, wide = w_gate.shape
    low = jnp.bfloat16
    meet([mate_dev, x_dev, y_dev])

    def remote(src, dst, send, recv, device):
        return pltpu.make_async_remote_copy(
            src_ref=src,
            dst_ref=dst,
            send_sem=send,
            recv_sem=recv,
            device_id=device,
            device_id_type=MESH,
        )

    own = [act_in.at[pl.ds(h * half, half)] for h in range(2)]

    def act_copy(t, other):
        if other:
            src, device = (own[t] if t < 2 else act.at[t, 0]), mate_dev
        else:
            src, device = {
                2: (own[0], x_dev),
                3: (own[1], y_dev),
                4: (own[1], x_dev),
                5: (own[0], y_dev),
                6: (act.at[2, 0], y_dev),
                7: (act.at[3, 0], x_dev),
            }[t]
        return remote(
            src, act.at[t, other], act_send.at[t, other], act_recv.at[t, other], device
        )

    for t in (2, 3, 4, 5):
        act_copy(t, 0).start()
    for t in (0, 1):
        act_copy(t, 1).start()
    own_copies = [pltpu.make_async_copy(own[t], act.at[t, 0], own_sem.at[t]) for t in range(2)]
    for copy in own_copies:
        copy.start()
    weights = [
        pltpu.make_async_copy(src, dst, weight_sem.at[k])
        for k, (src, dst) in enumerate(((gate_in, w_gate), (up_in, w_up), (down_in, w_down)))
    ]
    for copy in weights:
        copy.start()
    cot_copies = []
    for t in range(8):
        for other in range(2):
            owner = me ^ (2 * STEP_CHIP[t] + other)
            row = pl.multiple_of(owner * seq_len + STEP_HALF[t] * half, 16)
            copy = pltpu.make_async_copy(
                cot_in.at[pl.ds(row, half)], cot.at[t, other], cot_sem.at[t, other]
            )
            copy.start()
            cot_copies.append(copy)

    def pair_copy(kind, t):
        return remote(
            stage.at[kind], pair.at[kind, t], pair_send.at[kind], pair_recv.at[kind, t], mate_dev
        )

    def flow(kind, lane):
        src, dst, device = (
            (pair.at[kind, 2], final.at[kind, 0], x_dev),
            (pair.at[kind, 4], final.at[kind, 1], x_dev),
            (pair.at[kind, 5], final.at[kind, 2], y_dev),
            (pair.at[kind, 3], final.at[kind, 3], y_dev),
            (pair.at[kind, 6], passed.at[kind, 0], x_dev),
            (pair.at[kind, 7], passed.at[kind, 1], y_dev),
        )[lane]
        return remote(src, dst, flow_send.at[kind, lane], flow_recv.at[kind, lane], device)

    def add(*terms):
        total = terms[0].astype(jnp.float32)
        for term in terms[1:]:
            total = total + term.astype(jnp.float32)
        return total.astype(low)

    def forward_tiles(t):
        def tile(n, carry):
            cut = pl.ds(pl.multiple_of(n * TILE, TILE), TILE)
            tokens = act[t].reshape(seq_len, wide)
            gate = dot_nt(tokens, w_gate[cut])
            up = dot_nt(tokens, w_up[cut])
            d_hidden = dot_nt(cot[t].reshape(seq_len, wide), w_down[cut])
            sigmoid = 1.0 / (1.0 + jnp.exp(-gate))
            silu = gate * sigmoid
            hidden[t, :, cut] = (silu * up).astype(low)
            d_gate[t, :, cut] = (
                d_hidden * up * (sigmoid * (1.0 + gate * (1.0 - sigmoid)))
            ).astype(low)
            d_up[t, :, cut] = (d_hidden * silu).astype(low)
            return carry

        lax.fori_loop(0, rows // TILE, tile, 0)

    def backward_tiles(t):
        def tile(n, carry):
            cut = pl.ds(pl.multiple_of(n * TILE, TILE), TILE)
            out = dot(hidden[t], w_down[:, cut])
            mine[0, :, cut] = out[:half].astype(low)
            stage[0, :, cut] = out[half:].astype(low)
            dn = dot(d_gate[t], w_gate[:, cut]) + dot(d_up[t], w_up[:, cut])
            mine[1, :, cut] = dn[:half].astype(low)
            stage[1, :, cut] = dn[half:].astype(low)
            return carry

        lax.fori_loop(0, wide // TILE, tile, 0)

    def join(t, events):
        for kind in range(2):
            pair_copy(kind, t).wait()
            pair[kind, t] = add(pair[kind, t], mine[kind])
            for when, lane in events:
                if when is None:
                    flow(kind, lane).start()
                else:

                    @pl.when(t == when)
                    def _(kind=kind, lane=lane):
                        flow(kind, lane).start()

    for copy in own_copies + weights:
        copy.wait()

    def step(t, carry):
        for at in (2, 4, 6):

            @pl.when(t == at)
            def _(at=at):
                for u in (at, at + 1):
                    act_copy(u, 0).wait_recv()
                    if at == 2:
                        act_copy(u + 4, 0).start()
                    act_copy(u, 1).start()

        remote(
            act.at[t, 0], act.at[t, 1], act_send.at[t, 1], act_recv.at[t, 1], mate_dev
        ).wait_recv()
        for other in range(2):
            pltpu.make_async_copy(
                cot_in.at[pl.ds(0, half)], cot.at[t, other], cot_sem.at[t, other]
            ).wait()
        forward_tiles(t)

        @pl.when(t > 0)
        def _():
            join(t - 1, ((2, 0), (3, 3), (6, 4)))

        backward_tiles(t)
        for kind in range(2):
            pair_copy(kind, t).start()
        return carry

    lax.fori_loop(0, 8, step, 0)
    join(7, ((None, 5),))

    def write(target, slot, cut):
        return pltpu.make_async_copy(
            tile_buf.at[slot], target.at[:, cut], tile_sem.at[slot]
        )

    tiles = wide // TILE
    for k, (left, right, target) in enumerate(
        ((d_gate, act, grad_gate), (d_up, act, grad_up), (hidden, cot, grad_down))
    ):

        def tile(n, carry, k=k, left=left, right=right, target=target):
            cut = pl.ds(pl.multiple_of(n * TILE, TILE), TILE)
            slot = lax.rem(n, 2)

            @pl.when(k * tiles + n >= 2)
            def _():
                write(target, slot, cut).wait()

            tile_buf[slot] = dot_tn(
                left[...].reshape(8 * seq_len, rows),
                right[:, :, :, cut].reshape(8 * seq_len, TILE),
            ).astype(low)
            write(target, slot, cut).start()
            return carry

        lax.fori_loop(0, tiles, tile, 0)
    for slot in range(2):
        write(grad_down, slot, pl.ds(0, TILE)).wait()

    for kind in range(2):
        for lane, t, onward in ((4, 5, 2), (5, 4, 1)):
            flow(kind, lane).wait_recv()
            pair[kind, t] = add(pair[kind, t], passed[kind, lane - 4])
            flow(kind, onward).start()
    ends = []
    for kind, target in enumerate((out_ref, dn_ref)):
        for h in range(2):
            flow(kind, h).wait_recv()
            flow(kind, 2 + h).wait_recv()
            pair[kind, h] = add(pair[kind, h], final[kind, h], final[kind, 2 + h])
            copy = pltpu.make_async_copy(
                pair.at[kind, h], target.at[pl.ds(h * half, half)], end_sem.at[kind, h]
            )
            copy.start()
            ends.append(copy)
    for copy in ends:
        copy.wait()
    for kind in range(2):
        for lane in range(6):
            flow(kind, lane).wait_send()
    for t in range(8):
        act_copy(t, 1).wait_send()
        if t >= 2:
            act_copy(t, 0).wait_send()


def ffn_all(act, cot, w_gate, w_up, w_down):
    seq_len, wide = act.shape
    rows = w_gate.shape[0]
    half = seq_len // 2
    low = jnp.bfloat16
    hbm = pl.BlockSpec(memory_space=pltpu.HBM)
    dma = pltpu.SemaphoreType.DMA
    return pl.pallas_call(
        ffn_kernel,
        out_shape=[jax.ShapeDtypeStruct((seq_len, wide), low)] * 2
        + [jax.ShapeDtypeStruct((rows, wide), low)] * 3,
        in_specs=[hbm] * 5,
        out_specs=[hbm] * 5,
        scratch_shapes=[
            pltpu.VMEM((8, 2, half, wide), low),
            pltpu.VMEM((8, 2, half, wide), low),
            pltpu.VMEM((rows, wide), low),
            pltpu.VMEM((rows, wide), low),
            pltpu.VMEM((rows, wide), low),
            pltpu.VMEM((8, seq_len, rows), low),
            pltpu.VMEM((8, seq_len, rows), low),
            pltpu.VMEM((8, seq_len, rows), low),
            pltpu.VMEM((2, 8, half, wide), low),
            pltpu.VMEM((2, half, wide), low),
            pltpu.VMEM((2, half, wide), low),
            pltpu.VMEM((2, 2, half, wide), low),
            pltpu.VMEM((2, 4, half, wide), low),
            pltpu.VMEM((2, rows, TILE), low),
            dma((3,)),
            dma((8, 2)),
            dma((2,)),
            dma((8, 2)),
            dma((8, 2)),
            dma((2,)),
            dma((2, 8)),
            dma((2, 6)),
            dma((2, 6)),
            dma((2,)),
            dma((2, 2)),
        ],
        compiler_params=pltpu.CompilerParams(
            collective_id=2, has_side_effects=True, vmem_limit_bytes=VMEM_LIMIT
        ),
    )(act, cot, w_gate, w_up, w_down)


def per_device(
    inputs,
    conditioning,
    positions,
    slot_valid,
    cotangent,
    norm1_gain,
    norm1_shift,
    norm2_gain,
    norm2_shift,
    norm3_gain,
    norm3_shift,
    w_qkv,
    w_out,
    w_query2,
    w_kv2,
    w_out2,
    w_gate,
    w_up,
    w_down,
):
    tokens = inputs[0].astype(jnp.float32)
    seq_len = tokens.shape[0]
    cond_rows = conditioning[0]
    norms = jnp.stack(
        [norm1_gain, norm1_shift, norm2_gain, norm2_shift, norm3_gain, norm3_shift], axis=0
    )
    own_width = norms.shape[1]
    norms = jnp.pad(norms, ((0, 10), (0, -own_width % 128)))
    norms, full_qkv, full_out, full_kv2, full_query2, full_out2 = gather_all(
        [norms, w_qkv, w_out, w_kv2, w_query2, w_out2], [16, 48, 48, 96, 48, 48]
    )
    norms = jnp.swapaxes(norms[:, :6, :own_width], 0, 1).reshape(6, D).astype(jnp.float32)
    gain_one, shift_one, gain_two, shift_two, gain_three, shift_three = (norms[k] for k in range(6))
    full_qkv = full_qkv.reshape(-1, D)
    full_out = full_out.reshape(-1, D)
    full_kv2 = full_kv2.reshape(-1, cond_rows.shape[1])
    full_query2 = full_query2.reshape(-1, D)
    full_out2 = full_out2.reshape(-1, D)
    cosine, sin_table = angles(positions[0], HD)
    act_one = layer_norm(tokens, gain_one, shift_one).astype(jnp.bfloat16)
    qkv_rows = dot_nt(act_one, full_qkv)
    queries = rotate(qkv_rows[:, :D].reshape(seq_len, HEADS, HD), cosine, sin_table).astype(
        jnp.bfloat16
    )
    key_heads = rotate(
        qkv_rows[:, D : 2 * D].reshape(seq_len, HEADS, HD), cosine, sin_table
    ).astype(jnp.bfloat16)
    value_heads = qkv_rows[:, 2 * D :].reshape(seq_len, HEADS, HD).astype(jnp.bfloat16)
    attended, log_one = attend(queries, key_heads, value_heads)
    flat_one = attended.reshape(seq_len, D)
    section_one = tokens + dot_nt(flat_one, full_out)
    act_two = layer_norm(section_one, gain_two, shift_two).astype(jnp.bfloat16)
    query_two = dot_nt(act_two, full_query2).astype(jnp.bfloat16).reshape(seq_len, HEADS, HD)
    kv_two = dot_nt(cond_rows, full_kv2).astype(jnp.bfloat16)
    key_two = kv_two[:, :D].reshape(NC, HEADS, HD)
    value_two = kv_two[:, D:].reshape(NC, HEADS, HD)
    attended_two, log_two = attend(query_two, key_two, value_two)
    flat_two = attended_two.reshape(seq_len, D)
    section_two = section_one + dot_nt(flat_two, full_out2)
    act_three = layer_norm(section_two, gain_three, shift_three).astype(jnp.bfloat16)
    grad_out = cotangent[0].astype(jnp.float32) * slot_valid[0].astype(jnp.float32)
    grad_mlp = grad_out.astype(jnp.bfloat16)
    all_grad = lax.all_gather(grad_mlp, "grp", axis=0, tiled=True)
    if lax.axis_size("grp") == 8:
        mlp_out, d_norm3, grad_gate, grad_up, grad_down = ffn_all(
            act_three, all_grad, w_gate, w_up, w_down
        )
    else:
        all_act = lax.all_gather(act_three, "grp", axis=0, tiled=True)
        gate_pre = dot_nt(all_act, w_gate)
        up_pre = dot_nt(all_act, w_up)
        hidden = swiglu(gate_pre, up_pre).astype(jnp.bfloat16)
        mlp_part = dot(hidden, w_down).astype(jnp.bfloat16)
        mlp_out = lax.psum_scatter(mlp_part, "grp", scatter_dimension=0, tiled=True)
        d_hidden = dot_nt(all_grad, w_down)
        d_gate_full, d_up_full = swiglu_back(gate_pre, up_pre, d_hidden)
        d_gate = d_gate_full.astype(jnp.bfloat16)
        d_up = d_up_full.astype(jnp.bfloat16)
        d_norm3_part = (dot(d_gate, w_gate) + dot(d_up, w_up)).astype(jnp.bfloat16)
        d_norm3 = lax.psum_scatter(d_norm3_part, "grp", scatter_dimension=0, tiled=True)
        grad_gate = dot_tn(d_gate, all_act).astype(jnp.bfloat16)
        grad_up = dot_tn(d_up, all_act).astype(jnp.bfloat16)
        grad_down = dot_tn(hidden, all_grad).astype(jnp.bfloat16)
    outputs = (section_two + mlp_out.astype(jnp.float32)).astype(jnp.bfloat16)
    d_norm3 = d_norm3.astype(jnp.float32)
    ffn_sums = lax.psum((grad_gate, grad_up, grad_down), "rep")
    d_ln_three, d_gain_three, d_shift_three = norm_back(
        section_two, gain_three, shift_three, d_norm3
    )
    d_section_two = grad_out + d_ln_three
    d_cross = d_section_two.astype(jnp.bfloat16)
    grad_out_two = part_grad(d_cross, flat_two)
    d_att_two = dot(d_cross, full_out2).astype(jnp.bfloat16).reshape(seq_len, HEADS, HD)
    d_query_full, d_key_full, d_value_full = attend_back(
        query_two, key_two, value_two, log_two, d_att_two
    )
    d_query_two = d_query_full.reshape(seq_len, D).astype(jnp.bfloat16)
    d_kv_two = jnp.concatenate(
        [d_key_full.reshape(NC, D), d_value_full.reshape(NC, D)], axis=1
    ).astype(jnp.bfloat16)
    grad_query_two = part_grad(d_query_two, act_two)
    grad_kv_two = part_grad(d_kv_two, cond_rows)
    d_norm2 = dot(d_query_two, full_query2)
    d_ln_two, d_gain_two, d_shift_two = norm_back(section_one, gain_two, shift_two, d_norm2)
    d_section_one = d_section_two + d_ln_two
    d_attn = d_section_one.astype(jnp.bfloat16)
    grad_out_one = part_grad(d_attn, flat_one)
    d_att = dot(d_attn, full_out).astype(jnp.bfloat16).reshape(seq_len, HEADS, HD)
    d_query, d_key, d_value = attend_back(queries, key_heads, value_heads, log_one, d_att)
    d_qkv = jnp.concatenate(
        [
            rotate(d_query, cosine, -sin_table).reshape(seq_len, D),
            rotate(d_key, cosine, -sin_table).reshape(seq_len, D),
            d_value.reshape(seq_len, D),
        ],
        axis=1,
    ).astype(jnp.bfloat16)
    grad_qkv = part_grad(d_qkv, act_one)
    d_norm1 = dot(d_qkv, full_qkv)
    d_ln_one, d_gain_one, d_shift_one = norm_back(tokens, gain_one, shift_one, d_norm1)
    d_tokens = d_section_one + d_ln_one
    norm_stack = jnp.stack(
        [d_gain_one, d_shift_one, d_gain_two, d_shift_two, d_gain_three, d_shift_three], axis=0
    ).astype(jnp.bfloat16)
    groups = lax.axis_size("grp")
    attention_parts = [grad_qkv, grad_out_one, grad_query_two, grad_out_two, grad_kv_two]
    if groups == 8 and lax.axis_size("rep") == 4:
        norm_part = jnp.swapaxes(norm_stack.reshape(6, groups, own_width), 0, 1)
        norm_part = norm_part.reshape(groups, 1, 6 * own_width)
        norm_part = jnp.pad(norm_part, ((0, 0), (0, CUT - 1), (0, D - 6 * own_width)))
        kv2_rows = grad_kv_two.shape[0] // groups // 2
        kv2_part = grad_kv_two.reshape(groups, 2, kv2_rows, D // 2)
        kv2_part = jnp.swapaxes(kv2_part, 1, 2).reshape(groups, kv2_rows, D)
        parts = attention_parts[:4] + [kv2_part, norm_part]
        parts = [p.reshape(2, 2, 2, -1, D) for p in parts]
        (total_a,) = reduce_all(parts, [])
        ends = []
        for p in parts:
            ends.append((ends[-1] if ends else 0) + p.shape[3])
        pieces = [total_a[e - p.shape[3] : e] for e, p in zip(ends, parts)]
        norm_total = pieces[5][0, : 6 * own_width].reshape(6, own_width)
        kv2_total = jnp.swapaxes(pieces[4].reshape(kv2_rows, 2, D // 2), 0, 1)
        pieces[4] = kv2_total.reshape(2 * kv2_rows, D // 2)
        attention_sums = pieces[:5]
    else:
        norm_total = lax.psum(norm_stack, ("grp", "rep"))
        norm_total = lax.dynamic_slice_in_dim(
            norm_total, lax.axis_index("grp") * own_width, own_width, axis=1
        )
        attention_sums = [
            lax.psum_scatter(g, "grp", scatter_dimension=0, tiled=True) for g in attention_parts
        ]
        attention_sums = [lax.psum(g, "rep") for g in attention_sums]
    norm_total = norm_total.astype(jnp.float32)
    grad_qkv, grad_out_one, grad_query_two, grad_out_two, grad_kv_two = (
        g.astype(jnp.float32) for g in attention_sums
    )
    grad_gate, grad_up, grad_down = (g.astype(jnp.float32) for g in ffn_sums)
    return (
        outputs[None],
        d_tokens[None],
        norm_total[0],
        norm_total[1],
        norm_total[2],
        norm_total[3],
        norm_total[4],
        norm_total[5],
        grad_qkv,
        grad_out_one,
        grad_query_two,
        grad_kv_two,
        grad_out_two,
        grad_gate,
        grad_up,
        grad_down,
    )


def solution(mesh):
    return jax.shard_map(
        per_device,
        mesh=mesh,
        in_specs=(
            P(("grp", "rep"), None, None),
            P(("grp", "rep"), None, None),
            P(("grp", "rep"), None),
            P(("grp", "rep")),
            P(("grp", "rep"), None, None),
            P("grp"),
            P("grp"),
            P("grp"),
            P("grp"),
            P("grp"),
            P("grp"),
            P("grp", None),
            P("grp", None),
            P("grp", None),
            P("grp", None),
            P("grp", None),
            P("grp", None),
            P("grp", None),
            P("grp", None),
        ),
        out_specs=(
            P(("grp", "rep"), None, None),
            P(("grp", "rep"), None, None),
            P("grp"),
            P("grp"),
            P("grp"),
            P("grp"),
            P("grp"),
            P("grp"),
            P("grp", None),
            P("grp", None),
            P("grp", None),
            P("grp", None),
            P("grp", None),
            P("grp", None),
            P("grp", None),
            P("grp", None),
        ),
        check_vma=False,
    )
```

```python
import functools
import math

import jax
import jax.numpy as jnp
from jax import lax
from jax.experimental import pallas as pl
from jax.experimental.pallas import tpu as pltpu
from jax.sharding import PartitionSpec as P

MESH = pl.DeviceIdType.MESH
VMEM_LIMIT = 63 * 1024 * 1024

D = 1536
HEADS = 24
HD = 64
NC = 130


epsilon = 1e-05
score_scale = 0.125


def layer_norm(tensor, gain, shift):
    center = tensor - jnp.mean(tensor, axis=-1, keepdims=True)
    spread = jnp.mean(center * center, axis=-1, keepdims=True)
    return center * lax.rsqrt(spread + epsilon) * gain + shift


def swiglu(gate_part, up_part):
    return jax.nn.silu(gate_part) * up_part


def swiglu_back(gate_part, up_part, d_hidden):
    _, pullback = jax.vjp(swiglu, gate_part, up_part)
    return pullback(d_hidden)


def dot_nt(left_side, right_side):
    return lax.dot_general(
        left_side, right_side, (((1,), (1,)), ((), ())), preferred_element_type=jnp.float32
    )


def dot_tn(left_side, right_side):
    return lax.dot_general(
        left_side, right_side, (((0,), (0,)), ((), ())), preferred_element_type=jnp.float32
    )


def dot(left_side, right_side):
    return jnp.dot(left_side, right_side, preferred_element_type=jnp.float32)


def turn_tables(positions):
    quarter = HD // 4
    frequency = jnp.exp(jnp.arange(quarter, dtype=jnp.float32) * (-math.log(10000.0) / quarter))
    turned = positions.astype(jnp.float32)[:, None] * frequency[None, :]
    cosine, sine = jnp.cos(turned), jnp.sin(turned)
    none, one = jnp.zeros_like(sine), jnp.ones_like(sine)

    def heads(*parts):
        return jnp.tile(jnp.concatenate(parts, axis=1), (1, 2))

    return (
        heads(cosine, cosine, one, one),
        heads(-sine, none, none, none),
        heads(none, sine, none, none),
    )


def meet(peers, lower=None, upper=None, rep_index=None):
    barrier = pltpu.get_barrier_semaphore()
    for peer in peers:
        pl.semaphore_signal(barrier, inc=1, device_id=peer, device_id_type=MESH)
    if lower is not None:

        @pl.when(rep_index > 0)
        def _():
            pl.semaphore_signal(barrier, inc=1, device_id=lower, device_id_type=MESH)

        @pl.when(rep_index < 3)
        def _():
            pl.semaphore_signal(barrier, inc=1, device_id=upper, device_id_type=MESH)

    expected = len(peers)
    if lower is not None:
        expected = expected + jnp.where(rep_index > 0, 1, 0) + jnp.where(rep_index < 3, 1, 0)
    pl.semaphore_wait(barrier, expected)


GATHER_WINDOW = 4


class Gather:
    def __init__(self, pieces, sources, fulls, send_sem, recv_sem, local_sem):
        self.pieces, self.sources, self.fulls = pieces, sources, fulls
        self.send_sem, self.recv_sem, self.local_sem = send_sem, recv_sem, local_sem
        self.total = sum(n for n, _ in pieces)
        self.steps = self.total + GATHER_WINDOW + 2
        self.me = me = lax.axis_index("grp")
        self.plane = plane = lax.axis_index("rep")
        first_bit = 2 + 2 * lax.rem(plane, 2)
        self.first, self.second, self.across = me ^ first_bit, me ^ (6 - first_bit), me ^ 6
        self.first_dev = (self.first, plane)
        self.second_dev = (self.second, plane)
        self.rep_dev = (me, plane ^ 1)
        self.mate_dev = (me ^ 1, plane)

    def start(self):
        meet([self.first_dev, self.second_dev, self.rep_dev, self.mate_dev])

    def own_copy(self, k):
        n, rows = self.pieces[k]
        row = pl.multiple_of(self.me * (n * rows), 16)
        return pltpu.make_async_copy(
            self.sources[k], self.fulls[k].at[pl.ds(row, n * rows)], self.local_sem.at[k]
        )

    def each(self, i, body):
        base = 0
        for k, (n, rows) in enumerate(self.pieces):

            @pl.when((i >= base) & (i < base + n))
            def _(k=k, rows=rows, base=base):
                body(k, (i - base) * rows)

            base += n

    def push(self, k, offset, i, owner, lane, device, own=False):
        n, rows = self.pieces[k]
        cut = pl.ds(pl.multiple_of(offset, 16), rows)
        place = self.fulls[k].at[pl.ds(pl.multiple_of(owner * (n * rows) + offset, 16), rows)]
        return pltpu.make_async_remote_copy(
            src_ref=self.sources[k].at[cut] if own else place,
            dst_ref=place,
            send_sem=self.send_sem.at[lane, i],
            recv_sem=self.recv_sem.at[lane, i],
            device_id=device,
            device_id_type=MESH,
        )

    def stage_own(self, i):
        def body(k, offset):
            self.push(k, offset, i, self.me, 0, self.first_dev, own=True).start()
            self.push(k, offset, i, self.me, 3, self.mate_dev, own=True).start()

        self.each(i, body)

    def stage_first(self, i):
        def body(k, offset):
            self.push(k, offset, i, self.first, 0, self.first_dev).wait_recv()
            self.push(k, offset, i, self.first, 1, self.second_dev).start()
            self.push(k, offset, i, self.first, 2, self.rep_dev).start()
            self.push(k, offset, i, self.first, 4, self.mate_dev).start()

        self.each(i, body)

    def stage_rest(self, i):
        def body(k, offset):
            self.push(k, offset, i, self.across, 1, self.second_dev).wait_recv()
            self.push(k, offset, i, self.across, 5, self.mate_dev).start()
            self.push(k, offset, i, self.second, 2, self.rep_dev).wait_recv()
            self.push(k, offset, i, self.second, 6, self.mate_dev).start()

        self.each(i, body)

    def step(self, t):
        for stage, lag in (
            (self.stage_own, 0),
            (self.stage_first, GATHER_WINDOW),
            (self.stage_rest, GATHER_WINDOW + 2),
        ):
            i = t - lag

            @pl.when((i >= 0) & (i < self.total))
            def _(stage=stage, i=i):
                stage(i)

    def run(self, first, last):
        def body(t, carry):
            self.step(t)
            return carry

        lax.fori_loop(first, last, body, 0)

    def need(self, k):
        base = sum(n for n, _ in self.pieces[:k])
        n, rows = self.pieces[k]

        def body(j, carry):
            for lane in (3, 4, 5, 6):
                self.push(k, j * rows, base + j, self.me, lane, self.mate_dev).wait_recv()
            return carry

        lax.fori_loop(0, n, body, 0)
        self.own_copy(k).wait()

    def finish(self):
        def sent(i, carry):
            def body(k, offset):
                self.push(k, offset, i, self.me, 0, self.first_dev, own=True).wait_send()
                self.push(k, offset, i, self.me, 3, self.mate_dev, own=True).wait_send()
                for lane in (1, 2, 4, 5, 6):
                    self.push(k, offset, i, self.first, lane, self.mate_dev).wait_send()

            self.each(i, body)
            return carry

        lax.fori_loop(0, self.total, sent, 0)


class Loads:
    steps = 0

    def __init__(self, sources, fulls, local_sem):
        self.sources, self.fulls, self.local_sem = sources, fulls, local_sem

    def start(self):
        pass

    def own_copy(self, k):
        return pltpu.make_async_copy(self.sources[k], self.fulls[k], self.local_sem.at[k])

    def step(self, t):
        pass

    def run(self, first, last):
        pass

    def need(self, k):
        self.own_copy(k).wait()

    def finish(self):
        pass


CUT = 48
FCUT = 96
MATE_SLOTS = 6
OWN_SLOTS = 3
SUM_SLOTS = 8
FFN_SLOTS = 12


def reduce_kernel(pieces, ffn_pieces, *refs):
    count = len(pieces)
    parts = refs[:count]
    ffn_count = sum(ffn_pieces)
    ffn = refs[count : count + len(ffn_pieces)]
    refs = refs[len(ffn) :]
    out_a = refs[count]
    out_f = refs[count + 1] if ffn_count else None
    refs = refs[count + (2 if ffn_count else 1) :]
    (
        mate_buf,
        own_buf,
        sums,
        one_buf,
        two_buf,
        done,
        ffn_buf,
        low_a,
        up_a,
        low_f,
        up_f,
        mate_send,
        mate_recv,
        own_sem,
        one_send,
        one_recv,
        two_send,
        two_recv,
        ffn_sem,
        chain_send,
        chain_recv,
        out_sem,
        credit,
    ) = refs
    me = lax.axis_index("grp")
    plane = lax.axis_index("rep")
    core = lax.rem(me, 2)
    x = lax.rem(me // 2, 2)
    y = me // 4
    mate_dev = (me ^ 1, plane)
    x_dev = (me ^ 2, plane)
    y_dev = (me ^ 4, plane)
    low_dev = (me, plane - 1)
    up_dev = (me, plane + 1)
    meet([mate_dev, x_dev, y_dev], low_dev, up_dev, plane)
    total = sum(pieces)
    chain_total = ffn_count + total

    def each(i, body):
        base = 0
        for k, n in enumerate(pieces):

            @pl.when((i >= base) & (i < base + n))
            def _(k=k, base=base):
                body(k, pl.ds(pl.multiple_of((i - base) * CUT, 16), CUT))

            base += n

    def mate_copy(k, cut, slot):
        return pltpu.make_async_remote_copy(
            src_ref=parts[k].at[:, :, 1 - core, cut],
            dst_ref=mate_buf.at[slot],
            send_sem=mate_send.at[slot],
            recv_sem=mate_recv.at[slot],
            device_id=mate_dev,
            device_id_type=MESH,
        )

    def own_copy(k, cut, slot):
        return pltpu.make_async_copy(
            parts[k].at[:, :, core, cut], own_buf.at[slot], own_sem.at[slot]
        )

    def load(i):
        @pl.when(i >= MATE_SLOTS)
        def _():
            pl.semaphore_wait(credit, 1)
            mate_copy(0, pl.ds(0, CUT), lax.rem(i, MATE_SLOTS)).wait_send()

        def body(k, cut):
            mate_copy(k, cut, lax.rem(i, MATE_SLOTS)).start()
            own_copy(k, cut, lax.rem(i, OWN_SLOTS)).start()

        each(i, body)

    def one_copy(i, slot, by_x):
        return pltpu.make_async_remote_copy(
            src_ref=sums.at[slot, :, 1 - x] if by_x else sums.at[slot, 1 - y],
            dst_ref=one_buf.at[i],
            send_sem=one_send.at[slot],
            recv_sem=one_recv.at[i],
            device_id=x_dev if by_x else y_dev,
            device_id_type=MESH,
        )

    def two_copy(i, slot, by_x):
        return pltpu.make_async_remote_copy(
            src_ref=sums.at[slot, 1 - y, x] if by_x else sums.at[slot, y, 1 - x],
            dst_ref=two_buf.at[i],
            send_sem=two_send.at[slot],
            recv_sem=two_recv.at[i],
            device_id=y_dev if by_x else x_dev,
            device_id_type=MESH,
        )

    def either(i, body):
        @pl.when(lax.rem(i, 2) == 0)
        def _():
            body(True)

        @pl.when(lax.rem(i, 2) == 1)
        def _():
            body(False)

    def add(a, b):
        return (a.astype(jnp.float32) + b.astype(jnp.float32)).astype(jnp.bfloat16)

    def pair(i):
        mate_slot, own_slot, slot = (
            lax.rem(i, MATE_SLOTS),
            lax.rem(i, OWN_SLOTS),
            lax.rem(i, SUM_SLOTS),
        )
        mate_copy(0, pl.ds(0, CUT), mate_slot).wait_recv()
        own_copy(0, pl.ds(0, CUT), own_slot).wait()
        for u in range(2):
            for v in range(2):
                sums[slot, u, v] = add(own_buf[own_slot, u, v], mate_buf[mate_slot, u, v])

        @pl.when(i + MATE_SLOTS < total)
        def _():
            pl.semaphore_signal(credit, inc=1, device_id=mate_dev, device_id_type=MESH)

        either(i, lambda by_x: one_copy(i, slot, by_x).start())

    def plane_one(i):
        slot = lax.rem(i, SUM_SLOTS)

        def body(by_x):
            one_copy(i, slot, by_x).wait_recv()
            for u in range(2):
                if by_x:
                    sums[slot, u, x] = add(sums[slot, u, x], one_buf[i, u])
                else:
                    sums[slot, y, u] = add(sums[slot, y, u], one_buf[i, u])
            two_copy(i, slot, by_x).start()

        either(i, body)

    def plane_two(i):
        slot = lax.rem(i, SUM_SLOTS)

        def body(by_x):
            two_copy(i, slot, by_x).wait_recv()
            done[i] = add(sums[slot, y, x], two_buf[i])
            one_copy(i, slot, by_x).wait_send()
            two_copy(i, slot, by_x).wait_send()

        either(i, body)

    def ffn_load(j):
        base = 0
        for k, n in enumerate(ffn_pieces):

            @pl.when((j >= base) & (j < base + n))
            def _(k=k, base=base):
                row = pl.multiple_of((j - base) * FCUT, 16)
                pltpu.make_async_copy(
                    ffn[k].at[pl.ds(row, FCUT)],
                    ffn_buf.at[lax.rem(j, FFN_SLOTS)],
                    ffn_sem.at[lax.rem(j, FFN_SLOTS)],
                ).start()

            base += n

    def ffn_wait(j):
        pltpu.make_async_copy(
            ffn[0].at[pl.ds(0, FCUT)],
            ffn_buf.at[lax.rem(j, FFN_SLOTS)],
            ffn_sem.at[lax.rem(j, FFN_SLOTS)],
        ).wait()

    def views(j, is_ffn):
        if is_ffn:
            rows = pl.ds(pl.multiple_of(j * FCUT, 16), FCUT)
            return ffn_buf.at[lax.rem(j, FFN_SLOTS)], low_f.at[j], up_f.at[j], out_f.at[rows]
        i = j - ffn_count
        rows = pl.ds(pl.multiple_of(i * CUT, 16), CUT)
        return done.at[i], low_a.at[i], up_a.at[i], out_a.at[rows]

    def chain(j, lane, src, dst, device):
        return pltpu.make_async_remote_copy(
            src_ref=src,
            dst_ref=dst,
            send_sem=chain_send.at[lane, j],
            recv_sem=chain_recv.at[lane, j],
            device_id=device,
            device_id_type=MESH,
        )

    def kinds(j, body):
        if ffn_count:

            @pl.when(j < ffn_count)
            def _():
                body(*views(j, True))

        @pl.when(j >= ffn_count)
        def _():
            body(*views(j, False))

    def inward(j):
        if ffn_count:

            @pl.when(j < ffn_count)
            def _():
                ffn_wait(j)

        def body(mine, low, up, out):
            @pl.when(plane == 0)
            def _():
                chain(j, 0, mine, low, up_dev).start()

            @pl.when(plane == 3)
            def _():
                chain(j, 1, mine, up, low_dev).start()

        kinds(j, body)

    def middle(j):
        def body(mine, low, up, out):
            @pl.when(plane == 2)
            def _():
                chain(j, 1, mine, up, low_dev).wait_recv()
                mine[...] = add(mine[...], up[...])
                chain(j, 1, mine, up, low_dev).start()

        kinds(j, body)

    def root(j):
        def body(mine, low, up, out):
            @pl.when(plane == 1)
            def _():
                chain(j, 0, mine, low, up_dev).wait_recv()
                chain(j, 1, mine, up, low_dev).wait_recv()
                mine[...] = (
                    mine[...].astype(jnp.float32)
                    + low[...].astype(jnp.float32)
                    + up[...].astype(jnp.float32)
                ).astype(jnp.bfloat16)
                chain(j, 0, mine, out, up_dev).start()
                chain(j, 1, mine, out, low_dev).start()
                pltpu.make_async_copy(mine, out, out_sem.at[j]).start()

        kinds(j, body)

    def outward(j):
        def body(mine, low, up, out):
            @pl.when(plane == 2)
            def _():
                chain(j, 0, mine, out, up_dev).wait_recv()
                chain(j, 0, out, out, up_dev).start()

        kinds(j, body)

    def drain(j):
        def body(mine, low, up, out):
            @pl.when(plane == 0)
            def _():
                chain(j, 0, mine, low, up_dev).wait_send()
                chain(j, 1, mine, out, low_dev).wait_recv()

            @pl.when(plane == 3)
            def _():
                chain(j, 1, mine, up, low_dev).wait_send()
                chain(j, 0, mine, out, up_dev).wait_recv()

            @pl.when(plane == 1)
            def _():
                chain(j, 0, mine, out, up_dev).wait_send()
                chain(j, 1, mine, out, low_dev).wait_send()
                pltpu.make_async_copy(mine, out, out_sem.at[j]).wait()

            @pl.when(plane == 2)
            def _():
                chain(j, 1, mine, up, low_dev).wait_send()
                chain(j, 0, out, out, up_dev).wait_send()

        kinds(j, body)

    lag = max(1, 5 - ffn_count)
    stages = (
        (load, 0, total),
        (ffn_load, lag - 1, ffn_count),
        (pair, 1, total),
        (plane_one, 3, total),
        (plane_two, 5, total),
        (inward, lag, chain_total),
        (middle, lag + 2, chain_total),
        (root, lag + 4, chain_total),
        (outward, lag + 6, chain_total),
        (drain, lag + 8, chain_total),
    )

    def step(t, carry):
        for stage, behind, limit in stages:
            i = t - behind

            @pl.when((i >= 0) & (i < limit))
            def _(stage=stage, i=i):
                stage(i)

        return carry

    lax.fori_loop(0, chain_total + lag + 8, step, 0)
    for i in range(max(total - MATE_SLOTS, 0), total):
        mate_copy(0, pl.ds(0, CUT), i % MATE_SLOTS).wait_send()


def reduce_all(parts, ffn):
    pieces = tuple(p.shape[3] // CUT for p in parts)
    total = sum(pieces)
    wide = parts[0].shape[-1]
    ffn_rows = sum(f.shape[0] for f in ffn)
    ffn_pieces = tuple(f.shape[0] // FCUT for f in ffn)
    ffn_count = sum(ffn_pieces)
    chain_total = total + ffn_count
    hbm = pl.BlockSpec(memory_space=pltpu.HBM)
    low = jnp.bfloat16
    dma = pltpu.SemaphoreType.DMA
    return pl.pallas_call(
        functools.partial(reduce_kernel, pieces, ffn_pieces),
        out_shape=[
            jax.ShapeDtypeStruct((total * CUT, wide), low),
            jax.ShapeDtypeStruct((ffn_rows, wide), low),
        ][: 2 if ffn else 1],
        in_specs=[hbm] * (len(parts) + len(ffn)),
        out_specs=[hbm] * (2 if ffn else 1),
        scratch_shapes=[
            pltpu.VMEM((MATE_SLOTS, 2, 2, CUT, wide), low),
            pltpu.VMEM((OWN_SLOTS, 2, 2, CUT, wide), low),
            pltpu.VMEM((SUM_SLOTS, 2, 2, CUT, wide), low),
            pltpu.VMEM((total, 2, CUT, wide), low),
            pltpu.VMEM((total, CUT, wide), low),
            pltpu.VMEM((total, CUT, wide), low),
            pltpu.VMEM((FFN_SLOTS if ffn else 1, FCUT, wide), low),
            pltpu.VMEM((total, CUT, wide), low),
            pltpu.VMEM((total, CUT, wide), low),
            pltpu.VMEM((max(ffn_count, 1), FCUT, wide), low),
            pltpu.VMEM((max(ffn_count, 1), FCUT, wide), low),
            dma((MATE_SLOTS,)),
            dma((MATE_SLOTS,)),
            dma((OWN_SLOTS,)),
            dma((SUM_SLOTS,)),
            dma((total,)),
            dma((SUM_SLOTS,)),
            dma((total,)),
            dma((FFN_SLOTS,)),
            dma((2, chain_total)),
            dma((2, chain_total)),
            dma((chain_total,)),
            pltpu.SemaphoreType.REGULAR,
        ],
        compiler_params=pltpu.CompilerParams(
            collective_id=1, has_side_effects=True, vmem_limit_bytes=VMEM_LIMIT
        ),
    )(*parts, *ffn)


STEP_CHIP = (0, 0, 1, 2, 1, 2, 3, 3)
STEP_HALF = (0, 1, 0, 1, 1, 0, 0, 1)
TILE = 256


def ffn_kernel(
    act_in,
    cot_in,
    gate_in,
    up_in,
    down_in,
    out_ref,
    dn_ref,
    grad_gate,
    grad_up,
    grad_down,
    act,
    cot,
    w_gate,
    w_up,
    w_down,
    hidden,
    d_gate,
    d_up,
    pair,
    mine,
    stage,
    passed,
    final,
    tile_buf,
    weight_sem,
    cot_sem,
    own_sem,
    act_send,
    act_recv,
    pair_send,
    pair_recv,
    flow_send,
    flow_recv,
    tile_sem,
    end_sem,
):
    me = lax.axis_index("grp")
    plane = lax.axis_index("rep")
    mate_dev, x_dev, y_dev = (me ^ 1, plane), (me ^ 2, plane), (me ^ 4, plane)
    half = act.shape[2]
    seq_len = 2 * half
    rows, wide = w_gate.shape
    low = jnp.bfloat16
    meet([mate_dev, x_dev, y_dev])

    def remote(src, dst, send, recv, device):
        return pltpu.make_async_remote_copy(
            src_ref=src,
            dst_ref=dst,
            send_sem=send,
            recv_sem=recv,
            device_id=device,
            device_id_type=MESH,
        )

    own = [act_in.at[pl.ds(h * half, half)] for h in range(2)]

    def act_copy(t, other):
        if other:
            src, device = (own[t] if t < 2 else act.at[t, 0]), mate_dev
        else:
            src, device = {
                2: (own[0], x_dev),
                3: (own[1], y_dev),
                4: (own[1], x_dev),
                5: (own[0], y_dev),
                6: (act.at[2, 0], y_dev),
                7: (act.at[3, 0], x_dev),
            }[t]
        return remote(
            src, act.at[t, other], act_send.at[t, other], act_recv.at[t, other], device
        )

    for t in (2, 3, 4, 5):
        act_copy(t, 0).start()
    for t in (0, 1):
        act_copy(t, 1).start()
    own_copies = [pltpu.make_async_copy(own[t], act.at[t, 0], own_sem.at[t]) for t in range(2)]
    for copy in own_copies:
        copy.start()
    weights = [
        pltpu.make_async_copy(src, dst, weight_sem.at[k])
        for k, (src, dst) in enumerate(((gate_in, w_gate), (up_in, w_up), (down_in, w_down)))
    ]
    for copy in weights:
        copy.start()
    cot_copies = []
    for t in range(8):
        for other in range(2):
            owner = me ^ (2 * STEP_CHIP[t] + other)
            row = pl.multiple_of(owner * seq_len + STEP_HALF[t] * half, 16)
            copy = pltpu.make_async_copy(
                cot_in.at[pl.ds(row, half)], cot.at[t, other], cot_sem.at[t, other]
            )
            copy.start()
            cot_copies.append(copy)

    def pair_copy(kind, t):
        return remote(
            stage.at[kind], pair.at[kind, t], pair_send.at[kind], pair_recv.at[kind, t], mate_dev
        )

    def flow(kind, lane):
        src, dst, device = (
            (pair.at[kind, 2], final.at[kind, 0], x_dev),
            (pair.at[kind, 4], final.at[kind, 1], x_dev),
            (pair.at[kind, 5], final.at[kind, 2], y_dev),
            (pair.at[kind, 3], final.at[kind, 3], y_dev),
            (pair.at[kind, 6], passed.at[kind, 0], x_dev),
            (pair.at[kind, 7], passed.at[kind, 1], y_dev),
        )[lane]
        return remote(src, dst, flow_send.at[kind, lane], flow_recv.at[kind, lane], device)

    def add(*terms):
        total = terms[0].astype(jnp.float32)
        for term in terms[1:]:
            total = total + term.astype(jnp.float32)
        return total.astype(low)

    def forward_tiles(t):
        def tile(n, carry):
            cut = pl.ds(pl.multiple_of(n * TILE, TILE), TILE)
            tokens = act[t].reshape(seq_len, wide)
            gate = dot_nt(tokens, w_gate[cut])
            up = dot_nt(tokens, w_up[cut])
            d_hidden = dot_nt(cot[t].reshape(seq_len, wide), w_down[cut])
            sigmoid = 1.0 / (1.0 + jnp.exp(-gate))
            silu = gate * sigmoid
            hidden[t, :, cut] = (silu * up).astype(low)
            d_gate[t, :, cut] = (
                d_hidden * up * (sigmoid * (1.0 + gate * (1.0 - sigmoid)))
            ).astype(low)
            d_up[t, :, cut] = (d_hidden * silu).astype(low)
            return carry

        lax.fori_loop(0, rows // TILE, tile, 0)

    def backward_tiles(t):
        def tile(n, carry):
            cut = pl.ds(pl.multiple_of(n * TILE, TILE), TILE)
            out = dot(hidden[t], w_down[:, cut])
            mine[0, :, cut] = out[:half].astype(low)
            stage[0, :, cut] = out[half:].astype(low)
            dn = dot(d_gate[t], w_gate[:, cut]) + dot(d_up[t], w_up[:, cut])
            mine[1, :, cut] = dn[:half].astype(low)
            stage[1, :, cut] = dn[half:].astype(low)
            return carry

        lax.fori_loop(0, wide // TILE, tile, 0)

    def join(t, events):
        for kind in range(2):
            pair_copy(kind, t).wait()
            pair[kind, t] = add(pair[kind, t], mine[kind])
            for when, lane in events:
                if when is None:
                    flow(kind, lane).start()
                else:

                    @pl.when(t == when)
                    def _(kind=kind, lane=lane):
                        flow(kind, lane).start()

    for copy in own_copies + weights:
        copy.wait()

    def step(t, carry):
        for at in (2, 4, 6):

            @pl.when(t == at)
            def _(at=at):
                for u in (at, at + 1):
                    act_copy(u, 0).wait_recv()
                    if at == 2:
                        act_copy(u + 4, 0).start()
                    act_copy(u, 1).start()

        remote(
            act.at[t, 0], act.at[t, 1], act_send.at[t, 1], act_recv.at[t, 1], mate_dev
        ).wait_recv()
        for other in range(2):
            pltpu.make_async_copy(
                cot_in.at[pl.ds(0, half)], cot.at[t, other], cot_sem.at[t, other]
            ).wait()
        forward_tiles(t)

        @pl.when(t > 0)
        def _():
            join(t - 1, ((2, 0), (3, 3), (6, 4)))

        backward_tiles(t)
        for kind in range(2):
            pair_copy(kind, t).start()
        return carry

    lax.fori_loop(0, 8, step, 0)
    join(7, ((None, 5),))

    def write(target, slot, cut):
        return pltpu.make_async_copy(
            tile_buf.at[slot], target.at[:, cut], tile_sem.at[slot]
        )

    tiles = wide // TILE
    for k, (left, right, target) in enumerate(
        ((d_gate, act, grad_gate), (d_up, act, grad_up), (hidden, cot, grad_down))
    ):

        def tile(n, carry, k=k, left=left, right=right, target=target):
            cut = pl.ds(pl.multiple_of(n * TILE, TILE), TILE)
            slot = lax.rem(n, 2)

            @pl.when(k * tiles + n >= 2)
            def _():
                write(target, slot, cut).wait()

            tile_buf[slot] = dot_tn(
                left[...].reshape(8 * seq_len, rows),
                right[:, :, :, cut].reshape(8 * seq_len, TILE),
            ).astype(low)
            write(target, slot, cut).start()
            return carry

        lax.fori_loop(0, tiles, tile, 0)
    for slot in range(2):
        write(grad_down, slot, pl.ds(0, TILE)).wait()

    for kind in range(2):
        for lane, t, onward in ((4, 5, 2), (5, 4, 1)):
            flow(kind, lane).wait_recv()
            pair[kind, t] = add(pair[kind, t], passed[kind, lane - 4])
            flow(kind, onward).start()
    ends = []
    for kind, target in enumerate((out_ref, dn_ref)):
        for h in range(2):
            flow(kind, h).wait_recv()
            flow(kind, 2 + h).wait_recv()
            pair[kind, h] = add(pair[kind, h], final[kind, h], final[kind, 2 + h])
            copy = pltpu.make_async_copy(
                pair.at[kind, h], target.at[pl.ds(h * half, half)], end_sem.at[kind, h]
            )
            copy.start()
            ends.append(copy)
    for copy in ends:
        copy.wait()
    for kind in range(2):
        for lane in range(6):
            flow(kind, lane).wait_send()
    for t in range(8):
        act_copy(t, 1).wait_send()
        if t >= 2:
            act_copy(t, 0).wait_send()


def ffn_all(act, cot, w_gate, w_up, w_down):
    seq_len, wide = act.shape
    rows = w_gate.shape[0]
    half = seq_len // 2
    low = jnp.bfloat16
    hbm = pl.BlockSpec(memory_space=pltpu.HBM)
    dma = pltpu.SemaphoreType.DMA
    return pl.pallas_call(
        ffn_kernel,
        out_shape=[jax.ShapeDtypeStruct((seq_len, wide), low)] * 2
        + [jax.ShapeDtypeStruct((rows, wide), low)] * 3,
        in_specs=[hbm] * 5,
        out_specs=[hbm] * 5,
        scratch_shapes=[
            pltpu.VMEM((8, 2, half, wide), low),
            pltpu.VMEM((8, 2, half, wide), low),
            pltpu.VMEM((rows, wide), low),
            pltpu.VMEM((rows, wide), low),
            pltpu.VMEM((rows, wide), low),
            pltpu.VMEM((8, seq_len, rows), low),
            pltpu.VMEM((8, seq_len, rows), low),
            pltpu.VMEM((8, seq_len, rows), low),
            pltpu.VMEM((2, 8, half, wide), low),
            pltpu.VMEM((2, half, wide), low),
            pltpu.VMEM((2, half, wide), low),
            pltpu.VMEM((2, 2, half, wide), low),
            pltpu.VMEM((2, 4, half, wide), low),
            pltpu.VMEM((2, rows, TILE), low),
            dma((3,)),
            dma((8, 2)),
            dma((2,)),
            dma((8, 2)),
            dma((8, 2)),
            dma((2,)),
            dma((2, 8)),
            dma((2, 6)),
            dma((2, 6)),
            dma((2,)),
            dma((2, 2)),
        ],
        compiler_params=pltpu.CompilerParams(
            collective_id=2, has_side_effects=True, vmem_limit_bytes=VMEM_LIMIT
        ),
    )(act, cot, w_gate, w_up, w_down)


PAIR = 128
COND_ROWS = 256
NORM_ROWS = 32


def normalise(read, gain, shift, write, rows):
    def block(n, carry):
        cut = pl.ds(pl.multiple_of(n * NORM_ROWS, NORM_ROWS), NORM_ROWS)
        write[cut] = layer_norm(read[cut].astype(jnp.float32), gain[...], shift[...]).astype(
            write.dtype
        )
        return carry

    lax.fori_loop(0, rows // NORM_ROWS, block, 0)


def normalise_back(read, gain, d_read, straight, write, sums, row, rows):
    wide = read.shape[1]

    def block(n, carry):
        d_gain, d_shift = carry
        cut = pl.ds(pl.multiple_of(n * NORM_ROWS, NORM_ROWS), NORM_ROWS)
        tensor = read[cut].astype(jnp.float32)
        center = tensor - jnp.mean(tensor, axis=-1, keepdims=True)
        spread = jnp.mean(center * center, axis=-1, keepdims=True)
        inverse = lax.rsqrt(spread + epsilon)
        hat = center * inverse
        d_out = d_read[cut].astype(jnp.float32)
        scaled = d_out * gain[...]
        dv = inverse * (
            scaled
            - jnp.mean(scaled, axis=-1, keepdims=True)
            - hat * jnp.mean(scaled * hat, axis=-1, keepdims=True)
        )
        write[cut] = straight[cut].astype(jnp.float32) + dv
        d_gain = d_gain + jnp.sum((d_out * hat).reshape(NORM_ROWS // 8, 8, wide), axis=0)
        d_shift = d_shift + jnp.sum(d_out.reshape(NORM_ROWS // 8, 8, wide), axis=0)
        return d_gain, d_shift

    zero = jnp.zeros((8, wide), jnp.float32)
    d_gain, d_shift = lax.fori_loop(0, rows // NORM_ROWS, block, (zero, zero))
    sums[row : row + 1] = jnp.sum(d_gain, axis=0, keepdims=True)
    sums[row + 1 : row + 2] = jnp.sum(d_shift, axis=0, keepdims=True)


def turn(tensor, cosine, sine_left, sine_right):
    return (
        tensor * cosine
        + pltpu.roll(tensor, PAIR - HD // 4, 1) * sine_left
        + pltpu.roll(tensor, HD // 4, 1) * sine_right
    )


def tiles_of(count, body):
    def step(n, carry):
        body(pl.ds(pl.multiple_of(n * TILE, TILE), TILE))
        return carry

    lax.fori_loop(0, count // TILE, step, 0)


def pair_loop(body):
    def step(p, carry):
        body(p, pl.multiple_of(p * PAIR, PAIR))
        return carry

    lax.fori_loop(0, HEADS * HD // PAIR, step, 0)


def first_head(rows):
    return lax.broadcasted_iota(jnp.int32, (rows, PAIR), 1) < HD


def head_softmax(query, key, mine, keys):
    scores = dot_nt(jnp.where(mine, query, jnp.zeros_like(query)), key) * score_scale
    if keys < key.shape[0]:
        lanes = lax.broadcasted_iota(jnp.int32, scores.shape, 1)
        scores = jnp.where(lanes < keys, scores, -1e30)
    shifted = jnp.exp(scores - jnp.max(scores, axis=-1, keepdims=True))
    return (shifted * (1.0 / jnp.sum(shifted, axis=-1, keepdims=True))).astype(jnp.bfloat16)


def attend_pair(query, key, value, keys, keep):
    mask = first_head(query.shape[0])
    results = []
    for head in range(2):
        probability = head_softmax(query, key, mask if head == 0 else ~mask, keys)
        keep(head, probability)
        results.append(dot(probability, value))
    return jnp.where(mask, results[0], results[1]).astype(jnp.bfloat16)


def attend_pair_back(query, key, value, grad, probabilities):
    mask, key_mask = first_head(query.shape[0]), first_head(key.shape[0])
    d_queries, d_keys, d_values = [], [], []
    for head in range(2):
        probability = probabilities[head]
        mine = mask if head == 0 else ~mask
        d_prob = dot_nt(jnp.where(mine, grad, jnp.zeros_like(grad)), value)
        wide = probability.astype(jnp.float32)
        inner = jnp.sum(wide * d_prob, axis=-1, keepdims=True)
        d_scores = (wide * (d_prob - inner)).astype(jnp.bfloat16)
        d_queries.append(dot(d_scores, key))
        d_keys.append(dot_tn(d_scores, query))
        d_values.append(dot_tn(probability, grad))
    return (
        jnp.where(mask, d_queries[0], d_queries[1]) * score_scale,
        jnp.where(key_mask, d_keys[0], d_keys[1]) * score_scale,
        jnp.where(key_mask, d_values[0], d_values[1]),
    )


def attention_forward_kernel(
    pieces,
    x_in,
    cond_in,
    cosine,
    sine_left,
    sine_right,
    norms_in,
    qkv_in,
    out_in,
    kv2_in,
    query2_in,
    out2_in,
    norms_out,
    qkv_out,
    out_out,
    query2_out,
    out2_out,
    act_one_out,
    heads_out,
    prob_out,
    flat_one_out,
    section_one_out,
    act_two_out,
    query_two_out,
    kv_two_out,
    prob_two_out,
    flat_two_out,
    section_two_out,
    act_three_out,
    x,
    cond,
    norm_parts,
    w_qkv,
    w_out,
    w_kv2,
    w_query2,
    w_out2,
    act,
    heads,
    flat,
    section,
    query_two,
    kv_two,
    prob,
    prob_two,
    in_sem,
    out_sem,
    prob_sem,
    local_sem,
    *gather_sems,
):
    rows, wide = x.shape
    low = jnp.bfloat16
    sources = (norms_in, qkv_in, out_in, kv2_in, query2_in, out2_in)
    fulls = (norm_parts, w_qkv, w_out, w_kv2, w_query2, w_out2)
    if pieces is None:
        gather = Loads(sources, fulls, local_sem)
    else:
        gather = Gather(pieces, sources, fulls, *gather_sems, local_sem)
    gather.start()
    loads = []
    for k, (src, dst) in enumerate(((x_in, x), (cond_in, cond))):
        loads.append(pltpu.make_async_copy(src, dst, in_sem.at[k]))
        loads[-1].start()
    for k in range(len(sources)):
        gather.own_copy(k).start()
    stores = []

    def save(src, dst):
        stores.append(pltpu.make_async_copy(src, dst, out_sem.at[len(stores)]))
        stores[-1].start()
        return stores[-1]

    lead = GATHER_WINDOW + 2
    gather.run(0, 1 + lead)
    loads[0].wait()
    gather.need(0)
    norms_out[...] = jnp.sum(
        norm_parts[...].astype(jnp.float32).reshape(norm_parts.shape[0] // 16, 16, wide), axis=0
    )
    gains = [norms_out.at[pl.ds(k, 1)] for k in range(6)]
    normalise(x, gains[0], gains[1], act, rows)
    act_one_done = save(act, act_one_out)
    done = 13 + lead
    gather.run(1 + lead, done)
    gather.need(1)
    save(w_qkv, qkv_out)

    def project(cut, rotated):
        result = dot_nt(act[...], w_qkv[cut])
        for part in range(TILE // PAIR):
            piece = result[:, part * PAIR : (part + 1) * PAIR]
            if rotated:
                piece = turn(piece, cosine[...], sine_left[...], sine_right[...])
            heads[:, pl.ds(pl.multiple_of(cut.start + part * PAIR, PAIR), PAIR)] = piece.astype(low)

    for part in range(3):
        tiles_of(
            wide,
            lambda cut, part=part: project(
                pl.ds(pl.multiple_of(cut.start + part * wide, TILE), TILE), part < 2
            ),
        )
        gather.step(done + part)
    done += 3
    save(heads, heads_out)

    def prob_copy(buf, out, p, slot):
        return pltpu.make_async_copy(buf.at[slot], out.at[p], prob_sem.at[slot])

    def self_pair(p, lane):
        slot = lax.rem(p, 2)

        @pl.when(p >= 2)
        def _():
            prob_copy(prob, prob_out, p, slot).wait()

        def keep(head, probability):
            prob[slot, head] = probability

        cols = [pl.ds(pl.multiple_of(lane + k * wide, PAIR), PAIR) for k in range(3)]
        flat[:, cols[0]] = attend_pair(
            heads[:, cols[0]], heads[:, cols[1]], heads[:, cols[2]], rows, keep
        )
        prob_copy(prob, prob_out, p, slot).start()
        serve(p, SELF_EVERY)

    def serve(p, every):
        if gather.steps:

            @pl.when(lax.rem(p, every) == every - 1)
            def _():
                gather.step(done + p // every)

    pairs = wide // PAIR
    pair_loop(self_pair)
    done += pairs // SELF_EVERY
    for slot in range(2):
        prob_copy(prob, prob_out, 0, slot).wait()
    flat_one_done = save(flat, flat_one_out)
    gather.run(done, 17 + lead)
    done = max(done, 17 + lead)
    gather.need(2)
    save(w_out, out_out)

    def first_section(cut):
        section[:, cut] = x[:, cut].astype(jnp.float32) + dot_nt(flat[...], w_out[cut])

    tiles_of(wide, first_section)
    section_one_done = save(section, section_one_out)
    gather.run(done, 21 + lead)
    gather.step(max(done, 21 + lead))
    done = max(done, 21 + lead) + 1
    act_one_done.wait()
    normalise(section, gains[2], gains[3], act, rows)
    act_two_done = save(act, act_two_out)
    loads[1].wait()
    gather.need(3)

    def condition(cut):
        kv_two[:, cut] = dot_nt(cond[...], w_kv2[cut]).astype(low)

    tiles_of(2 * wide, condition)
    save(kv_two, kv_two_out)
    gather.run(done, 25 + lead)
    done = max(done, 25 + lead)
    gather.need(4)
    save(w_query2, query2_out)

    def query(cut):
        query_two[:, cut] = dot_nt(act[...], w_query2[cut]).astype(low)

    tiles_of(wide, query)
    save(query_two, query_two_out)
    flat_one_done.wait()

    def cross_pair(p, lane):
        slot = lax.rem(p, 2)

        @pl.when(p >= 2)
        def _():
            prob_copy(prob_two, prob_two_out, p, slot).wait()

        def keep(head, probability):
            prob_two[slot, head] = probability

        cols = [pl.ds(pl.multiple_of(lane + k * wide, PAIR), PAIR) for k in range(2)]
        flat[:, cols[0]] = attend_pair(
            query_two[:, cols[0]], kv_two[:, cols[0]], kv_two[:, cols[1]], NC, keep
        )
        prob_copy(prob_two, prob_two_out, p, slot).start()
        serve(p, CROSS_EVERY)

    pair_loop(cross_pair)
    done += pairs // CROSS_EVERY
    gather.run(done, 29 + lead)
    for slot in range(2):
        prob_copy(prob_two, prob_two_out, 0, slot).wait()
    save(flat, flat_two_out)
    gather.need(5)
    save(w_out2, out2_out)
    section_one_done.wait()

    def second_section(cut):
        section[:, cut] = section[:, cut] + dot_nt(flat[...], w_out2[cut])

    tiles_of(wide, second_section)
    save(section, section_two_out)
    act_two_done.wait()
    normalise(section, gains[4], gains[5], act, rows)
    save(act, act_three_out)
    waited = [id(c) for c in (act_one_done, flat_one_done, section_one_done, act_two_done)]
    gather.finish()
    for copy in stores:
        if id(copy) not in waited:
            copy.wait()


SELF_EVERY = 2
CROSS_EVERY = 3


def attention_forward(x, cond, tables, norms, weights):
    rows, wide = x.shape
    low, full = jnp.bfloat16, jnp.float32
    pairs = wide // PAIR
    hbm = pl.BlockSpec(memory_space=pltpu.HBM)
    vmem = pl.BlockSpec(memory_space=pltpu.VMEM)
    dma = pltpu.SemaphoreType.DMA
    shape = jax.ShapeDtypeStruct
    groups = lax.axis_size("grp")
    parameters = [norms] + list(weights)
    whole = [(groups * w.shape[0], w.shape[1]) for w in parameters]
    sems = []
    pieces = None
    options = {}
    if groups == 8 and lax.axis_size("rep") % 2 == 0:
        piece_rows = (16, 48, 48, 96, 48, 48)
        pieces = tuple((w.shape[0] // n, n) for w, n in zip(parameters, piece_rows))
        total = sum(n for n, _ in pieces)
        sems = [dma((7, total)), dma((7, total))]
        options = dict(collective_id=0, has_side_effects=True)
    else:
        parameters = [lax.all_gather(w, "grp", axis=0, tiled=True) for w in parameters]
    results = pl.pallas_call(
        functools.partial(attention_forward_kernel, pieces),
        out_shape=[
            shape((16, wide), full),
            *[shape(whole[k], low) for k in (1, 2, 4, 5)],
            shape((rows, wide), low),
            shape((rows, 3 * wide), low),
            shape((pairs, 2, rows, rows), low),
            shape((rows, wide), low),
            shape((rows, wide), full),
            shape((rows, wide), low),
            shape((rows, wide), low),
            shape((COND_ROWS, 2 * wide), low),
            shape((pairs, 2, rows, COND_ROWS), low),
            shape((rows, wide), low),
            shape((rows, wide), full),
            shape((rows, wide), low),
        ],
        in_specs=[hbm, hbm] + [vmem] * 3 + [hbm] * 6,
        out_specs=[vmem] + [hbm] * 16,
        scratch_shapes=[
            pltpu.VMEM((rows, wide), low),
            pltpu.VMEM(cond.shape, low),
            *[pltpu.VMEM(s, low) for s in whole],
            pltpu.VMEM((rows, wide), low),
            pltpu.VMEM((rows, 3 * wide), low),
            pltpu.VMEM((rows, wide), low),
            pltpu.VMEM((rows, wide), full),
            pltpu.VMEM((rows, wide), low),
            pltpu.VMEM((COND_ROWS, 2 * wide), low),
            pltpu.VMEM((2, 2, rows, rows), low),
            pltpu.VMEM((2, 2, rows, COND_ROWS), low),
            dma((2,)),
            dma((14,)),
            dma((2,)),
            dma((6,)),
            *sems,
        ],
        compiler_params=pltpu.CompilerParams(vmem_limit_bytes=VMEM_LIMIT, **options),
    )(x, cond, *tables, *parameters)
    return results[0], results[1:5], results[5:]


def attention_backward_kernel(
    x_in,
    cond_in,
    norms,
    cosine,
    sine_left,
    sine_right,
    qkv_in,
    out_in,
    query2_in,
    out2_in,
    act_one_in,
    heads_in,
    prob_in,
    flat_one_in,
    section_one_in,
    act_two_in,
    query_two_in,
    kv_two_in,
    prob_two_in,
    flat_two_in,
    section_two_in,
    d_norm_in,
    d_out_in,
    d_inputs_out,
    sums,
    grad_qkv,
    grad_out,
    grad_query2,
    grad_out2,
    grad_kv2,
    w_qkv,
    w_out,
    w_query2,
    w_out2,
    x,
    cond,
    act_one,
    heads,
    flat_one,
    section_one,
    act_two,
    query_two,
    kv_two,
    flat_two,
    section_two,
    d_norm,
    d_low,
    d_heads,
    d_kv,
    d_att,
    prob,
    prob_two,
    grad_buf,
    in_sem,
    prob_sem,
    grad_sem,
    end_sem,
):
    rows, wide = x.shape
    low = jnp.bfloat16
    loads = {}
    for k, (name, src, dst) in enumerate(
        (
            ("section_two", section_two_in, section_two),
            ("d_norm", d_norm_in, d_norm),
            ("d_out", d_out_in, d_low),
            ("w_out2", out2_in, w_out2),
            ("flat_two", flat_two_in, flat_two),
            ("query_two", query_two_in, query_two),
            ("kv_two", kv_two_in, kv_two),
            ("cond", cond_in, cond),
            ("act_two", act_two_in, act_two),
            ("w_query2", query2_in, w_query2),
            ("section_one", section_one_in, section_one),
            ("w_out", out_in, w_out),
            ("flat_one", flat_one_in, flat_one),
            ("heads", heads_in, heads),
            ("act_one", act_one_in, act_one),
            ("x", x_in, x),
            ("w_qkv", qkv_in, w_qkv),
        )
    ):
        loads[name] = pltpu.make_async_copy(src, dst, in_sem.at[k])
        loads[name].start()

    def need(*names):
        for name in names:
            loads[name].wait()

    gains = [norms.at[pl.ds(2 * k, 1)] for k in range(3)]

    def prob_copy(src, buf, p, slot):
        return pltpu.make_async_copy(src.at[p], buf.at[slot], prob_sem.at[slot])

    def prob_start(src, buf):
        for p in range(2):
            prob_copy(src, buf, p, p).start()

    pairs = wide // PAIR
    used = [0]

    def grad_copy(target, cut, slot):
        return pltpu.make_async_copy(grad_buf.at[slot], target.at[cut], grad_sem.at[slot])

    def weight_rows(left, right, target, count):
        before = used[0]

        def step(n, carry):
            cut = pl.ds(pl.multiple_of(n * TILE, TILE), TILE)
            slot = lax.rem(n + before, 2)

            @pl.when(n + before >= 2)
            def _():
                grad_copy(target, cut, slot).wait()

            columns = left[:, cut]
            for m in range(wide // 512):
                piece = slice(m * 512, (m + 1) * 512)
                grad_buf[slot, :, piece] = dot_tn(columns, right[:, piece]).astype(low)
            grad_copy(target, cut, slot).start()
            return carry

        lax.fori_loop(0, count // TILE, step, 0)
        used[0] = before + count // TILE

    prob_start(prob_two_in, prob_two)
    need("section_two", "d_norm", "d_out")
    normalise_back(section_two, gains[2], d_norm, d_low, section_two, sums, 4, rows)
    d_section = section_two

    def round_rows():
        def block(n, carry):
            cut = pl.ds(pl.multiple_of(n * NORM_ROWS, NORM_ROWS), NORM_ROWS)
            d_low[cut] = d_section[cut].astype(low)
            return carry

        lax.fori_loop(0, rows // NORM_ROWS, block, 0)

    round_rows()
    need("w_out2")

    def through(weight):
        def body(cut):
            d_att[:, cut] = dot(d_low[...], weight[:, cut]).astype(low)

        tiles_of(wide, body)

    through(w_out2)
    need("flat_two")
    weight_rows(d_low, flat_two, grad_out2, wide)
    need("query_two", "kv_two")

    def cross_pair(p, lane):
        slot = lax.rem(p, 2)
        prob_copy(prob_two_in, prob_two, p, slot).wait()
        cols = [pl.ds(pl.multiple_of(lane + k * wide, PAIR), PAIR) for k in range(2)]
        d_query, d_key, d_value = attend_pair_back(
            query_two[:, cols[0]],
            kv_two[:, cols[0]],
            kv_two[:, cols[1]],
            d_att[:, cols[0]],
            [prob_two[slot, head] for head in range(2)],
        )
        d_low[:, cols[0]] = d_query.astype(low)
        d_kv[:, cols[0]] = d_key.astype(low)
        d_kv[:, cols[1]] = d_value.astype(low)

        @pl.when(p + 2 < pairs)
        def _():
            prob_copy(prob_two_in, prob_two, p + 2, slot).start()

    pair_loop(cross_pair)
    prob_start(prob_in, prob)
    need("w_query2")

    def second_norm(cut):
        d_norm[:, cut] = dot(d_low[...], w_query2[:, cut]).astype(low)

    tiles_of(wide, second_norm)
    need("act_two")
    weight_rows(d_low, act_two, grad_query2, wide)
    need("cond")
    blocks = 2 * wide // 384
    before = used[0]

    def cond_rows(n, carry):
        slot = lax.rem(n + before, 2)
        part = grad_buf.at[slot, pl.ds(0, 192)]
        copy = pltpu.make_async_copy(
            part, grad_kv2.at[pl.ds(pl.multiple_of(n * 192, 16), 192)], grad_sem.at[slot]
        )

        @pl.when(n < 2)
        def _():
            grad_copy(grad_qkv, pl.ds(0, TILE), slot).wait()

        @pl.when(n >= 2)
        def _():
            copy.wait()

        result = dot_tn(d_kv[:, pl.ds(pl.multiple_of(n * 384, 128), 384)], cond[...]).astype(low)
        grad_buf[slot, :192, : wide // 2] = result[:192]
        grad_buf[slot, :192, wide // 2 :] = result[192:]
        copy.start()
        return carry

    lax.fori_loop(0, blocks, cond_rows, 0)
    for slot in range(2):
        pltpu.make_async_copy(
            grad_buf.at[slot, pl.ds(0, 192)], grad_kv2.at[pl.ds(0, 192)], grad_sem.at[slot]
        ).wait()
    used[0] = 0
    need("section_one")
    normalise_back(section_one, gains[1], d_norm, d_section, d_section, sums, 2, rows)
    round_rows()
    need("w_out")
    through(w_out)
    need("flat_one")
    weight_rows(d_low, flat_one, grad_out, wide)
    need("heads")

    def self_pair(p, lane):
        slot = lax.rem(p, 2)
        prob_copy(prob_in, prob, p, slot).wait()
        cols = [pl.ds(pl.multiple_of(lane + k * wide, PAIR), PAIR) for k in range(3)]
        d_query, d_key, d_value = attend_pair_back(
            heads[:, cols[0]],
            heads[:, cols[1]],
            heads[:, cols[2]],
            d_att[:, cols[0]],
            [prob[slot, head] for head in range(2)],
        )
        back = (cosine[...], -sine_left[...], -sine_right[...])
        d_heads[:, cols[0]] = turn(d_query, *back).astype(low)
        d_heads[:, cols[1]] = turn(d_key, *back).astype(low)
        d_heads[:, cols[2]] = d_value.astype(low)

        @pl.when(p + 2 < pairs)
        def _():
            prob_copy(prob_in, prob, p + 2, slot).start()

    pair_loop(self_pair)
    need("act_one")
    weight_rows(d_heads, act_one, grad_qkv, 3 * wide)
    need("w_qkv")

    def first_norm(cut):
        d_norm[:, cut] = dot(d_heads[...], w_qkv[:, cut]).astype(low)

    tiles_of(wide, first_norm)
    need("x")
    normalise_back(x, gains[0], d_norm, d_section, d_section, sums, 0, rows)
    end = pltpu.make_async_copy(d_section, d_inputs_out, end_sem)
    end.start()
    for slot in range(2):
        grad_copy(grad_qkv, pl.ds(0, TILE), slot).wait()
    end.wait()


def attention_backward(x, cond, norms, tables, weights, kept, d_norm, d_out):
    rows, wide = x.shape
    low, full = jnp.bfloat16, jnp.float32
    hbm = pl.BlockSpec(memory_space=pltpu.HBM)
    vmem = pl.BlockSpec(memory_space=pltpu.VMEM)
    dma = pltpu.SemaphoreType.DMA
    shape = jax.ShapeDtypeStruct
    buf = lambda s, t=low: pltpu.VMEM(s, t)
    return pl.pallas_call(
        attention_backward_kernel,
        out_shape=[
            shape((rows, wide), full),
            shape((8, wide), full),
            shape((3 * wide, wide), low),
            shape((wide, wide), low),
            shape((wide, wide), low),
            shape((wide, wide), low),
            shape((wide, wide), low),
        ],
        in_specs=[hbm, hbm] + [vmem] * 4 + [hbm] * 17,
        out_specs=[hbm, vmem] + [hbm] * 5,
        scratch_shapes=[
            *[buf(w.shape) for w in weights],
            buf((rows, wide)),
            buf(cond.shape),
            buf((rows, wide)),
            buf((rows, 3 * wide)),
            buf((rows, wide)),
            buf((rows, wide), full),
            buf((rows, wide)),
            buf((rows, wide)),
            buf((COND_ROWS, 2 * wide)),
            buf((rows, wide)),
            buf((rows, wide), full),
            buf((rows, wide)),
            buf((rows, wide)),
            buf((rows, 3 * wide)),
            buf((COND_ROWS, 2 * wide)),
            buf((rows, wide)),
            buf((2, 2, rows, rows)),
            buf((2, 2, rows, COND_ROWS)),
            buf((2, TILE, wide)),
            dma((17,)),
            dma((2,)),
            dma((2,)),
            dma,
        ],
        compiler_params=pltpu.CompilerParams(vmem_limit_bytes=VMEM_LIMIT),
    )(x, cond, norms, *tables, *weights, *kept, d_norm, d_out)


def per_device(
    inputs,
    conditioning,
    positions,
    slot_valid,
    cotangent,
    norm1_gain,
    norm1_shift,
    norm2_gain,
    norm2_shift,
    norm3_gain,
    norm3_shift,
    w_qkv,
    w_out,
    w_query2,
    w_kv2,
    w_out2,
    w_gate,
    w_up,
    w_down,
):
    cond_rows = conditioning[0]
    norms = jnp.stack(
        [norm1_gain, norm1_shift, norm2_gain, norm2_shift, norm3_gain, norm3_shift], axis=0
    )
    own_width = norms.shape[1]
    norms = lax.dynamic_update_slice(
        jnp.zeros((16, D), norms.dtype), norms, (0, lax.axis_index("grp") * own_width)
    )
    grad_mlp = (cotangent[0].astype(jnp.float32) * slot_valid[0].astype(jnp.float32)).astype(
        jnp.bfloat16
    )
    all_grad = lax.all_gather(grad_mlp, "grp", axis=0, tiled=True)
    tables = turn_tables(positions[0])
    padded_cond = jnp.pad(cond_rows, ((0, COND_ROWS - NC), (0, 0)))
    norms, whole, kept = attention_forward(
        inputs[0], padded_cond, tables, norms, [w_qkv, w_out, w_kv2, w_query2, w_out2]
    )
    act_three, section_two = kept[-1], kept[-2]
    if lax.axis_size("grp") == 8:
        mlp_out, d_norm3, grad_gate, grad_up, grad_down = ffn_all(
            act_three, all_grad, w_gate, w_up, w_down
        )
    else:
        all_act = lax.all_gather(act_three, "grp", axis=0, tiled=True)
        gate_pre = dot_nt(all_act, w_gate)
        up_pre = dot_nt(all_act, w_up)
        hidden = swiglu(gate_pre, up_pre).astype(jnp.bfloat16)
        mlp_part = dot(hidden, w_down).astype(jnp.bfloat16)
        mlp_out = lax.psum_scatter(mlp_part, "grp", scatter_dimension=0, tiled=True)
        d_hidden = dot_nt(all_grad, w_down)
        d_gate_full, d_up_full = swiglu_back(gate_pre, up_pre, d_hidden)
        d_gate = d_gate_full.astype(jnp.bfloat16)
        d_up = d_up_full.astype(jnp.bfloat16)
        d_norm3_part = (dot(d_gate, w_gate) + dot(d_up, w_up)).astype(jnp.bfloat16)
        d_norm3 = lax.psum_scatter(d_norm3_part, "grp", scatter_dimension=0, tiled=True)
        grad_gate = dot_tn(d_gate, all_act).astype(jnp.bfloat16)
        grad_up = dot_tn(d_up, all_act).astype(jnp.bfloat16)
        grad_down = dot_tn(hidden, all_grad).astype(jnp.bfloat16)
    outputs = (section_two + mlp_out.astype(jnp.float32)).astype(jnp.bfloat16)
    ffn_sums = list(lax.psum((grad_gate, grad_up), "rep"))
    d_tokens, norm_sums, grad_qkv, grad_out_one, grad_query_two, grad_out_two, grad_kv_two = (
        attention_backward(
            inputs[0],
            padded_cond,
            norms,
            tables,
            whole,
            kept[:-1],
            d_norm3,
            grad_mlp,
        )
    )
    norm_stack = norm_sums[:6].astype(jnp.bfloat16)
    groups = lax.axis_size("grp")
    attention_parts = [grad_qkv, grad_out_one, grad_query_two, grad_out_two, grad_kv_two]
    if groups == 8 and lax.axis_size("rep") == 4:
        norm_part = jnp.swapaxes(norm_stack.reshape(6, groups, own_width), 0, 1)
        norm_part = norm_part.reshape(groups, 1, 6 * own_width)
        norm_part = jnp.pad(norm_part, ((0, 0), (0, CUT - 1), (0, D - 6 * own_width)))
        kv2_rows = grad_kv_two.shape[0] // groups
        parts = attention_parts + [norm_part]
        parts = [p.reshape(2, 2, 2, -1, D) for p in parts]
        total_a, total_f = reduce_all(parts, [grad_down])
        ffn_sums.append(total_f)
        ends = []
        for p in parts:
            ends.append((ends[-1] if ends else 0) + p.shape[3])
        pieces = [total_a[e - p.shape[3] : e] for e, p in zip(ends, parts)]
        norm_total = pieces[5][0, : 6 * own_width].reshape(6, own_width)
        kv2_total = jnp.swapaxes(pieces[4].reshape(kv2_rows, 2, D // 2), 0, 1)
        pieces[4] = kv2_total.reshape(2 * kv2_rows, D // 2)
        attention_sums = pieces[:5]
    else:
        kv2_part = jnp.swapaxes(grad_kv_two.reshape(-1, 192, 2, D // 2), 1, 2)
        attention_parts[4] = kv2_part.reshape(2 * D, D // 2)
        norm_total = lax.psum(norm_stack, ("grp", "rep"))
        norm_total = lax.dynamic_slice_in_dim(
            norm_total, lax.axis_index("grp") * own_width, own_width, axis=1
        )
        attention_sums = [
            lax.psum_scatter(g, "grp", scatter_dimension=0, tiled=True) for g in attention_parts
        ]
        attention_sums = [lax.psum(g, "rep") for g in attention_sums]
        ffn_sums.append(lax.psum(grad_down, "rep"))
    norm_total = norm_total.astype(jnp.float32)
    grad_qkv, grad_out_one, grad_query_two, grad_out_two, grad_kv_two = (
        g.astype(jnp.float32) for g in attention_sums
    )
    grad_gate, grad_up, grad_down = (g.astype(jnp.float32) for g in ffn_sums)
    return (
        outputs[None],
        d_tokens[None],
        norm_total[0],
        norm_total[1],
        norm_total[2],
        norm_total[3],
        norm_total[4],
        norm_total[5],
        grad_qkv,
        grad_out_one,
        grad_query_two,
        grad_kv_two,
        grad_out_two,
        grad_gate,
        grad_up,
        grad_down,
    )


def solution(mesh):
    return jax.shard_map(
        per_device,
        mesh=mesh,
        in_specs=(
            P(("grp", "rep"), None, None),
            P(("grp", "rep"), None, None),
            P(("grp", "rep"), None),
            P(("grp", "rep")),
            P(("grp", "rep"), None, None),
            P("grp"),
            P("grp"),
            P("grp"),
            P("grp"),
            P("grp"),
            P("grp"),
            P("grp", None),
            P("grp", None),
            P("grp", None),
            P("grp", None),
            P("grp", None),
            P("grp", None),
            P("grp", None),
            P("grp", None),
        ),
        out_specs=(
            P(("grp", "rep"), None, None),
            P(("grp", "rep"), None, None),
            P("grp"),
            P("grp"),
            P("grp"),
            P("grp"),
            P("grp"),
            P("grp"),
            P("grp", None),
            P("grp", None),
            P("grp", None),
            P("grp", None),
            P("grp", None),
            P("grp", None),
            P("grp", None),
            P("grp", None),
        ),
        check_vma=False,
    )
```

```python
import functools
import math

import jax
import jax.numpy as jnp
from jax import lax
from jax.experimental import pallas as pl
from jax.experimental.pallas import tpu as pltpu
from jax.sharding import PartitionSpec as P

MESH = pl.DeviceIdType.MESH
VMEM_LIMIT = 63 * 1024 * 1024

D = 1536
HEADS = 24
HD = 64
NC = 130


epsilon = 1e-05
score_scale = 0.125


def layer_norm(tensor, gain, shift):
    center = tensor - jnp.mean(tensor, axis=-1, keepdims=True)
    spread = jnp.mean(center * center, axis=-1, keepdims=True)
    return center * lax.rsqrt(spread + epsilon) * gain + shift


def swiglu(gate_part, up_part):
    return jax.nn.silu(gate_part) * up_part


def swiglu_back(gate_part, up_part, d_hidden):
    _, pullback = jax.vjp(swiglu, gate_part, up_part)
    return pullback(d_hidden)


def dot_nt(left_side, right_side):
    return lax.dot_general(
        left_side, right_side, (((1,), (1,)), ((), ())), preferred_element_type=jnp.float32
    )


def dot_tn(left_side, right_side):
    return lax.dot_general(
        left_side, right_side, (((0,), (0,)), ((), ())), preferred_element_type=jnp.float32
    )


def dot(left_side, right_side):
    return jnp.dot(left_side, right_side, preferred_element_type=jnp.float32)


def turn_tables(positions):
    quarter = HD // 4
    frequency = jnp.exp(jnp.arange(quarter, dtype=jnp.float32) * (-math.log(10000.0) / quarter))
    turned = positions.astype(jnp.float32)[:, None] * frequency[None, :]
    cosine, sine = jnp.cos(turned), jnp.sin(turned)
    none, one = jnp.zeros_like(sine), jnp.ones_like(sine)

    def heads(*parts):
        return jnp.tile(jnp.concatenate(parts, axis=1), (1, 2))

    return (
        heads(cosine, cosine, one, one),
        heads(-sine, none, none, none),
        heads(none, sine, none, none),
    )


def meet(peers, lower=None, upper=None, rep_index=None):
    barrier = pltpu.get_barrier_semaphore()
    for peer in peers:
        pl.semaphore_signal(barrier, inc=1, device_id=peer, device_id_type=MESH)
    if lower is not None:

        @pl.when(rep_index > 0)
        def _():
            pl.semaphore_signal(barrier, inc=1, device_id=lower, device_id_type=MESH)

        @pl.when(rep_index < 3)
        def _():
            pl.semaphore_signal(barrier, inc=1, device_id=upper, device_id_type=MESH)

    expected = len(peers)
    if lower is not None:
        expected = expected + jnp.where(rep_index > 0, 1, 0) + jnp.where(rep_index < 3, 1, 0)
    pl.semaphore_wait(barrier, expected)


GATHER_WINDOW = 4


class Gather:
    def __init__(self, pieces, sources, fulls, send_sem, recv_sem, local_sem):
        self.pieces, self.sources, self.fulls = pieces, sources, fulls
        self.send_sem, self.recv_sem, self.local_sem = send_sem, recv_sem, local_sem
        self.total = sum(n for n, _ in pieces)
        self.steps = self.total + GATHER_WINDOW + 2
        self.me = me = lax.axis_index("grp")
        self.plane = plane = lax.axis_index("rep")
        first_bit = 2 + 2 * lax.rem(plane, 2)
        self.first, self.second, self.across = me ^ first_bit, me ^ (6 - first_bit), me ^ 6
        self.first_dev = (self.first, plane)
        self.second_dev = (self.second, plane)
        self.rep_dev = (me, plane ^ 1)
        self.mate_dev = (me ^ 1, plane)

    def start(self):
        meet([self.first_dev, self.second_dev, self.rep_dev, self.mate_dev])

    def own_copy(self, k):
        n, rows = self.pieces[k]
        row = pl.multiple_of(self.me * (n * rows), 16)
        return pltpu.make_async_copy(
            self.sources[k], self.fulls[k].at[pl.ds(row, n * rows)], self.local_sem.at[k]
        )

    def each(self, i, body):
        base = 0
        for k, (n, rows) in enumerate(self.pieces):

            @pl.when((i >= base) & (i < base + n))
            def _(k=k, rows=rows, base=base):
                body(k, (i - base) * rows)

            base += n

    def push(self, k, offset, i, owner, lane, device, own=False):
        n, rows = self.pieces[k]
        cut = pl.ds(pl.multiple_of(offset, 16), rows)
        place = self.fulls[k].at[pl.ds(pl.multiple_of(owner * (n * rows) + offset, 16), rows)]
        return pltpu.make_async_remote_copy(
            src_ref=self.sources[k].at[cut] if own else place,
            dst_ref=place,
            send_sem=self.send_sem.at[lane, i],
            recv_sem=self.recv_sem.at[lane, i],
            device_id=device,
            device_id_type=MESH,
        )

    def stage_own(self, i):
        def body(k, offset):
            self.push(k, offset, i, self.me, 0, self.first_dev, own=True).start()
            self.push(k, offset, i, self.me, 3, self.mate_dev, own=True).start()

        self.each(i, body)

    def stage_first(self, i):
        def body(k, offset):
            self.push(k, offset, i, self.first, 0, self.first_dev).wait_recv()
            self.push(k, offset, i, self.first, 1, self.second_dev).start()
            self.push(k, offset, i, self.first, 2, self.rep_dev).start()
            self.push(k, offset, i, self.first, 4, self.mate_dev).start()

        self.each(i, body)

    def stage_rest(self, i):
        def body(k, offset):
            self.push(k, offset, i, self.across, 1, self.second_dev).wait_recv()
            self.push(k, offset, i, self.across, 5, self.mate_dev).start()
            self.push(k, offset, i, self.second, 2, self.rep_dev).wait_recv()
            self.push(k, offset, i, self.second, 6, self.mate_dev).start()

        self.each(i, body)

    def step(self, t):
        for stage, lag in (
            (self.stage_own, 0),
            (self.stage_first, GATHER_WINDOW),
            (self.stage_rest, GATHER_WINDOW + 2),
        ):
            i = t - lag

            @pl.when((i >= 0) & (i < self.total))
            def _(stage=stage, i=i):
                stage(i)

    def run(self, first, last):
        def body(t, carry):
            self.step(t)
            return carry

        lax.fori_loop(first, last, body, 0)

    def need(self, k):
        base = sum(n for n, _ in self.pieces[:k])
        n, rows = self.pieces[k]

        def body(j, carry):
            for lane in (3, 4, 5, 6):
                self.push(k, j * rows, base + j, self.me, lane, self.mate_dev).wait_recv()
            return carry

        lax.fori_loop(0, n, body, 0)
        self.own_copy(k).wait()

    def finish(self):
        def sent(i, carry):
            def body(k, offset):
                self.push(k, offset, i, self.me, 0, self.first_dev, own=True).wait_send()
                self.push(k, offset, i, self.me, 3, self.mate_dev, own=True).wait_send()
                for lane in (1, 2, 4, 5, 6):
                    self.push(k, offset, i, self.first, lane, self.mate_dev).wait_send()

            self.each(i, body)
            return carry

        lax.fori_loop(0, self.total, sent, 0)


class Loads:
    steps = 0

    def __init__(self, sources, fulls, local_sem):
        self.sources, self.fulls, self.local_sem = sources, fulls, local_sem

    def start(self):
        pass

    def own_copy(self, k):
        return pltpu.make_async_copy(self.sources[k], self.fulls[k], self.local_sem.at[k])

    def step(self, t):
        pass

    def run(self, first, last):
        pass

    def need(self, k):
        self.own_copy(k).wait()

    def finish(self):
        pass


CUT = 48
FCUT = 64
UNIT = 192
MATE_SLOTS = 4
OWN_SLOTS = 2
SUM_SLOTS = 9
FFN_SLOTS = 14
LAND_SLOTS = 3


class Sums:
    def __init__(self, pieces, ffn_pieces, parts, ffn, outs, lands, bufs, sems):
        self.pieces, self.ffn_pieces, self.parts, self.ffn = pieces, ffn_pieces, parts, ffn
        self.out_a, self.out_f = outs
        self.one_land, self.two_land, self.low_a, self.up_a, self.low_f, self.up_f = lands
        (
            self.mate_buf,
            self.own_buf,
            self.sums,
            self.done,
            self.ffn_buf,
            self.one_buf,
            self.two_buf,
            self.low_buf,
            self.up_buf,
        ) = bufs
        (
            self.mate_send,
            self.mate_recv,
            self.own_sem,
            self.one_send,
            self.one_recv,
            self.one_sem,
            self.two_send,
            self.two_recv,
            self.two_sem,
            self.ffn_sem,
            self.chain_send,
            self.chain_recv,
            self.low_sem,
            self.up_sem,
            self.out_sem,
            self.credit,
        ) = sems
        me = lax.axis_index("grp")
        self.plane = plane = lax.axis_index("rep")
        self.core = lax.rem(me, 2)
        self.x = lax.rem(me // 2, 2)
        self.y = me // 4
        self.mate_dev = (me ^ 1, plane)
        self.x_dev = (me ^ 2, plane)
        self.y_dev = (me ^ 4, plane)
        self.low_dev = (me, plane - 1)
        self.up_dev = (me, plane + 1)
        self.total = sum(pieces)
        self.ffn_count = sum(ffn_pieces)
        self.chain_total = self.ffn_count + self.total

    def start(self):
        meet([self.mate_dev, self.x_dev, self.y_dev], self.low_dev, self.up_dev, self.plane)

    def each(self, i, body):
        base = 0
        for k, n in enumerate(self.pieces):

            @pl.when((i >= base) & (i < base + n))
            def _(k=k, base=base):
                body(k, pl.ds(pl.multiple_of((i - base) * CUT, 16), CUT))

            base += n

    def mate_copy(self, k, cut, slot):
        return pltpu.make_async_remote_copy(
            src_ref=self.parts[k].at[:, :, 1 - self.core, cut],
            dst_ref=self.mate_buf.at[slot],
            send_sem=self.mate_send.at[slot],
            recv_sem=self.mate_recv.at[slot],
            device_id=self.mate_dev,
            device_id_type=MESH,
        )

    def own_copy(self, k, cut, slot):
        return pltpu.make_async_copy(
            self.parts[k].at[:, :, self.core, cut], self.own_buf.at[slot], self.own_sem.at[slot]
        )

    def load(self, i):
        @pl.when(i >= MATE_SLOTS)
        def _():
            pl.semaphore_wait(self.credit, 1)
            self.mate_copy(0, pl.ds(0, CUT), lax.rem(i, MATE_SLOTS)).wait_send()

        def body(k, cut):
            self.mate_copy(k, cut, lax.rem(i, MATE_SLOTS)).start()
            self.own_copy(k, cut, lax.rem(i, OWN_SLOTS)).start()

        self.each(i, body)

    def one_copy(self, i, slot, by_x):
        return pltpu.make_async_remote_copy(
            src_ref=self.sums.at[slot, :, 1 - self.x] if by_x else self.sums.at[slot, 1 - self.y],
            dst_ref=self.one_land.at[i],
            send_sem=self.one_send.at[slot],
            recv_sem=self.one_recv.at[i],
            device_id=self.x_dev if by_x else self.y_dev,
            device_id_type=MESH,
        )

    def two_copy(self, i, slot, by_x):
        return pltpu.make_async_remote_copy(
            src_ref=self.sums.at[slot, 1 - self.y, self.x]
            if by_x
            else self.sums.at[slot, self.y, 1 - self.x],
            dst_ref=self.two_land.at[i],
            send_sem=self.two_send.at[slot],
            recv_sem=self.two_recv.at[i],
            device_id=self.y_dev if by_x else self.x_dev,
            device_id_type=MESH,
        )

    def either(self, i, body):
        @pl.when(lax.rem(i, 2) == 0)
        def _():
            body(True)

        @pl.when(lax.rem(i, 2) == 1)
        def _():
            body(False)

    def one_load(self, i):
        slot = lax.rem(i, LAND_SLOTS)
        return pltpu.make_async_copy(self.one_land.at[i], self.one_buf.at[slot], self.one_sem.at[slot])

    def two_load(self, i):
        slot = lax.rem(i, LAND_SLOTS)
        return pltpu.make_async_copy(self.two_land.at[i], self.two_buf.at[slot], self.two_sem.at[slot])

    def pair(self, i):
        mate_slot, own_slot = lax.rem(i, MATE_SLOTS), lax.rem(i, OWN_SLOTS)
        slot = lax.rem(i, SUM_SLOTS)
        self.mate_copy(0, pl.ds(0, CUT), mate_slot).wait_recv()
        self.own_copy(0, pl.ds(0, CUT), own_slot).wait()
        for u in range(2):
            for v in range(2):
                self.sums[slot, u, v] = add(
                    self.own_buf[own_slot, u, v], self.mate_buf[mate_slot, u, v]
                )

        @pl.when(i + MATE_SLOTS < self.total)
        def _():
            pl.semaphore_signal(
                self.credit, inc=1, device_id=self.mate_dev, device_id_type=MESH
            )

        self.either(i, lambda by_x: self.one_copy(i, slot, by_x).start())

    def one_arrives(self, i):
        self.either(i, lambda by_x: self.one_copy(i, lax.rem(i, SUM_SLOTS), by_x).wait_recv())
        self.one_load(i).start()

    def plane_one(self, i):
        slot, land = lax.rem(i, SUM_SLOTS), lax.rem(i, LAND_SLOTS)
        self.one_load(i).wait()

        def body(by_x):
            for u in range(2):
                at = (slot, u, self.x) if by_x else (slot, self.y, u)
                self.sums[at] = add(self.sums[at], self.one_buf[land, u])
            self.two_copy(i, slot, by_x).start()

        self.either(i, body)

    def two_arrives(self, i):
        self.either(i, lambda by_x: self.two_copy(i, lax.rem(i, SUM_SLOTS), by_x).wait_recv())
        self.two_load(i).start()

    def plane_two(self, i):
        slot = lax.rem(i, SUM_SLOTS)
        self.two_load(i).wait()
        self.done[i] = add(self.sums[slot, self.y, self.x], self.two_buf[lax.rem(i, LAND_SLOTS)])

        def body(by_x):
            self.one_copy(i, slot, by_x).wait_send()
            self.two_copy(i, slot, by_x).wait_send()

        self.either(i, body)

    def ffn_load(self, j):
        base = 0
        for k, n in enumerate(self.ffn_pieces):

            @pl.when((j >= base) & (j < base + n))
            def _(k=k, base=base):
                row = pl.multiple_of((j - base) * FCUT, 16)
                pltpu.make_async_copy(
                    self.ffn[k].at[pl.ds(row, FCUT)],
                    self.ffn_buf.at[lax.rem(j, FFN_SLOTS)],
                    self.ffn_sem.at[lax.rem(j, FFN_SLOTS)],
                ).start()

            base += n

    def ffn_wait(self, j):
        pltpu.make_async_copy(
            self.ffn[0].at[pl.ds(0, FCUT)],
            self.ffn_buf.at[lax.rem(j, FFN_SLOTS)],
            self.ffn_sem.at[lax.rem(j, FFN_SLOTS)],
        ).wait()

    def role(self, j, plane, body):
        slot = lax.rem(j, LAND_SLOTS)
        key = self.plane + jnp.where(j < self.ffn_count, 0, 4)
        key = jnp.where((j >= 0) & (j < self.chain_total), key, 8)

        @pl.when(key == plane)
        def _():
            rows = pl.ds(pl.multiple_of(j * FCUT, 16), FCUT)
            body(
                self.ffn_buf.at[lax.rem(j, FFN_SLOTS)],
                self.low_f.at[j],
                self.up_f.at[j],
                self.low_buf.at[slot],
                self.up_buf.at[slot],
                self.out_f.at[rows],
            )

        @pl.when(key == plane + 4)
        def _():
            i = j - self.ffn_count
            rows = pl.ds(pl.multiple_of(i * CUT, 16), CUT)
            part = pl.ds(0, CUT)
            body(
                self.done.at[i],
                self.low_a.at[i],
                self.up_a.at[i],
                self.low_buf.at[slot, part],
                self.up_buf.at[slot, part],
                self.out_a.at[rows],
            )

    def chain(self, j, lane, src, dst, device):
        return pltpu.make_async_remote_copy(
            src_ref=src,
            dst_ref=dst,
            send_sem=self.chain_send.at[lane, j],
            recv_sem=self.chain_recv.at[lane, j],
            device_id=device,
            device_id_type=MESH,
        )

    def low_load(self, j, land, buf):
        return pltpu.make_async_copy(land, buf, self.low_sem.at[lax.rem(j, LAND_SLOTS)])

    def up_load(self, j, land, buf):
        return pltpu.make_async_copy(land, buf, self.up_sem.at[lax.rem(j, LAND_SLOTS)])

    def inward(self, j):
        @pl.when((j >= 0) & (j < self.ffn_count))
        def _():
            self.ffn_wait(j)

        def lowest(mine, low, up, low_buf, up_buf, out):
            self.chain(j, 0, mine, low, self.up_dev).start()

        def highest(mine, low, up, low_buf, up_buf, out):
            self.chain(j, 1, mine, up, self.low_dev).start()

        self.role(j, 0, lowest)
        self.role(j, 3, highest)

    def middle_arrives(self, j):
        def body(mine, low, up, low_buf, up_buf, out):
            self.chain(j, 1, mine, up, self.low_dev).wait_recv()
            self.up_load(j, up, up_buf).start()

        self.role(j, 2, body)

    def middle(self, j):
        def body(mine, low, up, low_buf, up_buf, out):
            self.up_load(j, up, up_buf).wait()
            mine[...] = add(mine[...], up_buf[...])
            self.chain(j, 1, mine, up, self.low_dev).start()

        self.role(j, 2, body)

    def root_arrives(self, j):
        def body(mine, low, up, low_buf, up_buf, out):
            self.chain(j, 0, mine, low, self.up_dev).wait_recv()
            self.low_load(j, low, low_buf).start()
            self.chain(j, 1, mine, up, self.low_dev).wait_recv()
            self.up_load(j, up, up_buf).start()

        self.role(j, 1, body)

    def root(self, j):
        def body(mine, low, up, low_buf, up_buf, out):
            self.low_load(j, low, low_buf).wait()
            self.up_load(j, up, up_buf).wait()
            mine[...] = add(mine[...], low_buf[...], up_buf[...])
            self.chain(j, 0, mine, out, self.up_dev).start()
            self.chain(j, 1, mine, out, self.low_dev).start()
            pltpu.make_async_copy(mine, out, self.out_sem.at[j]).start()

        self.role(j, 1, body)

    def outward(self, j):
        def body(mine, low, up, low_buf, up_buf, out):
            self.chain(j, 0, mine, out, self.up_dev).wait_recv()
            self.chain(j, 0, out, out, self.up_dev).start()

        self.role(j, 2, body)

    def drain(self, j):
        def lowest(mine, low, up, low_buf, up_buf, out):
            self.chain(j, 0, mine, low, self.up_dev).wait_send()
            self.chain(j, 1, mine, out, self.low_dev).wait_recv()

        def holder(mine, low, up, low_buf, up_buf, out):
            self.chain(j, 0, mine, out, self.up_dev).wait_send()
            self.chain(j, 1, mine, out, self.low_dev).wait_send()
            pltpu.make_async_copy(mine, out, self.out_sem.at[j]).wait()

        def between(mine, low, up, low_buf, up_buf, out):
            self.chain(j, 1, mine, up, self.low_dev).wait_send()
            self.chain(j, 0, out, out, self.up_dev).wait_send()

        def highest(mine, low, up, low_buf, up_buf, out):
            self.chain(j, 1, mine, up, self.low_dev).wait_send()
            self.chain(j, 0, mine, out, self.up_dev).wait_recv()

        for plane, body in enumerate((lowest, holder, between, highest)):
            self.role(j, plane, body)

    def stages(self, at, limit, pairs):
        for stage, behind in pairs:
            i = at - behind

            @pl.when((i >= 0) & (i < limit))
            def _(stage=stage, i=i):
                stage(i)

    def xy_step(self, i):
        self.stages(
            i,
            self.total,
            (
                (self.load, 0),
                (self.pair, 1),
                (self.plane_two, 7),
                (self.plane_one, 4),
                (self.two_arrives, 6),
                (self.one_arrives, 3),
            ),
        )

    def z_step(self, j):
        self.stages(j + 1, self.ffn_count, ((self.ffn_load, 0),))
        for stage, behind in (
            (self.inward, 0),
            (self.root, 6),
            (self.middle, 3),
            (self.outward, 8),
            (self.root_arrives, 5),
            (self.middle_arrives, 2),
            (self.drain, 11),
        ):
            stage(j - behind)

    def begin(self):
        self.ffn_load(jnp.int32(0))

    def finish(self, z_next, xy_next):
        steps = self.chain_total + 12 - z_next

        def body(u, carry):
            self.z_step(z_next + u)
            self.xy_step(xy_next + u)
            return carry

        lax.fori_loop(0, steps, body, 0)
        for i in range(max(self.total - MATE_SLOTS, 0), self.total):
            self.mate_copy(0, pl.ds(0, CUT), i % MATE_SLOTS).wait_send()

    @staticmethod
    def shapes(pieces, ffn_pieces, wide):
        total, ffn_count = sum(pieces), sum(ffn_pieces)
        chain_total = total + ffn_count
        low = jnp.bfloat16
        dma = pltpu.SemaphoreType.DMA
        shape = lambda *s: jax.ShapeDtypeStruct(s, low)
        buf = lambda *s: pltpu.VMEM(s, low)
        outs = [shape(total * CUT, wide), shape(ffn_count * FCUT, wide)]
        lands = [
            shape(total, 2, CUT, wide),
            *[shape(total, CUT, wide)] * 3,
            *[shape(ffn_count, FCUT, wide)] * 2,
        ]
        bufs = [
            buf(MATE_SLOTS, 2, 2, CUT, wide),
            buf(OWN_SLOTS, 2, 2, CUT, wide),
            buf(SUM_SLOTS, 2, 2, CUT, wide),
            buf(total, CUT, wide),
            buf(FFN_SLOTS, FCUT, wide),
            buf(LAND_SLOTS, 2, CUT, wide),
            buf(LAND_SLOTS, CUT, wide),
            buf(LAND_SLOTS, FCUT, wide),
            buf(LAND_SLOTS, FCUT, wide),
        ]
        sems = [
            dma((MATE_SLOTS,)),
            dma((MATE_SLOTS,)),
            dma((OWN_SLOTS,)),
            dma((SUM_SLOTS,)),
            dma((total,)),
            dma((LAND_SLOTS,)),
            dma((SUM_SLOTS,)),
            dma((total,)),
            dma((LAND_SLOTS,)),
            dma((FFN_SLOTS,)),
            dma((2, chain_total)),
            dma((2, chain_total)),
            dma((LAND_SLOTS,)),
            dma((LAND_SLOTS,)),
            dma((chain_total,)),
            pltpu.SemaphoreType.REGULAR,
        ]
        return outs, lands, bufs, sems


class NoSums:
    def start(self):
        pass

    def begin(self):
        pass

    def z_step(self, j):
        pass

    def xy_step(self, i):
        pass

    def finish(self, z_next, xy_next):
        pass


def add(*terms):
    total = terms[0].astype(jnp.float32)
    for term in terms[1:]:
        total = total + term.astype(jnp.float32)
    return total.astype(jnp.bfloat16)


STEP_CHIP = (0, 0, 1, 2, 1, 2, 3, 3)
STEP_HALF = (0, 1, 0, 1, 1, 0, 0, 1)
TILE = 256


def ffn_kernel(
    act_in,
    cot_in,
    gate_in,
    up_in,
    down_in,
    out_ref,
    dn_ref,
    grad_gate,
    grad_up,
    grad_down,
    act,
    cot,
    w_gate,
    w_up,
    w_down,
    hidden,
    d_gate,
    d_up,
    pair,
    mine,
    stage,
    passed,
    final,
    tile_buf,
    weight_sem,
    cot_sem,
    own_sem,
    act_send,
    act_recv,
    pair_send,
    pair_recv,
    flow_send,
    flow_recv,
    tile_sem,
    end_sem,
):
    me = lax.axis_index("grp")
    plane = lax.axis_index("rep")
    mate_dev, x_dev, y_dev = (me ^ 1, plane), (me ^ 2, plane), (me ^ 4, plane)
    half = act.shape[2]
    seq_len = 2 * half
    rows, wide = w_gate.shape
    low = jnp.bfloat16
    meet([mate_dev, x_dev, y_dev])

    def remote(src, dst, send, recv, device):
        return pltpu.make_async_remote_copy(
            src_ref=src,
            dst_ref=dst,
            send_sem=send,
            recv_sem=recv,
            device_id=device,
            device_id_type=MESH,
        )

    own = [act_in.at[pl.ds(h * half, half)] for h in range(2)]

    def act_copy(t, other):
        if other:
            src, device = (own[t] if t < 2 else act.at[t, 0]), mate_dev
        else:
            src, device = {
                2: (own[0], x_dev),
                3: (own[1], y_dev),
                4: (own[1], x_dev),
                5: (own[0], y_dev),
                6: (act.at[2, 0], y_dev),
                7: (act.at[3, 0], x_dev),
            }[t]
        return remote(
            src, act.at[t, other], act_send.at[t, other], act_recv.at[t, other], device
        )

    for t in (2, 3, 4, 5):
        act_copy(t, 0).start()
    for t in (0, 1):
        act_copy(t, 1).start()
    own_copies = [pltpu.make_async_copy(own[t], act.at[t, 0], own_sem.at[t]) for t in range(2)]
    for copy in own_copies:
        copy.start()
    weights = [
        pltpu.make_async_copy(src, dst, weight_sem.at[k])
        for k, (src, dst) in enumerate(((gate_in, w_gate), (up_in, w_up), (down_in, w_down)))
    ]
    for copy in weights:
        copy.start()
    cot_copies = []
    for t in range(8):
        for other in range(2):
            owner = me ^ (2 * STEP_CHIP[t] + other)
            row = pl.multiple_of(owner * seq_len + STEP_HALF[t] * half, 16)
            copy = pltpu.make_async_copy(
                cot_in.at[pl.ds(row, half)], cot.at[t, other], cot_sem.at[t, other]
            )
            copy.start()
            cot_copies.append(copy)

    def pair_copy(kind, t):
        return remote(
            stage.at[kind], pair.at[kind, t], pair_send.at[kind], pair_recv.at[kind, t], mate_dev
        )

    def flow(kind, lane):
        src, dst, device = (
            (pair.at[kind, 2], final.at[kind, 0], x_dev),
            (pair.at[kind, 4], final.at[kind, 1], x_dev),
            (pair.at[kind, 5], final.at[kind, 2], y_dev),
            (pair.at[kind, 3], final.at[kind, 3], y_dev),
            (pair.at[kind, 6], passed.at[kind, 0], x_dev),
            (pair.at[kind, 7], passed.at[kind, 1], y_dev),
        )[lane]
        return remote(src, dst, flow_send.at[kind, lane], flow_recv.at[kind, lane], device)

    def forward_tiles(t):
        def tile(n, carry):
            cut = pl.ds(pl.multiple_of(n * TILE, TILE), TILE)
            tokens = act[t].reshape(seq_len, wide)
            gate = dot_nt(tokens, w_gate[cut])
            up = dot_nt(tokens, w_up[cut])
            d_hidden = dot_nt(cot[t].reshape(seq_len, wide), w_down[cut])
            sigmoid = 1.0 / (1.0 + jnp.exp(-gate))
            silu = gate * sigmoid
            hidden[t, :, cut] = (silu * up).astype(low)
            d_gate[t, :, cut] = (
                d_hidden * up * (sigmoid * (1.0 + gate * (1.0 - sigmoid)))
            ).astype(low)
            d_up[t, :, cut] = (d_hidden * silu).astype(low)
            return carry

        lax.fori_loop(0, rows // TILE, tile, 0)

    def backward_tiles(t):
        def tile(n, carry):
            cut = pl.ds(pl.multiple_of(n * TILE, TILE), TILE)
            out = dot(hidden[t], w_down[:, cut])
            mine[0, :, cut] = out[:half].astype(low)
            stage[0, :, cut] = out[half:].astype(low)
            dn = dot(d_gate[t], w_gate[:, cut]) + dot(d_up[t], w_up[:, cut])
            mine[1, :, cut] = dn[:half].astype(low)
            stage[1, :, cut] = dn[half:].astype(low)
            return carry

        lax.fori_loop(0, wide // TILE, tile, 0)

    def join(t, events):
        for kind in range(2):
            pair_copy(kind, t).wait()
            pair[kind, t] = add(pair[kind, t], mine[kind])
            for when, lane in events:
                if when is None:
                    flow(kind, lane).start()
                else:

                    @pl.when(t == when)
                    def _(kind=kind, lane=lane):
                        flow(kind, lane).start()

    for copy in own_copies + weights:
        copy.wait()

    def step(t, carry):
        for at in (2, 4, 6):

            @pl.when(t == at)
            def _(at=at):
                for u in (at, at + 1):
                    act_copy(u, 0).wait_recv()
                    if at == 2:
                        act_copy(u + 4, 0).start()
                    act_copy(u, 1).start()

        remote(
            act.at[t, 0], act.at[t, 1], act_send.at[t, 1], act_recv.at[t, 1], mate_dev
        ).wait_recv()
        for other in range(2):
            pltpu.make_async_copy(
                cot_in.at[pl.ds(0, half)], cot.at[t, other], cot_sem.at[t, other]
            ).wait()
        forward_tiles(t)

        @pl.when(t > 0)
        def _():
            join(t - 1, ((2, 0), (3, 3), (6, 4)))

        backward_tiles(t)
        for kind in range(2):
            pair_copy(kind, t).start()
        return carry

    lax.fori_loop(0, 8, step, 0)
    join(7, ((None, 5),))

    def write(target, slot, cut):
        return pltpu.make_async_copy(
            tile_buf.at[slot], target.at[:, cut], tile_sem.at[slot]
        )

    tiles = wide // TILE
    for k, (left, right, target) in enumerate(
        ((d_gate, act, grad_gate), (d_up, act, grad_up), (hidden, cot, grad_down))
    ):

        def tile(n, carry, k=k, left=left, right=right, target=target):
            cut = pl.ds(pl.multiple_of(n * TILE, TILE), TILE)
            slot = lax.rem(n, 2)

            @pl.when(k * tiles + n >= 2)
            def _():
                write(target, slot, cut).wait()

            tile_buf[slot] = dot_tn(
                left[...].reshape(8 * seq_len, rows),
                right[:, :, :, cut].reshape(8 * seq_len, TILE),
            ).astype(low)
            write(target, slot, cut).start()
            return carry

        lax.fori_loop(0, tiles, tile, 0)
    for slot in range(2):
        write(grad_down, slot, pl.ds(0, TILE)).wait()

    for kind in range(2):
        for lane, t, onward in ((4, 5, 2), (5, 4, 1)):
            flow(kind, lane).wait_recv()
            pair[kind, t] = add(pair[kind, t], passed[kind, lane - 4])
            flow(kind, onward).start()
    ends = []
    for kind, target in enumerate((out_ref, dn_ref)):
        for h in range(2):
            flow(kind, h).wait_recv()
            flow(kind, 2 + h).wait_recv()
            pair[kind, h] = add(pair[kind, h], final[kind, h], final[kind, 2 + h])
            copy = pltpu.make_async_copy(
                pair.at[kind, h], target.at[pl.ds(h * half, half)], end_sem.at[kind, h]
            )
            copy.start()
            ends.append(copy)
    for copy in ends:
        copy.wait()
    for kind in range(2):
        for lane in range(6):
            flow(kind, lane).wait_send()
    for t in range(8):
        act_copy(t, 1).wait_send()
        if t >= 2:
            act_copy(t, 0).wait_send()


def ffn_all(act, cot, w_gate, w_up, w_down):
    seq_len, wide = act.shape
    rows = w_gate.shape[0]
    half = seq_len // 2
    low = jnp.bfloat16
    hbm = pl.BlockSpec(memory_space=pltpu.HBM)
    dma = pltpu.SemaphoreType.DMA
    return pl.pallas_call(
        ffn_kernel,
        out_shape=[jax.ShapeDtypeStruct((seq_len, wide), low)] * 2
        + [jax.ShapeDtypeStruct((rows, wide), low)] * 3,
        in_specs=[hbm] * 5,
        out_specs=[hbm] * 5,
        scratch_shapes=[
            pltpu.VMEM((8, 2, half, wide), low),
            pltpu.VMEM((8, 2, half, wide), low),
            pltpu.VMEM((rows, wide), low),
            pltpu.VMEM((rows, wide), low),
            pltpu.VMEM((rows, wide), low),
            pltpu.VMEM((8, seq_len, rows), low),
            pltpu.VMEM((8, seq_len, rows), low),
            pltpu.VMEM((8, seq_len, rows), low),
            pltpu.VMEM((2, 8, half, wide), low),
            pltpu.VMEM((2, half, wide), low),
            pltpu.VMEM((2, half, wide), low),
            pltpu.VMEM((2, 2, half, wide), low),
            pltpu.VMEM((2, 4, half, wide), low),
            pltpu.VMEM((2, rows, TILE), low),
            dma((3,)),
            dma((8, 2)),
            dma((2,)),
            dma((8, 2)),
            dma((8, 2)),
            dma((2,)),
            dma((2, 8)),
            dma((2, 6)),
            dma((2, 6)),
            dma((2,)),
            dma((2, 2)),
        ],
        compiler_params=pltpu.CompilerParams(
            collective_id=2, has_side_effects=True, vmem_limit_bytes=VMEM_LIMIT
        ),
    )(act, cot, w_gate, w_up, w_down)


PAIR = 128
COND_ROWS = 256
NORM_ROWS = 32


def normalise(read, gain, shift, write, rows):
    def block(n, carry):
        cut = pl.ds(pl.multiple_of(n * NORM_ROWS, NORM_ROWS), NORM_ROWS)
        write[cut] = layer_norm(read[cut].astype(jnp.float32), gain[...], shift[...]).astype(
            write.dtype
        )
        return carry

    lax.fori_loop(0, rows // NORM_ROWS, block, 0)


def normalise_back(read, gain, d_read, straight, write, sums, row, rows):
    wide = read.shape[1]

    def block(n, carry):
        d_gain, d_shift = carry
        cut = pl.ds(pl.multiple_of(n * NORM_ROWS, NORM_ROWS), NORM_ROWS)
        tensor = read[cut].astype(jnp.float32)
        center = tensor - jnp.mean(tensor, axis=-1, keepdims=True)
        spread = jnp.mean(center * center, axis=-1, keepdims=True)
        inverse = lax.rsqrt(spread + epsilon)
        hat = center * inverse
        d_out = d_read[cut].astype(jnp.float32)
        scaled = d_out * gain[...]
        dv = inverse * (
            scaled
            - jnp.mean(scaled, axis=-1, keepdims=True)
            - hat * jnp.mean(scaled * hat, axis=-1, keepdims=True)
        )
        write[cut] = straight[cut].astype(jnp.float32) + dv
        d_gain = d_gain + jnp.sum((d_out * hat).reshape(NORM_ROWS // 8, 8, wide), axis=0)
        d_shift = d_shift + jnp.sum(d_out.reshape(NORM_ROWS // 8, 8, wide), axis=0)
        return d_gain, d_shift

    zero = jnp.zeros((8, wide), jnp.float32)
    d_gain, d_shift = lax.fori_loop(0, rows // NORM_ROWS, block, (zero, zero))
    sums[row : row + 1] = jnp.sum(d_gain, axis=0, keepdims=True)
    sums[row + 1 : row + 2] = jnp.sum(d_shift, axis=0, keepdims=True)


def turn(tensor, cosine, sine_left, sine_right):
    return (
        tensor * cosine
        + pltpu.roll(tensor, PAIR - HD // 4, 1) * sine_left
        + pltpu.roll(tensor, HD // 4, 1) * sine_right
    )


def tiles_of(count, body):
    def step(n, carry):
        body(pl.ds(pl.multiple_of(n * TILE, TILE), TILE))
        return carry

    lax.fori_loop(0, count // TILE, step, 0)


def pair_loop(body):
    def step(p, carry):
        body(p, pl.multiple_of(p * PAIR, PAIR))
        return carry

    lax.fori_loop(0, HEADS * HD // PAIR, step, 0)


def first_head(rows):
    return lax.broadcasted_iota(jnp.int32, (rows, PAIR), 1) < HD


def head_softmax(query, key, mine, keys):
    scores = dot_nt(jnp.where(mine, query, jnp.zeros_like(query)), key) * score_scale
    if keys < key.shape[0]:
        lanes = lax.broadcasted_iota(jnp.int32, scores.shape, 1)
        scores = jnp.where(lanes < keys, scores, -1e30)
    shifted = jnp.exp(scores - jnp.max(scores, axis=-1, keepdims=True))
    return (shifted * (1.0 / jnp.sum(shifted, axis=-1, keepdims=True))).astype(jnp.bfloat16)


def attend_pair(query, key, value, keys, keep):
    mask = first_head(query.shape[0])
    results = []
    for head in range(2):
        probability = head_softmax(query, key, mask if head == 0 else ~mask, keys)
        keep(head, probability)
        results.append(dot(probability, value))
    return jnp.where(mask, results[0], results[1]).astype(jnp.bfloat16)


def attend_pair_back(query, key, value, grad, probabilities):
    mask, key_mask = first_head(query.shape[0]), first_head(key.shape[0])
    d_queries, d_keys, d_values = [], [], []
    for head in range(2):
        probability = probabilities[head]
        mine = mask if head == 0 else ~mask
        d_prob = dot_nt(jnp.where(mine, grad, jnp.zeros_like(grad)), value)
        wide = probability.astype(jnp.float32)
        inner = jnp.sum(wide * d_prob, axis=-1, keepdims=True)
        d_scores = (wide * (d_prob - inner)).astype(jnp.bfloat16)
        d_queries.append(dot(d_scores, key))
        d_keys.append(dot_tn(d_scores, query))
        d_values.append(dot_tn(probability, grad))
    return (
        jnp.where(mask, d_queries[0], d_queries[1]) * score_scale,
        jnp.where(key_mask, d_keys[0], d_keys[1]) * score_scale,
        jnp.where(key_mask, d_values[0], d_values[1]),
    )


def attention_forward_kernel(
    pieces,
    x_in,
    cond_in,
    cosine,
    sine_left,
    sine_right,
    norms_in,
    qkv_in,
    out_in,
    kv2_in,
    query2_in,
    out2_in,
    norms_out,
    qkv_out,
    out_out,
    query2_out,
    out2_out,
    act_one_out,
    heads_out,
    prob_out,
    flat_one_out,
    section_one_out,
    act_two_out,
    query_two_out,
    kv_two_out,
    prob_two_out,
    flat_two_out,
    section_two_out,
    act_three_out,
    x,
    cond,
    norm_parts,
    w_qkv,
    w_out,
    w_kv2,
    w_query2,
    w_out2,
    act,
    heads,
    flat,
    section,
    query_two,
    kv_two,
    prob,
    prob_two,
    in_sem,
    out_sem,
    prob_sem,
    local_sem,
    *gather_sems,
):
    rows, wide = x.shape
    low = jnp.bfloat16
    sources = (norms_in, qkv_in, out_in, kv2_in, query2_in, out2_in)
    fulls = (norm_parts, w_qkv, w_out, w_kv2, w_query2, w_out2)
    if pieces is None:
        gather = Loads(sources, fulls, local_sem)
    else:
        gather = Gather(pieces, sources, fulls, *gather_sems, local_sem)
    gather.start()
    loads = []
    for k, (src, dst) in enumerate(((x_in, x), (cond_in, cond))):
        loads.append(pltpu.make_async_copy(src, dst, in_sem.at[k]))
        loads[-1].start()
    for k in range(len(sources)):
        gather.own_copy(k).start()
    stores = []

    def save(src, dst):
        stores.append(pltpu.make_async_copy(src, dst, out_sem.at[len(stores)]))
        stores[-1].start()
        return stores[-1]

    lead = GATHER_WINDOW + 2
    gather.run(0, 1 + lead)
    loads[0].wait()
    gather.need(0)
    norms_out[...] = jnp.sum(
        norm_parts[...].astype(jnp.float32).reshape(norm_parts.shape[0] // 16, 16, wide), axis=0
    )
    gains = [norms_out.at[pl.ds(k, 1)] for k in range(6)]
    normalise(x, gains[0], gains[1], act, rows)
    act_one_done = save(act, act_one_out)
    done = 13 + lead
    gather.run(1 + lead, done)
    gather.need(1)
    save(w_qkv, qkv_out)

    def project(cut, rotated):
        result = dot_nt(act[...], w_qkv[cut])
        for part in range(TILE // PAIR):
            piece = result[:, part * PAIR : (part + 1) * PAIR]
            if rotated:
                piece = turn(piece, cosine[...], sine_left[...], sine_right[...])
            heads[:, pl.ds(pl.multiple_of(cut.start + part * PAIR, PAIR), PAIR)] = piece.astype(low)

    for part in range(3):
        tiles_of(
            wide,
            lambda cut, part=part: project(
                pl.ds(pl.multiple_of(cut.start + part * wide, TILE), TILE), part < 2
            ),
        )
        gather.step(done + part)
    done += 3
    save(heads, heads_out)

    def prob_copy(buf, out, p, slot):
        return pltpu.make_async_copy(buf.at[slot], out.at[p], prob_sem.at[slot])

    def self_pair(p, lane):
        slot = lax.rem(p, 2)

        @pl.when(p >= 2)
        def _():
            prob_copy(prob, prob_out, p, slot).wait()

        def keep(head, probability):
            prob[slot, head] = probability

        cols = [pl.ds(pl.multiple_of(lane + k * wide, PAIR), PAIR) for k in range(3)]
        flat[:, cols[0]] = attend_pair(
            heads[:, cols[0]], heads[:, cols[1]], heads[:, cols[2]], rows, keep
        )
        prob_copy(prob, prob_out, p, slot).start()
        serve(p, SELF_EVERY)

    def serve(p, every):
        if gather.steps:

            @pl.when(lax.rem(p, every) == every - 1)
            def _():
                gather.step(done + p // every)

    pairs = wide // PAIR
    pair_loop(self_pair)
    done += pairs // SELF_EVERY
    for slot in range(2):
        prob_copy(prob, prob_out, 0, slot).wait()
    flat_one_done = save(flat, flat_one_out)
    gather.run(done, 17 + lead)
    done = max(done, 17 + lead)
    gather.need(2)
    save(w_out, out_out)

    def first_section(cut):
        section[:, cut] = x[:, cut].astype(jnp.float32) + dot_nt(flat[...], w_out[cut])

    tiles_of(wide, first_section)
    section_one_done = save(section, section_one_out)
    gather.run(done, 21 + lead)
    gather.step(max(done, 21 + lead))
    done = max(done, 21 + lead) + 1
    act_one_done.wait()
    normalise(section, gains[2], gains[3], act, rows)
    act_two_done = save(act, act_two_out)
    loads[1].wait()
    gather.need(3)

    def condition(cut):
        kv_two[:, cut] = dot_nt(cond[...], w_kv2[cut]).astype(low)

    tiles_of(2 * wide, condition)
    save(kv_two, kv_two_out)
    gather.run(done, 25 + lead)
    done = max(done, 25 + lead)
    gather.need(4)
    save(w_query2, query2_out)

    def query(cut):
        query_two[:, cut] = dot_nt(act[...], w_query2[cut]).astype(low)

    tiles_of(wide, query)
    save(query_two, query_two_out)
    flat_one_done.wait()

    def cross_pair(p, lane):
        slot = lax.rem(p, 2)

        @pl.when(p >= 2)
        def _():
            prob_copy(prob_two, prob_two_out, p, slot).wait()

        def keep(head, probability):
            prob_two[slot, head] = probability

        cols = [pl.ds(pl.multiple_of(lane + k * wide, PAIR), PAIR) for k in range(2)]
        flat[:, cols[0]] = attend_pair(
            query_two[:, cols[0]], kv_two[:, cols[0]], kv_two[:, cols[1]], NC, keep
        )
        prob_copy(prob_two, prob_two_out, p, slot).start()
        serve(p, CROSS_EVERY)

    pair_loop(cross_pair)
    done += pairs // CROSS_EVERY
    gather.run(done, 29 + lead)
    for slot in range(2):
        prob_copy(prob_two, prob_two_out, 0, slot).wait()
    save(flat, flat_two_out)
    gather.need(5)
    save(w_out2, out2_out)
    section_one_done.wait()

    def second_section(cut):
        section[:, cut] = section[:, cut] + dot_nt(flat[...], w_out2[cut])

    tiles_of(wide, second_section)
    save(section, section_two_out)
    act_two_done.wait()
    normalise(section, gains[4], gains[5], act, rows)
    save(act, act_three_out)
    waited = [id(c) for c in (act_one_done, flat_one_done, section_one_done, act_two_done)]
    gather.finish()
    for copy in stores:
        if id(copy) not in waited:
            copy.wait()


SELF_EVERY = 2
CROSS_EVERY = 3


def attention_forward(x, cond, tables, norms, weights):
    rows, wide = x.shape
    low, full = jnp.bfloat16, jnp.float32
    pairs = wide // PAIR
    hbm = pl.BlockSpec(memory_space=pltpu.HBM)
    vmem = pl.BlockSpec(memory_space=pltpu.VMEM)
    dma = pltpu.SemaphoreType.DMA
    shape = jax.ShapeDtypeStruct
    groups = lax.axis_size("grp")
    parameters = [norms] + list(weights)
    whole = [(groups * w.shape[0], w.shape[1]) for w in parameters]
    sems = []
    pieces = None
    options = {}
    if groups == 8 and lax.axis_size("rep") % 2 == 0:
        piece_rows = (16, 48, 48, 96, 48, 48)
        pieces = tuple((w.shape[0] // n, n) for w, n in zip(parameters, piece_rows))
        total = sum(n for n, _ in pieces)
        sems = [dma((7, total)), dma((7, total))]
        options = dict(collective_id=0, has_side_effects=True)
    else:
        parameters = [lax.all_gather(w, "grp", axis=0, tiled=True) for w in parameters]
    results = pl.pallas_call(
        functools.partial(attention_forward_kernel, pieces),
        out_shape=[
            shape((16, wide), full),
            *[shape(whole[k], low) for k in (1, 2, 4, 5)],
            shape((rows, wide), low),
            shape((rows, 3 * wide), low),
            shape((pairs, 2, rows, rows), low),
            shape((rows, wide), low),
            shape((rows, wide), full),
            shape((rows, wide), low),
            shape((rows, wide), low),
            shape((COND_ROWS, 2 * wide), low),
            shape((pairs, 2, rows, COND_ROWS), low),
            shape((rows, wide), low),
            shape((rows, wide), full),
            shape((rows, wide), low),
        ],
        in_specs=[hbm, hbm] + [vmem] * 3 + [hbm] * 6,
        out_specs=[vmem] + [hbm] * 16,
        scratch_shapes=[
            pltpu.VMEM((rows, wide), low),
            pltpu.VMEM(cond.shape, low),
            *[pltpu.VMEM(s, low) for s in whole],
            pltpu.VMEM((rows, wide), low),
            pltpu.VMEM((rows, 3 * wide), low),
            pltpu.VMEM((rows, wide), low),
            pltpu.VMEM((rows, wide), full),
            pltpu.VMEM((rows, wide), low),
            pltpu.VMEM((COND_ROWS, 2 * wide), low),
            pltpu.VMEM((2, 2, rows, rows), low),
            pltpu.VMEM((2, 2, rows, COND_ROWS), low),
            dma((2,)),
            dma((14,)),
            dma((2,)),
            dma((6,)),
            *sems,
        ],
        compiler_params=pltpu.CompilerParams(vmem_limit_bytes=VMEM_LIMIT, **options),
    )(x, cond, *tables, *parameters)
    return results[0], results[1:5], results[5:]


GRAD_TILE = 2 * UNIT


def attention_backward_kernel(plan, *refs):
    refs = list(refs)

    def take(n):
        taken = refs[:n]
        del refs[:n]
        return taken

    x_in, cond_in, norms, cosine, sine_left, sine_right = take(6)
    qkv_in, out_in, query2_in, out2_in = take(4)
    act_one_in, heads_in, prob_in, flat_one_in, section_one_in, act_two_in = take(6)
    query_two_in, kv_two_in, prob_two_in, flat_two_in, section_two_in = take(5)
    d_norm_in, d_out_in = take(2)
    ffn_in = take(3) if plan else []
    d_inputs_out, sums = take(2)
    grad_out2, grad_query2, grad_kv2, grad_out, grad_qkv = take(5)
    if plan:
        (grad_norm,) = take(1)
        sum_outs, lands = take(2), take(6)
    w_small, w_tile = take(2)
    x, cond, act_one, heads, flat_one, section_one, act_two = take(7)
    query_two, kv_two, flat_two, section_two, d_norm = take(5)
    d_low, d_heads, d_kv, d_att, prob, prob_two, grad_buf = take(7)
    in_sem, weight_sem, tile_sem, prob_sem, grad_sem, end_sem = take(6)
    if plan:
        norm_buf, norm_sem = take(2)
        bufs, sems = take(9), take(16)
        parts = (grad_out2, grad_query2, grad_kv2, grad_out, grad_qkv, grad_norm)
        work = Sums(plan[0], plan[1], parts, ffn_in, sum_outs, lands, bufs, sems)
    else:
        work = NoSums()
    rows, wide = x.shape
    pairs = wide // PAIR
    low = jnp.bfloat16
    work.start()
    work.begin()
    loads = {}
    for k, (name, src, dst) in enumerate(
        (
            ("section_two", section_two_in, section_two),
            ("d_norm", d_norm_in, d_norm),
            ("d_out", d_out_in, d_low),
            ("w_out2", out2_in, w_small),
            ("flat_two", flat_two_in, flat_two),
            ("query_two", query_two_in, query_two),
            ("kv_two", kv_two_in, kv_two),
            ("cond", cond_in, cond),
            ("act_two", act_two_in, act_two),
            ("section_one", section_one_in, section_one),
            ("flat_one", flat_one_in, flat_one),
            ("heads", heads_in, heads),
            ("act_one", act_one_in, act_one),
            ("x", x_in, x),
        )
    ):
        loads[name] = pltpu.make_async_copy(src, dst, in_sem.at[k])
        loads[name].start()

    def need(*names):
        for name in names:
            loads[name].wait()

    def next_weight(name, src, k):
        loads[name] = pltpu.make_async_copy(src, w_small, weight_sem.at[k])
        loads[name].start()

    gains = [norms.at[pl.ds(2 * k, 1)] for k in range(3)]

    def prob_copy(src, buf, p, slot):
        return pltpu.make_async_copy(src.at[p], buf.at[slot], prob_sem.at[slot])

    def prob_start(src, buf):
        for p in range(2):
            prob_copy(src, buf, p, p).start()

    def unit_copy(target, n, half, slot):
        src = grad_buf.at[slot, pl.ds(half * UNIT, UNIT)]
        unit = 2 * n + half
        if plan:
            per = target.shape[3] // UNIT
            block = unit // per
            row = pl.multiple_of(lax.rem(unit, per) * UNIT, 16)
            place = target.at[block // 4, lax.rem(block // 2, 2), lax.rem(block, 2), pl.ds(row, UNIT)]
        else:
            place = target.at[pl.ds(pl.multiple_of(unit * UNIT, 16), UNIT)]
        return pltpu.make_async_copy(src, place, grad_sem.at[slot, half])

    def grad_rows(target, count, compute):
        def step(n, carry):
            slot = lax.rem(n, 2)

            @pl.when(n >= 2)
            def _():
                for half in range(2):
                    unit_copy(target, n, half, slot).wait()

            compute(n, slot)
            for half in range(2):
                unit_copy(target, n, half, slot).start()
            return carry

        lax.fori_loop(0, count, step, 0)
        for slot in range(2):
            for half in range(2):
                unit_copy(target, 0, half, slot).wait()

    def weight_rows(left, right, target):
        def compute(n, slot):
            columns = left[:, pl.ds(pl.multiple_of(n * GRAD_TILE, 128), GRAD_TILE)]
            for m in range(wide // 512):
                piece = slice(m * 512, (m + 1) * 512)
                grad_buf[slot, :, piece] = dot_tn(columns, right[:, piece]).astype(low)

        grad_rows(target, left.shape[1] // GRAD_TILE, compute)

    def round_rows():
        def block(n, carry):
            cut = pl.ds(pl.multiple_of(n * NORM_ROWS, NORM_ROWS), NORM_ROWS)
            d_low[cut] = d_section[cut].astype(low)
            return carry

        lax.fori_loop(0, rows // NORM_ROWS, block, 0)

    def through(target):
        def body(cut):
            target[:, cut] = dot(d_low[...], w_small[:, cut]).astype(low)

        tiles_of(wide, body)

    at = {"z": 0, "xy": 0}

    def serve(*kinds):
        for kind in kinds:
            (work.z_step if kind == "z" else work.xy_step)(jnp.int32(at[kind]))
            at[kind] += 1

    def serve_pairs(p, kind, every):
        @pl.when(lax.rem(p, every) == every - 1)
        def _():
            (work.z_step if kind == "z" else work.xy_step)(at[kind] + p // every)

    prob_start(prob_two_in, prob_two)
    serve("z")
    need("section_two", "d_norm", "d_out")
    normalise_back(section_two, gains[2], d_norm, d_low, section_two, sums, 4, rows)
    d_section = section_two
    round_rows()
    need("w_out2")
    through(d_att)
    next_weight("w_query2", query2_in, 0)
    serve("z")
    need("flat_two")
    weight_rows(d_low, flat_two, grad_out2)
    serve("xy", "z")
    need("query_two", "kv_two")

    def cross_pair(p, lane):
        slot = lax.rem(p, 2)
        prob_copy(prob_two_in, prob_two, p, slot).wait()
        cols = [pl.ds(pl.multiple_of(lane + k * wide, PAIR), PAIR) for k in range(2)]
        d_query, d_key, d_value = attend_pair_back(
            query_two[:, cols[0]],
            kv_two[:, cols[0]],
            kv_two[:, cols[1]],
            d_att[:, cols[0]],
            [prob_two[slot, head] for head in range(2)],
        )
        d_low[:, cols[0]] = d_query.astype(low)
        d_kv[:, cols[0]] = d_key.astype(low)
        d_kv[:, cols[1]] = d_value.astype(low)

        @pl.when(p + 2 < pairs)
        def _():
            prob_copy(prob_two_in, prob_two, p + 2, slot).start()

        serve_pairs(p, "z", 3)
        serve_pairs(p, "xy", 4)

    pair_loop(cross_pair)
    at["z"] += 4
    at["xy"] += 3
    prob_start(prob_in, prob)
    need("w_query2")
    through(d_norm)
    next_weight("w_out", out_in, 1)
    serve("z")
    need("act_two")
    weight_rows(d_low, act_two, grad_query2)
    serve("z", "xy")
    need("cond")

    def cond_rows(n, slot):
        for half in range(2):
            columns = pl.ds(pl.multiple_of((2 * n + half) * GRAD_TILE, 128), GRAD_TILE)
            result = dot_tn(d_kv[:, columns], cond[...]).astype(low)
            at = slice(half * UNIT, (half + 1) * UNIT)
            grad_buf[slot, at, : wide // 2] = result[:UNIT]
            grad_buf[slot, at, wide // 2 :] = result[UNIT:]

    grad_rows(grad_kv2, wide // GRAD_TILE, cond_rows)
    serve("xy", "z")
    need("section_one")
    normalise_back(section_one, gains[1], d_norm, d_section, d_section, sums, 2, rows)
    serve("z", "xy")
    round_rows()
    need("w_out")
    through(d_att)

    def tile_copy(n, slot):
        cut = pl.ds(pl.multiple_of(n * TILE, TILE), TILE)
        return pltpu.make_async_copy(qkv_in.at[:, cut], w_tile.at[slot], tile_sem.at[slot])

    for n in range(2):
        tile_copy(n, n).start()
    serve("xy", "z")
    need("flat_one")
    weight_rows(d_low, flat_one, grad_out)
    serve("z", "xy")
    need("heads")

    def self_pair(p, lane):
        slot = lax.rem(p, 2)
        prob_copy(prob_in, prob, p, slot).wait()
        cols = [pl.ds(pl.multiple_of(lane + k * wide, PAIR), PAIR) for k in range(3)]
        d_query, d_key, d_value = attend_pair_back(
            heads[:, cols[0]],
            heads[:, cols[1]],
            heads[:, cols[2]],
            d_att[:, cols[0]],
            [prob[slot, head] for head in range(2)],
        )
        back = (cosine[...], -sine_left[...], -sine_right[...])
        d_heads[:, cols[0]] = turn(d_query, *back).astype(low)
        d_heads[:, cols[1]] = turn(d_key, *back).astype(low)
        d_heads[:, cols[2]] = d_value.astype(low)

        @pl.when(p + 2 < pairs)
        def _():
            prob_copy(prob_in, prob, p + 2, slot).start()

        serve_pairs(p, "z", 1)
        serve_pairs(p, "xy", 2)

    pair_loop(self_pair)
    at["z"] += pairs
    at["xy"] += 6
    need("act_one")
    weight_rows(d_heads, act_one, grad_qkv)
    serve("z", "xy")

    def first_norm(n, carry):
        slot = lax.rem(n, 2)
        cut = pl.ds(pl.multiple_of(n * TILE, TILE), TILE)
        tile_copy(n, slot).wait()
        d_norm[:, cut] = dot(d_heads[...], w_tile[slot]).astype(low)

        @pl.when(n + 2 < wide // TILE)
        def _():
            tile_copy(n + 2, slot).start()

        return carry

    lax.fori_loop(0, wide // TILE, first_norm, 0)
    serve("z", "xy")
    need("x")
    normalise_back(x, gains[0], d_norm, d_section, d_section, sums, 0, rows)
    end = pltpu.make_async_copy(d_section, d_inputs_out, end_sem)
    end.start()
    if plan:
        norm_buf[...] = jnp.zeros_like(norm_buf)
        norm_buf[:8] = sums[...].astype(low)
        copies = []
        for b in range(8):
            place = grad_norm.at[b // 4, b // 2 % 2, b % 2]
            copies.append(pltpu.make_async_copy(norm_buf, place, norm_sem.at[b]))
            copies[-1].start()
        for copy in copies:
            copy.wait()
    work.finish(at["z"], at["xy"])
    end.wait()


def attention_backward(x, cond, norms, tables, weights, kept, d_norm, d_out, ffn):
    rows, wide = x.shape
    low, full = jnp.bfloat16, jnp.float32
    hbm = pl.BlockSpec(memory_space=pltpu.HBM)
    vmem = pl.BlockSpec(memory_space=pltpu.VMEM)
    dma = pltpu.SemaphoreType.DMA
    shape = jax.ShapeDtypeStruct
    buf = lambda s, t=low: pltpu.VMEM(s, t)
    heights = (wide, wide, wide, wide, 3 * wide)
    more_outs, more_scratch = [], []
    plan = None
    options = {}
    if ffn:
        grads = [(2, 2, 2, h // 8, wide) for h in heights] + [(2, 2, 2, CUT, wide)]
        plan = (
            tuple(g[3] // CUT for g in grads),
            tuple(f.shape[0] // FCUT for f in ffn),
        )
        outs, lands, bufs, sems = Sums.shapes(*plan, wide)
        more_outs = outs + lands
        more_scratch = [buf((CUT, wide)), dma((8,))] + bufs + sems
        options = dict(collective_id=1, has_side_effects=True)
    else:
        grads = [(h, wide) for h in heights]
    ffn = list(ffn)
    results = pl.pallas_call(
        functools.partial(attention_backward_kernel, plan),
        out_shape=[shape((rows, wide), full), shape((8, wide), full)]
        + [shape(g, low) for g in grads]
        + more_outs,
        in_specs=[hbm, hbm] + [vmem] * 4 + [hbm] * (17 + len(ffn)),
        out_specs=[hbm, vmem] + [hbm] * (len(grads) + len(more_outs)),
        scratch_shapes=[
            buf((wide, wide)),
            buf((2, 3 * wide, TILE)),
            buf((rows, wide)),
            buf(cond.shape),
            buf((rows, wide)),
            buf((rows, 3 * wide)),
            buf((rows, wide)),
            buf((rows, wide), full),
            buf((rows, wide)),
            buf((rows, wide)),
            buf((COND_ROWS, 2 * wide)),
            buf((rows, wide)),
            buf((rows, wide), full),
            buf((rows, wide)),
            buf((rows, wide)),
            buf((rows, 3 * wide)),
            buf((COND_ROWS, 2 * wide)),
            buf((rows, wide)),
            buf((2, 2, rows, rows)),
            buf((2, 2, rows, COND_ROWS)),
            buf((2, GRAD_TILE, wide)),
            dma((14,)),
            dma((2,)),
            dma((2,)),
            dma((2,)),
            dma((2, 2)),
            dma,
            *more_scratch,
        ],
        compiler_params=pltpu.CompilerParams(vmem_limit_bytes=VMEM_LIMIT, **options),
    )(x, cond, norms, *tables, *weights, *kept, d_norm, d_out, *ffn)
    return results[0], results[1], results[2:7], results[8:10]


def per_device(
    inputs,
    conditioning,
    positions,
    slot_valid,
    cotangent,
    norm1_gain,
    norm1_shift,
    norm2_gain,
    norm2_shift,
    norm3_gain,
    norm3_shift,
    w_qkv,
    w_out,
    w_query2,
    w_kv2,
    w_out2,
    w_gate,
    w_up,
    w_down,
):
    cond_rows = conditioning[0]
    norms = jnp.stack(
        [norm1_gain, norm1_shift, norm2_gain, norm2_shift, norm3_gain, norm3_shift], axis=0
    )
    own_width = norms.shape[1]
    norms = lax.dynamic_update_slice(
        jnp.zeros((16, D), norms.dtype), norms, (0, lax.axis_index("grp") * own_width)
    )
    grad_mlp = (cotangent[0].astype(jnp.float32) * slot_valid[0].astype(jnp.float32)).astype(
        jnp.bfloat16
    )
    all_grad = lax.all_gather(grad_mlp, "grp", axis=0, tiled=True)
    tables = turn_tables(positions[0])
    padded_cond = jnp.pad(cond_rows, ((0, COND_ROWS - NC), (0, 0)))
    norms, whole, kept = attention_forward(
        inputs[0], padded_cond, tables, norms, [w_qkv, w_out, w_kv2, w_query2, w_out2]
    )
    act_three, section_two = kept[-1], kept[-2]
    if lax.axis_size("grp") == 8:
        mlp_out, d_norm3, grad_gate, grad_up, grad_down = ffn_all(
            act_three, all_grad, w_gate, w_up, w_down
        )
    else:
        all_act = lax.all_gather(act_three, "grp", axis=0, tiled=True)
        gate_pre = dot_nt(all_act, w_gate)
        up_pre = dot_nt(all_act, w_up)
        hidden = swiglu(gate_pre, up_pre).astype(jnp.bfloat16)
        mlp_part = dot(hidden, w_down).astype(jnp.bfloat16)
        mlp_out = lax.psum_scatter(mlp_part, "grp", scatter_dimension=0, tiled=True)
        d_hidden = dot_nt(all_grad, w_down)
        d_gate_full, d_up_full = swiglu_back(gate_pre, up_pre, d_hidden)
        d_gate = d_gate_full.astype(jnp.bfloat16)
        d_up = d_up_full.astype(jnp.bfloat16)
        d_norm3_part = (dot(d_gate, w_gate) + dot(d_up, w_up)).astype(jnp.bfloat16)
        d_norm3 = lax.psum_scatter(d_norm3_part, "grp", scatter_dimension=0, tiled=True)
        grad_gate = dot_tn(d_gate, all_act).astype(jnp.bfloat16)
        grad_up = dot_tn(d_up, all_act).astype(jnp.bfloat16)
        grad_down = dot_tn(hidden, all_grad).astype(jnp.bfloat16)
    outputs = (section_two + mlp_out.astype(jnp.float32)).astype(jnp.bfloat16)
    groups = lax.axis_size("grp")
    fused = groups == 8 and lax.axis_size("rep") == 4
    ffn_grads = [grad_gate, grad_up, grad_down]
    d_tokens, norm_sums, grads, totals = attention_backward(
        inputs[0],
        padded_cond,
        norms,
        tables,
        whole,
        kept[:-1],
        d_norm3,
        grad_mlp,
        ffn_grads if fused else [],
    )
    own_at = lax.axis_index("grp") * own_width
    if fused:
        total_a, total_f = totals
        ends = []
        for g in grads:
            ends.append((ends[-1] if ends else 0) + g.shape[3])
        grad_out_two, grad_query_two, kv2_total, grad_out_one, grad_qkv = (
            total_a[e - g.shape[3] : e] for e, g in zip(ends, grads)
        )
        norm_total = total_a[ends[-1] : ends[-1] + 6]
        own = w_gate.shape[0]
        ffn_sums = [total_f[k * own : (k + 1) * own] for k in range(3)]
        kv2_total = kv2_total.reshape(-1, UNIT, 2, D // 2)
        grad_kv_two = jnp.swapaxes(kv2_total, 1, 2).reshape(-1, D // 2)
    else:
        grads = list(grads)
        kv2_part = jnp.swapaxes(grads[2].reshape(-1, UNIT, 2, D // 2), 1, 2)
        grads[2] = kv2_part.reshape(2 * D, D // 2)
        norm_total = lax.psum(norm_sums[:6].astype(jnp.bfloat16), ("grp", "rep"))
        shards = [lax.psum_scatter(g, "grp", scatter_dimension=0, tiled=True) for g in grads]
        grad_out_two, grad_query_two, grad_kv_two, grad_out_one, grad_qkv = lax.psum(
            tuple(shards), "rep"
        )
        ffn_sums = lax.psum(tuple(ffn_grads), "rep")
    norm_total = lax.dynamic_slice_in_dim(norm_total, own_at, own_width, axis=1)
    grad_qkv, grad_out_one, grad_query_two, grad_out_two, grad_kv_two = (
        g.astype(jnp.float32)
        for g in (grad_qkv, grad_out_one, grad_query_two, grad_out_two, grad_kv_two)
    )
    norm_total = norm_total.astype(jnp.float32)
    grad_gate, grad_up, grad_down = (g.astype(jnp.float32) for g in ffn_sums)
    return (
        outputs[None],
        d_tokens[None],
        norm_total[0],
        norm_total[1],
        norm_total[2],
        norm_total[3],
        norm_total[4],
        norm_total[5],
        grad_qkv,
        grad_out_one,
        grad_query_two,
        grad_kv_two,
        grad_out_two,
        grad_gate,
        grad_up,
        grad_down,
    )


def solution(mesh):
    return jax.shard_map(
        per_device,
        mesh=mesh,
        in_specs=(
            P(("grp", "rep"), None, None),
            P(("grp", "rep"), None, None),
            P(("grp", "rep"), None),
            P(("grp", "rep")),
            P(("grp", "rep"), None, None),
            P("grp"),
            P("grp"),
            P("grp"),
            P("grp"),
            P("grp"),
            P("grp"),
            P("grp", None),
            P("grp", None),
            P("grp", None),
            P("grp", None),
            P("grp", None),
            P("grp", None),
            P("grp", None),
            P("grp", None),
        ),
        out_specs=(
            P(("grp", "rep"), None, None),
            P(("grp", "rep"), None, None),
            P("grp"),
            P("grp"),
            P("grp"),
            P("grp"),
            P("grp"),
            P("grp"),
            P("grp", None),
            P("grp", None),
            P("grp", None),
            P("grp", None),
            P("grp", None),
            P("grp", None),
            P("grp", None),
            P("grp", None),
        ),
        check_vma=False,
    )
```

```python
import functools
import math

import jax
import jax.numpy as jnp
from jax import lax
from jax.experimental import pallas as pl
from jax.experimental.pallas import tpu as pltpu
from jax.sharding import PartitionSpec as P

MESH = pl.DeviceIdType.MESH
VMEM_LIMIT = 63 * 1024 * 1024

D = 1536
HEADS = 24
HD = 64
NC = 130


epsilon = 1e-05
score_scale = 0.125


def layer_norm(tensor, gain, shift):
    center = tensor - jnp.mean(tensor, axis=-1, keepdims=True)
    spread = jnp.mean(center * center, axis=-1, keepdims=True)
    return center * lax.rsqrt(spread + epsilon) * gain + shift


def swiglu(gate_part, up_part):
    return jax.nn.silu(gate_part) * up_part


def swiglu_back(gate_part, up_part, d_hidden):
    _, pullback = jax.vjp(swiglu, gate_part, up_part)
    return pullback(d_hidden)


def dot_nt(left_side, right_side):
    return lax.dot_general(
        left_side, right_side, (((1,), (1,)), ((), ())), preferred_element_type=jnp.float32
    )


def dot_tn(left_side, right_side):
    return lax.dot_general(
        left_side, right_side, (((0,), (0,)), ((), ())), preferred_element_type=jnp.float32
    )


def dot(left_side, right_side):
    return jnp.dot(left_side, right_side, preferred_element_type=jnp.float32)


def turn_tables(positions):
    quarter = HD // 4
    frequency = jnp.exp(jnp.arange(quarter, dtype=jnp.float32) * (-math.log(10000.0) / quarter))
    turned = positions.astype(jnp.float32)[:, None] * frequency[None, :]
    cosine, sine = jnp.cos(turned), jnp.sin(turned)
    none, one = jnp.zeros_like(sine), jnp.ones_like(sine)

    def heads(*parts):
        return jnp.tile(jnp.concatenate(parts, axis=1), (1, 2))

    return (
        heads(cosine, cosine, one, one),
        heads(-sine, none, none, none),
        heads(none, sine, none, none),
    )


def meet(peers, lower=None, upper=None, rep_index=None):
    barrier = pltpu.get_barrier_semaphore()
    for peer in peers:
        pl.semaphore_signal(barrier, inc=1, device_id=peer, device_id_type=MESH)
    if lower is not None:

        @pl.when(rep_index > 0)
        def _():
            pl.semaphore_signal(barrier, inc=1, device_id=lower, device_id_type=MESH)

        @pl.when(rep_index < 3)
        def _():
            pl.semaphore_signal(barrier, inc=1, device_id=upper, device_id_type=MESH)

    expected = len(peers)
    if lower is not None:
        expected = expected + jnp.where(rep_index > 0, 1, 0) + jnp.where(rep_index < 3, 1, 0)
    pl.semaphore_wait(barrier, expected)


GATHER_WINDOW = 4


class Gather:
    def __init__(self, pieces, sources, fulls, send_sem, recv_sem, local_sem):
        self.pieces, self.sources, self.fulls = pieces, sources, fulls
        self.send_sem, self.recv_sem, self.local_sem = send_sem, recv_sem, local_sem
        self.total = sum(n for n, _ in pieces)
        self.steps = self.total + GATHER_WINDOW + 2
        self.me = me = lax.axis_index("grp")
        self.plane = plane = lax.axis_index("rep")
        first_bit = 2 + 2 * lax.rem(plane, 2)
        self.first, self.second, self.across = me ^ first_bit, me ^ (6 - first_bit), me ^ 6
        self.first_dev = (self.first, plane)
        self.second_dev = (self.second, plane)
        self.rep_dev = (me, plane ^ 1)
        self.mate_dev = (me ^ 1, plane)

    def start(self):
        meet([self.first_dev, self.second_dev, self.rep_dev, self.mate_dev])

    def own_copy(self, k):
        n, rows = self.pieces[k]
        row = pl.multiple_of(self.me * (n * rows), 16)
        return pltpu.make_async_copy(
            self.sources[k], self.fulls[k].at[pl.ds(row, n * rows)], self.local_sem.at[k]
        )

    def each(self, i, body):
        base = 0
        for k, (n, rows) in enumerate(self.pieces):

            @pl.when((i >= base) & (i < base + n))
            def _(k=k, rows=rows, base=base):
                body(k, (i - base) * rows)

            base += n

    def push(self, k, offset, i, owner, lane, device, own=False):
        n, rows = self.pieces[k]
        cut = pl.ds(pl.multiple_of(offset, 16), rows)
        place = self.fulls[k].at[pl.ds(pl.multiple_of(owner * (n * rows) + offset, 16), rows)]
        return pltpu.make_async_remote_copy(
            src_ref=self.sources[k].at[cut] if own else place,
            dst_ref=place,
            send_sem=self.send_sem.at[lane, i],
            recv_sem=self.recv_sem.at[lane, i],
            device_id=device,
            device_id_type=MESH,
        )

    def stage_own(self, i):
        def body(k, offset):
            self.push(k, offset, i, self.me, 0, self.first_dev, own=True).start()
            self.push(k, offset, i, self.me, 3, self.mate_dev, own=True).start()

        self.each(i, body)

    def stage_first(self, i):
        def body(k, offset):
            self.push(k, offset, i, self.first, 0, self.first_dev).wait_recv()
            self.push(k, offset, i, self.first, 1, self.second_dev).start()
            self.push(k, offset, i, self.first, 2, self.rep_dev).start()
            self.push(k, offset, i, self.first, 4, self.mate_dev).start()

        self.each(i, body)

    def stage_rest(self, i):
        def body(k, offset):
            self.push(k, offset, i, self.across, 1, self.second_dev).wait_recv()
            self.push(k, offset, i, self.across, 5, self.mate_dev).start()
            self.push(k, offset, i, self.second, 2, self.rep_dev).wait_recv()
            self.push(k, offset, i, self.second, 6, self.mate_dev).start()

        self.each(i, body)

    def step(self, t):
        for stage, lag in (
            (self.stage_own, 0),
            (self.stage_first, GATHER_WINDOW),
            (self.stage_rest, GATHER_WINDOW + 2),
        ):
            i = t - lag

            @pl.when((i >= 0) & (i < self.total))
            def _(stage=stage, i=i):
                stage(i)

    def run(self, first, last):
        def body(t, carry):
            self.step(t)
            return carry

        lax.fori_loop(first, last, body, 0)

    def need(self, k):
        base = sum(n for n, _ in self.pieces[:k])
        n, rows = self.pieces[k]

        def body(j, carry):
            for lane in (3, 4, 5, 6):
                self.push(k, j * rows, base + j, self.me, lane, self.mate_dev).wait_recv()
            return carry

        lax.fori_loop(0, n, body, 0)
        self.own_copy(k).wait()

    def finish(self):
        def sent(i, carry):
            def body(k, offset):
                self.push(k, offset, i, self.me, 0, self.first_dev, own=True).wait_send()
                self.push(k, offset, i, self.me, 3, self.mate_dev, own=True).wait_send()
                for lane in (1, 2, 4, 5, 6):
                    self.push(k, offset, i, self.first, lane, self.mate_dev).wait_send()

            self.each(i, body)
            return carry

        lax.fori_loop(0, self.total, sent, 0)


class Loads:
    steps = 0

    def __init__(self, sources, fulls, local_sem):
        self.sources, self.fulls, self.local_sem = sources, fulls, local_sem

    def start(self):
        pass

    def own_copy(self, k):
        return pltpu.make_async_copy(self.sources[k], self.fulls[k], self.local_sem.at[k])

    def step(self, t):
        pass

    def run(self, first, last):
        pass

    def need(self, k):
        self.own_copy(k).wait()

    def finish(self):
        pass


CUT = 48
FCUT = 48
UNIT = 192
MATE_SLOTS = 4
OWN_SLOTS = 2
SUM_SLOTS = 9
FFN_SLOTS = 14
LAND_SLOTS = 3


class Sums:
    def __init__(self, pieces, ffn_pieces, parts, ffn, outs, lands, bufs, sems):
        self.near = pieces[0]
        self.pieces, self.ffn_pieces, self.parts, self.ffn = pieces, ffn_pieces, parts, ffn
        self.out_n, self.out_a, self.out_f = outs
        self.one_land, self.two_land, self.low_a, self.up_a, self.low_f, self.up_f = lands
        (
            self.mate_buf,
            self.own_buf,
            self.sums,
            self.done,
            self.ffn_buf,
            self.one_buf,
            self.two_buf,
            self.low_buf,
            self.up_buf,
        ) = bufs
        (
            self.mate_send,
            self.mate_recv,
            self.own_sem,
            self.one_send,
            self.one_recv,
            self.one_sem,
            self.two_send,
            self.two_recv,
            self.two_sem,
            self.ffn_sem,
            self.chain_send,
            self.chain_recv,
            self.low_sem,
            self.up_sem,
            self.out_sem,
            self.near_sem,
            self.credit,
        ) = sems
        me = lax.axis_index("grp")
        self.plane = plane = lax.axis_index("rep")
        self.core = lax.rem(me, 2)
        self.x = lax.rem(me // 2, 2)
        self.y = me // 4
        self.mate_dev = (me ^ 1, plane)
        self.x_dev = (me ^ 2, plane)
        self.y_dev = (me ^ 4, plane)
        self.low_dev = (me, plane - 1)
        self.up_dev = (me, plane + 1)
        self.total = sum(pieces)
        self.ffn_count = sum(ffn_pieces)
        self.chain_total = self.ffn_count + self.total - self.near

    def start(self):
        meet([self.mate_dev, self.x_dev, self.y_dev], self.low_dev, self.up_dev, self.plane)

    def each(self, i, body):
        base = 0
        for k, n in enumerate(self.pieces):

            @pl.when((i >= base) & (i < base + n))
            def _(k=k, base=base):
                body(k, pl.ds(pl.multiple_of((i - base) * CUT, 16), CUT))

            base += n

    def mate_copy(self, k, cut, slot):
        return pltpu.make_async_remote_copy(
            src_ref=self.parts[k].at[:, :, 1 - self.core, cut],
            dst_ref=self.mate_buf.at[slot],
            send_sem=self.mate_send.at[slot],
            recv_sem=self.mate_recv.at[slot],
            device_id=self.mate_dev,
            device_id_type=MESH,
        )

    def own_copy(self, k, cut, slot):
        return pltpu.make_async_copy(
            self.parts[k].at[:, :, self.core, cut], self.own_buf.at[slot], self.own_sem.at[slot]
        )

    def load(self, i):
        @pl.when(i >= MATE_SLOTS)
        def _():
            pl.semaphore_wait(self.credit, 1)
            self.mate_copy(0, pl.ds(0, CUT), lax.rem(i, MATE_SLOTS)).wait_send()

        def body(k, cut):
            self.mate_copy(k, cut, lax.rem(i, MATE_SLOTS)).start()
            self.own_copy(k, cut, lax.rem(i, OWN_SLOTS)).start()

        self.each(i, body)

    def one_copy(self, i, slot, by_x):
        return pltpu.make_async_remote_copy(
            src_ref=self.sums.at[slot, :, 1 - self.x] if by_x else self.sums.at[slot, 1 - self.y],
            dst_ref=self.one_land.at[i],
            send_sem=self.one_send.at[slot],
            recv_sem=self.one_recv.at[i],
            device_id=self.x_dev if by_x else self.y_dev,
            device_id_type=MESH,
        )

    def two_copy(self, i, slot, by_x):
        return pltpu.make_async_remote_copy(
            src_ref=self.sums.at[slot, 1 - self.y, self.x]
            if by_x
            else self.sums.at[slot, self.y, 1 - self.x],
            dst_ref=self.two_land.at[i],
            send_sem=self.two_send.at[slot],
            recv_sem=self.two_recv.at[i],
            device_id=self.y_dev if by_x else self.x_dev,
            device_id_type=MESH,
        )

    def either(self, i, body):
        @pl.when(lax.rem(i, 2) == 0)
        def _():
            body(True)

        @pl.when(lax.rem(i, 2) == 1)
        def _():
            body(False)

    def one_load(self, i):
        slot = lax.rem(i, LAND_SLOTS)
        return pltpu.make_async_copy(self.one_land.at[i], self.one_buf.at[slot], self.one_sem.at[slot])

    def two_load(self, i):
        slot = lax.rem(i, LAND_SLOTS)
        return pltpu.make_async_copy(self.two_land.at[i], self.two_buf.at[slot], self.two_sem.at[slot])

    def pair(self, i):
        mate_slot, own_slot = lax.rem(i, MATE_SLOTS), lax.rem(i, OWN_SLOTS)
        slot = lax.rem(i, SUM_SLOTS)
        self.mate_copy(0, pl.ds(0, CUT), mate_slot).wait_recv()
        self.own_copy(0, pl.ds(0, CUT), own_slot).wait()
        for u in range(2):
            for v in range(2):
                self.sums[slot, u, v] = add(
                    self.own_buf[own_slot, u, v], self.mate_buf[mate_slot, u, v]
                )

        @pl.when(i + MATE_SLOTS < self.total)
        def _():
            pl.semaphore_signal(
                self.credit, inc=1, device_id=self.mate_dev, device_id_type=MESH
            )

        self.either(i, lambda by_x: self.one_copy(i, slot, by_x).start())

    def one_arrives(self, i):
        self.either(i, lambda by_x: self.one_copy(i, lax.rem(i, SUM_SLOTS), by_x).wait_recv())
        self.one_load(i).start()

    def plane_one(self, i):
        slot, land = lax.rem(i, SUM_SLOTS), lax.rem(i, LAND_SLOTS)
        self.one_load(i).wait()

        def body(by_x):
            for u in range(2):
                at = (slot, u, self.x) if by_x else (slot, self.y, u)
                self.sums[at] = add(self.sums[at], self.one_buf[land, u])
            self.two_copy(i, slot, by_x).start()

        self.either(i, body)

    def two_arrives(self, i):
        self.either(i, lambda by_x: self.two_copy(i, lax.rem(i, SUM_SLOTS), by_x).wait_recv())
        self.two_load(i).start()

    def plane_two(self, i):
        slot = lax.rem(i, SUM_SLOTS)
        self.two_load(i).wait()
        self.done[i] = add(self.sums[slot, self.y, self.x], self.two_buf[lax.rem(i, LAND_SLOTS)])

        @pl.when(i < self.near)
        def _():
            self.near_copy(i).start()

        def body(by_x):
            self.one_copy(i, slot, by_x).wait_send()
            self.two_copy(i, slot, by_x).wait_send()

        self.either(i, body)

    def near_copy(self, i):
        rows = pl.ds(pl.multiple_of(i * CUT, 16), CUT)
        return pltpu.make_async_copy(self.done.at[i], self.out_n.at[rows], self.near_sem.at[i])

    def ffn_load(self, j):
        base = 0
        for k, n in enumerate(self.ffn_pieces):

            @pl.when((j >= base) & (j < base + n))
            def _(k=k, base=base):
                row = pl.multiple_of((j - base) * FCUT, 16)
                pltpu.make_async_copy(
                    self.ffn[k].at[pl.ds(row, FCUT)],
                    self.ffn_buf.at[lax.rem(j, FFN_SLOTS)],
                    self.ffn_sem.at[lax.rem(j, FFN_SLOTS)],
                ).start()

            base += n

    def ffn_wait(self, j):
        pltpu.make_async_copy(
            self.ffn[0].at[pl.ds(0, FCUT)],
            self.ffn_buf.at[lax.rem(j, FFN_SLOTS)],
            self.ffn_sem.at[lax.rem(j, FFN_SLOTS)],
        ).wait()

    def role(self, j, plane, body):
        slot = lax.rem(j, LAND_SLOTS)
        key = self.plane + jnp.where(j < self.ffn_count, 0, 4)
        key = jnp.where((j >= 0) & (j < self.chain_total), key, 8)

        @pl.when(key == plane)
        def _():
            rows = pl.ds(pl.multiple_of(j * FCUT, 16), FCUT)
            body(
                self.ffn_buf.at[lax.rem(j, FFN_SLOTS)],
                self.low_f.at[j],
                self.up_f.at[j],
                self.low_buf.at[slot],
                self.up_buf.at[slot],
                self.out_f.at[rows],
            )

        @pl.when(key == plane + 4)
        def _():
            i = j - self.ffn_count
            rows = pl.ds(pl.multiple_of(i * CUT, 16), CUT)
            part = pl.ds(0, CUT)
            body(
                self.done.at[i + self.near],
                self.low_a.at[i],
                self.up_a.at[i],
                self.low_buf.at[slot, part],
                self.up_buf.at[slot, part],
                self.out_a.at[rows],
            )

    def chain(self, j, lane, src, dst, device):
        return pltpu.make_async_remote_copy(
            src_ref=src,
            dst_ref=dst,
            send_sem=self.chain_send.at[lane, j],
            recv_sem=self.chain_recv.at[lane, j],
            device_id=device,
            device_id_type=MESH,
        )

    def low_load(self, j, land, buf):
        return pltpu.make_async_copy(land, buf, self.low_sem.at[lax.rem(j, LAND_SLOTS)])

    def up_load(self, j, land, buf):
        return pltpu.make_async_copy(land, buf, self.up_sem.at[lax.rem(j, LAND_SLOTS)])

    def inward(self, j):
        @pl.when((j >= 0) & (j < self.ffn_count))
        def _():
            self.ffn_wait(j)

        def lowest(mine, low, up, low_buf, up_buf, out):
            self.chain(j, 0, mine, low, self.up_dev).start()

        def highest(mine, low, up, low_buf, up_buf, out):
            self.chain(j, 1, mine, up, self.low_dev).start()

        self.role(j, 0, lowest)
        self.role(j, 3, highest)

    def middle_arrives(self, j):
        def body(mine, low, up, low_buf, up_buf, out):
            self.chain(j, 1, mine, up, self.low_dev).wait_recv()
            self.up_load(j, up, up_buf).start()

        self.role(j, 2, body)

    def middle(self, j):
        def body(mine, low, up, low_buf, up_buf, out):
            self.up_load(j, up, up_buf).wait()
            mine[...] = add(mine[...], up_buf[...])
            self.chain(j, 1, mine, up, self.low_dev).start()

        self.role(j, 2, body)

    def root_arrives(self, j):
        def body(mine, low, up, low_buf, up_buf, out):
            self.chain(j, 0, mine, low, self.up_dev).wait_recv()
            self.low_load(j, low, low_buf).start()
            self.chain(j, 1, mine, up, self.low_dev).wait_recv()
            self.up_load(j, up, up_buf).start()

        self.role(j, 1, body)

    def root(self, j):
        def body(mine, low, up, low_buf, up_buf, out):
            self.low_load(j, low, low_buf).wait()
            self.up_load(j, up, up_buf).wait()
            mine[...] = add(mine[...], low_buf[...], up_buf[...])
            self.chain(j, 0, mine, out, self.up_dev).start()
            self.chain(j, 1, mine, out, self.low_dev).start()
            pltpu.make_async_copy(mine, out, self.out_sem.at[j]).start()

        self.role(j, 1, body)

    def outward(self, j):
        def body(mine, low, up, low_buf, up_buf, out):
            self.chain(j, 0, mine, out, self.up_dev).wait_recv()
            self.chain(j, 0, out, out, self.up_dev).start()

        self.role(j, 2, body)

    def drain(self, j):
        def lowest(mine, low, up, low_buf, up_buf, out):
            self.chain(j, 0, mine, low, self.up_dev).wait_send()
            self.chain(j, 1, mine, out, self.low_dev).wait_recv()

        def holder(mine, low, up, low_buf, up_buf, out):
            self.chain(j, 0, mine, out, self.up_dev).wait_send()
            self.chain(j, 1, mine, out, self.low_dev).wait_send()
            pltpu.make_async_copy(mine, out, self.out_sem.at[j]).wait()

        def between(mine, low, up, low_buf, up_buf, out):
            self.chain(j, 1, mine, up, self.low_dev).wait_send()
            self.chain(j, 0, out, out, self.up_dev).wait_send()

        def highest(mine, low, up, low_buf, up_buf, out):
            self.chain(j, 1, mine, up, self.low_dev).wait_send()
            self.chain(j, 0, mine, out, self.up_dev).wait_recv()

        for plane, body in enumerate((lowest, holder, between, highest)):
            self.role(j, plane, body)

    def stages(self, at, limit, pairs):
        for stage, behind in pairs:
            i = at - behind

            @pl.when((i >= 0) & (i < limit))
            def _(stage=stage, i=i):
                stage(i)

    def xy_step(self, i):
        self.stages(
            i,
            self.total,
            (
                (self.load, 0),
                (self.pair, 1),
                (self.plane_two, 7),
                (self.plane_one, 4),
                (self.two_arrives, 6),
                (self.one_arrives, 3),
            ),
        )

    def z_step(self, j):
        self.stages(j + 1, self.ffn_count, ((self.ffn_load, 0),))
        for stage, behind in (
            (self.inward, 0),
            (self.outward, 8),
            (self.root, 6),
            (self.middle, 3),
            (self.root_arrives, 5),
            (self.middle_arrives, 2),
            (self.drain, 11),
        ):
            stage(j - behind)

    def begin(self):
        self.ffn_load(jnp.int32(0))

    def finish(self, z_next, xy_next):
        both = (self.total + 8 - xy_next + 1) // 2

        def body(u, carry):
            self.z_step(z_next + 3 * u)
            self.xy_step(xy_next + 2 * u)
            self.z_step(z_next + 3 * u + 1)
            self.xy_step(xy_next + 2 * u + 1)
            self.z_step(z_next + 3 * u + 2)
            return carry

        def chain_only(u, carry):
            self.z_step(u)
            return carry

        lax.fori_loop(0, both, body, 0)
        lax.fori_loop(z_next + 3 * both, self.chain_total + 12, chain_only, 0)
        for i in range(max(self.total - MATE_SLOTS, 0), self.total):
            self.mate_copy(0, pl.ds(0, CUT), i % MATE_SLOTS).wait_send()
        for i in range(self.near):
            self.near_copy(i).wait()

    @staticmethod
    def shapes(pieces, ffn_pieces, wide):
        total, ffn_count = sum(pieces), sum(ffn_pieces)
        near = pieces[0]
        far = total - near
        chain_total = far + ffn_count
        low = jnp.bfloat16
        dma = pltpu.SemaphoreType.DMA
        shape = lambda *s: jax.ShapeDtypeStruct(s, low)
        buf = lambda *s: pltpu.VMEM(s, low)
        outs = [shape(n, wide) for n in (near * CUT, far * CUT, ffn_count * FCUT)]
        lands = [
            shape(total, 2, CUT, wide),
            shape(total, CUT, wide),
            *[shape(far, CUT, wide)] * 2,
            *[shape(ffn_count, FCUT, wide)] * 2,
        ]
        bufs = [
            buf(MATE_SLOTS, 2, 2, CUT, wide),
            buf(OWN_SLOTS, 2, 2, CUT, wide),
            buf(SUM_SLOTS, 2, 2, CUT, wide),
            buf(total, CUT, wide),
            buf(FFN_SLOTS, FCUT, wide),
            buf(LAND_SLOTS, 2, CUT, wide),
            buf(LAND_SLOTS, CUT, wide),
            buf(LAND_SLOTS, FCUT, wide),
            buf(LAND_SLOTS, FCUT, wide),
        ]
        sems = [
            dma((MATE_SLOTS,)),
            dma((MATE_SLOTS,)),
            dma((OWN_SLOTS,)),
            dma((SUM_SLOTS,)),
            dma((total,)),
            dma((LAND_SLOTS,)),
            dma((SUM_SLOTS,)),
            dma((total,)),
            dma((LAND_SLOTS,)),
            dma((FFN_SLOTS,)),
            dma((2, chain_total)),
            dma((2, chain_total)),
            dma((LAND_SLOTS,)),
            dma((LAND_SLOTS,)),
            dma((chain_total,)),
            dma((near,)),
            pltpu.SemaphoreType.REGULAR,
        ]
        return outs, lands, bufs, sems


class NoSums:
    def start(self):
        pass

    def begin(self):
        pass

    def z_step(self, j):
        pass

    def xy_step(self, i):
        pass

    def finish(self, z_next, xy_next):
        pass


def add(*terms):
    total = terms[0].astype(jnp.float32)
    for term in terms[1:]:
        total = total + term.astype(jnp.float32)
    return total.astype(jnp.bfloat16)


STEP_CHIP = (0, 0, 1, 2, 1, 2, 3, 3)
STEP_HALF = (0, 1, 0, 1, 1, 0, 0, 1)
TILE = 256


def ffn_kernel(
    act_in,
    cot_in,
    gate_in,
    up_in,
    down_in,
    out_part,
    dn_ref,
    grad_gate,
    grad_up,
    grad_down,
    act,
    cot,
    w_gate,
    w_up,
    w_down,
    hidden,
    d_gate,
    d_up,
    pair,
    mine,
    stage,
    out_buf,
    passed,
    final,
    tile_buf,
    weight_sem,
    cot_sem,
    own_sem,
    act_send,
    act_recv,
    pair_send,
    pair_recv,
    flow_send,
    flow_recv,
    tile_sem,
    end_sem,
    part_sem,
):
    me = lax.axis_index("grp")
    plane = lax.axis_index("rep")
    mate_dev, x_dev, y_dev = (me ^ 1, plane), (me ^ 2, plane), (me ^ 4, plane)
    half = act.shape[2]
    seq_len = 2 * half
    rows, wide = w_gate.shape
    low = jnp.bfloat16
    meet([mate_dev, x_dev, y_dev])

    def remote(src, dst, send, recv, device):
        return pltpu.make_async_remote_copy(
            src_ref=src,
            dst_ref=dst,
            send_sem=send,
            recv_sem=recv,
            device_id=device,
            device_id_type=MESH,
        )

    own = [act_in.at[pl.ds(h * half, half)] for h in range(2)]

    def act_copy(t, other):
        if other:
            src, device = (own[t] if t < 2 else act.at[t, 0]), mate_dev
        else:
            src, device = {
                2: (own[0], x_dev),
                3: (own[1], y_dev),
                4: (own[1], x_dev),
                5: (own[0], y_dev),
                6: (act.at[2, 0], y_dev),
                7: (act.at[3, 0], x_dev),
            }[t]
        return remote(
            src, act.at[t, other], act_send.at[t, other], act_recv.at[t, other], device
        )

    for t in (2, 3, 4, 5):
        act_copy(t, 0).start()
    for t in (0, 1):
        act_copy(t, 1).start()
    own_copies = [pltpu.make_async_copy(own[t], act.at[t, 0], own_sem.at[t]) for t in range(2)]
    for copy in own_copies:
        copy.start()
    weights = [
        pltpu.make_async_copy(src, dst, weight_sem.at[k])
        for k, (src, dst) in enumerate(((gate_in, w_gate), (up_in, w_up), (down_in, w_down)))
    ]
    for copy in weights:
        copy.start()
    cot_copies = []
    for t in range(8):
        for other in range(2):
            owner = me ^ (2 * STEP_CHIP[t] + other)
            row = pl.multiple_of(owner * seq_len + STEP_HALF[t] * half, 16)
            copy = pltpu.make_async_copy(
                cot_in.at[pl.ds(row, half)], cot.at[t, other], cot_sem.at[t, other]
            )
            copy.start()
            cot_copies.append(copy)

    def pair_copy(t):
        return remote(stage, pair.at[t], pair_send, pair_recv.at[t], mate_dev)

    def flow(lane):
        src, dst, device = (
            (pair.at[2], final.at[0], x_dev),
            (pair.at[4], final.at[1], x_dev),
            (pair.at[5], final.at[2], y_dev),
            (pair.at[3], final.at[3], y_dev),
            (pair.at[6], passed.at[0], x_dev),
            (pair.at[7], passed.at[1], y_dev),
        )[lane]
        return remote(src, dst, flow_send.at[lane], flow_recv.at[lane], device)

    def part_copy(t, other):
        owner = me ^ (2 * STEP_CHIP[t] + other)
        place = out_part.at[owner // 4, lax.rem(owner // 2, 2), lax.rem(owner, 2)]
        return pltpu.make_async_copy(
            out_buf.at[t % 2, pl.ds(other * half, half)],
            place.at[pl.ds(STEP_HALF[t] * half, half)],
            part_sem.at[t % 2, other],
        )

    def forward_tiles(t):
        def tile(n, carry):
            cut = pl.ds(pl.multiple_of(n * TILE, TILE), TILE)
            tokens = act[t].reshape(seq_len, wide)
            gate = dot_nt(tokens, w_gate[cut])
            up = dot_nt(tokens, w_up[cut])
            d_hidden = dot_nt(cot[t].reshape(seq_len, wide), w_down[cut])
            sigmoid = 1.0 / (1.0 + jnp.exp(-gate))
            silu = gate * sigmoid
            hidden[t, :, cut] = (silu * up).astype(low)
            d_gate[t, :, cut] = (
                d_hidden * up * (sigmoid * (1.0 + gate * (1.0 - sigmoid)))
            ).astype(low)
            d_up[t, :, cut] = (d_hidden * silu).astype(low)
            return carry

        lax.fori_loop(0, rows // TILE, tile, 0)

    def backward_tiles(t):
        def tile(n, carry):
            cut = pl.ds(pl.multiple_of(n * TILE, TILE), TILE)
            out_buf[lax.rem(t, 2), :, cut] = dot(hidden[t], w_down[:, cut]).astype(low)
            dn = dot(d_gate[t], w_gate[:, cut]) + dot(d_up[t], w_up[:, cut])
            mine[:, cut] = dn[:half].astype(low)
            stage[:, cut] = dn[half:].astype(low)
            return carry

        lax.fori_loop(0, wide // TILE, tile, 0)

    def join(t, events):
        pair_copy(t).wait()
        pair[t] = add(pair[t], mine[...])
        for when, lane in events:
            if when is None:
                flow(lane).start()
            else:

                @pl.when(t == when)
                def _(lane=lane):
                    flow(lane).start()

    for copy in own_copies + weights:
        copy.wait()

    def step(t, carry):
        for at in (2, 4, 6):

            @pl.when(t == at)
            def _(at=at):
                for u in (at, at + 1):
                    act_copy(u, 0).wait_recv()
                    if at == 2:
                        act_copy(u + 4, 0).start()
                    act_copy(u, 1).start()

        remote(
            act.at[t, 0], act.at[t, 1], act_send.at[t, 1], act_recv.at[t, 1], mate_dev
        ).wait_recv()
        for other in range(2):
            pltpu.make_async_copy(
                cot_in.at[pl.ds(0, half)], cot.at[t, other], cot_sem.at[t, other]
            ).wait()
        forward_tiles(t)

        @pl.when(t > 0)
        def _():
            join(t - 1, ((2, 0), (3, 3), (6, 4)))

        @pl.when(t >= 2)
        def _():
            for other in range(2):
                pltpu.make_async_copy(
                    out_buf.at[lax.rem(t, 2), pl.ds(other * half, half)],
                    out_part.at[0, 0, 0, pl.ds(0, half)],
                    part_sem.at[lax.rem(t, 2), other],
                ).wait()

        backward_tiles(t)
        pair_copy(t).start()
        for u in range(8):

            @pl.when(t == u)
            def _(u=u):
                for other in range(2):
                    part_copy(u, other).start()

        return carry

    lax.fori_loop(0, 8, step, 0)
    join(7, ((None, 5),))

    def write(target, slot, cut):
        return pltpu.make_async_copy(
            tile_buf.at[slot], target.at[:, cut], tile_sem.at[slot]
        )

    def pass_on():
        for lane, t, onward in ((4, 5, 2), (5, 4, 1)):
            flow(lane).wait_recv()
            pair[t] = add(pair[t], passed[lane - 4])
            flow(onward).start()

    tiles = wide // TILE
    for k, (left, right, target) in enumerate(
        ((d_gate, act, grad_gate), (d_up, act, grad_up), (hidden, cot, grad_down))
    ):

        def tile(n, carry, k=k, left=left, right=right, target=target):
            cut = pl.ds(pl.multiple_of(n * TILE, TILE), TILE)
            slot = lax.rem(n, 2)

            @pl.when(k * tiles + n >= 2)
            def _():
                write(target, slot, cut).wait()

            tile_buf[slot] = dot_tn(
                left[...].reshape(8 * seq_len, rows),
                right[:, :, :, cut].reshape(8 * seq_len, TILE),
            ).astype(low)
            write(target, slot, cut).start()
            return carry

        lax.fori_loop(0, tiles, tile, 0)
        if k == 1:
            pass_on()
    for slot in range(2):
        write(grad_down, slot, pl.ds(0, TILE)).wait()

    ends = []
    for h in range(2):
        flow(h).wait_recv()
        flow(2 + h).wait_recv()
        pair[h] = add(pair[h], final[h], final[2 + h])
        copy = pltpu.make_async_copy(pair.at[h], dn_ref.at[pl.ds(h * half, half)], end_sem.at[h])
        copy.start()
        ends.append(copy)
    for copy in ends:
        copy.wait()
    for t in (6, 7):
        for other in range(2):
            part_copy(t, other).wait()
    for lane in range(6):
        flow(lane).wait_send()
    for t in range(8):
        act_copy(t, 1).wait_send()
        if t >= 2:
            act_copy(t, 0).wait_send()


def ffn_all(act, cot, w_gate, w_up, w_down):
    seq_len, wide = act.shape
    rows = w_gate.shape[0]
    half = seq_len // 2
    low = jnp.bfloat16
    hbm = pl.BlockSpec(memory_space=pltpu.HBM)
    dma = pltpu.SemaphoreType.DMA
    return pl.pallas_call(
        ffn_kernel,
        out_shape=[
            jax.ShapeDtypeStruct((2, 2, 2, seq_len, wide), low),
            jax.ShapeDtypeStruct((seq_len, wide), low),
        ]
        + [jax.ShapeDtypeStruct((rows, wide), low)] * 3,
        in_specs=[hbm] * 5,
        out_specs=[hbm] * 5,
        scratch_shapes=[
            pltpu.VMEM((8, 2, half, wide), low),
            pltpu.VMEM((8, 2, half, wide), low),
            pltpu.VMEM((rows, wide), low),
            pltpu.VMEM((rows, wide), low),
            pltpu.VMEM((rows, wide), low),
            pltpu.VMEM((8, seq_len, rows), low),
            pltpu.VMEM((8, seq_len, rows), low),
            pltpu.VMEM((8, seq_len, rows), low),
            pltpu.VMEM((8, half, wide), low),
            pltpu.VMEM((half, wide), low),
            pltpu.VMEM((half, wide), low),
            pltpu.VMEM((2, seq_len, wide), low),
            pltpu.VMEM((2, half, wide), low),
            pltpu.VMEM((4, half, wide), low),
            pltpu.VMEM((2, rows, TILE), low),
            dma((3,)),
            dma((8, 2)),
            dma((2,)),
            dma((8, 2)),
            dma((8, 2)),
            dma,
            dma((8,)),
            dma((6,)),
            dma((6,)),
            dma((2,)),
            dma((2,)),
            dma((2, 2)),
        ],
        compiler_params=pltpu.CompilerParams(
            collective_id=2, has_side_effects=True, vmem_limit_bytes=VMEM_LIMIT
        ),
    )(act, cot, w_gate, w_up, w_down)


PAIR = 128
COND_ROWS = 256
NORM_ROWS = 32


def normalise(read, gain, shift, write, rows):
    def block(n, carry):
        cut = pl.ds(pl.multiple_of(n * NORM_ROWS, NORM_ROWS), NORM_ROWS)
        write[cut] = layer_norm(read[cut].astype(jnp.float32), gain[...], shift[...]).astype(
            write.dtype
        )
        return carry

    lax.fori_loop(0, rows // NORM_ROWS, block, 0)


def normalise_back(read, gain, d_read, straight, write, sums, row, rows):
    wide = read.shape[1]

    def block(n, carry):
        d_gain, d_shift = carry
        cut = pl.ds(pl.multiple_of(n * NORM_ROWS, NORM_ROWS), NORM_ROWS)
        tensor = read[cut].astype(jnp.float32)
        center = tensor - jnp.mean(tensor, axis=-1, keepdims=True)
        spread = jnp.mean(center * center, axis=-1, keepdims=True)
        inverse = lax.rsqrt(spread + epsilon)
        hat = center * inverse
        d_out = d_read[cut].astype(jnp.float32)
        scaled = d_out * gain[...]
        dv = inverse * (
            scaled
            - jnp.mean(scaled, axis=-1, keepdims=True)
            - hat * jnp.mean(scaled * hat, axis=-1, keepdims=True)
        )
        write[cut] = straight[cut].astype(jnp.float32) + dv
        d_gain = d_gain + jnp.sum((d_out * hat).reshape(NORM_ROWS // 8, 8, wide), axis=0)
        d_shift = d_shift + jnp.sum(d_out.reshape(NORM_ROWS // 8, 8, wide), axis=0)
        return d_gain, d_shift

    zero = jnp.zeros((8, wide), jnp.float32)
    d_gain, d_shift = lax.fori_loop(0, rows // NORM_ROWS, block, (zero, zero))
    sums[row : row + 1] = jnp.sum(d_gain, axis=0, keepdims=True)
    sums[row + 1 : row + 2] = jnp.sum(d_shift, axis=0, keepdims=True)


def turn(tensor, cosine, sine_left, sine_right):
    return (
        tensor * cosine
        + pltpu.roll(tensor, PAIR - HD // 4, 1) * sine_left
        + pltpu.roll(tensor, HD // 4, 1) * sine_right
    )


def tiles_of(count, body):
    def step(n, carry):
        body(pl.ds(pl.multiple_of(n * TILE, TILE), TILE))
        return carry

    lax.fori_loop(0, count // TILE, step, 0)


def pair_loop(body):
    def step(p, carry):
        body(p, pl.multiple_of(p * PAIR, PAIR))
        return carry

    lax.fori_loop(0, HEADS * HD // PAIR, step, 0)


def first_head(rows):
    return lax.broadcasted_iota(jnp.int32, (rows, PAIR), 1) < HD


def head_softmax(query, key, mine, keys):
    scores = dot_nt(jnp.where(mine, query, jnp.zeros_like(query)), key) * score_scale
    if keys < key.shape[0]:
        lanes = lax.broadcasted_iota(jnp.int32, scores.shape, 1)
        scores = jnp.where(lanes < keys, scores, -1e30)
    shifted = jnp.exp(scores - jnp.max(scores, axis=-1, keepdims=True))
    return (shifted * (1.0 / jnp.sum(shifted, axis=-1, keepdims=True))).astype(jnp.bfloat16)


def attend_pair(query, key, value, keys, keep):
    mask = first_head(query.shape[0])
    results = []
    for head in range(2):
        probability = head_softmax(query, key, mask if head == 0 else ~mask, keys)
        keep(head, probability)
        results.append(dot(probability, value))
    return jnp.where(mask, results[0], results[1]).astype(jnp.bfloat16)


def attend_pair_back(query, key, value, grad, probabilities):
    mask, key_mask = first_head(query.shape[0]), first_head(key.shape[0])
    d_queries, d_keys, d_values = [], [], []
    for head in range(2):
        probability = probabilities[head]
        mine = mask if head == 0 else ~mask
        d_prob = dot_nt(jnp.where(mine, grad, jnp.zeros_like(grad)), value)
        wide = probability.astype(jnp.float32)
        inner = jnp.sum(wide * d_prob, axis=-1, keepdims=True)
        d_scores = (wide * (d_prob - inner)).astype(jnp.bfloat16)
        d_queries.append(dot(d_scores, key))
        d_keys.append(dot_tn(d_scores, query))
        d_values.append(dot_tn(probability, grad))
    return (
        jnp.where(mask, d_queries[0], d_queries[1]) * score_scale,
        jnp.where(key_mask, d_keys[0], d_keys[1]) * score_scale,
        jnp.where(key_mask, d_values[0], d_values[1]),
    )


def attention_forward_kernel(
    pieces,
    x_in,
    cond_in,
    cosine,
    sine_left,
    sine_right,
    norms_in,
    qkv_in,
    out_in,
    kv2_in,
    query2_in,
    out2_in,
    norms_out,
    qkv_out,
    out_out,
    query2_out,
    out2_out,
    act_one_out,
    heads_out,
    prob_out,
    flat_one_out,
    section_one_out,
    act_two_out,
    query_two_out,
    kv_two_out,
    prob_two_out,
    flat_two_out,
    section_two_out,
    act_three_out,
    x,
    cond,
    norm_parts,
    w_qkv,
    w_out,
    w_kv2,
    w_query2,
    w_out2,
    act,
    heads,
    flat,
    section,
    query_two,
    kv_two,
    prob,
    prob_two,
    in_sem,
    out_sem,
    prob_sem,
    local_sem,
    *gather_sems,
):
    rows, wide = x.shape
    low = jnp.bfloat16
    sources = (norms_in, qkv_in, out_in, kv2_in, query2_in, out2_in)
    fulls = (norm_parts, w_qkv, w_out, w_kv2, w_query2, w_out2)
    if pieces is None:
        gather = Loads(sources, fulls, local_sem)
    else:
        gather = Gather(pieces, sources, fulls, *gather_sems, local_sem)
    gather.start()
    loads = []
    for k, (src, dst) in enumerate(((x_in, x), (cond_in, cond))):
        loads.append(pltpu.make_async_copy(src, dst, in_sem.at[k]))
        loads[-1].start()
    for k in range(len(sources)):
        gather.own_copy(k).start()
    stores = []

    def save(src, dst):
        stores.append(pltpu.make_async_copy(src, dst, out_sem.at[len(stores)]))
        stores[-1].start()
        return stores[-1]

    lead = GATHER_WINDOW + 2
    gather.run(0, 1 + lead)
    loads[0].wait()
    gather.need(0)
    norms_out[...] = jnp.sum(
        norm_parts[...].astype(jnp.float32).reshape(norm_parts.shape[0] // 16, 16, wide), axis=0
    )
    gains = [norms_out.at[pl.ds(k, 1)] for k in range(6)]
    normalise(x, gains[0], gains[1], act, rows)
    act_one_done = save(act, act_one_out)
    done = 13 + lead
    gather.run(1 + lead, done)
    gather.need(1)
    save(w_qkv, qkv_out)

    def project(cut, rotated):
        result = dot_nt(act[...], w_qkv[cut])
        for part in range(TILE // PAIR):
            piece = result[:, part * PAIR : (part + 1) * PAIR]
            if rotated:
                piece = turn(piece, cosine[...], sine_left[...], sine_right[...])
            heads[:, pl.ds(pl.multiple_of(cut.start + part * PAIR, PAIR), PAIR)] = piece.astype(low)

    for part in range(3):
        tiles_of(
            wide,
            lambda cut, part=part: project(
                pl.ds(pl.multiple_of(cut.start + part * wide, TILE), TILE), part < 2
            ),
        )
        gather.step(done + part)
    done += 3
    save(heads, heads_out)

    def prob_copy(buf, out, p, slot):
        return pltpu.make_async_copy(buf.at[slot], out.at[p], prob_sem.at[slot])

    def self_pair(p, lane):
        slot = lax.rem(p, 2)

        @pl.when(p >= 2)
        def _():
            prob_copy(prob, prob_out, p, slot).wait()

        def keep(head, probability):
            prob[slot, head] = probability

        cols = [pl.ds(pl.multiple_of(lane + k * wide, PAIR), PAIR) for k in range(3)]
        flat[:, cols[0]] = attend_pair(
            heads[:, cols[0]], heads[:, cols[1]], heads[:, cols[2]], rows, keep
        )
        prob_copy(prob, prob_out, p, slot).start()
        serve(p, SELF_EVERY)

    def serve(p, every):
        if gather.steps:

            @pl.when(lax.rem(p, every) == every - 1)
            def _():
                gather.step(done + p // every)

    pairs = wide // PAIR
    pair_loop(self_pair)
    done += pairs // SELF_EVERY
    for slot in range(2):
        prob_copy(prob, prob_out, 0, slot).wait()
    flat_one_done = save(flat, flat_one_out)
    gather.run(done, 17 + lead)
    done = max(done, 17 + lead)
    gather.need(2)
    save(w_out, out_out)

    def first_section(cut):
        section[:, cut] = x[:, cut].astype(jnp.float32) + dot_nt(flat[...], w_out[cut])

    tiles_of(wide, first_section)
    section_one_done = save(section, section_one_out)
    gather.run(done, 21 + lead)
    gather.step(max(done, 21 + lead))
    done = max(done, 21 + lead) + 1
    act_one_done.wait()
    normalise(section, gains[2], gains[3], act, rows)
    act_two_done = save(act, act_two_out)
    loads[1].wait()
    gather.need(3)

    def condition(cut):
        kv_two[:, cut] = dot_nt(cond[...], w_kv2[cut]).astype(low)

    tiles_of(2 * wide, condition)
    save(kv_two, kv_two_out)
    gather.run(done, 25 + lead)
    done = max(done, 25 + lead)
    gather.need(4)
    save(w_query2, query2_out)

    def query(cut):
        query_two[:, cut] = dot_nt(act[...], w_query2[cut]).astype(low)

    tiles_of(wide, query)
    save(query_two, query_two_out)
    flat_one_done.wait()

    def cross_pair(p, lane):
        slot = lax.rem(p, 2)

        @pl.when(p >= 2)
        def _():
            prob_copy(prob_two, prob_two_out, p, slot).wait()

        def keep(head, probability):
            prob_two[slot, head] = probability

        cols = [pl.ds(pl.multiple_of(lane + k * wide, PAIR), PAIR) for k in range(2)]
        flat[:, cols[0]] = attend_pair(
            query_two[:, cols[0]], kv_two[:, cols[0]], kv_two[:, cols[1]], NC, keep
        )
        prob_copy(prob_two, prob_two_out, p, slot).start()
        serve(p, CROSS_EVERY)

    pair_loop(cross_pair)
    done += pairs // CROSS_EVERY
    gather.run(done, 29 + lead)
    for slot in range(2):
        prob_copy(prob_two, prob_two_out, 0, slot).wait()
    save(flat, flat_two_out)
    gather.need(5)
    save(w_out2, out2_out)
    section_one_done.wait()

    def second_section(cut):
        section[:, cut] = section[:, cut] + dot_nt(flat[...], w_out2[cut])

    tiles_of(wide, second_section)
    save(section, section_two_out)
    act_two_done.wait()
    normalise(section, gains[4], gains[5], act, rows)
    save(act, act_three_out)
    waited = [id(c) for c in (act_one_done, flat_one_done, section_one_done, act_two_done)]
    gather.finish()
    for copy in stores:
        if id(copy) not in waited:
            copy.wait()


SELF_EVERY = 2
CROSS_EVERY = 3


def attention_forward(x, cond, tables, norms, weights):
    rows, wide = x.shape
    low, full = jnp.bfloat16, jnp.float32
    pairs = wide // PAIR
    hbm = pl.BlockSpec(memory_space=pltpu.HBM)
    vmem = pl.BlockSpec(memory_space=pltpu.VMEM)
    dma = pltpu.SemaphoreType.DMA
    shape = jax.ShapeDtypeStruct
    groups = lax.axis_size("grp")
    parameters = [norms] + list(weights)
    whole = [(groups * w.shape[0], w.shape[1]) for w in parameters]
    sems = []
    pieces = None
    options = {}
    if groups == 8 and lax.axis_size("rep") % 2 == 0:
        piece_rows = (16, 48, 48, 96, 48, 48)
        pieces = tuple((w.shape[0] // n, n) for w, n in zip(parameters, piece_rows))
        total = sum(n for n, _ in pieces)
        sems = [dma((7, total)), dma((7, total))]
        options = dict(collective_id=0, has_side_effects=True)
    else:
        parameters = [lax.all_gather(w, "grp", axis=0, tiled=True) for w in parameters]
    results = pl.pallas_call(
        functools.partial(attention_forward_kernel, pieces),
        out_shape=[
            shape((16, wide), full),
            *[shape(whole[k], low) for k in (1, 2, 4, 5)],
            shape((rows, wide), low),
            shape((rows, 3 * wide), low),
            shape((pairs, 2, rows, rows), low),
            shape((rows, wide), low),
            shape((rows, wide), full),
            shape((rows, wide), low),
            shape((rows, wide), low),
            shape((COND_ROWS, 2 * wide), low),
            shape((pairs, 2, rows, COND_ROWS), low),
            shape((rows, wide), low),
            shape((rows, wide), full),
            shape((rows, wide), low),
        ],
        in_specs=[hbm, hbm] + [vmem] * 3 + [hbm] * 6,
        out_specs=[vmem] + [hbm] * 16,
        scratch_shapes=[
            pltpu.VMEM((rows, wide), low),
            pltpu.VMEM(cond.shape, low),
            *[pltpu.VMEM(s, low) for s in whole],
            pltpu.VMEM((rows, wide), low),
            pltpu.VMEM((rows, 3 * wide), low),
            pltpu.VMEM((rows, wide), low),
            pltpu.VMEM((rows, wide), full),
            pltpu.VMEM((rows, wide), low),
            pltpu.VMEM((COND_ROWS, 2 * wide), low),
            pltpu.VMEM((2, 2, rows, rows), low),
            pltpu.VMEM((2, 2, rows, COND_ROWS), low),
            dma((2,)),
            dma((14,)),
            dma((2,)),
            dma((6,)),
            *sems,
        ],
        compiler_params=pltpu.CompilerParams(vmem_limit_bytes=VMEM_LIMIT, **options),
    )(x, cond, *tables, *parameters)
    return results[0], results[1:5], results[5:]


GRAD_TILE = 2 * UNIT


def attention_backward_kernel(plan, *refs):
    refs = list(refs)

    def take(n):
        taken = refs[:n]
        del refs[:n]
        return taken

    x_in, cond_in, norms, cosine, sine_left, sine_right = take(6)
    qkv_in, out_in, query2_in, out2_in = take(4)
    act_one_in, heads_in, prob_in, flat_one_in, section_one_in, act_two_in = take(6)
    query_two_in, kv_two_in, prob_two_in, flat_two_in, section_two_in = take(5)
    d_norm_in, d_out_in = take(2)
    out_part, *ffn_in = take(4) if plan else [None]
    d_inputs_out, sums = take(2)
    grad_out2, grad_query2, grad_kv2, grad_out, grad_qkv = take(5)
    if plan:
        (grad_norm,) = take(1)
        sum_outs, lands = take(3), take(6)
    w_small, w_tile = take(2)
    x, cond, act_one, heads, flat_one, section_one, act_two = take(7)
    query_two, kv_two, flat_two, section_two, d_norm = take(5)
    d_low, d_heads, d_kv, d_att, prob, prob_two, grad_buf = take(7)
    in_sem, weight_sem, tile_sem, prob_sem, grad_sem, end_sem = take(6)
    if plan:
        norm_buf, norm_sem = take(2)
        bufs, sems = take(9), take(17)
        parts = (out_part, grad_out2, grad_query2, grad_kv2, grad_out, grad_qkv, grad_norm)
        work = Sums(plan[0], plan[1], parts, ffn_in, sum_outs, lands, bufs, sems)
    else:
        work = NoSums()
    rows, wide = x.shape
    pairs = wide // PAIR
    low = jnp.bfloat16
    work.start()
    work.begin()
    loads = {}
    for k, (name, src, dst) in enumerate(
        (
            ("section_two", section_two_in, section_two),
            ("d_norm", d_norm_in, d_norm),
            ("d_out", d_out_in, d_low),
            ("w_out2", out2_in, w_small),
            ("flat_two", flat_two_in, flat_two),
            ("query_two", query_two_in, query_two),
            ("kv_two", kv_two_in, kv_two),
            ("cond", cond_in, cond),
            ("act_two", act_two_in, act_two),
            ("section_one", section_one_in, section_one),
            ("flat_one", flat_one_in, flat_one),
            ("heads", heads_in, heads),
            ("act_one", act_one_in, act_one),
            ("x", x_in, x),
        )
    ):
        loads[name] = pltpu.make_async_copy(src, dst, in_sem.at[k])
        loads[name].start()

    def need(*names):
        for name in names:
            loads[name].wait()

    def next_weight(name, src, k):
        loads[name] = pltpu.make_async_copy(src, w_small, weight_sem.at[k])
        loads[name].start()

    gains = [norms.at[pl.ds(2 * k, 1)] for k in range(3)]

    def prob_copy(src, buf, p, slot):
        return pltpu.make_async_copy(src.at[p], buf.at[slot], prob_sem.at[slot])

    def prob_start(src, buf):
        for p in range(2):
            prob_copy(src, buf, p, p).start()

    at = {"z": 0, "xy": 0}

    def serve(*kinds):
        for kind in kinds:
            (work.z_step if kind == "z" else work.xy_step)(jnp.int32(at[kind]))
            at[kind] += 1

    def serve_pairs(p, kind, every):
        @pl.when(lax.rem(p, every) == every - 1)
        def _():
            (work.z_step if kind == "z" else work.xy_step)(at[kind] + p // every)

    def unit_copy(target, n, half, slot):
        src = grad_buf.at[slot, pl.ds(half * UNIT, UNIT)]
        unit = 2 * n + half
        if plan:
            per = target.shape[3] // UNIT
            block = unit // per
            row = pl.multiple_of(lax.rem(unit, per) * UNIT, 16)
            place = target.at[block // 4, lax.rem(block // 2, 2), lax.rem(block, 2), pl.ds(row, UNIT)]
        else:
            place = target.at[pl.ds(pl.multiple_of(unit * UNIT, 16), UNIT)]
        return pltpu.make_async_copy(src, place, grad_sem.at[slot, half])

    def grad_rows(target, count, compute, every=0):
        def step(n, carry):
            slot = lax.rem(n, 2)

            @pl.when(n >= 2)
            def _():
                for half in range(2):
                    unit_copy(target, n, half, slot).wait()

            compute(n, slot)
            for half in range(2):
                unit_copy(target, n, half, slot).start()
            if every:
                serve_pairs(n, "z", every)
            return carry

        lax.fori_loop(0, count, step, 0)
        for slot in range(2):
            for half in range(2):
                unit_copy(target, 0, half, slot).wait()

    def weight_rows(left, right, target, every=0):
        def compute(n, slot):
            columns = left[:, pl.ds(pl.multiple_of(n * GRAD_TILE, 128), GRAD_TILE)]
            for m in range(wide // 512):
                piece = slice(m * 512, (m + 1) * 512)
                grad_buf[slot, :, piece] = dot_tn(columns, right[:, piece]).astype(low)

        grad_rows(target, left.shape[1] // GRAD_TILE, compute, every)

    def round_rows():
        def block(n, carry):
            cut = pl.ds(pl.multiple_of(n * NORM_ROWS, NORM_ROWS), NORM_ROWS)
            d_low[cut] = d_section[cut].astype(low)
            return carry

        lax.fori_loop(0, rows // NORM_ROWS, block, 0)

    def through(target):
        def body(cut):
            target[:, cut] = dot(d_low[...], w_small[:, cut]).astype(low)

        tiles_of(wide, body)

    prob_start(prob_two_in, prob_two)
    serve("z", "xy")
    need("section_two", "d_norm", "d_out")
    normalise_back(section_two, gains[2], d_norm, d_low, section_two, sums, 4, rows)
    d_section = section_two
    round_rows()
    serve("z", "xy")
    need("w_out2")
    through(d_att)
    next_weight("w_query2", query2_in, 0)
    serve("z", "xy")
    need("flat_two")
    weight_rows(d_low, flat_two, grad_out2)
    serve("xy", "z")
    need("query_two", "kv_two")

    def cross_pair(p, lane):
        slot = lax.rem(p, 2)
        prob_copy(prob_two_in, prob_two, p, slot).wait()
        cols = [pl.ds(pl.multiple_of(lane + k * wide, PAIR), PAIR) for k in range(2)]
        d_query, d_key, d_value = attend_pair_back(
            query_two[:, cols[0]],
            kv_two[:, cols[0]],
            kv_two[:, cols[1]],
            d_att[:, cols[0]],
            [prob_two[slot, head] for head in range(2)],
        )
        d_low[:, cols[0]] = d_query.astype(low)
        d_kv[:, cols[0]] = d_key.astype(low)
        d_kv[:, cols[1]] = d_value.astype(low)

        @pl.when(p + 2 < pairs)
        def _():
            prob_copy(prob_two_in, prob_two, p + 2, slot).start()

        serve_pairs(p, "z", 2)
        serve_pairs(p, "xy", 3)

    pair_loop(cross_pair)
    at["z"] += 6
    at["xy"] += 4
    prob_start(prob_in, prob)
    need("w_query2")
    through(d_norm)
    next_weight("w_out", out_in, 1)
    serve("z", "xy")
    need("act_two")
    weight_rows(d_low, act_two, grad_query2)
    serve("z", "xy")
    need("cond")

    def cond_rows(n, slot):
        for half in range(2):
            columns = pl.ds(pl.multiple_of((2 * n + half) * GRAD_TILE, 128), GRAD_TILE)
            result = dot_tn(d_kv[:, columns], cond[...]).astype(low)
            at = slice(half * UNIT, (half + 1) * UNIT)
            grad_buf[slot, at, : wide // 2] = result[:UNIT]
            grad_buf[slot, at, wide // 2 :] = result[UNIT:]

    grad_rows(grad_kv2, wide // GRAD_TILE, cond_rows)
    serve("xy", "z")
    need("section_one")
    normalise_back(section_one, gains[1], d_norm, d_section, d_section, sums, 2, rows)
    serve("z", "xy")
    round_rows()
    need("w_out")
    through(d_att)

    def tile_copy(n, slot):
        cut = pl.ds(pl.multiple_of(n * TILE, TILE), TILE)
        return pltpu.make_async_copy(qkv_in.at[:, cut], w_tile.at[slot], tile_sem.at[slot])

    for n in range(2):
        tile_copy(n, n).start()
    serve("xy", "z")
    need("flat_one")
    weight_rows(d_low, flat_one, grad_out)
    serve("z", "xy")
    need("heads")

    def self_pair(p, lane):
        slot = lax.rem(p, 2)
        prob_copy(prob_in, prob, p, slot).wait()
        cols = [pl.ds(pl.multiple_of(lane + k * wide, PAIR), PAIR) for k in range(3)]
        d_query, d_key, d_value = attend_pair_back(
            heads[:, cols[0]],
            heads[:, cols[1]],
            heads[:, cols[2]],
            d_att[:, cols[0]],
            [prob[slot, head] for head in range(2)],
        )
        back = (cosine[...], -sine_left[...], -sine_right[...])
        d_heads[:, cols[0]] = turn(d_query, *back).astype(low)
        d_heads[:, cols[1]] = turn(d_key, *back).astype(low)
        d_heads[:, cols[2]] = d_value.astype(low)

        @pl.when(p + 2 < pairs)
        def _():
            prob_copy(prob_in, prob, p + 2, slot).start()

        work.z_step(at["z"] + p + (p + 1) // 2)

        @pl.when(lax.rem(p, 2) == 0)
        def _():
            work.z_step(at["z"] + p + 1 + p // 2)

        @pl.when(p < 10)
        def _():
            serve_pairs(p, "xy", 1)


    pair_loop(self_pair)
    at["z"] += pairs * 3 // 2
    at["xy"] += 10
    need("act_one")
    weight_rows(d_heads, act_one, grad_qkv, 4)
    at["z"] += 3
    serve("z", "xy")

    def first_norm(n, carry):
        slot = lax.rem(n, 2)
        cut = pl.ds(pl.multiple_of(n * TILE, TILE), TILE)
        tile_copy(n, slot).wait()
        d_norm[:, cut] = dot(d_heads[...], w_tile[slot]).astype(low)
        serve_pairs(n, "z", 3)

        @pl.when(n + 2 < wide // TILE)
        def _():
            tile_copy(n + 2, slot).start()

        return carry

    lax.fori_loop(0, wide // TILE, first_norm, 0)
    at["z"] += 2
    serve("z", "xy")
    need("x")
    normalise_back(x, gains[0], d_norm, d_section, d_section, sums, 0, rows)
    end = pltpu.make_async_copy(d_section, d_inputs_out, end_sem)
    end.start()
    if plan:
        norm_buf[...] = jnp.zeros_like(norm_buf)
        norm_buf[:8] = sums[...].astype(low)
        copies = []
        for b in range(8):
            place = grad_norm.at[b // 4, b // 2 % 2, b % 2]
            copies.append(pltpu.make_async_copy(norm_buf, place, norm_sem.at[b]))
            copies[-1].start()
        for copy in copies:
            copy.wait()
    work.finish(at["z"], at["xy"])
    end.wait()


def attention_backward(x, cond, norms, tables, weights, kept, d_norm, d_out, out_part, ffn):
    rows, wide = x.shape
    low, full = jnp.bfloat16, jnp.float32
    hbm = pl.BlockSpec(memory_space=pltpu.HBM)
    vmem = pl.BlockSpec(memory_space=pltpu.VMEM)
    dma = pltpu.SemaphoreType.DMA
    shape = jax.ShapeDtypeStruct
    buf = lambda s, t=low: pltpu.VMEM(s, t)
    heights = (wide, wide, wide, wide, 3 * wide)
    more_outs, more_scratch = [], []
    plan = None
    options = {}
    if ffn:
        grads = [(2, 2, 2, h // 8, wide) for h in heights] + [(2, 2, 2, CUT, wide)]
        plan = (
            tuple(g[3] // CUT for g in [out_part.shape] + grads),
            tuple(f.shape[0] // FCUT for f in ffn),
        )
        outs, lands, bufs, sems = Sums.shapes(*plan, wide)
        more_outs = outs + lands
        more_scratch = [buf((CUT, wide)), dma((8,))] + bufs + sems
        options = dict(collective_id=1, has_side_effects=True)
    else:
        grads = [(h, wide) for h in heights]
    ffn = [out_part] + list(ffn) if ffn else []
    results = pl.pallas_call(
        functools.partial(attention_backward_kernel, plan),
        out_shape=[shape((rows, wide), full), shape((8, wide), full)]
        + [shape(g, low) for g in grads]
        + more_outs,
        in_specs=[hbm, hbm] + [vmem] * 4 + [hbm] * (17 + len(ffn)),
        out_specs=[hbm, vmem] + [hbm] * (len(grads) + len(more_outs)),
        scratch_shapes=[
            buf((wide, wide)),
            buf((2, 3 * wide, TILE)),
            buf((rows, wide)),
            buf(cond.shape),
            buf((rows, wide)),
            buf((rows, 3 * wide)),
            buf((rows, wide)),
            buf((rows, wide), full),
            buf((rows, wide)),
            buf((rows, wide)),
            buf((COND_ROWS, 2 * wide)),
            buf((rows, wide)),
            buf((rows, wide), full),
            buf((rows, wide)),
            buf((rows, wide)),
            buf((rows, 3 * wide)),
            buf((COND_ROWS, 2 * wide)),
            buf((rows, wide)),
            buf((2, 2, rows, rows)),
            buf((2, 2, rows, COND_ROWS)),
            buf((2, GRAD_TILE, wide)),
            dma((14,)),
            dma((2,)),
            dma((2,)),
            dma((2,)),
            dma((2, 2)),
            dma,
            *more_scratch,
        ],
        compiler_params=pltpu.CompilerParams(vmem_limit_bytes=VMEM_LIMIT, **options),
    )(x, cond, norms, *tables, *weights, *kept, d_norm, d_out, *ffn)
    return results[0], results[1], results[2:7], results[8:11]


END_SLOTS = 4


def end_kernel(near, far, ffn, section, *refs):
    outs, (low_buf, full_buf, in_sem, out_sem) = refs[:9], refs[9:]
    outputs, out2, query2, kv2, out, qkv, gate, up, down = outs
    wide = low_buf.shape[2]
    jobs = []
    base = 0
    for target in (out2, query2, kv2, out, qkv):
        rows = target.shape[0] * target.shape[1] // wide
        jobs += [(far, base + r, target, r) for r in range(0, rows, UNIT)]
        base += rows
    base = 0
    for target in (gate, up, down):
        jobs += [(ffn, base + r, target, r) for r in range(0, target.shape[0], UNIT)]
        base += target.shape[0]
    jobs += [(near, r, outputs, r) for r in range(0, outputs.shape[0], UNIT)]

    def loads(n):
        source, row, target, place = jobs[n]
        slot = n % END_SLOTS
        copies = [
            pltpu.make_async_copy(
                source.at[pl.ds(row, UNIT)], low_buf.at[slot], in_sem.at[slot, 0]
            )
        ]
        if target is outputs:
            copies.append(
                pltpu.make_async_copy(
                    section.at[pl.ds(place, UNIT)], full_buf.at[slot], in_sem.at[slot, 1]
                )
            )
        return copies

    def stores(n):
        _, _, target, place = jobs[n]
        slot = n % END_SLOTS
        if target is outputs:
            pairs = [(low_buf.at[slot], target.at[pl.ds(place, UNIT)])]
        elif target is kv2:
            pairs = [
                (
                    full_buf.at[slot, :, pl.ds(h * (wide // 2), wide // 2)],
                    target.at[pl.ds(2 * place + h * UNIT, UNIT)],
                )
                for h in range(2)
            ]
        else:
            pairs = [(full_buf.at[slot], target.at[pl.ds(place, UNIT)])]
        return [
            pltpu.make_async_copy(src, dst, out_sem.at[slot, k])
            for k, (src, dst) in enumerate(pairs)
        ]

    ahead = END_SLOTS - 2
    for n in range(ahead):
        for copy in loads(n):
            copy.start()
    for n in range(len(jobs)):
        if n + ahead < len(jobs):
            if n + ahead >= END_SLOTS:
                for copy in stores(n + ahead - END_SLOTS):
                    copy.wait()
            for copy in loads(n + ahead):
                copy.start()
        for copy in loads(n):
            copy.wait()
        slot = n % END_SLOTS
        is_output = jobs[n][2] is outputs

        def block(m, carry, slot=slot, is_output=is_output):
            cut = pl.ds(pl.multiple_of(m * 32, 32), 32)
            value = low_buf[slot, cut].astype(jnp.float32)
            if is_output:
                low_buf[slot, cut] = (full_buf[slot, cut] + value).astype(low_buf.dtype)
            else:
                full_buf[slot, cut] = value
            return carry

        lax.fori_loop(0, UNIT // 32, block, 0)
        for copy in stores(n):
            copy.start()
    for n in range(max(len(jobs) - END_SLOTS, 0), len(jobs)):
        for copy in stores(n):
            copy.wait()


def end_all(near, far, ffn, section, out_shapes):
    hbm = pl.BlockSpec(memory_space=pltpu.HBM)
    wide = near.shape[1]
    dma = pltpu.SemaphoreType.DMA
    return pl.pallas_call(
        end_kernel,
        out_shape=[jax.ShapeDtypeStruct(near.shape, near.dtype)]
        + [jax.ShapeDtypeStruct(s, jnp.float32) for s in out_shapes],
        in_specs=[hbm] * 4,
        out_specs=[hbm] * 9,
        scratch_shapes=[
            pltpu.VMEM((END_SLOTS, UNIT, wide), near.dtype),
            pltpu.VMEM((END_SLOTS, UNIT, wide), jnp.float32),
            dma((END_SLOTS, 2)),
            dma((END_SLOTS, 2)),
        ],
        compiler_params=pltpu.CompilerParams(vmem_limit_bytes=VMEM_LIMIT),
    )(near, far, ffn, section)


def per_device(
    inputs,
    conditioning,
    positions,
    slot_valid,
    cotangent,
    norm1_gain,
    norm1_shift,
    norm2_gain,
    norm2_shift,
    norm3_gain,
    norm3_shift,
    w_qkv,
    w_out,
    w_query2,
    w_kv2,
    w_out2,
    w_gate,
    w_up,
    w_down,
):
    cond_rows = conditioning[0]
    norms = jnp.stack(
        [norm1_gain, norm1_shift, norm2_gain, norm2_shift, norm3_gain, norm3_shift], axis=0
    )
    own_width = norms.shape[1]
    norms = lax.dynamic_update_slice(
        jnp.zeros((16, D), norms.dtype), norms, (0, lax.axis_index("grp") * own_width)
    )
    grad_mlp = (cotangent[0].astype(jnp.float32) * slot_valid[0].astype(jnp.float32)).astype(
        jnp.bfloat16
    )
    all_grad = lax.all_gather(grad_mlp, "grp", axis=0, tiled=True)
    tables = turn_tables(positions[0])
    padded_cond = jnp.pad(cond_rows, ((0, COND_ROWS - NC), (0, 0)))
    norms, whole, kept = attention_forward(
        inputs[0], padded_cond, tables, norms, [w_qkv, w_out, w_kv2, w_query2, w_out2]
    )
    act_three, section_two = kept[-1], kept[-2]
    if lax.axis_size("grp") == 8:
        mlp_out, d_norm3, grad_gate, grad_up, grad_down = ffn_all(
            act_three, all_grad, w_gate, w_up, w_down
        )
    else:
        all_act = lax.all_gather(act_three, "grp", axis=0, tiled=True)
        gate_pre = dot_nt(all_act, w_gate)
        up_pre = dot_nt(all_act, w_up)
        hidden = swiglu(gate_pre, up_pre).astype(jnp.bfloat16)
        mlp_part = dot(hidden, w_down).astype(jnp.bfloat16)
        mlp_out = lax.psum_scatter(mlp_part, "grp", scatter_dimension=0, tiled=True)
        d_hidden = dot_nt(all_grad, w_down)
        d_gate_full, d_up_full = swiglu_back(gate_pre, up_pre, d_hidden)
        d_gate = d_gate_full.astype(jnp.bfloat16)
        d_up = d_up_full.astype(jnp.bfloat16)
        d_norm3_part = (dot(d_gate, w_gate) + dot(d_up, w_up)).astype(jnp.bfloat16)
        d_norm3 = lax.psum_scatter(d_norm3_part, "grp", scatter_dimension=0, tiled=True)
        grad_gate = dot_tn(d_gate, all_act).astype(jnp.bfloat16)
        grad_up = dot_tn(d_up, all_act).astype(jnp.bfloat16)
        grad_down = dot_tn(hidden, all_grad).astype(jnp.bfloat16)
    groups = lax.axis_size("grp")
    fused = groups == 8 and lax.axis_size("rep") == 4
    ffn_grads = [grad_gate, grad_up, grad_down]
    if groups == 8 and not fused:
        mlp_out = lax.psum_scatter(
            mlp_out.reshape(-1, D), "grp", scatter_dimension=0, tiled=True
        )
    d_tokens, norm_sums, grads, totals = attention_backward(
        inputs[0],
        padded_cond,
        norms,
        tables,
        whole,
        kept[:-1],
        d_norm3,
        grad_mlp,
        mlp_out,
        ffn_grads if fused else [],
    )
    own_at = lax.axis_index("grp") * own_width
    if fused:
        mlp_out, total_a, total_f = totals
        norm_total = total_a[total_a.shape[0] - CUT :][:6]
        (
            outputs,
            grad_out_two,
            grad_query_two,
            grad_kv_two,
            grad_out_one,
            grad_qkv,
            *ffn_sums,
        ) = end_all(
            mlp_out,
            total_a,
            total_f,
            section_two,
            [w.shape for w in (w_out2, w_query2, w_kv2, w_out, w_qkv, w_gate, w_up, w_down)],
        )
    else:
        grads = list(grads)
        kv2_part = jnp.swapaxes(grads[2].reshape(-1, UNIT, 2, D // 2), 1, 2)
        grads[2] = kv2_part.reshape(2 * D, D // 2)
        norm_total = lax.psum(norm_sums[:6].astype(jnp.bfloat16), ("grp", "rep"))
        shards = [lax.psum_scatter(g, "grp", scatter_dimension=0, tiled=True) for g in grads]
        grad_out_two, grad_query_two, grad_kv_two, grad_out_one, grad_qkv = lax.psum(
            tuple(shards), "rep"
        )
        ffn_sums = lax.psum(tuple(ffn_grads), "rep")
        outputs = (section_two + mlp_out.astype(jnp.float32)).astype(jnp.bfloat16)
    norm_total = lax.dynamic_slice_in_dim(norm_total, own_at, own_width, axis=1)
    grad_qkv, grad_out_one, grad_query_two, grad_out_two, grad_kv_two = (
        g.astype(jnp.float32)
        for g in (grad_qkv, grad_out_one, grad_query_two, grad_out_two, grad_kv_two)
    )
    norm_total = norm_total.astype(jnp.float32)
    grad_gate, grad_up, grad_down = (g.astype(jnp.float32) for g in ffn_sums)
    return (
        outputs[None],
        d_tokens[None],
        norm_total[0],
        norm_total[1],
        norm_total[2],
        norm_total[3],
        norm_total[4],
        norm_total[5],
        grad_qkv,
        grad_out_one,
        grad_query_two,
        grad_kv_two,
        grad_out_two,
        grad_gate,
        grad_up,
        grad_down,
    )


def solution(mesh):
    return jax.shard_map(
        per_device,
        mesh=mesh,
        in_specs=(
            P(("grp", "rep"), None, None),
            P(("grp", "rep"), None, None),
            P(("grp", "rep"), None),
            P(("grp", "rep")),
            P(("grp", "rep"), None, None),
            P("grp"),
            P("grp"),
            P("grp"),
            P("grp"),
            P("grp"),
            P("grp"),
            P("grp", None),
            P("grp", None),
            P("grp", None),
            P("grp", None),
            P("grp", None),
            P("grp", None),
            P("grp", None),
            P("grp", None),
        ),
        out_specs=(
            P(("grp", "rep"), None, None),
            P(("grp", "rep"), None, None),
            P("grp"),
            P("grp"),
            P("grp"),
            P("grp"),
            P("grp"),
            P("grp"),
            P("grp", None),
            P("grp", None),
            P("grp", None),
            P("grp", None),
            P("grp", None),
            P("grp", None),
            P("grp", None),
            P("grp", None),
        ),
        check_vma=False,
    )
```

```python
import functools
import math

import jax
import jax.numpy as jnp
from jax import lax
from jax.experimental import pallas as pl
from jax.experimental.pallas import tpu as pltpu
from jax.sharding import PartitionSpec as P

MESH = pl.DeviceIdType.MESH
VMEM_LIMIT = 63 * 1024 * 1024

D = 1536
HEADS = 24
HD = 64
NC = 130


epsilon = 1e-05
score_scale = 0.125


def layer_norm(tensor, gain, shift):
    center = tensor - jnp.mean(tensor, axis=-1, keepdims=True)
    spread = jnp.mean(center * center, axis=-1, keepdims=True)
    return center * lax.rsqrt(spread + epsilon) * gain + shift


def swiglu(gate_part, up_part):
    return jax.nn.silu(gate_part) * up_part


def swiglu_back(gate_part, up_part, d_hidden):
    _, pullback = jax.vjp(swiglu, gate_part, up_part)
    return pullback(d_hidden)


def dot_nt(left_side, right_side):
    return lax.dot_general(
        left_side, right_side, (((1,), (1,)), ((), ())), preferred_element_type=jnp.float32
    )


def dot_tn(left_side, right_side):
    return lax.dot_general(
        left_side, right_side, (((0,), (0,)), ((), ())), preferred_element_type=jnp.float32
    )


def dot(left_side, right_side):
    return jnp.dot(left_side, right_side, preferred_element_type=jnp.float32)


def turn_tables(positions):
    quarter = HD // 4
    frequency = jnp.exp(jnp.arange(quarter, dtype=jnp.float32) * (-math.log(10000.0) / quarter))
    turned = positions.astype(jnp.float32)[:, None] * frequency[None, :]
    cosine, sine = jnp.cos(turned), jnp.sin(turned)
    none, one = jnp.zeros_like(sine), jnp.ones_like(sine)

    def heads(*parts):
        return jnp.tile(jnp.concatenate(parts, axis=1), (1, 2))

    return (
        heads(cosine, cosine, one, one),
        heads(-sine, none, none, none),
        heads(none, sine, none, none),
    )


def meet(peers, lower=None, upper=None, rep_index=None):
    barrier = pltpu.get_barrier_semaphore()
    for peer in peers:
        pl.semaphore_signal(barrier, inc=1, device_id=peer, device_id_type=MESH)
    if lower is not None:

        @pl.when(rep_index > 0)
        def _():
            pl.semaphore_signal(barrier, inc=1, device_id=lower, device_id_type=MESH)

        @pl.when(rep_index < 3)
        def _():
            pl.semaphore_signal(barrier, inc=1, device_id=upper, device_id_type=MESH)

    expected = len(peers)
    if lower is not None:
        expected = expected + jnp.where(rep_index > 0, 1, 0) + jnp.where(rep_index < 3, 1, 0)
    pl.semaphore_wait(barrier, expected)


GATHER_WINDOW = 4


class Gather:
    def __init__(self, pieces, sources, fulls, send_sem, recv_sem, local_sem):
        self.pieces, self.sources, self.fulls = pieces, sources, fulls
        self.send_sem, self.recv_sem, self.local_sem = send_sem, recv_sem, local_sem
        self.total = sum(n for n, _ in pieces)
        self.steps = self.total + GATHER_WINDOW + 2
        self.me = me = lax.axis_index("grp")
        self.plane = plane = lax.axis_index("rep")
        first_bit = 2 + 2 * lax.rem(plane, 2)
        self.first, self.second, self.across = me ^ first_bit, me ^ (6 - first_bit), me ^ 6
        self.first_dev = (self.first, plane)
        self.second_dev = (self.second, plane)
        self.rep_dev = (me, plane ^ 1)
        self.mate_dev = (me ^ 1, plane)

    def start(self):
        meet([self.first_dev, self.second_dev, self.rep_dev, self.mate_dev])

    def own_copy(self, k):
        n, rows = self.pieces[k]
        row = pl.multiple_of(self.me * (n * rows), 16)
        return pltpu.make_async_copy(
            self.sources[k], self.fulls[k].at[pl.ds(row, n * rows)], self.local_sem.at[k]
        )

    def each(self, i, body):
        base = 0
        for k, (n, rows) in enumerate(self.pieces):

            @pl.when((i >= base) & (i < base + n))
            def _(k=k, rows=rows, base=base):
                body(k, (i - base) * rows)

            base += n

    def push(self, k, offset, i, owner, lane, device, own=False):
        n, rows = self.pieces[k]
        cut = pl.ds(pl.multiple_of(offset, 16), rows)
        place = self.fulls[k].at[pl.ds(pl.multiple_of(owner * (n * rows) + offset, 16), rows)]
        return pltpu.make_async_remote_copy(
            src_ref=self.sources[k].at[cut] if own else place,
            dst_ref=place,
            send_sem=self.send_sem.at[lane, i],
            recv_sem=self.recv_sem.at[lane, i],
            device_id=device,
            device_id_type=MESH,
        )

    def stage_own(self, i):
        def body(k, offset):
            self.push(k, offset, i, self.me, 0, self.first_dev, own=True).start()
            self.push(k, offset, i, self.me, 3, self.mate_dev, own=True).start()

        self.each(i, body)

    def stage_first(self, i):
        def body(k, offset):
            self.push(k, offset, i, self.first, 0, self.first_dev).wait_recv()
            self.push(k, offset, i, self.first, 1, self.second_dev).start()
            self.push(k, offset, i, self.first, 2, self.rep_dev).start()
            self.push(k, offset, i, self.first, 4, self.mate_dev).start()

        self.each(i, body)

    def stage_rest(self, i):
        def body(k, offset):
            self.push(k, offset, i, self.across, 1, self.second_dev).wait_recv()
            self.push(k, offset, i, self.across, 5, self.mate_dev).start()
            self.push(k, offset, i, self.second, 2, self.rep_dev).wait_recv()
            self.push(k, offset, i, self.second, 6, self.mate_dev).start()

        self.each(i, body)

    def step(self, t):
        for stage, lag in (
            (self.stage_own, 0),
            (self.stage_first, GATHER_WINDOW),
            (self.stage_rest, GATHER_WINDOW + 2),
        ):
            i = t - lag

            @pl.when((i >= 0) & (i < self.total))
            def _(stage=stage, i=i):
                stage(i)

    def run(self, first, last):
        def body(t, carry):
            self.step(t)
            return carry

        lax.fori_loop(first, last, body, 0)

    def need(self, k):
        base = sum(n for n, _ in self.pieces[:k])
        n, rows = self.pieces[k]

        def body(j, carry):
            for lane in (3, 4, 5, 6):
                self.push(k, j * rows, base + j, self.me, lane, self.mate_dev).wait_recv()
            return carry

        lax.fori_loop(0, n, body, 0)
        self.own_copy(k).wait()

    def finish(self):
        def sent(i, carry):
            def body(k, offset):
                self.push(k, offset, i, self.me, 0, self.first_dev, own=True).wait_send()
                self.push(k, offset, i, self.me, 3, self.mate_dev, own=True).wait_send()
                for lane in (1, 2, 4, 5, 6):
                    self.push(k, offset, i, self.first, lane, self.mate_dev).wait_send()

            self.each(i, body)
            return carry

        lax.fori_loop(0, self.total, sent, 0)


class Loads:
    steps = 0

    def __init__(self, sources, fulls, local_sem):
        self.sources, self.fulls, self.local_sem = sources, fulls, local_sem

    def start(self):
        pass

    def own_copy(self, k):
        return pltpu.make_async_copy(self.sources[k], self.fulls[k], self.local_sem.at[k])

    def step(self, t):
        pass

    def run(self, first, last):
        pass

    def need(self, k):
        self.own_copy(k).wait()

    def finish(self):
        pass


CUT = 48
FCUT = 48
UNIT = 192
MATE_SLOTS = 4
OWN_SLOTS = 2
SUM_SLOTS = 9
FFN_SLOTS = 14
LAND_SLOTS = 3


class Sums:
    def __init__(self, pieces, ffn_pieces, parts, ffn, outs, lands, bufs, sems):
        self.near = pieces[0]
        self.pieces, self.ffn_pieces, self.parts, self.ffn = pieces, ffn_pieces, parts, ffn
        self.out_n, self.out_a, self.out_f = outs
        self.one_land, self.two_land, self.low_a, self.up_a, self.low_f, self.up_f = lands
        (
            self.mate_buf,
            self.own_buf,
            self.sums,
            self.done,
            self.ffn_buf,
            self.one_buf,
            self.two_buf,
            self.low_buf,
            self.up_buf,
        ) = bufs
        (
            self.mate_send,
            self.mate_recv,
            self.own_sem,
            self.one_send,
            self.one_recv,
            self.one_sem,
            self.two_send,
            self.two_recv,
            self.two_sem,
            self.ffn_sem,
            self.chain_send,
            self.chain_recv,
            self.low_sem,
            self.up_sem,
            self.out_sem,
            self.near_sem,
            self.credit,
        ) = sems
        me = lax.axis_index("grp")
        self.plane = plane = lax.axis_index("rep")
        self.core = lax.rem(me, 2)
        self.x = lax.rem(me // 2, 2)
        self.y = me // 4
        self.mate_dev = (me ^ 1, plane)
        self.x_dev = (me ^ 2, plane)
        self.y_dev = (me ^ 4, plane)
        self.low_dev = (me, plane - 1)
        self.up_dev = (me, plane + 1)
        self.total = sum(pieces)
        self.ffn_count = sum(ffn_pieces)
        self.chain_total = self.ffn_count + self.total - self.near

    def start(self):
        meet([self.mate_dev, self.x_dev, self.y_dev], self.low_dev, self.up_dev, self.plane)

    def each(self, i, body):
        base = 0
        for k, n in enumerate(self.pieces):

            @pl.when((i >= base) & (i < base + n))
            def _(k=k, base=base):
                body(k, pl.ds(pl.multiple_of((i - base) * CUT, 16), CUT))

            base += n

    def mate_copy(self, k, cut, slot):
        return pltpu.make_async_remote_copy(
            src_ref=self.parts[k].at[:, :, 1 - self.core, cut],
            dst_ref=self.mate_buf.at[slot],
            send_sem=self.mate_send.at[slot],
            recv_sem=self.mate_recv.at[slot],
            device_id=self.mate_dev,
            device_id_type=MESH,
        )

    def own_copy(self, k, cut, slot):
        return pltpu.make_async_copy(
            self.parts[k].at[:, :, self.core, cut], self.own_buf.at[slot], self.own_sem.at[slot]
        )

    def load(self, i):
        @pl.when(i >= MATE_SLOTS)
        def _():
            pl.semaphore_wait(self.credit, 1)
            self.mate_copy(0, pl.ds(0, CUT), lax.rem(i, MATE_SLOTS)).wait_send()

        def body(k, cut):
            self.mate_copy(k, cut, lax.rem(i, MATE_SLOTS)).start()
            self.own_copy(k, cut, lax.rem(i, OWN_SLOTS)).start()

        self.each(i, body)

    def one_copy(self, i, slot, by_x):
        return pltpu.make_async_remote_copy(
            src_ref=self.sums.at[slot, :, 1 - self.x] if by_x else self.sums.at[slot, 1 - self.y],
            dst_ref=self.one_land.at[i],
            send_sem=self.one_send.at[slot],
            recv_sem=self.one_recv.at[i],
            device_id=self.x_dev if by_x else self.y_dev,
            device_id_type=MESH,
        )

    def two_copy(self, i, slot, by_x):
        return pltpu.make_async_remote_copy(
            src_ref=self.sums.at[slot, 1 - self.y, self.x]
            if by_x
            else self.sums.at[slot, self.y, 1 - self.x],
            dst_ref=self.two_land.at[i],
            send_sem=self.two_send.at[slot],
            recv_sem=self.two_recv.at[i],
            device_id=self.y_dev if by_x else self.x_dev,
            device_id_type=MESH,
        )

    def either(self, i, body):
        @pl.when(lax.rem(i, 2) == 0)
        def _():
            body(True)

        @pl.when(lax.rem(i, 2) == 1)
        def _():
            body(False)

    def one_load(self, i):
        slot = lax.rem(i, LAND_SLOTS)
        return pltpu.make_async_copy(self.one_land.at[i], self.one_buf.at[slot], self.one_sem.at[slot])

    def two_load(self, i):
        slot = lax.rem(i, LAND_SLOTS)
        return pltpu.make_async_copy(self.two_land.at[i], self.two_buf.at[slot], self.two_sem.at[slot])

    def pair(self, i):
        mate_slot, own_slot = lax.rem(i, MATE_SLOTS), lax.rem(i, OWN_SLOTS)
        slot = lax.rem(i, SUM_SLOTS)
        self.mate_copy(0, pl.ds(0, CUT), mate_slot).wait_recv()
        self.own_copy(0, pl.ds(0, CUT), own_slot).wait()
        for u in range(2):
            for v in range(2):
                self.sums[slot, u, v] = add(
                    self.own_buf[own_slot, u, v], self.mate_buf[mate_slot, u, v]
                )

        @pl.when(i + MATE_SLOTS < self.total)
        def _():
            pl.semaphore_signal(
                self.credit, inc=1, device_id=self.mate_dev, device_id_type=MESH
            )

        self.either(i, lambda by_x: self.one_copy(i, slot, by_x).start())

    def one_arrives(self, i):
        self.either(i, lambda by_x: self.one_copy(i, lax.rem(i, SUM_SLOTS), by_x).wait_recv())
        self.one_load(i).start()

    def plane_one(self, i):
        slot, land = lax.rem(i, SUM_SLOTS), lax.rem(i, LAND_SLOTS)
        self.one_load(i).wait()

        def body(by_x):
            for u in range(2):
                at = (slot, u, self.x) if by_x else (slot, self.y, u)
                self.sums[at] = add(self.sums[at], self.one_buf[land, u])
            self.two_copy(i, slot, by_x).start()

        self.either(i, body)

    def two_arrives(self, i):
        self.either(i, lambda by_x: self.two_copy(i, lax.rem(i, SUM_SLOTS), by_x).wait_recv())
        self.two_load(i).start()

    def plane_two(self, i):
        slot = lax.rem(i, SUM_SLOTS)
        self.two_load(i).wait()
        self.done[i] = add(self.sums[slot, self.y, self.x], self.two_buf[lax.rem(i, LAND_SLOTS)])

        @pl.when(i < self.near)
        def _():
            self.near_copy(i).start()

        def body(by_x):
            self.one_copy(i, slot, by_x).wait_send()
            self.two_copy(i, slot, by_x).wait_send()

        self.either(i, body)

    def near_copy(self, i):
        rows = pl.ds(pl.multiple_of(i * CUT, 16), CUT)
        return pltpu.make_async_copy(self.done.at[i], self.out_n.at[rows], self.near_sem.at[i])

    def ffn_load(self, j):
        base = 0
        for k, n in enumerate(self.ffn_pieces):

            @pl.when((j >= base) & (j < base + n))
            def _(k=k, base=base):
                row = pl.multiple_of((j - base) * FCUT, 16)
                pltpu.make_async_copy(
                    self.ffn[k].at[pl.ds(row, FCUT)],
                    self.ffn_buf.at[lax.rem(j, FFN_SLOTS)],
                    self.ffn_sem.at[lax.rem(j, FFN_SLOTS)],
                ).start()

            base += n

    def ffn_wait(self, j):
        pltpu.make_async_copy(
            self.ffn[0].at[pl.ds(0, FCUT)],
            self.ffn_buf.at[lax.rem(j, FFN_SLOTS)],
            self.ffn_sem.at[lax.rem(j, FFN_SLOTS)],
        ).wait()

    def role(self, j, plane, body):
        slot = lax.rem(j, LAND_SLOTS)
        key = self.plane + jnp.where(j < self.ffn_count, 0, 4)
        key = jnp.where((j >= 0) & (j < self.chain_total), key, 8)

        @pl.when(key == plane)
        def _():
            rows = pl.ds(pl.multiple_of(j * FCUT, 16), FCUT)
            body(
                self.ffn_buf.at[lax.rem(j, FFN_SLOTS)],
                self.low_f.at[j],
                self.up_f.at[j],
                self.low_buf.at[slot],
                self.up_buf.at[slot],
                self.out_f.at[rows],
            )

        @pl.when(key == plane + 4)
        def _():
            i = j - self.ffn_count
            rows = pl.ds(pl.multiple_of(i * CUT, 16), CUT)
            part = pl.ds(0, CUT)
            body(
                self.done.at[i + self.near],
                self.low_a.at[i],
                self.up_a.at[i],
                self.low_buf.at[slot, part],
                self.up_buf.at[slot, part],
                self.out_a.at[rows],
            )

    def chain(self, j, lane, src, dst, device):
        return pltpu.make_async_remote_copy(
            src_ref=src,
            dst_ref=dst,
            send_sem=self.chain_send.at[lane, j],
            recv_sem=self.chain_recv.at[lane, j],
            device_id=device,
            device_id_type=MESH,
        )

    def low_load(self, j, land, buf):
        return pltpu.make_async_copy(land, buf, self.low_sem.at[lax.rem(j, LAND_SLOTS)])

    def up_load(self, j, land, buf):
        return pltpu.make_async_copy(land, buf, self.up_sem.at[lax.rem(j, LAND_SLOTS)])

    def inward(self, j):
        @pl.when((j >= 0) & (j < self.ffn_count))
        def _():
            self.ffn_wait(j)

        def lowest(mine, low, up, low_buf, up_buf, out):
            self.chain(j, 0, mine, low, self.up_dev).start()

        def highest(mine, low, up, low_buf, up_buf, out):
            self.chain(j, 1, mine, up, self.low_dev).start()

        self.role(j, 0, lowest)
        self.role(j, 3, highest)

    def middle_arrives(self, j):
        def body(mine, low, up, low_buf, up_buf, out):
            self.chain(j, 1, mine, up, self.low_dev).wait_recv()
            self.up_load(j, up, up_buf).start()

        self.role(j, 2, body)

    def middle(self, j):
        def body(mine, low, up, low_buf, up_buf, out):
            self.up_load(j, up, up_buf).wait()
            mine[...] = add(mine[...], up_buf[...])
            self.chain(j, 1, mine, up, self.low_dev).start()

        self.role(j, 2, body)

    def root_arrives(self, j):
        def body(mine, low, up, low_buf, up_buf, out):
            self.chain(j, 0, mine, low, self.up_dev).wait_recv()
            self.low_load(j, low, low_buf).start()
            self.chain(j, 1, mine, up, self.low_dev).wait_recv()
            self.up_load(j, up, up_buf).start()

        self.role(j, 1, body)

    def root(self, j):
        def body(mine, low, up, low_buf, up_buf, out):
            self.low_load(j, low, low_buf).wait()
            self.up_load(j, up, up_buf).wait()
            mine[...] = add(mine[...], low_buf[...], up_buf[...])
            self.chain(j, 0, mine, out, self.up_dev).start()
            self.chain(j, 1, mine, out, self.low_dev).start()
            pltpu.make_async_copy(mine, out, self.out_sem.at[j]).start()

        self.role(j, 1, body)

    def outward(self, j):
        def body(mine, low, up, low_buf, up_buf, out):
            self.chain(j, 0, mine, out, self.up_dev).wait_recv()
            self.chain(j, 0, out, out, self.up_dev).start()

        self.role(j, 2, body)

    def drain(self, j):
        def lowest(mine, low, up, low_buf, up_buf, out):
            self.chain(j, 0, mine, low, self.up_dev).wait_send()
            self.chain(j, 1, mine, out, self.low_dev).wait_recv()

        def holder(mine, low, up, low_buf, up_buf, out):
            self.chain(j, 0, mine, out, self.up_dev).wait_send()
            self.chain(j, 1, mine, out, self.low_dev).wait_send()
            pltpu.make_async_copy(mine, out, self.out_sem.at[j]).wait()

        def between(mine, low, up, low_buf, up_buf, out):
            self.chain(j, 1, mine, up, self.low_dev).wait_send()
            self.chain(j, 0, out, out, self.up_dev).wait_send()

        def highest(mine, low, up, low_buf, up_buf, out):
            self.chain(j, 1, mine, up, self.low_dev).wait_send()
            self.chain(j, 0, mine, out, self.up_dev).wait_recv()

        for plane, body in enumerate((lowest, holder, between, highest)):
            self.role(j, plane, body)

    def stages(self, at, limit, pairs):
        for stage, behind in pairs:
            i = at - behind

            @pl.when((i >= 0) & (i < limit))
            def _(stage=stage, i=i):
                stage(i)

    def xy_step(self, i):
        self.stages(
            i,
            self.total,
            (
                (self.load, 0),
                (self.pair, 1),
                (self.plane_two, 7),
                (self.plane_one, 4),
                (self.two_arrives, 6),
                (self.one_arrives, 3),
            ),
        )

    def z_step(self, j):
        self.stages(j + 1, self.ffn_count, ((self.ffn_load, 0),))
        for stage, behind in (
            (self.inward, 0),
            (self.outward, 8),
            (self.root, 6),
            (self.middle, 3),
            (self.root_arrives, 5),
            (self.middle_arrives, 2),
            (self.drain, 11),
        ):
            stage(j - behind)

    def begin(self):
        self.ffn_load(jnp.int32(0))

    def finish(self, z_next, xy_next):
        both = (self.total + 8 - xy_next + 1) // 2

        def body(u, carry):
            self.z_step(z_next + 3 * u)
            self.xy_step(xy_next + 2 * u)
            self.z_step(z_next + 3 * u + 1)
            self.xy_step(xy_next + 2 * u + 1)
            self.z_step(z_next + 3 * u + 2)
            return carry

        def chain_only(u, carry):
            self.z_step(u)
            return carry

        lax.fori_loop(0, both, body, 0)
        lax.fori_loop(z_next + 3 * both, self.chain_total + 12, chain_only, 0)
        for i in range(max(self.total - MATE_SLOTS, 0), self.total):
            self.mate_copy(0, pl.ds(0, CUT), i % MATE_SLOTS).wait_send()
        for i in range(self.near):
            self.near_copy(i).wait()

    @staticmethod
    def shapes(pieces, ffn_pieces, wide):
        total, ffn_count = sum(pieces), sum(ffn_pieces)
        near = pieces[0]
        far = total - near
        chain_total = far + ffn_count
        low = jnp.bfloat16
        dma = pltpu.SemaphoreType.DMA
        shape = lambda *s: jax.ShapeDtypeStruct(s, low)
        buf = lambda *s: pltpu.VMEM(s, low)
        outs = [shape(n, wide) for n in (near * CUT, far * CUT, ffn_count * FCUT)]
        lands = [
            shape(total, 2, CUT, wide),
            shape(total, CUT, wide),
            *[shape(far, CUT, wide)] * 2,
            *[shape(ffn_count, FCUT, wide)] * 2,
        ]
        bufs = [
            buf(MATE_SLOTS, 2, 2, CUT, wide),
            buf(OWN_SLOTS, 2, 2, CUT, wide),
            buf(SUM_SLOTS, 2, 2, CUT, wide),
            buf(total, CUT, wide),
            buf(FFN_SLOTS, FCUT, wide),
            buf(LAND_SLOTS, 2, CUT, wide),
            buf(LAND_SLOTS, CUT, wide),
            buf(LAND_SLOTS, FCUT, wide),
            buf(LAND_SLOTS, FCUT, wide),
        ]
        sems = [
            dma((MATE_SLOTS,)),
            dma((MATE_SLOTS,)),
            dma((OWN_SLOTS,)),
            dma((SUM_SLOTS,)),
            dma((total,)),
            dma((LAND_SLOTS,)),
            dma((SUM_SLOTS,)),
            dma((total,)),
            dma((LAND_SLOTS,)),
            dma((FFN_SLOTS,)),
            dma((2, chain_total)),
            dma((2, chain_total)),
            dma((LAND_SLOTS,)),
            dma((LAND_SLOTS,)),
            dma((chain_total,)),
            dma((near,)),
            pltpu.SemaphoreType.REGULAR,
        ]
        return outs, lands, bufs, sems


class NoSums:
    def start(self):
        pass

    def begin(self):
        pass

    def z_step(self, j):
        pass

    def xy_step(self, i):
        pass

    def finish(self, z_next, xy_next):
        pass


def add(*terms):
    total = terms[0].astype(jnp.float32)
    for term in terms[1:]:
        total = total + term.astype(jnp.float32)
    return total.astype(jnp.bfloat16)


STEP_CHIP = (0, 0, 1, 2, 1, 2, 3, 3)
STEP_HALF = (0, 1, 0, 1, 1, 0, 0, 1)
FFN_TILE = 512
TILE = 256


def ffn_kernel(
    act_in,
    cot_in,
    gate_in,
    up_in,
    down_in,
    out_part,
    dn_ref,
    grad_gate,
    grad_up,
    grad_down,
    act,
    cot,
    w_gate,
    w_up,
    w_down,
    hidden,
    d_gate,
    d_up,
    pair,
    mine,
    stage,
    out_buf,
    passed,
    final,
    tile_buf,
    weight_sem,
    cot_sem,
    own_sem,
    act_send,
    act_recv,
    pair_send,
    pair_recv,
    flow_send,
    flow_recv,
    tile_sem,
    end_sem,
    part_sem,
):
    me = lax.axis_index("grp")
    plane = lax.axis_index("rep")
    mate_dev, x_dev, y_dev = (me ^ 1, plane), (me ^ 2, plane), (me ^ 4, plane)
    half = act.shape[2]
    seq_len = 2 * half
    rows, wide = w_gate.shape
    low = jnp.bfloat16
    meet([mate_dev, x_dev, y_dev])

    def remote(src, dst, send, recv, device):
        return pltpu.make_async_remote_copy(
            src_ref=src,
            dst_ref=dst,
            send_sem=send,
            recv_sem=recv,
            device_id=device,
            device_id_type=MESH,
        )

    own = [act_in.at[pl.ds(h * half, half)] for h in range(2)]

    def act_copy(t, other):
        if other:
            src, device = (own[t] if t < 2 else act.at[t, 0]), mate_dev
        else:
            src, device = {
                2: (own[0], x_dev),
                3: (own[1], y_dev),
                4: (own[1], x_dev),
                5: (own[0], y_dev),
                6: (act.at[2, 0], y_dev),
                7: (act.at[3, 0], x_dev),
            }[t]
        return remote(
            src, act.at[t, other], act_send.at[t, other], act_recv.at[t, other], device
        )

    for t in (2, 3, 4, 5):
        act_copy(t, 0).start()
    for t in (0, 1):
        act_copy(t, 1).start()
    own_copies = [pltpu.make_async_copy(own[t], act.at[t, 0], own_sem.at[t]) for t in range(2)]
    for copy in own_copies:
        copy.start()
    weights = [
        pltpu.make_async_copy(src, dst, weight_sem.at[k])
        for k, (src, dst) in enumerate(((gate_in, w_gate), (up_in, w_up), (down_in, w_down)))
    ]
    for copy in weights:
        copy.start()
    cot_copies = []
    for t in range(8):
        for other in range(2):
            owner = me ^ (2 * STEP_CHIP[t] + other)
            row = pl.multiple_of(owner * seq_len + STEP_HALF[t] * half, 16)
            copy = pltpu.make_async_copy(
                cot_in.at[pl.ds(row, half)], cot.at[t, other], cot_sem.at[t, other]
            )
            copy.start()
            cot_copies.append(copy)

    def pair_copy(t):
        return remote(stage, pair.at[t], pair_send, pair_recv.at[t], mate_dev)

    def flow(lane):
        src, dst, device = (
            (pair.at[2], final.at[0], x_dev),
            (pair.at[4], final.at[1], x_dev),
            (pair.at[5], final.at[2], y_dev),
            (pair.at[3], final.at[3], y_dev),
            (pair.at[6], passed.at[0], x_dev),
            (pair.at[7], passed.at[1], y_dev),
        )[lane]
        return remote(src, dst, flow_send.at[lane], flow_recv.at[lane], device)

    def part_copy(t, other):
        owner = me ^ (2 * STEP_CHIP[t] + other)
        place = out_part.at[owner // 4, lax.rem(owner // 2, 2), lax.rem(owner, 2)]
        return pltpu.make_async_copy(
            out_buf.at[t % 2, pl.ds(other * half, half)],
            place.at[pl.ds(STEP_HALF[t] * half, half)],
            part_sem.at[t % 2, other],
        )

    def forward_part(t):
        tokens = act[t].reshape(seq_len, wide)
        gate = dot_nt(tokens, w_gate[...])
        up = dot_nt(tokens, w_up[...])
        d_hidden = dot_nt(cot[t].reshape(seq_len, wide), w_down[...])
        sigmoid = 1.0 / (1.0 + jnp.exp(-gate))
        silu = gate * sigmoid
        hidden[t] = (silu * up).astype(low)
        d_gate[t] = (d_hidden * up * (sigmoid * (1.0 + gate * (1.0 - sigmoid)))).astype(low)
        d_up[t] = (d_hidden * silu).astype(low)

    def backward_part(t):
        out_buf[lax.rem(t, 2)] = dot(hidden[t], w_down[...]).astype(low)
        dn = dot(d_gate[t], w_gate[...]) + dot(d_up[t], w_up[...])
        mine[...] = dn[:half].astype(low)
        stage[...] = dn[half:].astype(low)

    def join(t, events):
        pair_copy(t).wait()
        pair[t] = add(pair[t], mine[...])
        for when, lane in events:
            if when is None:
                flow(lane).start()
            else:

                @pl.when(t == when)
                def _(lane=lane):
                    flow(lane).start()

    for copy in own_copies + weights:
        copy.wait()

    def step(t, carry):
        for at in (2, 4, 6):

            @pl.when(t == at)
            def _(at=at):
                for u in (at, at + 1):
                    act_copy(u, 0).wait_recv()
                    if at == 2:
                        act_copy(u + 4, 0).start()
                    act_copy(u, 1).start()

        remote(
            act.at[t, 0], act.at[t, 1], act_send.at[t, 1], act_recv.at[t, 1], mate_dev
        ).wait_recv()
        for other in range(2):
            pltpu.make_async_copy(
                cot_in.at[pl.ds(0, half)], cot.at[t, other], cot_sem.at[t, other]
            ).wait()
        forward_part(t)

        @pl.when(t > 0)
        def _():
            join(t - 1, ((2, 0), (3, 3), (6, 4)))

        @pl.when(t >= 2)
        def _():
            for other in range(2):
                pltpu.make_async_copy(
                    out_buf.at[lax.rem(t, 2), pl.ds(other * half, half)],
                    out_part.at[0, 0, 0, pl.ds(0, half)],
                    part_sem.at[lax.rem(t, 2), other],
                ).wait()

        backward_part(t)
        pair_copy(t).start()
        for u in range(8):

            @pl.when(t == u)
            def _(u=u):
                for other in range(2):
                    part_copy(u, other).start()

        return carry

    lax.fori_loop(0, 8, step, 0)
    join(7, ((None, 5),))

    def write(target, slot, cut):
        return pltpu.make_async_copy(
            tile_buf.at[slot], target.at[:, cut], tile_sem.at[slot]
        )

    def pass_on():
        for lane, t, onward in ((4, 5, 2), (5, 4, 1)):
            flow(lane).wait_recv()
            pair[t] = add(pair[t], passed[lane - 4])
            flow(onward).start()

    tiles = wide // FFN_TILE
    for k, (left, right, target) in enumerate(
        ((d_gate, act, grad_gate), (d_up, act, grad_up), (hidden, cot, grad_down))
    ):

        def tile(n, carry, k=k, left=left, right=right, target=target):
            cut = pl.ds(pl.multiple_of(n * FFN_TILE, FFN_TILE), FFN_TILE)
            slot = lax.rem(n, 2)

            @pl.when(k * tiles + n >= 2)
            def _():
                write(target, slot, cut).wait()

            tile_buf[slot] = dot_tn(
                left[...].reshape(8 * seq_len, rows),
                right[:, :, :, cut].reshape(8 * seq_len, FFN_TILE),
            ).astype(low)
            write(target, slot, cut).start()
            return carry

        lax.fori_loop(0, tiles, tile, 0)
        if k == 1:
            pass_on()
    for slot in range(2):
        write(grad_down, slot, pl.ds(0, FFN_TILE)).wait()

    ends = []
    for h in range(2):
        flow(h).wait_recv()
        flow(2 + h).wait_recv()
        pair[h] = add(pair[h], final[h], final[2 + h])
        copy = pltpu.make_async_copy(pair.at[h], dn_ref.at[pl.ds(h * half, half)], end_sem.at[h])
        copy.start()
        ends.append(copy)
    for copy in ends:
        copy.wait()
    for t in (6, 7):
        for other in range(2):
            part_copy(t, other).wait()
    for lane in range(6):
        flow(lane).wait_send()
    for t in range(8):
        act_copy(t, 1).wait_send()
        if t >= 2:
            act_copy(t, 0).wait_send()


def ffn_all(act, cot, w_gate, w_up, w_down):
    seq_len, wide = act.shape
    rows = w_gate.shape[0]
    half = seq_len // 2
    low = jnp.bfloat16
    hbm = pl.BlockSpec(memory_space=pltpu.HBM)
    dma = pltpu.SemaphoreType.DMA
    return pl.pallas_call(
        ffn_kernel,
        out_shape=[
            jax.ShapeDtypeStruct((2, 2, 2, seq_len, wide), low),
            jax.ShapeDtypeStruct((seq_len, wide), low),
        ]
        + [jax.ShapeDtypeStruct((rows, wide), low)] * 3,
        in_specs=[hbm] * 5,
        out_specs=[hbm] * 5,
        scratch_shapes=[
            pltpu.VMEM((8, 2, half, wide), low),
            pltpu.VMEM((8, 2, half, wide), low),
            pltpu.VMEM((rows, wide), low),
            pltpu.VMEM((rows, wide), low),
            pltpu.VMEM((rows, wide), low),
            pltpu.VMEM((8, seq_len, rows), low),
            pltpu.VMEM((8, seq_len, rows), low),
            pltpu.VMEM((8, seq_len, rows), low),
            pltpu.VMEM((8, half, wide), low),
            pltpu.VMEM((half, wide), low),
            pltpu.VMEM((half, wide), low),
            pltpu.VMEM((2, seq_len, wide), low),
            pltpu.VMEM((2, half, wide), low),
            pltpu.VMEM((4, half, wide), low),
            pltpu.VMEM((2, rows, FFN_TILE), low),
            dma((3,)),
            dma((8, 2)),
            dma((2,)),
            dma((8, 2)),
            dma((8, 2)),
            dma,
            dma((8,)),
            dma((6,)),
            dma((6,)),
            dma((2,)),
            dma((2,)),
            dma((2, 2)),
        ],
        compiler_params=pltpu.CompilerParams(
            collective_id=2, has_side_effects=True, vmem_limit_bytes=VMEM_LIMIT
        ),
    )(act, cot, w_gate, w_up, w_down)


PAIR = 128
COND_ROWS = 256
NORM_ROWS = 32


def normalise(read, gain, shift, write, rows):
    def block(n, carry):
        cut = pl.ds(pl.multiple_of(n * NORM_ROWS, NORM_ROWS), NORM_ROWS)
        write[cut] = layer_norm(read[cut].astype(jnp.float32), gain[...], shift[...]).astype(
            write.dtype
        )
        return carry

    lax.fori_loop(0, rows // NORM_ROWS, block, 0)


def normalise_back(read, gain, d_read, straight, write, sums, row, rows):
    wide = read.shape[1]

    def block(n, carry):
        d_gain, d_shift = carry
        cut = pl.ds(pl.multiple_of(n * NORM_ROWS, NORM_ROWS), NORM_ROWS)
        tensor = read[cut].astype(jnp.float32)
        center = tensor - jnp.mean(tensor, axis=-1, keepdims=True)
        spread = jnp.mean(center * center, axis=-1, keepdims=True)
        inverse = lax.rsqrt(spread + epsilon)
        hat = center * inverse
        d_out = d_read[cut].astype(jnp.float32)
        scaled = d_out * gain[...]
        dv = inverse * (
            scaled
            - jnp.mean(scaled, axis=-1, keepdims=True)
            - hat * jnp.mean(scaled * hat, axis=-1, keepdims=True)
        )
        write[cut] = straight[cut].astype(jnp.float32) + dv
        d_gain = d_gain + jnp.sum((d_out * hat).reshape(NORM_ROWS // 8, 8, wide), axis=0)
        d_shift = d_shift + jnp.sum(d_out.reshape(NORM_ROWS // 8, 8, wide), axis=0)
        return d_gain, d_shift

    zero = jnp.zeros((8, wide), jnp.float32)
    d_gain, d_shift = lax.fori_loop(0, rows // NORM_ROWS, block, (zero, zero))
    sums[row : row + 1] = jnp.sum(d_gain, axis=0, keepdims=True)
    sums[row + 1 : row + 2] = jnp.sum(d_shift, axis=0, keepdims=True)


def turn(tensor, cosine, sine_left, sine_right):
    return (
        tensor * cosine
        + pltpu.roll(tensor, PAIR - HD // 4, 1) * sine_left
        + pltpu.roll(tensor, HD // 4, 1) * sine_right
    )


def tiles_of(count, body, size=768):
    def step(n, carry):
        body(pl.ds(pl.multiple_of(n * size, size), size))
        return carry

    lax.fori_loop(0, count // size, step, 0)


def pair_loop(body):
    def step(p, carry):
        body(p, pl.multiple_of(p * PAIR, PAIR))
        return carry

    lax.fori_loop(0, HEADS * HD // PAIR, step, 0)


def first_head(rows):
    return lax.broadcasted_iota(jnp.int32, (rows, PAIR), 1) < HD


def head_softmax(query, key, mine, keys):
    scores = dot_nt(jnp.where(mine, query, jnp.zeros_like(query)), key) * score_scale
    if keys < key.shape[0]:
        lanes = lax.broadcasted_iota(jnp.int32, scores.shape, 1)
        scores = jnp.where(lanes < keys, scores, -1e30)
    shifted = jnp.exp(scores - jnp.max(scores, axis=-1, keepdims=True))
    return (shifted * (1.0 / jnp.sum(shifted, axis=-1, keepdims=True))).astype(jnp.bfloat16)


def attend_pair(query, key, value, keys, keep):
    mask = first_head(query.shape[0])
    results = []
    for head in range(2):
        probability = head_softmax(query, key, mask if head == 0 else ~mask, keys)
        keep(head, probability)
        results.append(dot(probability, value))
    return jnp.where(mask, results[0], results[1]).astype(jnp.bfloat16)


def attend_pair_back(query, key, value, grad, probabilities):
    mask, key_mask = first_head(query.shape[0]), first_head(key.shape[0])
    d_queries, d_keys, d_values = [], [], []
    for head in range(2):
        probability = probabilities[head]
        mine = mask if head == 0 else ~mask
        d_prob = dot_nt(jnp.where(mine, grad, jnp.zeros_like(grad)), value)
        wide = probability.astype(jnp.float32)
        inner = jnp.sum(wide * d_prob, axis=-1, keepdims=True)
        d_scores = (wide * (d_prob - inner)).astype(jnp.bfloat16)
        d_queries.append(dot(d_scores, key))
        d_keys.append(dot_tn(d_scores, query))
        d_values.append(dot_tn(probability, grad))
    return (
        jnp.where(mask, d_queries[0], d_queries[1]) * score_scale,
        jnp.where(key_mask, d_keys[0], d_keys[1]) * score_scale,
        jnp.where(key_mask, d_values[0], d_values[1]),
    )


def attention_forward_kernel(
    pieces,
    x_in,
    cond_in,
    cosine,
    sine_left,
    sine_right,
    norms_in,
    qkv_in,
    out_in,
    kv2_in,
    query2_in,
    out2_in,
    norms_out,
    qkv_out,
    out_out,
    query2_out,
    out2_out,
    act_one_out,
    heads_out,
    prob_out,
    flat_one_out,
    section_one_out,
    act_two_out,
    query_two_out,
    kv_two_out,
    prob_two_out,
    flat_two_out,
    section_two_out,
    act_three_out,
    x,
    cond,
    norm_parts,
    w_qkv,
    w_out,
    w_kv2,
    w_query2,
    w_out2,
    act,
    heads,
    flat,
    section,
    query_two,
    kv_two,
    prob,
    prob_two,
    in_sem,
    out_sem,
    prob_sem,
    local_sem,
    *gather_sems,
):
    rows, wide = x.shape
    low = jnp.bfloat16
    sources = (norms_in, qkv_in, out_in, kv2_in, query2_in, out2_in)
    fulls = (norm_parts, w_qkv, w_out, w_kv2, w_query2, w_out2)
    if pieces is None:
        gather = Loads(sources, fulls, local_sem)
    else:
        gather = Gather(pieces, sources, fulls, *gather_sems, local_sem)
    gather.start()
    loads = []
    for k, (src, dst) in enumerate(((x_in, x), (cond_in, cond))):
        loads.append(pltpu.make_async_copy(src, dst, in_sem.at[k]))
        loads[-1].start()
    for k in range(len(sources)):
        gather.own_copy(k).start()
    stores = []

    def save(src, dst):
        stores.append(pltpu.make_async_copy(src, dst, out_sem.at[len(stores)]))
        stores[-1].start()
        return stores[-1]

    lead = GATHER_WINDOW + 2
    gather.run(0, 1 + lead)
    loads[0].wait()
    gather.need(0)
    norms_out[...] = jnp.sum(
        norm_parts[...].astype(jnp.float32).reshape(norm_parts.shape[0] // 16, 16, wide), axis=0
    )
    gains = [norms_out.at[pl.ds(k, 1)] for k in range(6)]
    normalise(x, gains[0], gains[1], act, rows)
    act_one_done = save(act, act_one_out)
    done = 13 + lead
    gather.run(1 + lead, done)
    gather.need(1)
    save(w_qkv, qkv_out)

    def project(cut, rotated):
        result = dot_nt(act[...], w_qkv[cut])
        for part in range(cut.size // PAIR):
            piece = result[:, part * PAIR : (part + 1) * PAIR]
            if rotated:
                piece = turn(piece, cosine[...], sine_left[...], sine_right[...])
            heads[:, pl.ds(pl.multiple_of(cut.start + part * PAIR, PAIR), PAIR)] = piece.astype(low)

    for part in range(3):
        tiles_of(
            wide,
            lambda cut, part=part: project(
                pl.ds(pl.multiple_of(cut.start + part * wide, PAIR), cut.size), part < 2
            ),
        )
        gather.step(done + part)
    done += 3
    save(heads, heads_out)

    def prob_copy(buf, out, p, slot):
        return pltpu.make_async_copy(buf.at[slot], out.at[p], prob_sem.at[slot])

    def self_pair(p, lane):
        slot = lax.rem(p, 2)

        @pl.when(p >= 2)
        def _():
            prob_copy(prob, prob_out, p, slot).wait()

        def keep(head, probability):
            prob[slot, head] = probability

        cols = [pl.ds(pl.multiple_of(lane + k * wide, PAIR), PAIR) for k in range(3)]
        flat[:, cols[0]] = attend_pair(
            heads[:, cols[0]], heads[:, cols[1]], heads[:, cols[2]], rows, keep
        )
        prob_copy(prob, prob_out, p, slot).start()
        serve(p, SELF_EVERY)

    def serve(p, every):
        if gather.steps:

            @pl.when(lax.rem(p, every) == every - 1)
            def _():
                gather.step(done + p // every)

    pairs = wide // PAIR
    pair_loop(self_pair)
    done += pairs // SELF_EVERY
    for slot in range(2):
        prob_copy(prob, prob_out, 0, slot).wait()
    flat_one_done = save(flat, flat_one_out)
    gather.run(done, 17 + lead)
    done = max(done, 17 + lead)
    gather.need(2)
    save(w_out, out_out)

    def first_section(cut):
        section[:, cut] = x[:, cut].astype(jnp.float32) + dot_nt(flat[...], w_out[cut])

    tiles_of(wide, first_section)
    section_one_done = save(section, section_one_out)
    gather.run(done, 21 + lead)
    gather.step(max(done, 21 + lead))
    done = max(done, 21 + lead) + 1
    act_one_done.wait()
    normalise(section, gains[2], gains[3], act, rows)
    act_two_done = save(act, act_two_out)
    loads[1].wait()
    gather.need(3)

    def condition(cut):
        kv_two[:, cut] = dot_nt(cond[...], w_kv2[cut]).astype(low)

    tiles_of(2 * wide, condition)
    save(kv_two, kv_two_out)
    gather.run(done, 25 + lead)
    done = max(done, 25 + lead)
    gather.need(4)
    save(w_query2, query2_out)

    def query(cut):
        query_two[:, cut] = dot_nt(act[...], w_query2[cut]).astype(low)

    tiles_of(wide, query)
    save(query_two, query_two_out)
    flat_one_done.wait()

    def cross_pair(p, lane):
        slot = lax.rem(p, 2)

        @pl.when(p >= 2)
        def _():
            prob_copy(prob_two, prob_two_out, p, slot).wait()

        def keep(head, probability):
            prob_two[slot, head] = probability

        cols = [pl.ds(pl.multiple_of(lane + k * wide, PAIR), PAIR) for k in range(2)]
        flat[:, cols[0]] = attend_pair(
            query_two[:, cols[0]], kv_two[:, cols[0]], kv_two[:, cols[1]], NC, keep
        )
        prob_copy(prob_two, prob_two_out, p, slot).start()
        serve(p, CROSS_EVERY)

    pair_loop(cross_pair)
    done += pairs // CROSS_EVERY
    gather.run(done, 29 + lead)
    for slot in range(2):
        prob_copy(prob_two, prob_two_out, 0, slot).wait()
    save(flat, flat_two_out)
    gather.need(5)
    save(w_out2, out2_out)
    section_one_done.wait()

    def second_section(cut):
        section[:, cut] = section[:, cut] + dot_nt(flat[...], w_out2[cut])

    tiles_of(wide, second_section)
    save(section, section_two_out)
    act_two_done.wait()
    normalise(section, gains[4], gains[5], act, rows)
    save(act, act_three_out)
    waited = [id(c) for c in (act_one_done, flat_one_done, section_one_done, act_two_done)]
    gather.finish()
    for copy in stores:
        if id(copy) not in waited:
            copy.wait()


SELF_EVERY = 2
CROSS_EVERY = 3


def attention_forward(x, cond, tables, norms, weights):
    rows, wide = x.shape
    low, full = jnp.bfloat16, jnp.float32
    pairs = wide // PAIR
    hbm = pl.BlockSpec(memory_space=pltpu.HBM)
    vmem = pl.BlockSpec(memory_space=pltpu.VMEM)
    dma = pltpu.SemaphoreType.DMA
    shape = jax.ShapeDtypeStruct
    groups = lax.axis_size("grp")
    parameters = [norms] + list(weights)
    whole = [(groups * w.shape[0], w.shape[1]) for w in parameters]
    sems = []
    pieces = None
    options = {}
    if groups == 8 and lax.axis_size("rep") % 2 == 0:
        piece_rows = (16, 48, 48, 96, 48, 48)
        pieces = tuple((w.shape[0] // n, n) for w, n in zip(parameters, piece_rows))
        total = sum(n for n, _ in pieces)
        sems = [dma((7, total)), dma((7, total))]
        options = dict(collective_id=0, has_side_effects=True)
    else:
        parameters = [lax.all_gather(w, "grp", axis=0, tiled=True) for w in parameters]
    results = pl.pallas_call(
        functools.partial(attention_forward_kernel, pieces),
        out_shape=[
            shape((16, wide), full),
            *[shape(whole[k], low) for k in (1, 2, 4, 5)],
            shape((rows, wide), low),
            shape((rows, 3 * wide), low),
            shape((pairs, 2, rows, rows), low),
            shape((rows, wide), low),
            shape((rows, wide), full),
            shape((rows, wide), low),
            shape((rows, wide), low),
            shape((COND_ROWS, 2 * wide), low),
            shape((pairs, 2, rows, COND_ROWS), low),
            shape((rows, wide), low),
            shape((rows, wide), full),
            shape((rows, wide), low),
        ],
        in_specs=[hbm, hbm] + [vmem] * 3 + [hbm] * 6,
        out_specs=[vmem] + [hbm] * 16,
        scratch_shapes=[
            pltpu.VMEM((rows, wide), low),
            pltpu.VMEM(cond.shape, low),
            *[pltpu.VMEM(s, low) for s in whole],
            pltpu.VMEM((rows, wide), low),
            pltpu.VMEM((rows, 3 * wide), low),
            pltpu.VMEM((rows, wide), low),
            pltpu.VMEM((rows, wide), full),
            pltpu.VMEM((rows, wide), low),
            pltpu.VMEM((COND_ROWS, 2 * wide), low),
            pltpu.VMEM((2, 2, rows, rows), low),
            pltpu.VMEM((2, 2, rows, COND_ROWS), low),
            dma((2,)),
            dma((14,)),
            dma((2,)),
            dma((6,)),
            *sems,
        ],
        compiler_params=pltpu.CompilerParams(vmem_limit_bytes=VMEM_LIMIT, **options),
    )(x, cond, *tables, *parameters)
    return results[0], results[1:5], results[5:]


GRAD_TILE = 2 * UNIT


def attention_backward_kernel(plan, *refs):
    refs = list(refs)

    def take(n):
        taken = refs[:n]
        del refs[:n]
        return taken

    x_in, cond_in, norms, cosine, sine_left, sine_right = take(6)
    qkv_in, out_in, query2_in, out2_in = take(4)
    act_one_in, heads_in, prob_in, flat_one_in, section_one_in, act_two_in = take(6)
    query_two_in, kv_two_in, prob_two_in, flat_two_in, section_two_in = take(5)
    d_norm_in, d_out_in = take(2)
    out_part, *ffn_in = take(4) if plan else [None]
    d_inputs_out, sums = take(2)
    grad_out2, grad_query2, grad_kv2, grad_out, grad_qkv = take(5)
    if plan:
        (grad_norm,) = take(1)
        sum_outs, lands = take(3), take(6)
    w_small, w_tile = take(2)
    x, cond, act_one, heads, flat_one, section_one, act_two = take(7)
    query_two, kv_two, flat_two, section_two, d_norm = take(5)
    d_low, d_heads, d_kv, d_att, prob, prob_two, grad_buf = take(7)
    in_sem, weight_sem, tile_sem, prob_sem, grad_sem, end_sem = take(6)
    if plan:
        norm_buf, norm_sem = take(2)
        bufs, sems = take(9), take(17)
        parts = (out_part, grad_out2, grad_query2, grad_kv2, grad_out, grad_qkv, grad_norm)
        work = Sums(plan[0], plan[1], parts, ffn_in, sum_outs, lands, bufs, sems)
    else:
        work = NoSums()
    rows, wide = x.shape
    pairs = wide // PAIR
    low = jnp.bfloat16
    work.start()
    work.begin()
    loads = {}
    for k, (name, src, dst) in enumerate(
        (
            ("section_two", section_two_in, section_two),
            ("d_norm", d_norm_in, d_norm),
            ("d_out", d_out_in, d_low),
            ("w_out2", out2_in, w_small),
            ("flat_two", flat_two_in, flat_two),
            ("query_two", query_two_in, query_two),
            ("kv_two", kv_two_in, kv_two),
            ("cond", cond_in, cond),
            ("act_two", act_two_in, act_two),
            ("section_one", section_one_in, section_one),
            ("flat_one", flat_one_in, flat_one),
            ("heads", heads_in, heads),
            ("act_one", act_one_in, act_one),
            ("x", x_in, x),
        )
    ):
        loads[name] = pltpu.make_async_copy(src, dst, in_sem.at[k])
        loads[name].start()

    def need(*names):
        for name in names:
            loads[name].wait()

    def next_weight(name, src, k):
        loads[name] = pltpu.make_async_copy(src, w_small, weight_sem.at[k])
        loads[name].start()

    gains = [norms.at[pl.ds(2 * k, 1)] for k in range(3)]

    def prob_copy(src, buf, p, slot):
        return pltpu.make_async_copy(src.at[p], buf.at[slot], prob_sem.at[slot])

    def prob_start(src, buf):
        for p in range(2):
            prob_copy(src, buf, p, p).start()

    at = {"z": 0, "xy": 0}

    def serve(*kinds):
        for kind in kinds:
            (work.z_step if kind == "z" else work.xy_step)(jnp.int32(at[kind]))
            at[kind] += 1

    def serve_pairs(p, kind, every):
        @pl.when(lax.rem(p, every) == every - 1)
        def _():
            (work.z_step if kind == "z" else work.xy_step)(at[kind] + p // every)

    def unit_copy(target, n, half, slot):
        src = grad_buf.at[slot, pl.ds(half * UNIT, UNIT)]
        unit = 2 * n + half
        if plan:
            per = target.shape[3] // UNIT
            block = unit // per
            row = pl.multiple_of(lax.rem(unit, per) * UNIT, 16)
            place = target.at[block // 4, lax.rem(block // 2, 2), lax.rem(block, 2), pl.ds(row, UNIT)]
        else:
            place = target.at[pl.ds(pl.multiple_of(unit * UNIT, 16), UNIT)]
        return pltpu.make_async_copy(src, place, grad_sem.at[slot, half])

    def grad_rows(target, count, compute, every=0):
        def step(n, carry):
            slot = lax.rem(n, 2)

            @pl.when(n >= 2)
            def _():
                for half in range(2):
                    unit_copy(target, n, half, slot).wait()

            compute(n, slot)
            for half in range(2):
                unit_copy(target, n, half, slot).start()
            if every:
                serve_pairs(n, "z", every)
            return carry

        lax.fori_loop(0, count, step, 0)
        for slot in range(2):
            for half in range(2):
                unit_copy(target, 0, half, slot).wait()

    def weight_rows(left, right, target, every=0):
        def compute(n, slot):
            columns = left[:, pl.ds(pl.multiple_of(n * GRAD_TILE, 128), GRAD_TILE)]
            for m in range(wide // 512):
                piece = slice(m * 512, (m + 1) * 512)
                grad_buf[slot, :, piece] = dot_tn(columns, right[:, piece]).astype(low)

        grad_rows(target, left.shape[1] // GRAD_TILE, compute, every)

    def round_rows():
        def block(n, carry):
            cut = pl.ds(pl.multiple_of(n * NORM_ROWS, NORM_ROWS), NORM_ROWS)
            d_low[cut] = d_section[cut].astype(low)
            return carry

        lax.fori_loop(0, rows // NORM_ROWS, block, 0)

    def through(target):
        def body(cut):
            target[:, cut] = dot(d_low[...], w_small[:, cut]).astype(low)

        tiles_of(wide, body)

    prob_start(prob_two_in, prob_two)
    serve("z", "xy")
    need("section_two", "d_norm", "d_out")
    normalise_back(section_two, gains[2], d_norm, d_low, section_two, sums, 4, rows)
    d_section = section_two
    round_rows()
    serve("z", "xy")
    need("w_out2")
    through(d_att)
    next_weight("w_query2", query2_in, 0)
    serve("z", "xy")
    need("flat_two")
    weight_rows(d_low, flat_two, grad_out2)
    serve("xy", "z")
    need("query_two", "kv_two")

    def cross_pair(p, lane):
        slot = lax.rem(p, 2)
        prob_copy(prob_two_in, prob_two, p, slot).wait()
        cols = [pl.ds(pl.multiple_of(lane + k * wide, PAIR), PAIR) for k in range(2)]
        d_query, d_key, d_value = attend_pair_back(
            query_two[:, cols[0]],
            kv_two[:, cols[0]],
            kv_two[:, cols[1]],
            d_att[:, cols[0]],
            [prob_two[slot, head] for head in range(2)],
        )
        d_low[:, cols[0]] = d_query.astype(low)
        d_kv[:, cols[0]] = d_key.astype(low)
        d_kv[:, cols[1]] = d_value.astype(low)

        @pl.when(p + 2 < pairs)
        def _():
            prob_copy(prob_two_in, prob_two, p + 2, slot).start()

        serve_pairs(p, "z", 1)
        serve_pairs(p, "xy", 3)

    pair_loop(cross_pair)
    at["z"] += 12
    at["xy"] += 4
    prob_start(prob_in, prob)
    need("w_query2")
    through(d_norm)
    next_weight("w_out", out_in, 1)
    serve("z", "xy")
    need("act_two")
    weight_rows(d_low, act_two, grad_query2)
    serve("z", "xy")
    need("cond")

    def cond_rows(n, slot):
        for half in range(2):
            columns = pl.ds(pl.multiple_of((2 * n + half) * GRAD_TILE, 128), GRAD_TILE)
            result = dot_tn(d_kv[:, columns], cond[...]).astype(low)
            at = slice(half * UNIT, (half + 1) * UNIT)
            grad_buf[slot, at, : wide // 2] = result[:UNIT]
            grad_buf[slot, at, wide // 2 :] = result[UNIT:]

    grad_rows(grad_kv2, wide // GRAD_TILE, cond_rows)
    serve("xy", "z")
    need("section_one")
    normalise_back(section_one, gains[1], d_norm, d_section, d_section, sums, 2, rows)
    serve("z", "xy")
    round_rows()
    need("w_out")
    through(d_att)

    def tile_copy(n, slot):
        cut = pl.ds(pl.multiple_of(n * TILE, TILE), TILE)
        return pltpu.make_async_copy(qkv_in.at[:, cut], w_tile.at[slot], tile_sem.at[slot])

    for n in range(2):
        tile_copy(n, n).start()
    serve("xy", "z")
    need("flat_one")
    weight_rows(d_low, flat_one, grad_out)
    serve("z", "xy")
    need("heads")

    def self_pair(p, lane):
        slot = lax.rem(p, 2)
        prob_copy(prob_in, prob, p, slot).wait()
        cols = [pl.ds(pl.multiple_of(lane + k * wide, PAIR), PAIR) for k in range(3)]
        d_query, d_key, d_value = attend_pair_back(
            heads[:, cols[0]],
            heads[:, cols[1]],
            heads[:, cols[2]],
            d_att[:, cols[0]],
            [prob[slot, head] for head in range(2)],
        )
        back = (cosine[...], -sine_left[...], -sine_right[...])
        d_heads[:, cols[0]] = turn(d_query, *back).astype(low)
        d_heads[:, cols[1]] = turn(d_key, *back).astype(low)
        d_heads[:, cols[2]] = d_value.astype(low)

        @pl.when(p + 2 < pairs)
        def _():
            prob_copy(prob_in, prob, p + 2, slot).start()

        work.z_step(at["z"] + p + (p + 1) // 2)

        @pl.when(lax.rem(p, 2) == 0)
        def _():
            work.z_step(at["z"] + p + 1 + p // 2)

        @pl.when(p < 10)
        def _():
            serve_pairs(p, "xy", 1)


    pair_loop(self_pair)
    at["z"] += pairs * 3 // 2
    at["xy"] += 10
    need("act_one")
    weight_rows(d_heads, act_one, grad_qkv, 4)
    at["z"] += 3
    serve("z", "xy")

    def first_norm(n, carry):
        slot = lax.rem(n, 2)
        cut = pl.ds(pl.multiple_of(n * TILE, TILE), TILE)
        tile_copy(n, slot).wait()
        d_norm[:, cut] = dot(d_heads[...], w_tile[slot]).astype(low)
        serve_pairs(n, "z", 3)

        @pl.when(n + 2 < wide // TILE)
        def _():
            tile_copy(n + 2, slot).start()

        return carry

    lax.fori_loop(0, wide // TILE, first_norm, 0)
    at["z"] += 2
    serve("z", "xy")
    need("x")
    normalise_back(x, gains[0], d_norm, d_section, d_section, sums, 0, rows)
    end = pltpu.make_async_copy(d_section, d_inputs_out, end_sem)
    end.start()
    if plan:
        norm_buf[...] = jnp.zeros_like(norm_buf)
        norm_buf[:8] = sums[...].astype(low)
        copies = []
        for b in range(8):
            place = grad_norm.at[b // 4, b // 2 % 2, b % 2]
            copies.append(pltpu.make_async_copy(norm_buf, place, norm_sem.at[b]))
            copies[-1].start()
        for copy in copies:
            copy.wait()
    work.finish(at["z"], at["xy"])
    end.wait()


def attention_backward(x, cond, norms, tables, weights, kept, d_norm, d_out, out_part, ffn):
    rows, wide = x.shape
    low, full = jnp.bfloat16, jnp.float32
    hbm = pl.BlockSpec(memory_space=pltpu.HBM)
    vmem = pl.BlockSpec(memory_space=pltpu.VMEM)
    dma = pltpu.SemaphoreType.DMA
    shape = jax.ShapeDtypeStruct
    buf = lambda s, t=low: pltpu.VMEM(s, t)
    heights = (wide, wide, wide, wide, 3 * wide)
    more_outs, more_scratch = [], []
    plan = None
    options = {}
    if ffn:
        grads = [(2, 2, 2, h // 8, wide) for h in heights] + [(2, 2, 2, CUT, wide)]
        plan = (
            tuple(g[3] // CUT for g in [out_part.shape] + grads),
            tuple(f.shape[0] // FCUT for f in ffn),
        )
        outs, lands, bufs, sems = Sums.shapes(*plan, wide)
        more_outs = outs + lands
        more_scratch = [buf((CUT, wide)), dma((8,))] + bufs + sems
        options = dict(collective_id=1, has_side_effects=True)
    else:
        grads = [(h, wide) for h in heights]
    ffn = [out_part] + list(ffn) if ffn else []
    results = pl.pallas_call(
        functools.partial(attention_backward_kernel, plan),
        out_shape=[shape((rows, wide), full), shape((8, wide), full)]
        + [shape(g, low) for g in grads]
        + more_outs,
        in_specs=[hbm, hbm] + [vmem] * 4 + [hbm] * (17 + len(ffn)),
        out_specs=[hbm, vmem] + [hbm] * (len(grads) + len(more_outs)),
        scratch_shapes=[
            buf((wide, wide)),
            buf((2, 3 * wide, TILE)),
            buf((rows, wide)),
            buf(cond.shape),
            buf((rows, wide)),
            buf((rows, 3 * wide)),
            buf((rows, wide)),
            buf((rows, wide), full),
            buf((rows, wide)),
            buf((rows, wide)),
            buf((COND_ROWS, 2 * wide)),
            buf((rows, wide)),
            buf((rows, wide), full),
            buf((rows, wide)),
            buf((rows, wide)),
            buf((rows, 3 * wide)),
            buf((COND_ROWS, 2 * wide)),
            buf((rows, wide)),
            buf((2, 2, rows, rows)),
            buf((2, 2, rows, COND_ROWS)),
            buf((2, GRAD_TILE, wide)),
            dma((14,)),
            dma((2,)),
            dma((2,)),
            dma((2,)),
            dma((2, 2)),
            dma,
            *more_scratch,
        ],
        compiler_params=pltpu.CompilerParams(vmem_limit_bytes=VMEM_LIMIT, **options),
    )(x, cond, norms, *tables, *weights, *kept, d_norm, d_out, *ffn)
    return results[0], results[1], results[2:7], results[8:11]


END_SLOTS = 4


def end_kernel(near, far, ffn, section, d_in, *refs):
    d_out, *outs = refs[:10]
    low_buf, full_buf, in_sem, out_sem = refs[10:]
    outputs, out2, query2, kv2, out, qkv, gate, up, down = outs
    wide = low_buf.shape[2]
    jobs = []
    base = 0
    for target in (out2, query2, kv2, out, qkv):
        rows = target.shape[0] * target.shape[1] // wide
        jobs += [(far, base + r, target, r) for r in range(0, rows, UNIT)]
        base += rows
    base = 0
    for target in (gate, up, down):
        jobs += [(ffn, base + r, target, r) for r in range(0, target.shape[0], UNIT)]
        base += target.shape[0]
    jobs += [(near, r, outputs, r) for r in range(0, outputs.shape[0], UNIT)]
    jobs += [(d_in, r, d_out, r) for r in range(0, d_out.shape[0], UNIT)]

    def loads(n):
        source, row, target, place = jobs[n]
        slot = n % END_SLOTS
        buf = full_buf if source is d_in else low_buf
        copies = [
            pltpu.make_async_copy(source.at[pl.ds(row, UNIT)], buf.at[slot], in_sem.at[slot, 0])
        ]
        if target is outputs:
            copies.append(
                pltpu.make_async_copy(
                    section.at[pl.ds(place, UNIT)], full_buf.at[slot], in_sem.at[slot, 1]
                )
            )
        return copies

    def stores(n):
        _, _, target, place = jobs[n]
        slot = n % END_SLOTS
        if target is outputs:
            pairs = [(low_buf.at[slot], target.at[pl.ds(place, UNIT)])]
        elif target is kv2:
            pairs = [
                (
                    full_buf.at[slot, :, pl.ds(h * (wide // 2), wide // 2)],
                    target.at[pl.ds(2 * place + h * UNIT, UNIT)],
                )
                for h in range(2)
            ]
        else:
            pairs = [(full_buf.at[slot], target.at[pl.ds(place, UNIT)])]
        return [
            pltpu.make_async_copy(src, dst, out_sem.at[slot, k])
            for k, (src, dst) in enumerate(pairs)
        ]

    ahead = END_SLOTS - 2
    for n in range(ahead):
        for copy in loads(n):
            copy.start()
    for n in range(len(jobs)):
        if n + ahead < len(jobs):
            if n + ahead >= END_SLOTS:
                for copy in stores(n + ahead - END_SLOTS):
                    copy.wait()
            for copy in loads(n + ahead):
                copy.start()
        for copy in loads(n):
            copy.wait()
        slot = n % END_SLOTS
        is_output = jobs[n][2] is outputs

        def block(m, carry, slot=slot, is_output=is_output):
            cut = pl.ds(pl.multiple_of(m * 32, 32), 32)
            value = low_buf[slot, cut].astype(jnp.float32)
            if is_output:
                low_buf[slot, cut] = (full_buf[slot, cut] + value).astype(low_buf.dtype)
            else:
                full_buf[slot, cut] = value
            return carry

        if jobs[n][0] is not d_in:
            lax.fori_loop(0, UNIT // 32, block, 0)
        for copy in stores(n):
            copy.start()
    for n in range(max(len(jobs) - END_SLOTS, 0), len(jobs)):
        for copy in stores(n):
            copy.wait()


def end_all(near, far, ffn, section, d_in, out_shapes):
    hbm = pl.BlockSpec(memory_space=pltpu.HBM)
    wide = near.shape[1]
    dma = pltpu.SemaphoreType.DMA
    return pl.pallas_call(
        end_kernel,
        out_shape=[
            jax.ShapeDtypeStruct(d_in.shape, d_in.dtype),
            jax.ShapeDtypeStruct(near.shape, near.dtype),
        ]
        + [jax.ShapeDtypeStruct(s, jnp.float32) for s in out_shapes],
        in_specs=[hbm] * 5,
        out_specs=[hbm] * 10,
        scratch_shapes=[
            pltpu.VMEM((END_SLOTS, UNIT, wide), near.dtype),
            pltpu.VMEM((END_SLOTS, UNIT, wide), jnp.float32),
            dma((END_SLOTS, 2)),
            dma((END_SLOTS, 2)),
        ],
        compiler_params=pltpu.CompilerParams(vmem_limit_bytes=VMEM_LIMIT),
    )(near, far, ffn, section, d_in)


def per_device(
    inputs,
    conditioning,
    positions,
    slot_valid,
    cotangent,
    norm1_gain,
    norm1_shift,
    norm2_gain,
    norm2_shift,
    norm3_gain,
    norm3_shift,
    w_qkv,
    w_out,
    w_query2,
    w_kv2,
    w_out2,
    w_gate,
    w_up,
    w_down,
):
    cond_rows = conditioning[0]
    norms = jnp.stack(
        [norm1_gain, norm1_shift, norm2_gain, norm2_shift, norm3_gain, norm3_shift], axis=0
    )
    own_width = norms.shape[1]
    norms = lax.dynamic_update_slice(
        jnp.zeros((16, D), norms.dtype), norms, (0, lax.axis_index("grp") * own_width)
    )
    grad_mlp = (cotangent[0].astype(jnp.float32) * slot_valid[0].astype(jnp.float32)).astype(
        jnp.bfloat16
    )
    grad_mlp = lax.optimization_barrier(grad_mlp)
    all_grad = lax.all_gather(grad_mlp, "grp", axis=0, tiled=True)
    tables = turn_tables(positions[0])
    padded_cond = jnp.pad(cond_rows, ((0, COND_ROWS - NC), (0, 0)))
    norms, whole, kept = attention_forward(
        inputs[0], padded_cond, tables, norms, [w_qkv, w_out, w_kv2, w_query2, w_out2]
    )
    act_three, section_two = kept[-1], kept[-2]
    if lax.axis_size("grp") == 8:
        mlp_out, d_norm3, grad_gate, grad_up, grad_down = ffn_all(
            act_three, all_grad, w_gate, w_up, w_down
        )
    else:
        all_act = lax.all_gather(act_three, "grp", axis=0, tiled=True)
        gate_pre = dot_nt(all_act, w_gate)
        up_pre = dot_nt(all_act, w_up)
        hidden = swiglu(gate_pre, up_pre).astype(jnp.bfloat16)
        mlp_part = dot(hidden, w_down).astype(jnp.bfloat16)
        mlp_out = lax.psum_scatter(mlp_part, "grp", scatter_dimension=0, tiled=True)
        d_hidden = dot_nt(all_grad, w_down)
        d_gate_full, d_up_full = swiglu_back(gate_pre, up_pre, d_hidden)
        d_gate = d_gate_full.astype(jnp.bfloat16)
        d_up = d_up_full.astype(jnp.bfloat16)
        d_norm3_part = (dot(d_gate, w_gate) + dot(d_up, w_up)).astype(jnp.bfloat16)
        d_norm3 = lax.psum_scatter(d_norm3_part, "grp", scatter_dimension=0, tiled=True)
        grad_gate = dot_tn(d_gate, all_act).astype(jnp.bfloat16)
        grad_up = dot_tn(d_up, all_act).astype(jnp.bfloat16)
        grad_down = dot_tn(hidden, all_grad).astype(jnp.bfloat16)
    groups = lax.axis_size("grp")
    fused = groups == 8 and lax.axis_size("rep") == 4
    ffn_grads = [grad_gate, grad_up, grad_down]
    if groups == 8 and not fused:
        mlp_out = lax.psum_scatter(
            mlp_out.reshape(-1, D), "grp", scatter_dimension=0, tiled=True
        )
    d_tokens, norm_sums, grads, totals = attention_backward(
        inputs[0],
        padded_cond,
        norms,
        tables,
        whole,
        kept[:-1],
        d_norm3,
        grad_mlp,
        mlp_out,
        ffn_grads if fused else [],
    )
    own_at = lax.axis_index("grp") * own_width
    if fused:
        mlp_out, total_a, total_f = totals
        norm_total = total_a[total_a.shape[0] - CUT :][:6]
        (
            d_tokens,
            outputs,
            grad_out_two,
            grad_query_two,
            grad_kv_two,
            grad_out_one,
            grad_qkv,
            *ffn_sums,
        ) = end_all(
            mlp_out,
            total_a,
            total_f,
            section_two,
            d_tokens,
            [w.shape for w in (w_out2, w_query2, w_kv2, w_out, w_qkv, w_gate, w_up, w_down)],
        )
    else:
        grads = list(grads)
        kv2_part = jnp.swapaxes(grads[2].reshape(-1, UNIT, 2, D // 2), 1, 2)
        grads[2] = kv2_part.reshape(2 * D, D // 2)
        norm_total = lax.psum(norm_sums[:6].astype(jnp.bfloat16), ("grp", "rep"))
        shards = [lax.psum_scatter(g, "grp", scatter_dimension=0, tiled=True) for g in grads]
        grad_out_two, grad_query_two, grad_kv_two, grad_out_one, grad_qkv = lax.psum(
            tuple(shards), "rep"
        )
        ffn_sums = lax.psum(tuple(ffn_grads), "rep")
        outputs = (section_two + mlp_out.astype(jnp.float32)).astype(jnp.bfloat16)
    norm_total = lax.dynamic_slice_in_dim(norm_total, own_at, own_width, axis=1)
    grad_qkv, grad_out_one, grad_query_two, grad_out_two, grad_kv_two = (
        g.astype(jnp.float32)
        for g in (grad_qkv, grad_out_one, grad_query_two, grad_out_two, grad_kv_two)
    )
    norm_total = norm_total.astype(jnp.float32)
    grad_gate, grad_up, grad_down = (g.astype(jnp.float32) for g in ffn_sums)
    return (
        outputs[None],
        d_tokens[None],
        norm_total[0],
        norm_total[1],
        norm_total[2],
        norm_total[3],
        norm_total[4],
        norm_total[5],
        grad_qkv,
        grad_out_one,
        grad_query_two,
        grad_kv_two,
        grad_out_two,
        grad_gate,
        grad_up,
        grad_down,
    )


def solution(mesh):
    return jax.shard_map(
        per_device,
        mesh=mesh,
        in_specs=(
            P(("grp", "rep"), None, None),
            P(("grp", "rep"), None, None),
            P(("grp", "rep"), None),
            P(("grp", "rep")),
            P(("grp", "rep"), None, None),
            P("grp"),
            P("grp"),
            P("grp"),
            P("grp"),
            P("grp"),
            P("grp"),
            P("grp", None),
            P("grp", None),
            P("grp", None),
            P("grp", None),
            P("grp", None),
            P("grp", None),
            P("grp", None),
            P("grp", None),
        ),
        out_specs=(
            P(("grp", "rep"), None, None),
            P(("grp", "rep"), None, None),
            P("grp"),
            P("grp"),
            P("grp"),
            P("grp"),
            P("grp"),
            P("grp"),
            P("grp", None),
            P("grp", None),
            P("grp", None),
            P("grp", None),
            P("grp", None),
            P("grp", None),
            P("grp", None),
            P("grp", None),
        ),
        check_vma=False,
    )
```

```python
import functools
import math

import jax
import jax.numpy as jnp
from jax import lax
from jax.experimental import pallas as pl
from jax.experimental.pallas import tpu as pltpu
from jax.sharding import PartitionSpec as P

MESH = pl.DeviceIdType.MESH
VMEM_LIMIT = 63 * 1024 * 1024

D = 1536
HEADS = 24
HD = 64
NC = 130


epsilon = 1e-05
score_scale = 0.125


def layer_norm(tensor, gain, shift):
    center = tensor - jnp.mean(tensor, axis=-1, keepdims=True)
    spread = jnp.mean(center * center, axis=-1, keepdims=True)
    return center * lax.rsqrt(spread + epsilon) * gain + shift


def swiglu(gate_part, up_part):
    return jax.nn.silu(gate_part) * up_part


def swiglu_back(gate_part, up_part, d_hidden):
    _, pullback = jax.vjp(swiglu, gate_part, up_part)
    return pullback(d_hidden)


def dot_nt(left_side, right_side):
    return lax.dot_general(
        left_side, right_side, (((1,), (1,)), ((), ())), preferred_element_type=jnp.float32
    )


def dot_tn(left_side, right_side):
    return lax.dot_general(
        left_side, right_side, (((0,), (0,)), ((), ())), preferred_element_type=jnp.float32
    )


def dot(left_side, right_side):
    return jnp.dot(left_side, right_side, preferred_element_type=jnp.float32)


def turn_tables(positions):
    quarter = HD // 4
    frequency = jnp.exp(jnp.arange(quarter, dtype=jnp.float32) * (-math.log(10000.0) / quarter))
    turned = positions.astype(jnp.float32)[:, None] * frequency[None, :]
    cosine, sine = jnp.cos(turned), jnp.sin(turned)
    none, one = jnp.zeros_like(sine), jnp.ones_like(sine)

    def heads(*parts):
        return jnp.tile(jnp.concatenate(parts, axis=1), (1, 2))

    return (
        heads(cosine, cosine, one, one),
        heads(-sine, none, none, none),
        heads(none, sine, none, none),
    )


def meet(peers, lower=None, upper=None, rep_index=None):
    barrier = pltpu.get_barrier_semaphore()
    for peer in peers:
        pl.semaphore_signal(barrier, inc=1, device_id=peer, device_id_type=MESH)
    if lower is not None:

        @pl.when(rep_index > 0)
        def _():
            pl.semaphore_signal(barrier, inc=1, device_id=lower, device_id_type=MESH)

        @pl.when(rep_index < 3)
        def _():
            pl.semaphore_signal(barrier, inc=1, device_id=upper, device_id_type=MESH)

    expected = len(peers)
    if lower is not None:
        expected = expected + jnp.where(rep_index > 0, 1, 0) + jnp.where(rep_index < 3, 1, 0)
    pl.semaphore_wait(barrier, expected)


GATHER_WINDOW = 4


class Gather:
    def __init__(self, pieces, sources, fulls, send_sem, recv_sem, local_sem):
        self.pieces, self.sources, self.fulls = pieces, sources, fulls
        self.send_sem, self.recv_sem, self.local_sem = send_sem, recv_sem, local_sem
        self.total = sum(n for n, _ in pieces)
        self.steps = self.total + GATHER_WINDOW + 2
        self.me = me = lax.axis_index("grp")
        self.plane = plane = lax.axis_index("rep")
        first_bit = 2 + 2 * lax.rem(plane, 2)
        self.first, self.second, self.across = me ^ first_bit, me ^ (6 - first_bit), me ^ 6
        self.first_dev = (self.first, plane)
        self.second_dev = (self.second, plane)
        self.rep_dev = (me, plane ^ 1)
        self.mate_dev = (me ^ 1, plane)

    def start(self):
        meet([self.first_dev, self.second_dev, self.rep_dev, self.mate_dev])

    def own_copy(self, k):
        n, rows = self.pieces[k]
        row = pl.multiple_of(self.me * (n * rows), 16)
        return pltpu.make_async_copy(
            self.sources[k], self.fulls[k].at[pl.ds(row, n * rows)], self.local_sem.at[k]
        )

    def each(self, i, body):
        base = 0
        for k, (n, rows) in enumerate(self.pieces):

            @pl.when((i >= base) & (i < base + n))
            def _(k=k, rows=rows, base=base):
                body(k, (i - base) * rows)

            base += n

    def push(self, k, offset, i, owner, lane, device, own=False):
        n, rows = self.pieces[k]
        cut = pl.ds(pl.multiple_of(offset, 16), rows)
        place = self.fulls[k].at[pl.ds(pl.multiple_of(owner * (n * rows) + offset, 16), rows)]
        return pltpu.make_async_remote_copy(
            src_ref=self.sources[k].at[cut] if own else place,
            dst_ref=place,
            send_sem=self.send_sem.at[lane, i],
            recv_sem=self.recv_sem.at[lane, i],
            device_id=device,
            device_id_type=MESH,
        )

    def stage_own(self, i):
        def body(k, offset):
            self.push(k, offset, i, self.me, 0, self.first_dev, own=True).start()
            self.push(k, offset, i, self.me, 3, self.mate_dev, own=True).start()

        self.each(i, body)

    def stage_first(self, i):
        def body(k, offset):
            self.push(k, offset, i, self.first, 0, self.first_dev).wait_recv()
            self.push(k, offset, i, self.first, 1, self.second_dev).start()
            self.push(k, offset, i, self.first, 2, self.rep_dev).start()
            self.push(k, offset, i, self.first, 4, self.mate_dev).start()

        self.each(i, body)

    def stage_rest(self, i):
        def body(k, offset):
            self.push(k, offset, i, self.across, 1, self.second_dev).wait_recv()
            self.push(k, offset, i, self.across, 5, self.mate_dev).start()
            self.push(k, offset, i, self.second, 2, self.rep_dev).wait_recv()
            self.push(k, offset, i, self.second, 6, self.mate_dev).start()

        self.each(i, body)

    def step(self, t):
        for stage, lag in (
            (self.stage_own, 0),
            (self.stage_first, GATHER_WINDOW),
            (self.stage_rest, GATHER_WINDOW + 2),
        ):
            i = t - lag

            @pl.when((i >= 0) & (i < self.total))
            def _(stage=stage, i=i):
                stage(i)

    def run(self, first, last):
        def body(t, carry):
            self.step(t)
            return carry

        lax.fori_loop(first, last, body, 0)

    def need(self, k):
        base = sum(n for n, _ in self.pieces[:k])
        n, rows = self.pieces[k]

        def body(j, carry):
            for lane in (3, 4, 5, 6):
                self.push(k, j * rows, base + j, self.me, lane, self.mate_dev).wait_recv()
            return carry

        lax.fori_loop(0, n, body, 0)
        self.own_copy(k).wait()

    def finish(self):
        def sent(i, carry):
            def body(k, offset):
                self.push(k, offset, i, self.me, 0, self.first_dev, own=True).wait_send()
                self.push(k, offset, i, self.me, 3, self.mate_dev, own=True).wait_send()
                for lane in (1, 2, 4, 5, 6):
                    self.push(k, offset, i, self.first, lane, self.mate_dev).wait_send()

            self.each(i, body)
            return carry

        lax.fori_loop(0, self.total, sent, 0)


class Loads:
    steps = 0

    def __init__(self, sources, fulls, local_sem):
        self.sources, self.fulls, self.local_sem = sources, fulls, local_sem

    def start(self):
        pass

    def own_copy(self, k):
        return pltpu.make_async_copy(self.sources[k], self.fulls[k], self.local_sem.at[k])

    def step(self, t):
        pass

    def run(self, first, last):
        pass

    def need(self, k):
        self.own_copy(k).wait()

    def finish(self):
        pass


CUT = 48
FCUT = 48
UNIT = 192
MATE_SLOTS = 4
OWN_SLOTS = 2
SUM_SLOTS = 9
FFN_SLOTS = 14
LAND_SLOTS = 3


class Sums:
    def __init__(self, pieces, ffn_pieces, parts, ffn, outs, lands, bufs, sems):
        self.near = pieces[0]
        self.pieces, self.ffn_pieces, self.parts, self.ffn = pieces, ffn_pieces, parts, ffn
        self.out_n, self.out_a, self.out_f = outs
        self.one_land, self.two_land, self.low_a, self.up_a, self.low_f, self.up_f = lands
        (
            self.mate_buf,
            self.own_buf,
            self.sums,
            self.done,
            self.ffn_buf,
            self.one_buf,
            self.two_buf,
            self.low_buf,
            self.up_buf,
        ) = bufs
        (
            self.mate_send,
            self.mate_recv,
            self.own_sem,
            self.one_send,
            self.one_recv,
            self.one_sem,
            self.two_send,
            self.two_recv,
            self.two_sem,
            self.ffn_sem,
            self.chain_send,
            self.chain_recv,
            self.low_sem,
            self.up_sem,
            self.out_sem,
            self.near_sem,
            self.credit,
        ) = sems
        me = lax.axis_index("grp")
        self.plane = plane = lax.axis_index("rep")
        self.core = lax.rem(me, 2)
        self.x = lax.rem(me // 2, 2)
        self.y = me // 4
        self.mate_dev = (me ^ 1, plane)
        self.x_dev = (me ^ 2, plane)
        self.y_dev = (me ^ 4, plane)
        self.low_dev = (me, plane - 1)
        self.up_dev = (me, plane + 1)
        self.total = sum(pieces)
        self.ffn_count = sum(ffn_pieces)
        self.chain_total = self.ffn_count + self.total - self.near

    def start(self):
        meet([self.mate_dev, self.x_dev, self.y_dev], self.low_dev, self.up_dev, self.plane)

    def each(self, i, body):
        base = 0
        for k, n in enumerate(self.pieces):

            @pl.when((i >= base) & (i < base + n))
            def _(k=k, base=base):
                body(k, pl.ds(pl.multiple_of((i - base) * CUT, 16), CUT))

            base += n

    def mate_copy(self, k, cut, slot):
        return pltpu.make_async_remote_copy(
            src_ref=self.parts[k].at[:, :, 1 - self.core, cut],
            dst_ref=self.mate_buf.at[slot],
            send_sem=self.mate_send.at[slot],
            recv_sem=self.mate_recv.at[slot],
            device_id=self.mate_dev,
            device_id_type=MESH,
        )

    def own_copy(self, k, cut, slot):
        return pltpu.make_async_copy(
            self.parts[k].at[:, :, self.core, cut], self.own_buf.at[slot], self.own_sem.at[slot]
        )

    def load(self, i):
        @pl.when(i >= MATE_SLOTS)
        def _():
            pl.semaphore_wait(self.credit, 1)
            self.mate_copy(0, pl.ds(0, CUT), lax.rem(i, MATE_SLOTS)).wait_send()

        def body(k, cut):
            self.mate_copy(k, cut, lax.rem(i, MATE_SLOTS)).start()
            self.own_copy(k, cut, lax.rem(i, OWN_SLOTS)).start()

        self.each(i, body)

    def one_copy(self, i, slot, by_x):
        return pltpu.make_async_remote_copy(
            src_ref=self.sums.at[slot, :, 1 - self.x] if by_x else self.sums.at[slot, 1 - self.y],
            dst_ref=self.one_land.at[i],
            send_sem=self.one_send.at[slot],
            recv_sem=self.one_recv.at[i],
            device_id=self.x_dev if by_x else self.y_dev,
            device_id_type=MESH,
        )

    def two_copy(self, i, slot, by_x):
        return pltpu.make_async_remote_copy(
            src_ref=self.sums.at[slot, 1 - self.y, self.x]
            if by_x
            else self.sums.at[slot, self.y, 1 - self.x],
            dst_ref=self.two_land.at[i],
            send_sem=self.two_send.at[slot],
            recv_sem=self.two_recv.at[i],
            device_id=self.y_dev if by_x else self.x_dev,
            device_id_type=MESH,
        )

    def either(self, i, body):
        @pl.when(lax.rem(i, 2) == 0)
        def _():
            body(True)

        @pl.when(lax.rem(i, 2) == 1)
        def _():
            body(False)

    def one_load(self, i):
        slot = lax.rem(i, LAND_SLOTS)
        return pltpu.make_async_copy(self.one_land.at[i], self.one_buf.at[slot], self.one_sem.at[slot])

    def two_load(self, i):
        slot = lax.rem(i, LAND_SLOTS)
        return pltpu.make_async_copy(self.two_land.at[i], self.two_buf.at[slot], self.two_sem.at[slot])

    def pair(self, i):
        mate_slot, own_slot = lax.rem(i, MATE_SLOTS), lax.rem(i, OWN_SLOTS)
        slot = lax.rem(i, SUM_SLOTS)
        self.mate_copy(0, pl.ds(0, CUT), mate_slot).wait_recv()
        self.own_copy(0, pl.ds(0, CUT), own_slot).wait()
        for u in range(2):
            for v in range(2):
                self.sums[slot, u, v] = add(
                    self.own_buf[own_slot, u, v], self.mate_buf[mate_slot, u, v]
                )

        @pl.when(i + MATE_SLOTS < self.total)
        def _():
            pl.semaphore_signal(
                self.credit, inc=1, device_id=self.mate_dev, device_id_type=MESH
            )

        self.either(i, lambda by_x: self.one_copy(i, slot, by_x).start())

    def one_arrives(self, i):
        self.either(i, lambda by_x: self.one_copy(i, lax.rem(i, SUM_SLOTS), by_x).wait_recv())
        self.one_load(i).start()

    def plane_one(self, i):
        slot, land = lax.rem(i, SUM_SLOTS), lax.rem(i, LAND_SLOTS)
        self.one_load(i).wait()

        def body(by_x):
            for u in range(2):
                at = (slot, u, self.x) if by_x else (slot, self.y, u)
                self.sums[at] = add(self.sums[at], self.one_buf[land, u])
            self.two_copy(i, slot, by_x).start()

        self.either(i, body)

    def two_arrives(self, i):
        self.either(i, lambda by_x: self.two_copy(i, lax.rem(i, SUM_SLOTS), by_x).wait_recv())
        self.two_load(i).start()

    def plane_two(self, i):
        slot = lax.rem(i, SUM_SLOTS)
        self.two_load(i).wait()
        self.done[i] = add(self.sums[slot, self.y, self.x], self.two_buf[lax.rem(i, LAND_SLOTS)])

        @pl.when(i < self.near)
        def _():
            self.near_copy(i).start()

        def body(by_x):
            self.one_copy(i, slot, by_x).wait_send()
            self.two_copy(i, slot, by_x).wait_send()

        self.either(i, body)

    def near_copy(self, i):
        rows = pl.ds(pl.multiple_of(i * CUT, 16), CUT)
        return pltpu.make_async_copy(self.done.at[i], self.out_n.at[rows], self.near_sem.at[i])

    def ffn_load(self, j):
        base = 0
        for k, n in enumerate(self.ffn_pieces):

            @pl.when((j >= base) & (j < base + n))
            def _(k=k, base=base):
                row = pl.multiple_of((j - base) * FCUT, 16)
                pltpu.make_async_copy(
                    self.ffn[k].at[pl.ds(row, FCUT)],
                    self.ffn_buf.at[lax.rem(j, FFN_SLOTS)],
                    self.ffn_sem.at[lax.rem(j, FFN_SLOTS)],
                ).start()

            base += n

    def ffn_wait(self, j):
        pltpu.make_async_copy(
            self.ffn[0].at[pl.ds(0, FCUT)],
            self.ffn_buf.at[lax.rem(j, FFN_SLOTS)],
            self.ffn_sem.at[lax.rem(j, FFN_SLOTS)],
        ).wait()

    def role(self, j, plane, body):
        slot = lax.rem(j, LAND_SLOTS)
        key = self.plane + jnp.where(j < self.ffn_count, 0, 4)
        key = jnp.where((j >= 0) & (j < self.chain_total), key, 8)

        @pl.when(key == plane)
        def _():
            rows = pl.ds(pl.multiple_of(j * FCUT, 16), FCUT)
            body(
                self.ffn_buf.at[lax.rem(j, FFN_SLOTS)],
                self.low_f.at[j],
                self.up_f.at[j],
                self.low_buf.at[slot],
                self.up_buf.at[slot],
                self.out_f.at[rows],
            )

        @pl.when(key == plane + 4)
        def _():
            i = j - self.ffn_count
            rows = pl.ds(pl.multiple_of(i * CUT, 16), CUT)
            part = pl.ds(0, CUT)
            body(
                self.done.at[i + self.near],
                self.low_a.at[i],
                self.up_a.at[i],
                self.low_buf.at[slot, part],
                self.up_buf.at[slot, part],
                self.out_a.at[rows],
            )

    def chain(self, j, lane, src, dst, device):
        return pltpu.make_async_remote_copy(
            src_ref=src,
            dst_ref=dst,
            send_sem=self.chain_send.at[lane, j],
            recv_sem=self.chain_recv.at[lane, j],
            device_id=device,
            device_id_type=MESH,
        )

    def low_load(self, j, land, buf):
        return pltpu.make_async_copy(land, buf, self.low_sem.at[lax.rem(j, LAND_SLOTS)])

    def up_load(self, j, land, buf):
        return pltpu.make_async_copy(land, buf, self.up_sem.at[lax.rem(j, LAND_SLOTS)])

    def inward(self, j):
        @pl.when((j >= 0) & (j < self.ffn_count))
        def _():
            self.ffn_wait(j)

        def lowest(mine, low, up, low_buf, up_buf, out):
            self.chain(j, 0, mine, low, self.up_dev).start()

        def highest(mine, low, up, low_buf, up_buf, out):
            self.chain(j, 1, mine, up, self.low_dev).start()

        self.role(j, 0, lowest)
        self.role(j, 3, highest)

    def middle_arrives(self, j):
        def body(mine, low, up, low_buf, up_buf, out):
            self.chain(j, 1, mine, up, self.low_dev).wait_recv()
            self.up_load(j, up, up_buf).start()

        self.role(j, 2, body)

    def middle(self, j):
        def body(mine, low, up, low_buf, up_buf, out):
            self.up_load(j, up, up_buf).wait()
            mine[...] = add(mine[...], up_buf[...])
            self.chain(j, 1, mine, up, self.low_dev).start()

        self.role(j, 2, body)

    def root_arrives(self, j):
        def body(mine, low, up, low_buf, up_buf, out):
            self.chain(j, 0, mine, low, self.up_dev).wait_recv()
            self.low_load(j, low, low_buf).start()
            self.chain(j, 1, mine, up, self.low_dev).wait_recv()
            self.up_load(j, up, up_buf).start()

        self.role(j, 1, body)

    def root(self, j):
        def body(mine, low, up, low_buf, up_buf, out):
            self.low_load(j, low, low_buf).wait()
            self.up_load(j, up, up_buf).wait()
            mine[...] = add(mine[...], low_buf[...], up_buf[...])
            self.chain(j, 0, mine, out, self.up_dev).start()
            self.chain(j, 1, mine, out, self.low_dev).start()
            pltpu.make_async_copy(mine, out, self.out_sem.at[j]).start()

        self.role(j, 1, body)

    def outward(self, j):
        def body(mine, low, up, low_buf, up_buf, out):
            self.chain(j, 0, mine, out, self.up_dev).wait_recv()
            self.chain(j, 0, out, out, self.up_dev).start()

        self.role(j, 2, body)

    def drain(self, j):
        def lowest(mine, low, up, low_buf, up_buf, out):
            self.chain(j, 0, mine, low, self.up_dev).wait_send()
            self.chain(j, 1, mine, out, self.low_dev).wait_recv()

        def holder(mine, low, up, low_buf, up_buf, out):
            self.chain(j, 0, mine, out, self.up_dev).wait_send()
            self.chain(j, 1, mine, out, self.low_dev).wait_send()
            pltpu.make_async_copy(mine, out, self.out_sem.at[j]).wait()

        def between(mine, low, up, low_buf, up_buf, out):
            self.chain(j, 1, mine, up, self.low_dev).wait_send()
            self.chain(j, 0, out, out, self.up_dev).wait_send()

        def highest(mine, low, up, low_buf, up_buf, out):
            self.chain(j, 1, mine, up, self.low_dev).wait_send()
            self.chain(j, 0, mine, out, self.up_dev).wait_recv()

        for plane, body in enumerate((lowest, holder, between, highest)):
            self.role(j, plane, body)

    def stages(self, at, limit, pairs):
        for stage, behind in pairs:
            i = at - behind

            @pl.when((i >= 0) & (i < limit))
            def _(stage=stage, i=i):
                stage(i)

    def xy_step(self, i):
        self.stages(
            i,
            self.total,
            (
                (self.load, 0),
                (self.pair, 1),
                (self.plane_two, 7),
                (self.plane_one, 4),
                (self.two_arrives, 6),
                (self.one_arrives, 3),
            ),
        )

    def z_step(self, j):
        self.stages(j + 1, self.ffn_count, ((self.ffn_load, 0),))
        for stage, behind in (
            (self.inward, 0),
            (self.outward, 8),
            (self.root, 6),
            (self.middle, 3),
            (self.root_arrives, 5),
            (self.middle_arrives, 2),
            (self.drain, 11),
        ):
            stage(j - behind)

    def begin(self):
        self.ffn_load(jnp.int32(0))

    def finish(self, z_next, xy_next):
        both = (self.total + 8 - xy_next + 1) // 2

        def body(u, carry):
            self.z_step(z_next + 3 * u)
            self.xy_step(xy_next + 2 * u)
            self.z_step(z_next + 3 * u + 1)
            self.xy_step(xy_next + 2 * u + 1)
            self.z_step(z_next + 3 * u + 2)
            return carry

        def chain_only(u, carry):
            self.z_step(u)
            return carry

        lax.fori_loop(0, both, body, 0)
        lax.fori_loop(z_next + 3 * both, self.chain_total + 12, chain_only, 0)
        for i in range(max(self.total - MATE_SLOTS, 0), self.total):
            self.mate_copy(0, pl.ds(0, CUT), i % MATE_SLOTS).wait_send()
        for i in range(self.near):
            self.near_copy(i).wait()

    @staticmethod
    def shapes(pieces, ffn_pieces, wide):
        total, ffn_count = sum(pieces), sum(ffn_pieces)
        near = pieces[0]
        far = total - near
        chain_total = far + ffn_count
        low = jnp.bfloat16
        dma = pltpu.SemaphoreType.DMA
        shape = lambda *s: jax.ShapeDtypeStruct(s, low)
        buf = lambda *s: pltpu.VMEM(s, low)
        outs = [shape(n, wide) for n in (near * CUT, far * CUT, ffn_count * FCUT)]
        lands = [
            shape(total, 2, CUT, wide),
            shape(total, CUT, wide),
            *[shape(far, CUT, wide)] * 2,
            *[shape(ffn_count, FCUT, wide)] * 2,
        ]
        bufs = [
            buf(MATE_SLOTS, 2, 2, CUT, wide),
            buf(OWN_SLOTS, 2, 2, CUT, wide),
            buf(SUM_SLOTS, 2, 2, CUT, wide),
            buf(total, CUT, wide),
            buf(FFN_SLOTS, FCUT, wide),
            buf(LAND_SLOTS, 2, CUT, wide),
            buf(LAND_SLOTS, CUT, wide),
            buf(LAND_SLOTS, FCUT, wide),
            buf(LAND_SLOTS, FCUT, wide),
        ]
        sems = [
            dma((MATE_SLOTS,)),
            dma((MATE_SLOTS,)),
            dma((OWN_SLOTS,)),
            dma((SUM_SLOTS,)),
            dma((total,)),
            dma((LAND_SLOTS,)),
            dma((SUM_SLOTS,)),
            dma((total,)),
            dma((LAND_SLOTS,)),
            dma((FFN_SLOTS,)),
            dma((2, chain_total)),
            dma((2, chain_total)),
            dma((LAND_SLOTS,)),
            dma((LAND_SLOTS,)),
            dma((chain_total,)),
            dma((near,)),
            pltpu.SemaphoreType.REGULAR,
        ]
        return outs, lands, bufs, sems


class NoSums:
    def start(self):
        pass

    def begin(self):
        pass

    def z_step(self, j):
        pass

    def xy_step(self, i):
        pass

    def finish(self, z_next, xy_next):
        pass


def add(*terms):
    total = terms[0].astype(jnp.float32)
    for term in terms[1:]:
        total = total + term.astype(jnp.float32)
    return total.astype(jnp.bfloat16)


STEP_CHIP = (0, 0, 1, 2, 1, 2, 3, 3)
STEP_HALF = (0, 1, 0, 1, 1, 0, 0, 1)
FFN_TILE = 512
TILE = 256


def ffn_kernel(
    act_in,
    cot_in,
    gate_in,
    up_in,
    down_in,
    out_part,
    dn_ref,
    grad_gate,
    grad_up,
    grad_down,
    act,
    cot,
    w_gate,
    w_up,
    w_down,
    hidden,
    d_gate,
    d_up,
    pair,
    mine,
    stage,
    out_buf,
    passed,
    final,
    tile_buf,
    weight_sem,
    cot_sem,
    own_sem,
    act_send,
    act_recv,
    pair_send,
    pair_recv,
    flow_send,
    flow_recv,
    tile_sem,
    end_sem,
    part_sem,
):
    me = lax.axis_index("grp")
    plane = lax.axis_index("rep")
    mate_dev, x_dev, y_dev = (me ^ 1, plane), (me ^ 2, plane), (me ^ 4, plane)
    half = act.shape[2]
    seq_len = 2 * half
    rows, wide = w_gate.shape
    low = jnp.bfloat16
    meet([mate_dev, x_dev, y_dev])

    def remote(src, dst, send, recv, device):
        return pltpu.make_async_remote_copy(
            src_ref=src,
            dst_ref=dst,
            send_sem=send,
            recv_sem=recv,
            device_id=device,
            device_id_type=MESH,
        )

    own = [act_in.at[pl.ds(h * half, half)] for h in range(2)]

    def act_copy(t, other):
        if other:
            src, device = (own[t] if t < 2 else act.at[t, 0]), mate_dev
        else:
            src, device = {
                2: (own[0], x_dev),
                3: (own[1], y_dev),
                4: (own[1], x_dev),
                5: (own[0], y_dev),
                6: (act.at[2, 0], y_dev),
                7: (act.at[3, 0], x_dev),
            }[t]
        return remote(
            src, act.at[t, other], act_send.at[t, other], act_recv.at[t, other], device
        )

    for t in (2, 3, 4, 5):
        act_copy(t, 0).start()
    for t in (0, 1):
        act_copy(t, 1).start()
    own_copies = [pltpu.make_async_copy(own[t], act.at[t, 0], own_sem.at[t]) for t in range(2)]
    for copy in own_copies:
        copy.start()
    weights = [
        pltpu.make_async_copy(src, dst, weight_sem.at[k])
        for k, (src, dst) in enumerate(((gate_in, w_gate), (up_in, w_up), (down_in, w_down)))
    ]
    for copy in weights:
        copy.start()
    cot_copies = []
    for t in range(8):
        for other in range(2):
            owner = me ^ (2 * STEP_CHIP[t] + other)
            row = pl.multiple_of(owner * seq_len + STEP_HALF[t] * half, 16)
            copy = pltpu.make_async_copy(
                cot_in.at[pl.ds(row, half)], cot.at[t, other], cot_sem.at[t, other]
            )
            copy.start()
            cot_copies.append(copy)

    def pair_copy(t):
        return remote(stage, pair.at[t], pair_send, pair_recv.at[t], mate_dev)

    def flow(lane):
        src, dst, device = (
            (pair.at[2], final.at[0], x_dev),
            (pair.at[4], final.at[1], x_dev),
            (pair.at[5], final.at[2], y_dev),
            (pair.at[3], final.at[3], y_dev),
            (pair.at[6], passed.at[0], x_dev),
            (pair.at[7], passed.at[1], y_dev),
        )[lane]
        return remote(src, dst, flow_send.at[lane], flow_recv.at[lane], device)

    def part_copy(t, other):
        owner = me ^ (2 * STEP_CHIP[t] + other)
        place = out_part.at[owner // 4, lax.rem(owner // 2, 2), lax.rem(owner, 2)]
        return pltpu.make_async_copy(
            out_buf.at[t % 2, pl.ds(other * half, half)],
            place.at[pl.ds(STEP_HALF[t] * half, half)],
            part_sem.at[t % 2, other],
        )

    def forward_part(t):
        tokens = act[t].reshape(seq_len, wide)
        gate = dot_nt(tokens, w_gate[...])
        up = dot_nt(tokens, w_up[...])
        d_hidden = dot_nt(cot[t].reshape(seq_len, wide), w_down[...])
        sigmoid = 1.0 / (1.0 + jnp.exp(-gate))
        silu = gate * sigmoid
        hidden[t] = (silu * up).astype(low)
        d_gate[t] = (d_hidden * up * (sigmoid * (1.0 + gate * (1.0 - sigmoid)))).astype(low)
        d_up[t] = (d_hidden * silu).astype(low)

    def backward_part(t):
        out_buf[lax.rem(t, 2)] = dot(hidden[t], w_down[...]).astype(low)
        dn = dot(d_gate[t], w_gate[...]) + dot(d_up[t], w_up[...])
        mine[...] = dn[:half].astype(low)
        stage[...] = dn[half:].astype(low)

    def join(t, events):
        pair_copy(t).wait()
        pair[t] = add(pair[t], mine[...])
        for when, lane in events:
            if when is None:
                flow(lane).start()
            else:

                @pl.when(t == when)
                def _(lane=lane):
                    flow(lane).start()

    for copy in own_copies + weights:
        copy.wait()

    def step(t, carry):
        for at in (2, 4, 6):

            @pl.when(t == at)
            def _(at=at):
                for u in (at, at + 1):
                    act_copy(u, 0).wait_recv()
                    if at == 2:
                        act_copy(u + 4, 0).start()
                    act_copy(u, 1).start()

        remote(
            act.at[t, 0], act.at[t, 1], act_send.at[t, 1], act_recv.at[t, 1], mate_dev
        ).wait_recv()
        for other in range(2):
            pltpu.make_async_copy(
                cot_in.at[pl.ds(0, half)], cot.at[t, other], cot_sem.at[t, other]
            ).wait()
        forward_part(t)

        @pl.when(t > 0)
        def _():
            join(t - 1, ((2, 0), (3, 3), (6, 4)))

        @pl.when(t >= 2)
        def _():
            for other in range(2):
                pltpu.make_async_copy(
                    out_buf.at[lax.rem(t, 2), pl.ds(other * half, half)],
                    out_part.at[0, 0, 0, pl.ds(0, half)],
                    part_sem.at[lax.rem(t, 2), other],
                ).wait()

        backward_part(t)
        pair_copy(t).start()
        for u in range(8):

            @pl.when(t == u)
            def _(u=u):
                for other in range(2):
                    part_copy(u, other).start()

        return carry

    lax.fori_loop(0, 8, step, 0)
    join(7, ((None, 5),))

    def write(target, slot, cut):
        return pltpu.make_async_copy(
            tile_buf.at[slot], target.at[:, cut], tile_sem.at[slot]
        )

    def pass_on():
        for lane, t, onward in ((4, 5, 2), (5, 4, 1)):
            flow(lane).wait_recv()
            pair[t] = add(pair[t], passed[lane - 4])
            flow(onward).start()

    tiles = wide // FFN_TILE
    for k, (left, right, target) in enumerate(
        ((d_gate, act, grad_gate), (d_up, act, grad_up), (hidden, cot, grad_down))
    ):

        def tile(n, carry, k=k, left=left, right=right, target=target):
            cut = pl.ds(pl.multiple_of(n * FFN_TILE, FFN_TILE), FFN_TILE)
            slot = lax.rem(n, 2)

            @pl.when(k * tiles + n >= 2)
            def _():
                write(target, slot, cut).wait()

            tile_buf[slot] = dot_tn(
                left[...].reshape(8 * seq_len, rows),
                right[:, :, :, cut].reshape(8 * seq_len, FFN_TILE),
            ).astype(low)
            write(target, slot, cut).start()
            return carry

        lax.fori_loop(0, tiles, tile, 0)
        if k == 1:
            pass_on()
    for slot in range(2):
        write(grad_down, slot, pl.ds(0, FFN_TILE)).wait()

    ends = []
    for h in range(2):
        flow(h).wait_recv()
        flow(2 + h).wait_recv()
        pair[h] = add(pair[h], final[h], final[2 + h])
        copy = pltpu.make_async_copy(pair.at[h], dn_ref.at[pl.ds(h * half, half)], end_sem.at[h])
        copy.start()
        ends.append(copy)
    for copy in ends:
        copy.wait()
    for t in (6, 7):
        for other in range(2):
            part_copy(t, other).wait()
    for lane in range(6):
        flow(lane).wait_send()
    for t in range(8):
        act_copy(t, 1).wait_send()
        if t >= 2:
            act_copy(t, 0).wait_send()


def ffn_all(act, cot, w_gate, w_up, w_down):
    seq_len, wide = act.shape
    rows = w_gate.shape[0]
    half = seq_len // 2
    low = jnp.bfloat16
    hbm = pl.BlockSpec(memory_space=pltpu.HBM)
    dma = pltpu.SemaphoreType.DMA
    return pl.pallas_call(
        ffn_kernel,
        out_shape=[
            jax.ShapeDtypeStruct((2, 2, 2, seq_len, wide), low),
            jax.ShapeDtypeStruct((seq_len, wide), low),
        ]
        + [jax.ShapeDtypeStruct((rows, wide), low)] * 3,
        in_specs=[hbm] * 5,
        out_specs=[hbm] * 5,
        scratch_shapes=[
            pltpu.VMEM((8, 2, half, wide), low),
            pltpu.VMEM((8, 2, half, wide), low),
            pltpu.VMEM((rows, wide), low),
            pltpu.VMEM((rows, wide), low),
            pltpu.VMEM((rows, wide), low),
            pltpu.VMEM((8, seq_len, rows), low),
            pltpu.VMEM((8, seq_len, rows), low),
            pltpu.VMEM((8, seq_len, rows), low),
            pltpu.VMEM((8, half, wide), low),
            pltpu.VMEM((half, wide), low),
            pltpu.VMEM((half, wide), low),
            pltpu.VMEM((2, seq_len, wide), low),
            pltpu.VMEM((2, half, wide), low),
            pltpu.VMEM((4, half, wide), low),
            pltpu.VMEM((2, rows, FFN_TILE), low),
            dma((3,)),
            dma((8, 2)),
            dma((2,)),
            dma((8, 2)),
            dma((8, 2)),
            dma,
            dma((8,)),
            dma((6,)),
            dma((6,)),
            dma((2,)),
            dma((2,)),
            dma((2, 2)),
        ],
        compiler_params=pltpu.CompilerParams(
            collective_id=2, has_side_effects=True, vmem_limit_bytes=VMEM_LIMIT
        ),
    )(act, cot, w_gate, w_up, w_down)


PAIR = 128
COND_ROWS = 256
NORM_ROWS = 128


def normalise(read, gain, shift, write, rows):
    def block(n, carry):
        cut = pl.ds(pl.multiple_of(n * NORM_ROWS, NORM_ROWS), NORM_ROWS)
        write[cut] = layer_norm(read[cut].astype(jnp.float32), gain[...], shift[...]).astype(
            write.dtype
        )
        return carry

    lax.fori_loop(0, rows // NORM_ROWS, block, 0)


def normalise_back(read, gain, d_read, straight, write, sums, row, rows):
    wide = read.shape[1]

    def block(n, carry):
        d_gain, d_shift = carry
        cut = pl.ds(pl.multiple_of(n * NORM_ROWS, NORM_ROWS), NORM_ROWS)
        tensor = read[cut].astype(jnp.float32)
        center = tensor - jnp.mean(tensor, axis=-1, keepdims=True)
        spread = jnp.mean(center * center, axis=-1, keepdims=True)
        inverse = lax.rsqrt(spread + epsilon)
        hat = center * inverse
        d_out = d_read[cut].astype(jnp.float32)
        scaled = d_out * gain[...]
        dv = inverse * (
            scaled
            - jnp.mean(scaled, axis=-1, keepdims=True)
            - hat * jnp.mean(scaled * hat, axis=-1, keepdims=True)
        )
        write[cut] = straight[cut].astype(jnp.float32) + dv
        d_gain = d_gain + jnp.sum((d_out * hat).reshape(NORM_ROWS // 8, 8, wide), axis=0)
        d_shift = d_shift + jnp.sum(d_out.reshape(NORM_ROWS // 8, 8, wide), axis=0)
        return d_gain, d_shift

    zero = jnp.zeros((8, wide), jnp.float32)
    d_gain, d_shift = lax.fori_loop(0, rows // NORM_ROWS, block, (zero, zero))
    sums[row : row + 1] = jnp.sum(d_gain, axis=0, keepdims=True)
    sums[row + 1 : row + 2] = jnp.sum(d_shift, axis=0, keepdims=True)


def turn(tensor, cosine, sine_left, sine_right):
    return (
        tensor * cosine
        + pltpu.roll(tensor, PAIR - HD // 4, 1) * sine_left
        + pltpu.roll(tensor, HD // 4, 1) * sine_right
    )


def tiles_of(count, body, size=768):
    def step(n, carry):
        body(pl.ds(pl.multiple_of(n * size, size), size))
        return carry

    lax.fori_loop(0, count // size, step, 0)


def pair_loop(body):
    def step(p, carry):
        body(p, pl.multiple_of(p * PAIR, PAIR))
        return carry

    lax.fori_loop(0, HEADS * HD // PAIR, step, 0)


def first_head(rows):
    return lax.broadcasted_iota(jnp.int32, (rows, PAIR), 1) < HD


def head_softmax(query, key, mine, keys):
    scores = dot_nt(jnp.where(mine, query, jnp.zeros_like(query)), key) * score_scale
    if keys < key.shape[0]:
        lanes = lax.broadcasted_iota(jnp.int32, scores.shape, 1)
        scores = jnp.where(lanes < keys, scores, -1e30)
    shifted = jnp.exp(scores - jnp.max(scores, axis=-1, keepdims=True))
    return (shifted * (1.0 / jnp.sum(shifted, axis=-1, keepdims=True))).astype(jnp.bfloat16)


def attend_pair(query, key, value, keys, keep):
    mask = first_head(query.shape[0])
    results = []
    for head in range(2):
        probability = head_softmax(query, key, mask if head == 0 else ~mask, keys)
        keep(head, probability)
        results.append(dot(probability, value))
    return jnp.where(mask, results[0], results[1]).astype(jnp.bfloat16)


def attend_pair_back(query, key, value, grad, probabilities):
    mask, key_mask = first_head(query.shape[0]), first_head(key.shape[0])
    d_queries, d_keys, d_values = [], [], []
    for head in range(2):
        probability = probabilities[head]
        mine = mask if head == 0 else ~mask
        d_prob = dot_nt(jnp.where(mine, grad, jnp.zeros_like(grad)), value)
        wide = probability.astype(jnp.float32)
        inner = jnp.sum(wide * d_prob, axis=-1, keepdims=True)
        d_scores = (wide * (d_prob - inner)).astype(jnp.bfloat16)
        d_queries.append(dot(d_scores, key))
        d_keys.append(dot_tn(d_scores, query))
        d_values.append(dot_tn(probability, grad))
    return (
        jnp.where(mask, d_queries[0], d_queries[1]) * score_scale,
        jnp.where(key_mask, d_keys[0], d_keys[1]) * score_scale,
        jnp.where(key_mask, d_values[0], d_values[1]),
    )


def attention_forward_kernel(
    pieces,
    x_in,
    cond_in,
    cosine,
    sine_left,
    sine_right,
    norms_in,
    qkv_in,
    out_in,
    kv2_in,
    query2_in,
    out2_in,
    norms_out,
    qkv_out,
    out_out,
    query2_out,
    out2_out,
    act_one_out,
    heads_out,
    prob_out,
    flat_one_out,
    section_one_out,
    act_two_out,
    query_two_out,
    kv_two_out,
    prob_two_out,
    flat_two_out,
    section_two_out,
    act_three_out,
    x,
    cond,
    norm_parts,
    w_qkv,
    w_out,
    w_kv2,
    w_query2,
    w_out2,
    act,
    heads,
    flat,
    section,
    query_two,
    kv_two,
    prob,
    prob_two,
    in_sem,
    out_sem,
    prob_sem,
    local_sem,
    *gather_sems,
):
    rows, wide = x.shape
    low = jnp.bfloat16
    sources = (norms_in, qkv_in, out_in, kv2_in, query2_in, out2_in)
    fulls = (norm_parts, w_qkv, w_out, w_kv2, w_query2, w_out2)
    if pieces is None:
        gather = Loads(sources, fulls, local_sem)
    else:
        gather = Gather(pieces, sources, fulls, *gather_sems, local_sem)
    gather.start()
    loads = []
    for k, (src, dst) in enumerate(((x_in, x), (cond_in, cond))):
        loads.append(pltpu.make_async_copy(src, dst, in_sem.at[k]))
        loads[-1].start()
    for k in range(len(sources)):
        gather.own_copy(k).start()
    stores = []

    def save(src, dst):
        stores.append(pltpu.make_async_copy(src, dst, out_sem.at[len(stores)]))
        stores[-1].start()
        return stores[-1]

    lead = GATHER_WINDOW + 2
    gather.run(0, 1 + lead)
    loads[0].wait()
    gather.need(0)
    norms_out[...] = jnp.sum(
        norm_parts[...].astype(jnp.float32).reshape(norm_parts.shape[0] // 16, 16, wide), axis=0
    )
    gains = [norms_out.at[pl.ds(k, 1)] for k in range(6)]
    normalise(x, gains[0], gains[1], act, rows)
    act_one_done = save(act, act_one_out)
    done = 13 + lead
    gather.run(1 + lead, done)
    gather.need(1)
    save(w_qkv, qkv_out)

    def project(cut, rotated):
        result = dot_nt(act[...], w_qkv[cut])
        for part in range(cut.size // PAIR):
            piece = result[:, part * PAIR : (part + 1) * PAIR]
            if rotated:
                piece = turn(piece, cosine[...], sine_left[...], sine_right[...])
            heads[:, pl.ds(pl.multiple_of(cut.start + part * PAIR, PAIR), PAIR)] = piece.astype(low)

    for part in range(3):
        tiles_of(
            wide,
            lambda cut, part=part: project(
                pl.ds(pl.multiple_of(cut.start + part * wide, PAIR), cut.size), part < 2
            ),
        )
        gather.step(done + part)
    done += 3
    save(heads, heads_out)

    def prob_copy(buf, out, p, slot):
        return pltpu.make_async_copy(buf.at[slot], out.at[p], prob_sem.at[slot])

    def self_pair(p, lane):
        slot = lax.rem(p, 2)

        @pl.when(p >= 2)
        def _():
            prob_copy(prob, prob_out, p, slot).wait()

        def keep(head, probability):
            prob[slot, head] = probability

        cols = [pl.ds(pl.multiple_of(lane + k * wide, PAIR), PAIR) for k in range(3)]
        flat[:, cols[0]] = attend_pair(
            heads[:, cols[0]], heads[:, cols[1]], heads[:, cols[2]], rows, keep
        )
        prob_copy(prob, prob_out, p, slot).start()
        serve(p, SELF_EVERY)

    def serve(p, every):
        if gather.steps:

            @pl.when(lax.rem(p, every) == every - 1)
            def _():
                gather.step(done + p // every)

    pairs = wide // PAIR
    pair_loop(self_pair)
    done += pairs // SELF_EVERY
    for slot in range(2):
        prob_copy(prob, prob_out, 0, slot).wait()
    flat_one_done = save(flat, flat_one_out)
    gather.run(done, 17 + lead)
    done = max(done, 17 + lead)
    gather.need(2)
    save(w_out, out_out)

    def first_section(cut):
        section[:, cut] = x[:, cut].astype(jnp.float32) + dot_nt(flat[...], w_out[cut])

    tiles_of(wide, first_section)
    section_one_done = save(section, section_one_out)
    gather.run(done, 21 + lead)
    gather.step(max(done, 21 + lead))
    done = max(done, 21 + lead) + 1
    act_one_done.wait()
    normalise(section, gains[2], gains[3], act, rows)
    act_two_done = save(act, act_two_out)
    loads[1].wait()
    gather.need(3)

    def condition(cut):
        kv_two[:, cut] = dot_nt(cond[...], w_kv2[cut]).astype(low)

    tiles_of(2 * wide, condition)
    save(kv_two, kv_two_out)
    gather.run(done, 25 + lead)
    done = max(done, 25 + lead)
    gather.need(4)
    save(w_query2, query2_out)

    def query(cut):
        query_two[:, cut] = dot_nt(act[...], w_query2[cut]).astype(low)

    tiles_of(wide, query)
    save(query_two, query_two_out)
    flat_one_done.wait()

    def cross_pair(p, lane):
        slot = lax.rem(p, 2)

        @pl.when(p >= 2)
        def _():
            prob_copy(prob_two, prob_two_out, p, slot).wait()

        def keep(head, probability):
            prob_two[slot, head] = probability

        cols = [pl.ds(pl.multiple_of(lane + k * wide, PAIR), PAIR) for k in range(2)]
        flat[:, cols[0]] = attend_pair(
            query_two[:, cols[0]], kv_two[:, cols[0]], kv_two[:, cols[1]], NC, keep
        )
        prob_copy(prob_two, prob_two_out, p, slot).start()
        serve(p, CROSS_EVERY)

    pair_loop(cross_pair)
    done += pairs // CROSS_EVERY
    gather.run(done, 29 + lead)
    for slot in range(2):
        prob_copy(prob_two, prob_two_out, 0, slot).wait()
    save(flat, flat_two_out)
    gather.need(5)
    save(w_out2, out2_out)
    section_one_done.wait()

    def second_section(cut):
        section[:, cut] = section[:, cut] + dot_nt(flat[...], w_out2[cut])

    tiles_of(wide, second_section)
    save(section, section_two_out)
    act_two_done.wait()
    normalise(section, gains[4], gains[5], act, rows)
    save(act, act_three_out)
    waited = [id(c) for c in (act_one_done, flat_one_done, section_one_done, act_two_done)]
    gather.finish()
    for copy in stores:
        if id(copy) not in waited:
            copy.wait()


SELF_EVERY = 2
CROSS_EVERY = 3


def attention_forward(x, cond, tables, norms, weights):
    rows, wide = x.shape
    low, full = jnp.bfloat16, jnp.float32
    pairs = wide // PAIR
    hbm = pl.BlockSpec(memory_space=pltpu.HBM)
    vmem = pl.BlockSpec(memory_space=pltpu.VMEM)
    dma = pltpu.SemaphoreType.DMA
    shape = jax.ShapeDtypeStruct
    groups = lax.axis_size("grp")
    parameters = [norms] + list(weights)
    whole = [(groups * w.shape[0], w.shape[1]) for w in parameters]
    sems = []
    pieces = None
    options = {}
    if groups == 8 and lax.axis_size("rep") % 2 == 0:
        piece_rows = (16, 48, 48, 96, 48, 48)
        pieces = tuple((w.shape[0] // n, n) for w, n in zip(parameters, piece_rows))
        total = sum(n for n, _ in pieces)
        sems = [dma((7, total)), dma((7, total))]
        options = dict(collective_id=0, has_side_effects=True)
    else:
        parameters = [lax.all_gather(w, "grp", axis=0, tiled=True) for w in parameters]
    results = pl.pallas_call(
        functools.partial(attention_forward_kernel, pieces),
        out_shape=[
            shape((16, wide), full),
            *[shape(whole[k], low) for k in (1, 2, 4, 5)],
            shape((rows, wide), low),
            shape((rows, 3 * wide), low),
            shape((pairs, 2, rows, rows), low),
            shape((rows, wide), low),
            shape((rows, wide), full),
            shape((rows, wide), low),
            shape((rows, wide), low),
            shape((COND_ROWS, 2 * wide), low),
            shape((pairs, 2, rows, COND_ROWS), low),
            shape((rows, wide), low),
            shape((rows, wide), full),
            shape((rows, wide), low),
        ],
        in_specs=[hbm, hbm] + [vmem] * 3 + [hbm] * 6,
        out_specs=[vmem] + [hbm] * 16,
        scratch_shapes=[
            pltpu.VMEM((rows, wide), low),
            pltpu.VMEM(cond.shape, low),
            *[pltpu.VMEM(s, low) for s in whole],
            pltpu.VMEM((rows, wide), low),
            pltpu.VMEM((rows, 3 * wide), low),
            pltpu.VMEM((rows, wide), low),
            pltpu.VMEM((rows, wide), full),
            pltpu.VMEM((rows, wide), low),
            pltpu.VMEM((COND_ROWS, 2 * wide), low),
            pltpu.VMEM((2, 2, rows, rows), low),
            pltpu.VMEM((2, 2, rows, COND_ROWS), low),
            dma((2,)),
            dma((14,)),
            dma((2,)),
            dma((6,)),
            *sems,
        ],
        compiler_params=pltpu.CompilerParams(vmem_limit_bytes=VMEM_LIMIT, **options),
    )(x, cond, *tables, *parameters)
    return results[0], results[1:5], results[5:]


GRAD_TILE = 2 * UNIT


def attention_backward_kernel(plan, *refs):
    refs = list(refs)

    def take(n):
        taken = refs[:n]
        del refs[:n]
        return taken

    x_in, cond_in, norms, cosine, sine_left, sine_right = take(6)
    qkv_in, out_in, query2_in, out2_in = take(4)
    act_one_in, heads_in, prob_in, flat_one_in, section_one_in, act_two_in = take(6)
    query_two_in, kv_two_in, prob_two_in, flat_two_in, section_two_in = take(5)
    d_norm_in, d_out_in = take(2)
    out_part, *ffn_in = take(4) if plan else [None]
    d_inputs_out, sums = take(2)
    grad_out2, grad_query2, grad_kv2, grad_out, grad_qkv = take(5)
    if plan:
        (grad_norm,) = take(1)
        sum_outs, lands = take(3), take(6)
    w_small, w_tile = take(2)
    x, cond, act_one, heads, flat_one, section_one, act_two = take(7)
    query_two, kv_two, flat_two, section_two, d_norm = take(5)
    d_low, d_heads, d_kv, d_att, prob, prob_two, grad_buf = take(7)
    in_sem, weight_sem, tile_sem, prob_sem, grad_sem, end_sem = take(6)
    if plan:
        norm_buf, norm_sem = take(2)
        bufs, sems = take(9), take(17)
        parts = (out_part, grad_out2, grad_query2, grad_kv2, grad_out, grad_qkv, grad_norm)
        work = Sums(plan[0], plan[1], parts, ffn_in, sum_outs, lands, bufs, sems)
    else:
        work = NoSums()
    rows, wide = x.shape
    pairs = wide // PAIR
    low = jnp.bfloat16
    work.start()
    work.begin()
    loads = {}
    for k, (name, src, dst) in enumerate(
        (
            ("section_two", section_two_in, section_two),
            ("d_norm", d_norm_in, d_norm),
            ("d_out", d_out_in, d_low),
            ("w_out2", out2_in, w_small),
            ("flat_two", flat_two_in, flat_two),
            ("query_two", query_two_in, query_two),
            ("kv_two", kv_two_in, kv_two),
            ("cond", cond_in, cond),
            ("act_two", act_two_in, act_two),
            ("section_one", section_one_in, section_one),
            ("flat_one", flat_one_in, flat_one),
            ("heads", heads_in, heads),
            ("act_one", act_one_in, act_one),
            ("x", x_in, x),
        )
    ):
        loads[name] = pltpu.make_async_copy(src, dst, in_sem.at[k])
        loads[name].start()

    def need(*names):
        for name in names:
            loads[name].wait()

    def next_weight(name, src, k):
        loads[name] = pltpu.make_async_copy(src, w_small, weight_sem.at[k])
        loads[name].start()

    gains = [norms.at[pl.ds(2 * k, 1)] for k in range(3)]

    def prob_copy(src, buf, p, slot):
        return pltpu.make_async_copy(src.at[p], buf.at[slot], prob_sem.at[slot])

    def prob_start(src, buf):
        for p in range(2):
            prob_copy(src, buf, p, p).start()

    at = {"z": 0, "xy": 0}

    def serve(*kinds):
        for kind in kinds:
            (work.z_step if kind == "z" else work.xy_step)(jnp.int32(at[kind]))
            at[kind] += 1

    def serve_pairs(p, kind, every):
        @pl.when(lax.rem(p, every) == every - 1)
        def _():
            (work.z_step if kind == "z" else work.xy_step)(at[kind] + p // every)

    def unit_copy(target, n, half, slot):
        src = grad_buf.at[slot, pl.ds(half * UNIT, UNIT)]
        unit = 2 * n + half
        if plan:
            per = target.shape[3] // UNIT
            block = unit // per
            row = pl.multiple_of(lax.rem(unit, per) * UNIT, 16)
            place = target.at[block // 4, lax.rem(block // 2, 2), lax.rem(block, 2), pl.ds(row, UNIT)]
        else:
            place = target.at[pl.ds(pl.multiple_of(unit * UNIT, 16), UNIT)]
        return pltpu.make_async_copy(src, place, grad_sem.at[slot, half])

    def grad_rows(target, count, compute, every=0):
        def step(n, carry):
            slot = lax.rem(n, 2)

            @pl.when(n >= 2)
            def _():
                for half in range(2):
                    unit_copy(target, n, half, slot).wait()

            compute(n, slot)
            for half in range(2):
                unit_copy(target, n, half, slot).start()
            if every:
                serve_pairs(n, "z", every)
            return carry

        lax.fori_loop(0, count, step, 0)
        for slot in range(2):
            for half in range(2):
                unit_copy(target, 0, half, slot).wait()

    def weight_rows(left, right, target, every=0):
        def compute(n, slot):
            columns = left[:, pl.ds(pl.multiple_of(n * GRAD_TILE, 128), GRAD_TILE)]
            for m in range(wide // 512):
                piece = slice(m * 512, (m + 1) * 512)
                grad_buf[slot, :, piece] = dot_tn(columns, right[:, piece]).astype(low)

        grad_rows(target, left.shape[1] // GRAD_TILE, compute, every)

    def round_rows():
        def block(n, carry):
            cut = pl.ds(pl.multiple_of(n * NORM_ROWS, NORM_ROWS), NORM_ROWS)
            d_low[cut] = d_section[cut].astype(low)
            return carry

        lax.fori_loop(0, rows // NORM_ROWS, block, 0)

    def through(target):
        def body(cut):
            target[:, cut] = dot(d_low[...], w_small[:, cut]).astype(low)

        tiles_of(wide, body)

    prob_start(prob_two_in, prob_two)
    serve("z", "xy")
    need("section_two", "d_norm", "d_out")
    normalise_back(section_two, gains[2], d_norm, d_low, section_two, sums, 4, rows)
    d_section = section_two
    round_rows()
    serve("z", "xy")
    need("w_out2")
    through(d_att)
    next_weight("w_query2", query2_in, 0)
    serve("z", "xy")
    need("flat_two")
    weight_rows(d_low, flat_two, grad_out2)
    serve("xy", "z")
    need("query_two", "kv_two")

    def cross_pair(p, lane):
        slot = lax.rem(p, 2)
        prob_copy(prob_two_in, prob_two, p, slot).wait()
        cols = [pl.ds(pl.multiple_of(lane + k * wide, PAIR), PAIR) for k in range(2)]
        d_query, d_key, d_value = attend_pair_back(
            query_two[:, cols[0]],
            kv_two[:, cols[0]],
            kv_two[:, cols[1]],
            d_att[:, cols[0]],
            [prob_two[slot, head] for head in range(2)],
        )
        d_low[:, cols[0]] = d_query.astype(low)
        d_kv[:, cols[0]] = d_key.astype(low)
        d_kv[:, cols[1]] = d_value.astype(low)

        @pl.when(p + 2 < pairs)
        def _():
            prob_copy(prob_two_in, prob_two, p + 2, slot).start()

        serve_pairs(p, "z", 1)
        serve_pairs(p, "xy", 3)

    pair_loop(cross_pair)
    at["z"] += 12
    at["xy"] += 4
    prob_start(prob_in, prob)
    need("w_query2")
    through(d_norm)
    next_weight("w_out", out_in, 1)
    serve("z", "xy")
    need("act_two")
    weight_rows(d_low, act_two, grad_query2)
    serve("z", "xy")
    need("cond")

    def cond_rows(n, slot):
        for half in range(2):
            columns = pl.ds(pl.multiple_of((2 * n + half) * GRAD_TILE, 128), GRAD_TILE)
            result = dot_tn(d_kv[:, columns], cond[...]).astype(low)
            at = slice(half * UNIT, (half + 1) * UNIT)
            grad_buf[slot, at, : wide // 2] = result[:UNIT]
            grad_buf[slot, at, wide // 2 :] = result[UNIT:]

    grad_rows(grad_kv2, wide // GRAD_TILE, cond_rows)
    serve("xy", "z")
    need("section_one")
    normalise_back(section_one, gains[1], d_norm, d_section, d_section, sums, 2, rows)
    serve("z", "xy")
    round_rows()
    need("w_out")
    through(d_att)

    def tile_copy(n, slot):
        cut = pl.ds(pl.multiple_of(n * TILE, TILE), TILE)
        return pltpu.make_async_copy(qkv_in.at[:, cut], w_tile.at[slot], tile_sem.at[slot])

    for n in range(2):
        tile_copy(n, n).start()
    serve("xy", "z")
    need("flat_one")
    weight_rows(d_low, flat_one, grad_out)
    serve("z", "xy")
    need("heads")

    def self_pair(p, lane):
        slot = lax.rem(p, 2)
        prob_copy(prob_in, prob, p, slot).wait()
        cols = [pl.ds(pl.multiple_of(lane + k * wide, PAIR), PAIR) for k in range(3)]
        d_query, d_key, d_value = attend_pair_back(
            heads[:, cols[0]],
            heads[:, cols[1]],
            heads[:, cols[2]],
            d_att[:, cols[0]],
            [prob[slot, head] for head in range(2)],
        )
        back = (cosine[...], -sine_left[...], -sine_right[...])
        d_heads[:, cols[0]] = turn(d_query, *back).astype(low)
        d_heads[:, cols[1]] = turn(d_key, *back).astype(low)
        d_heads[:, cols[2]] = d_value.astype(low)

        @pl.when(p + 2 < pairs)
        def _():
            prob_copy(prob_in, prob, p + 2, slot).start()

        work.z_step(at["z"] + p + (p + 1) // 2)

        @pl.when(lax.rem(p, 2) == 0)
        def _():
            work.z_step(at["z"] + p + 1 + p // 2)

        @pl.when(p < 10)
        def _():
            serve_pairs(p, "xy", 1)


    pair_loop(self_pair)
    at["z"] += pairs * 3 // 2
    at["xy"] += 10
    need("act_one")
    weight_rows(d_heads, act_one, grad_qkv, 4)
    at["z"] += 3
    serve("z", "xy")

    def first_norm(n, carry):
        slot = lax.rem(n, 2)
        cut = pl.ds(pl.multiple_of(n * TILE, TILE), TILE)
        tile_copy(n, slot).wait()
        d_norm[:, cut] = dot(d_heads[...], w_tile[slot]).astype(low)
        serve_pairs(n, "z", 3)

        @pl.when(n + 2 < wide // TILE)
        def _():
            tile_copy(n + 2, slot).start()

        return carry

    lax.fori_loop(0, wide // TILE, first_norm, 0)
    at["z"] += 2
    serve("z", "xy")
    need("x")
    normalise_back(x, gains[0], d_norm, d_section, d_section, sums, 0, rows)
    end = pltpu.make_async_copy(d_section, d_inputs_out, end_sem)
    end.start()
    if plan:
        norm_buf[...] = jnp.zeros_like(norm_buf)
        norm_buf[:8] = sums[...].astype(low)
        copies = []
        for b in range(8):
            place = grad_norm.at[b // 4, b // 2 % 2, b % 2]
            copies.append(pltpu.make_async_copy(norm_buf, place, norm_sem.at[b]))
            copies[-1].start()
        for copy in copies:
            copy.wait()
    work.finish(at["z"], at["xy"])
    end.wait()


def attention_backward(x, cond, norms, tables, weights, kept, d_norm, d_out, out_part, ffn):
    rows, wide = x.shape
    low, full = jnp.bfloat16, jnp.float32
    hbm = pl.BlockSpec(memory_space=pltpu.HBM)
    vmem = pl.BlockSpec(memory_space=pltpu.VMEM)
    dma = pltpu.SemaphoreType.DMA
    shape = jax.ShapeDtypeStruct
    buf = lambda s, t=low: pltpu.VMEM(s, t)
    heights = (wide, wide, wide, wide, 3 * wide)
    more_outs, more_scratch = [], []
    plan = None
    options = {}
    if ffn:
        grads = [(2, 2, 2, h // 8, wide) for h in heights] + [(2, 2, 2, CUT, wide)]
        plan = (
            tuple(g[3] // CUT for g in [out_part.shape] + grads),
            tuple(f.shape[0] // FCUT for f in ffn),
        )
        outs, lands, bufs, sems = Sums.shapes(*plan, wide)
        more_outs = outs + lands
        more_scratch = [buf((CUT, wide)), dma((8,))] + bufs + sems
        options = dict(collective_id=1, has_side_effects=True)
    else:
        grads = [(h, wide) for h in heights]
    ffn = [out_part] + list(ffn) if ffn else []
    results = pl.pallas_call(
        functools.partial(attention_backward_kernel, plan),
        out_shape=[shape((rows, wide), full), shape((8, wide), full)]
        + [shape(g, low) for g in grads]
        + more_outs,
        in_specs=[hbm, hbm] + [vmem] * 4 + [hbm] * (17 + len(ffn)),
        out_specs=[hbm, vmem] + [hbm] * (len(grads) + len(more_outs)),
        scratch_shapes=[
            buf((wide, wide)),
            buf((2, 3 * wide, TILE)),
            buf((rows, wide)),
            buf(cond.shape),
            buf((rows, wide)),
            buf((rows, 3 * wide)),
            buf((rows, wide)),
            buf((rows, wide), full),
            buf((rows, wide)),
            buf((rows, wide)),
            buf((COND_ROWS, 2 * wide)),
            buf((rows, wide)),
            buf((rows, wide), full),
            buf((rows, wide)),
            buf((rows, wide)),
            buf((rows, 3 * wide)),
            buf((COND_ROWS, 2 * wide)),
            buf((rows, wide)),
            buf((2, 2, rows, rows)),
            buf((2, 2, rows, COND_ROWS)),
            buf((2, GRAD_TILE, wide)),
            dma((14,)),
            dma((2,)),
            dma((2,)),
            dma((2,)),
            dma((2, 2)),
            dma,
            *more_scratch,
        ],
        compiler_params=pltpu.CompilerParams(vmem_limit_bytes=VMEM_LIMIT, **options),
    )(x, cond, norms, *tables, *weights, *kept, d_norm, d_out, *ffn)
    return results[0], results[1], results[2:7], results[8:11]


END_SLOTS = 6


def end_kernel(near, far, ffn, section, d_in, *refs):
    d_out, *outs = refs[:10]
    low_buf, full_buf, in_sem, out_sem = refs[10:]
    outputs, out2, query2, kv2, out, qkv, gate, up, down = outs
    wide = low_buf.shape[2]
    jobs = []
    base = 0
    for target in (out2, query2, kv2, out, qkv):
        rows = target.shape[0] * target.shape[1] // wide
        jobs += [(far, base + r, target, r) for r in range(0, rows, UNIT)]
        base += rows
    base = 0
    for target in (gate, up, down):
        jobs += [(ffn, base + r, target, r) for r in range(0, target.shape[0], UNIT)]
        base += target.shape[0]
    jobs += [(near, r, outputs, r) for r in range(0, outputs.shape[0], UNIT)]
    jobs += [(d_in, r, d_out, r) for r in range(0, d_out.shape[0], UNIT)]

    def loads(n):
        source, row, target, place = jobs[n]
        slot = n % END_SLOTS
        buf = full_buf if source is d_in else low_buf
        copies = [
            pltpu.make_async_copy(source.at[pl.ds(row, UNIT)], buf.at[slot], in_sem.at[slot, 0])
        ]
        if target is outputs:
            copies.append(
                pltpu.make_async_copy(
                    section.at[pl.ds(place, UNIT)], full_buf.at[slot], in_sem.at[slot, 1]
                )
            )
        return copies

    def stores(n):
        _, _, target, place = jobs[n]
        slot = n % END_SLOTS
        if target is outputs:
            pairs = [(low_buf.at[slot], target.at[pl.ds(place, UNIT)])]
        elif target is kv2:
            pairs = [
                (
                    full_buf.at[slot, :, pl.ds(h * (wide // 2), wide // 2)],
                    target.at[pl.ds(2 * place + h * UNIT, UNIT)],
                )
                for h in range(2)
            ]
        else:
            pairs = [(full_buf.at[slot], target.at[pl.ds(place, UNIT)])]
        return [
            pltpu.make_async_copy(src, dst, out_sem.at[slot, k])
            for k, (src, dst) in enumerate(pairs)
        ]

    ahead = END_SLOTS - 2
    for n in range(ahead):
        for copy in loads(n):
            copy.start()
    for n in range(len(jobs)):
        if n + ahead < len(jobs):
            if n + ahead >= END_SLOTS:
                for copy in stores(n + ahead - END_SLOTS):
                    copy.wait()
            for copy in loads(n + ahead):
                copy.start()
        for copy in loads(n):
            copy.wait()
        slot = n % END_SLOTS
        is_output = jobs[n][2] is outputs

        def block(m, carry, slot=slot, is_output=is_output):
            cut = pl.ds(pl.multiple_of(m * 32, 32), 32)
            value = low_buf[slot, cut].astype(jnp.float32)
            if is_output:
                low_buf[slot, cut] = (full_buf[slot, cut] + value).astype(low_buf.dtype)
            else:
                full_buf[slot, cut] = value
            return carry

        if jobs[n][0] is not d_in:
            lax.fori_loop(0, UNIT // 32, block, 0)
        for copy in stores(n):
            copy.start()
    for n in range(max(len(jobs) - END_SLOTS, 0), len(jobs)):
        for copy in stores(n):
            copy.wait()


def end_all(near, far, ffn, section, d_in, out_shapes):
    hbm = pl.BlockSpec(memory_space=pltpu.HBM)
    wide = near.shape[1]
    dma = pltpu.SemaphoreType.DMA
    return pl.pallas_call(
        end_kernel,
        out_shape=[
            jax.ShapeDtypeStruct(d_in.shape, d_in.dtype),
            jax.ShapeDtypeStruct(near.shape, near.dtype),
        ]
        + [jax.ShapeDtypeStruct(s, jnp.float32) for s in out_shapes],
        in_specs=[hbm] * 5,
        out_specs=[hbm] * 10,
        scratch_shapes=[
            pltpu.VMEM((END_SLOTS, UNIT, wide), near.dtype),
            pltpu.VMEM((END_SLOTS, UNIT, wide), jnp.float32),
            dma((END_SLOTS, 2)),
            dma((END_SLOTS, 2)),
        ],
        compiler_params=pltpu.CompilerParams(vmem_limit_bytes=VMEM_LIMIT),
    )(near, far, ffn, section, d_in)


def per_device(
    inputs,
    conditioning,
    positions,
    slot_valid,
    cotangent,
    norm1_gain,
    norm1_shift,
    norm2_gain,
    norm2_shift,
    norm3_gain,
    norm3_shift,
    w_qkv,
    w_out,
    w_query2,
    w_kv2,
    w_out2,
    w_gate,
    w_up,
    w_down,
):
    cond_rows = conditioning[0]
    norms = jnp.stack(
        [norm1_gain, norm1_shift, norm2_gain, norm2_shift, norm3_gain, norm3_shift], axis=0
    )
    own_width = norms.shape[1]
    norms = lax.dynamic_update_slice(
        jnp.zeros((16, D), norms.dtype), norms, (0, lax.axis_index("grp") * own_width)
    )
    grad_mlp = (cotangent[0].astype(jnp.float32) * slot_valid[0].astype(jnp.float32)).astype(
        jnp.bfloat16
    )
    grad_mlp = lax.optimization_barrier(grad_mlp)
    all_grad = lax.all_gather(grad_mlp, "grp", axis=0, tiled=True)
    tables = turn_tables(positions[0])
    padded_cond = jnp.pad(cond_rows, ((0, COND_ROWS - NC), (0, 0)))
    norms, whole, kept = attention_forward(
        inputs[0], padded_cond, tables, norms, [w_qkv, w_out, w_kv2, w_query2, w_out2]
    )
    act_three, section_two = kept[-1], kept[-2]
    if lax.axis_size("grp") == 8:
        mlp_out, d_norm3, grad_gate, grad_up, grad_down = ffn_all(
            act_three, all_grad, w_gate, w_up, w_down
        )
    else:
        all_act = lax.all_gather(act_three, "grp", axis=0, tiled=True)
        gate_pre = dot_nt(all_act, w_gate)
        up_pre = dot_nt(all_act, w_up)
        hidden = swiglu(gate_pre, up_pre).astype(jnp.bfloat16)
        mlp_part = dot(hidden, w_down).astype(jnp.bfloat16)
        mlp_out = lax.psum_scatter(mlp_part, "grp", scatter_dimension=0, tiled=True)
        d_hidden = dot_nt(all_grad, w_down)
        d_gate_full, d_up_full = swiglu_back(gate_pre, up_pre, d_hidden)
        d_gate = d_gate_full.astype(jnp.bfloat16)
        d_up = d_up_full.astype(jnp.bfloat16)
        d_norm3_part = (dot(d_gate, w_gate) + dot(d_up, w_up)).astype(jnp.bfloat16)
        d_norm3 = lax.psum_scatter(d_norm3_part, "grp", scatter_dimension=0, tiled=True)
        grad_gate = dot_tn(d_gate, all_act).astype(jnp.bfloat16)
        grad_up = dot_tn(d_up, all_act).astype(jnp.bfloat16)
        grad_down = dot_tn(hidden, all_grad).astype(jnp.bfloat16)
    groups = lax.axis_size("grp")
    fused = groups == 8 and lax.axis_size("rep") == 4
    ffn_grads = [grad_gate, grad_up, grad_down]
    if groups == 8 and not fused:
        mlp_out = lax.psum_scatter(
            mlp_out.reshape(-1, D), "grp", scatter_dimension=0, tiled=True
        )
    d_tokens, norm_sums, grads, totals = attention_backward(
        inputs[0],
        padded_cond,
        norms,
        tables,
        whole,
        kept[:-1],
        d_norm3,
        grad_mlp,
        mlp_out,
        ffn_grads if fused else [],
    )
    own_at = lax.axis_index("grp") * own_width
    if fused:
        mlp_out, total_a, total_f = totals
        norm_total = total_a[total_a.shape[0] - CUT :][:6]
        (
            d_tokens,
            outputs,
            grad_out_two,
            grad_query_two,
            grad_kv_two,
            grad_out_one,
            grad_qkv,
            *ffn_sums,
        ) = end_all(
            mlp_out,
            total_a,
            total_f,
            section_two,
            d_tokens,
            [w.shape for w in (w_out2, w_query2, w_kv2, w_out, w_qkv, w_gate, w_up, w_down)],
        )
    else:
        grads = list(grads)
        kv2_part = jnp.swapaxes(grads[2].reshape(-1, UNIT, 2, D // 2), 1, 2)
        grads[2] = kv2_part.reshape(2 * D, D // 2)
        norm_total = lax.psum(norm_sums[:6].astype(jnp.bfloat16), ("grp", "rep"))
        shards = [lax.psum_scatter(g, "grp", scatter_dimension=0, tiled=True) for g in grads]
        grad_out_two, grad_query_two, grad_kv_two, grad_out_one, grad_qkv = lax.psum(
            tuple(shards), "rep"
        )
        ffn_sums = lax.psum(tuple(ffn_grads), "rep")
        outputs = (section_two + mlp_out.astype(jnp.float32)).astype(jnp.bfloat16)
    norm_total = lax.dynamic_slice_in_dim(norm_total, own_at, own_width, axis=1)
    grad_qkv, grad_out_one, grad_query_two, grad_out_two, grad_kv_two = (
        g.astype(jnp.float32)
        for g in (grad_qkv, grad_out_one, grad_query_two, grad_out_two, grad_kv_two)
    )
    norm_total = norm_total.astype(jnp.float32)
    grad_gate, grad_up, grad_down = (g.astype(jnp.float32) for g in ffn_sums)
    return (
        outputs[None],
        d_tokens[None],
        norm_total[0],
        norm_total[1],
        norm_total[2],
        norm_total[3],
        norm_total[4],
        norm_total[5],
        grad_qkv,
        grad_out_one,
        grad_query_two,
        grad_kv_two,
        grad_out_two,
        grad_gate,
        grad_up,
        grad_down,
    )


def solution(mesh):
    return jax.shard_map(
        per_device,
        mesh=mesh,
        in_specs=(
            P(("grp", "rep"), None, None),
            P(("grp", "rep"), None, None),
            P(("grp", "rep"), None),
            P(("grp", "rep")),
            P(("grp", "rep"), None, None),
            P("grp"),
            P("grp"),
            P("grp"),
            P("grp"),
            P("grp"),
            P("grp"),
            P("grp", None),
            P("grp", None),
            P("grp", None),
            P("grp", None),
            P("grp", None),
            P("grp", None),
            P("grp", None),
            P("grp", None),
        ),
        out_specs=(
            P(("grp", "rep"), None, None),
            P(("grp", "rep"), None, None),
            P("grp"),
            P("grp"),
            P("grp"),
            P("grp"),
            P("grp"),
            P("grp"),
            P("grp", None),
            P("grp", None),
            P("grp", None),
            P("grp", None),
            P("grp", None),
            P("grp", None),
            P("grp", None),
            P("grp", None),
        ),
        check_vma=False,
    )
```
